32 devices in a mesh: dp: 8 (over z, x), head: 4 (over y, core).
Axes of the slice: x: 2, y: 2, z: 4, core: 2. Of those that a mesh axis runs over, the one named last changes fastest.
Arguments:
- tokens: bfloat16 [16384, 1024], P(('dp', 'head')), may hold values from -6 to 6
- lengths: int32 [8, 8], P('dp'), may hold values from 1 to 1536, as said below
- attn_gain: float32 [1024], replicated, may hold values from 0.5 to 1.5
- w_query: bfloat16 [1024, 1024], P('dp', 'head'), may hold values from -0.1875 to 0.1875
- w_key: bfloat16 [1024, 1024], P('dp', 'head'), may hold values from -0.1875 to 0.1875
- w_value: bfloat16 [1024, 1024], P('dp', 'head'), may hold values from -0.1875 to 0.1875
- w_beta: bfloat16 [1024, 8], P('dp', 'head'), may hold values from -0.1875 to 0.1875
- w_gate_out: bfloat16 [1024, 1024], P('dp', 'head'), may hold values from -0.1875 to 0.1875
- conv_weight: bfloat16 [3, 4, 1024], P(None, None, 'head'), may hold values from -3 to 3
- head_gain: float32 [128], replicated, may hold values from 0.5 to 1.5
- w_out: bfloat16 [1024, 1024], P('head', 'dp'), may hold values from -0.1875 to 0.1875
- mlp_gain: float32 [1024], replicated, may hold values from 0.5 to 1.5
- w_mlp_gate: bfloat16 [1024, 2816], P('dp', 'head'), may hold values from -0.1875 to 0.1875
- w_mlp_up: bfloat16 [1024, 2816], P('dp', 'head'), may hold values from -0.1875 to 0.1875
- w_down: bfloat16 [2816, 1024], P('head', 'dp'), may hold values from -0.109375 to 0.109375
- cotangent: bfloat16 [16384, 1024], P(('dp', 'head')), may hold values from -6 to 6
Outputs:
- output: bfloat16 [16384, 1024], P(('dp', 'head'))
- input_grad: float32 [16384, 1024], P(('dp', 'head'))
- attn_gain_grad: float32 [1024], replicated
- w_query_grad: float32 [1024, 1024], P('dp', 'head')
- w_key_grad: float32 [1024, 1024], P('dp', 'head')
- w_value_grad: float32 [1024, 1024], P('dp', 'head')
- w_beta_grad: float32 [1024, 8], P('dp', 'head')
- w_gate_out_grad: float32 [1024, 1024], P('dp', 'head')
- conv_grad: float32 [3, 4, 1024], P(None, None, 'head')
- head_gain_grad: float32 [128], replicated
- w_out_grad: float32 [1024, 1024], P('head', 'dp')
- mlp_gain_grad: float32 [1024], replicated
- w_mlp_gate_grad: float32 [1024, 2816], P('dp', 'head')
- w_mlp_up_grad: float32 [1024, 2816], P('dp', 'head')
- w_down_grad: float32 [2816, 1024], P('head', 'dp')
The draws below stay inside these ranges and needn't reach their ends.
Inputs may be any that keep to these rules, and one draw needn't show every extreme that they name: Each row of lengths sums to 2048; its first entry is at most 256 and its second is 1536.
All inputs are finite; a program needn't handle non-finite values.
Results may differ from the reference program's by a relative error of at most 0.015.
Values may be sent and summed in bfloat16 or wider, within the bound.
A program may use at most 192 MiB of HBM per device.

```python
import jax
import jax.numpy as jnp
from jax import lax

D = 1024
HEADS = 8
HEAD_DIM = 128
FF = 2816
CONV = 4
GROUP = 64
ROW = 2048
DOCS = 8
HID = 1024
ROWS = 8
TOKENS = 16384


def draw_lengths(key, part):
    key = jax.random.fold_in(key, 11)
    first_key, piece_key = jax.random.split(key)
    leading = jax.random.randint(first_key, (ROWS, 1), 1, ROW // 8 + 1).astype(jnp.int32)
    spanning = jnp.full((ROWS, 1), 3 * ROW // 4, jnp.int32)
    pieces = jax.random.randint(piece_key, (ROWS, DOCS - 3), 1, ROW // (16 * DOCS) + 2).astype(jnp.int32)
    trailing = ROW - leading - spanning - jnp.sum(pieces, axis=1, keepdims=True).astype(jnp.int32)
    return jnp.concatenate([leading, spanning, pieces, trailing], axis=1).astype(jnp.int32)


def level_of(key, dims, cuts, least, top_value):
    def one(dim, blocks):
        draws = jax.random.uniform(jax.random.fold_in(jax.random.fold_in(key, 6), dim), (blocks,), jnp.float32, least / len(cuts), top_value / len(cuts))
        return jnp.repeat(jnp.exp(draws), dims[dim] // blocks).reshape((-1,) + (1,) * (len(dims) - dim - 1))

    loudness = one(*cuts[0])
    for cut in cuts[1:]:
        loudness = loudness * one(*cut)
    return loudness


def noise(rng, extent, spread, reach, cuts=(), kind=jnp.bfloat16):
    level = level_of(rng, extent, cuts, -0.22, 0.18) if cuts else 1.0
    result = jax.random.normal(rng, extent, jnp.float32) * spread * level
    return jnp.minimum(jnp.maximum(result, -reach), reach).astype(kind)


def setup_inputs(seed: int = 0) -> dict:
    splits = jax.random.split(jax.random.key(seed), 17)
    tokens = noise(splits[0], (TOKENS, D), 1.0, 6.0, ((0, 32),))
    lengths = draw_lengths(jax.random.fold_in(splits[16], 71), 0)
    attn_gain = jnp.clip(1.0 + 0.1 * jax.random.normal(splits[2], (D,), jnp.float32), 0.5, 1.5)
    w_query = noise(splits[3], (D, HID), D ** -0.5, 0.1875, ((0, 8), (1, 4)))
    w_key = noise(splits[4], (D, HID), D ** -0.5, 0.1875, ((0, 8), (1, 4)))
    w_value = noise(splits[5], (D, HID), D ** -0.5, 0.1875, ((0, 8), (1, 4)))
    w_beta = noise(splits[6], (D, HEADS), D ** -0.5, 0.1875, ((0, 8), (1, 4)))
    w_gate_out = noise(splits[7], (D, HID), D ** -0.5, 0.1875, ((0, 8), (1, 4)))
    conv_weight = noise(splits[8], (3, CONV, HID), CONV ** -0.5, 3.0, ((2, 4),))
    head_gain = jnp.clip(1.0 + 0.1 * jax.random.normal(splits[9], (HEAD_DIM,), jnp.float32), 0.5, 1.5)
    w_out = noise(splits[10], (HID, D), HID ** -0.5, 0.1875, ((0, 4), (1, 8)))
    mlp_gain = jnp.clip(1.0 + 0.1 * jax.random.normal(splits[11], (D,), jnp.float32), 0.5, 1.5)
    w_mlp_gate = noise(splits[12], (D, FF), D ** -0.5, 0.1875, ((0, 8), (1, 4)))
    w_mlp_up = noise(splits[13], (D, FF), D ** -0.5, 0.1875, ((0, 8), (1, 4)))
    w_down = noise(splits[14], (FF, D), FF ** -0.5, 0.109375, ((0, 4), (1, 8)))
    cotangent = noise(splits[15], (TOKENS, D), 1.0, 6.0, ((0, 32),))
    return dict(tokens=tokens, lengths=lengths, attn_gain=attn_gain, w_query=w_query, w_key=w_key, w_value=w_value, w_beta=w_beta, w_gate_out=w_gate_out, conv_weight=conv_weight, head_gain=head_gain, w_out=w_out, mlp_gain=mlp_gain, w_mlp_gate=w_mlp_gate, w_mlp_up=w_mlp_up, w_down=w_down, cotangent=cotangent)


HIGH_ACCURACY = lax.Precision.HIGHEST

@jax.custom_vjp
def low(v):
    return lax.optimization_barrier(v.astype(jnp.bfloat16)).astype(jnp.float32)

@jax.custom_vjp
def low_back(v):
    return v

def low_keep(v):
    return (low(v), None)

def low_pass(kept, grad):
    return (grad,)

def back_keep(v):
    return (v, None)

def back_low(kept, grad):
    return (low(grad),)
low.defvjp(low_keep, low_pass)
low_back.defvjp(back_keep, back_low)

def scaled_norm(values, norm_weight, epsilon):
    return values * lax.rsqrt(lax.optimization_barrier(jnp.mean(values * values, axis=-1, keepdims=True)) + epsilon) * norm_weight

def doc_ids(lengths):
    doc_ends = jnp.cumsum(lengths, axis=-1).astype(jnp.int32)
    position = jnp.arange(ROW, dtype=jnp.int32)
    return lax.optimization_barrier(jnp.sum((position[:, None] >= doc_ends[..., None, :]).astype(jnp.int32), axis=-1)).astype(jnp.int32)

def short_conv(linear, kernel, doc_index):
    conv_width = kernel.shape[0]
    summed = linear * kernel[conv_width - 1]
    for offset in range(1, conv_width):
        shifted = jnp.concatenate([jnp.zeros((offset, linear.shape[1]), linear.dtype), linear[:-offset]], axis=0)
        prior_doc = jnp.concatenate([jnp.full((offset,), -1, jnp.int32), doc_index[:-offset]], axis=0)
        same_doc = (prior_doc == doc_index).astype(linear.dtype)
        summed = summed + shifted * same_doc[:, None] * kernel[conv_width - 1 - offset]
    return summed

def group_step(carried_state, inputs):
    query_segment, key_segment, value_part, beta_part, doc_part, prior_doc = inputs
    position = jnp.arange(doc_part.shape[0], dtype=jnp.int32)
    same_doc = doc_part[:, None] == doc_part[None, :]
    strict_mask = jnp.logical_and(same_doc, position[:, None] > position[None, :])
    causal_mask = jnp.logical_and(same_doc, position[:, None] >= position[None, :])
    entering_state = (doc_part == prior_doc).astype(query_segment.dtype)
    leaving_state = (doc_part == doc_part[-1]).astype(query_segment.dtype)
    key_gram = jnp.einsum('hik,hjk->hij', key_segment, key_segment, precision=HIGH_ACCURACY)
    coupled = jnp.where(strict_mask, key_gram * beta_part[:, :, None], 0.0)
    targets = jnp.concatenate([key_segment, value_part], axis=2) * beta_part[:, :, None]
    solved = jax.scipy.linalg.solve_triangular(coupled, targets, lower=True, unit_diagonal=True)
    key_dim = key_segment.shape[2]
    key_rows_weighted = solved[:, :, :key_dim]
    value_rows_weighted = solved[:, :, key_dim:]
    corrected_rows = value_rows_weighted - entering_state[None, :, None] * jnp.einsum('nyl,nlm->nym', key_rows_weighted, carried_state, precision=HIGH_ACCURACY)
    scores = jnp.where(causal_mask, jnp.einsum('hik,hjk->hij', query_segment, key_segment, precision=HIGH_ACCURACY), 0.0)
    layer_output = entering_state[None, :, None] * jnp.einsum('nyl,nlm->nym', query_segment, carried_state, precision=HIGH_ACCURACY)
    layer_output = layer_output + jnp.einsum('hij,hjv->hiv', scores, corrected_rows, precision=HIGH_ACCURACY)
    updated_state = entering_state[-1] * carried_state + jnp.einsum('lxo,lxb->lob', key_segment * leaving_state[None, :, None], corrected_rows, precision=HIGH_ACCURACY)
    return (updated_state, layer_output)

def delta_row(queries, key_rows, value_rows, beta_rows, doc_index):
    head_count, length, key_dim = queries.shape
    block_count = length // GROUP

    def blocked(stacked):
        return jnp.swapaxes(stacked.reshape((head_count, block_count, GROUP) + stacked.shape[2:]), 0, 1)
    doc_blocks = doc_index.reshape(block_count, GROUP)
    prior_docs = jnp.concatenate([jnp.full((1,), -1, jnp.int32), doc_blocks[:-1, -1]], axis=0)
    initial = jnp.zeros((head_count, key_dim, value_rows.shape[2]), queries.dtype)
    final_state, outputs = lax.scan(jax.checkpoint(group_step), initial, (blocked(queries), blocked(key_rows), blocked(value_rows), blocked(beta_rows), doc_blocks, prior_docs))
    return jnp.swapaxes(outputs, 0, 1).reshape(head_count, length, value_rows.shape[2])

def mixer(query_pre, key_pre, value_pre, gate_pre, beta_pre, conv_kernel, head_gain, doc_index):
    head_count = beta_pre.shape[1]
    length = beta_pre.shape[0]

    def prepare(linear, channel, unit_norm):
        activated = jax.nn.silu(short_conv(linear, conv_kernel[channel], doc_index)).reshape(length, head_count, HEAD_DIM)
        if unit_norm:
            activated = activated * lax.rsqrt(lax.optimization_barrier(jnp.sum(activated * activated, axis=-1, keepdims=True)) + 1e-06)
        return jnp.swapaxes(activated, 0, 1)
    queries = prepare(query_pre, 0, True) * HEAD_DIM ** (-0.5)
    key_rows = prepare(key_pre, 1, True)
    value_rows = prepare(value_pre, 2, False)
    beta_rows = jnp.swapaxes(jax.nn.sigmoid(beta_pre), 0, 1)
    mixed = delta_row(queries, key_rows, value_rows, beta_rows, doc_index)
    normed = scaled_norm(jnp.swapaxes(mixed, 0, 1), head_gain, 1e-05).reshape(length, head_count * HEAD_DIM)
    return normed * jax.nn.silu(gate_pre)

def forward(tokens, attn_gain, w_query, w_key, w_value, w_beta, w_gate_out, conv_weight, head_gain, w_out, mlp_gain, w_mlp_gate, w_mlp_up, w_down, doc_index):
    normed = low_back(low(scaled_norm(tokens, attn_gain, 1e-06)))

    def project(weight):
        linear = low_back(jnp.dot(normed, weight, precision=HIGH_ACCURACY))
        return linear.reshape((ROWS, ROW) + linear.shape[1:])
    pieces = tuple((project(weight) for weight in (w_query, w_key, w_value, w_gate_out, w_beta)))

    def one_row(packed):
        return mixer(packed[0], packed[1], packed[2], packed[3], packed[4], conv_weight, head_gain, packed[5])
    mixed = lax.map(one_row, pieces + (doc_index,)).reshape(ROWS * ROW, HID)
    attention = low_back(jnp.dot(low_back(low(mixed)), w_out, precision=HIGH_ACCURACY))
    hidden = tokens + attention
    second = low_back(low(scaled_norm(hidden, mlp_gain, 1e-06)))
    gate_val = low_back(jnp.dot(second, w_mlp_gate, precision=HIGH_ACCURACY))
    up_val = low_back(jnp.dot(second, w_mlp_up, precision=HIGH_ACCURACY))
    middle = low_back(low(jax.nn.silu(gate_val) * up_val))
    return hidden + low_back(jnp.dot(middle, w_down, precision=HIGH_ACCURACY))

def reference(tokens, lengths, attn_gain, w_query, w_key, w_value, w_beta, w_gate_out, conv_weight, head_gain, w_out, mlp_gain, w_mlp_gate, w_mlp_up, w_down, cotangent):
    doc_index = doc_ids(lengths)

    def whole_layer(*floats):
        return forward(*floats, doc_index)
    floats = (tokens.astype(jnp.float32), attn_gain.astype(jnp.float32), w_query.astype(jnp.float32), w_key.astype(jnp.float32), w_value.astype(jnp.float32), w_beta.astype(jnp.float32), w_gate_out.astype(jnp.float32), conv_weight.astype(jnp.float32), head_gain.astype(jnp.float32), w_out.astype(jnp.float32), mlp_gain.astype(jnp.float32), w_mlp_gate.astype(jnp.float32), w_mlp_up.astype(jnp.float32), w_down.astype(jnp.float32))
    layer_output, pullback = jax.vjp(whole_layer, *floats)
    gradients = pullback(cotangent.astype(jnp.float32))
    return (layer_output.astype(jnp.bfloat16), gradients[0], gradients[1], gradients[2], gradients[3], gradients[4], gradients[5], gradients[6], gradients[7], gradients[8], gradients[9], gradients[10], gradients[11], gradients[12], gradients[13])
```

```python
from functools import partial

import jax
import jax.numpy as jnp
from jax import lax
from jax.experimental import pallas as pl
from jax.experimental.pallas import tpu as pltpu
from jax.sharding import PartitionSpec as P

HEAD_DIM = 128
CHUNK = 128
GROUP = 4
STEP = CHUNK * GROUP
PAD = 8
F32 = jnp.float32
BF16 = jnp.bfloat16
VMEM_LIMIT = 56 * 1024 * 1024
SOLVE_PASSES = 1


def dot(left, right, dims):
    return lax.dot_general(left, right, (dims, ((), ())), preferred_element_type=F32)


def mul(left, right):
    return dot(left.astype(BF16), right.astype(BF16), ((1,), (0,)))


def mul_t(left, right):
    return dot(left.astype(BF16), right.astype(BF16), ((1,), (1,)))


def t_mul(left, right):
    return dot(left.astype(BF16), right.astype(BF16), ((0,), (0,)))


def mul_split(left, right):
    lead_l = left.astype(BF16)
    rest_l = (left - lead_l.astype(F32)).astype(BF16)
    lead_r = right.astype(BF16)
    rest_r = (right - lead_r.astype(F32)).astype(BF16)
    dims = ((1,), (0,))
    return dot(lead_l, lead_r, dims) + (dot(rest_l, lead_r, dims) + dot(lead_l, rest_r, dims))


solve_mul = mul if SOLVE_PASSES == 1 else mul_split


def unit_inverses(lowers):
    row = lax.broadcasted_iota(jnp.int32, (CHUNK, CHUNK), 0)
    col = lax.broadcasted_iota(jnp.int32, (CHUNK, CHUNK), 1)
    eye = (row == col).astype(F32)
    level = lambda bit: jnp.logical_and(
        (row >> (bit + 1)) == (col >> (bit + 1)), (row >> bit) > (col >> bit)
    )
    first = level(0)
    solved = [eye - jnp.where(first, a, 0.0) for a in lowers]
    for bit in range(1, CHUNK.bit_length() - 1):
        mask = level(bit)
        right = [solve_mul(jnp.where(mask, a, 0.0), t) for a, t in zip(lowers, solved)]
        solved = [t - solve_mul(t, r) for t, r in zip(solved, right)]
    return solved


def conv_parts(pre, ext, conv, aux):
    summed = pre * conv[3:4, :]
    for offset in range(1, 4):
        shifted = ext[PAD - offset : PAD - offset + STEP, :]
        summed = summed + shifted * aux[:, offset - 1 : offset] * conv[3 - offset : 4 - offset, :]
    return summed


def unit_rows(act, scale):
    out = []
    for h in range(act.shape[1] // HEAD_DIM):
        part = act[:, h * HEAD_DIM : (h + 1) * HEAD_DIM]
        inv = lax.rsqrt(jnp.sum(part * part, axis=-1, keepdims=True) + 1e-6)
        out.append((part * inv * scale, inv))
    return out


def chunk_masks(aux, docrow):
    row = lax.broadcasted_iota(jnp.int32, (CHUNK, CHUNK), 0)
    col = lax.broadcasted_iota(jnp.int32, (CHUNK, CHUNK), 1)
    made = []
    for c in range(GROUP):
        same = aux[c * CHUNK : (c + 1) * CHUNK, 8:9] == docrow[c : c + 1, :]
        made.append((jnp.logical_and(same, row > col), jnp.logical_and(same, row >= col)))
    return made


def mixer_fwd_kernel(
    x_ref, w_ref, aux_ref, docrow_ref, conv_ref, gain_ref,
    pre_ref, mixed_ref, o_ref, t_ref, phi_ref, s_ref, p_ref, d_ref, ew_ref,
    ext, state,
):
    heads = mixed_ref.shape[1] // HEAD_DIM
    hid = heads * HEAD_DIM

    @pl.when(pl.program_id(0) == 0)
    def _():
        ext[0:PAD, :] = jnp.zeros((PAD, 3 * hid), F32)
        state[...] = jnp.zeros_like(state)

    pre_ref[...] = dot(x_ref[...], w_ref[...], ((1,), (0,)))
    aux = aux_ref[...]
    conv = conv_ref[...]
    pre = pre_ref[:, : 3 * hid]
    ext[PAD:, :] = pre
    act = conv_parts(pre, ext, conv, aux)
    act = act * jax.nn.sigmoid(act)
    ext[0:PAD, :] = ext[STEP:, :]
    q = unit_rows(act[:, :hid], HEAD_DIM**-0.5)
    k = unit_rows(act[:, hid : 2 * hid], 1.0)
    beta = jax.nn.sigmoid(pre_ref[:, 4 * hid : 4 * hid + 8])
    masks = chunk_masks(aux, docrow_ref[0])

    items = [(c, h) for c in range(GROUP) for h in range(heads)]
    rows = [slice(c * CHUNK, (c + 1) * CHUNK) for c in range(GROUP)]
    lowers, scores = [], []
    for c, h in items:
        key, query = k[h][0][rows[c]], q[h][0][rows[c]]
        both = mul_t(jnp.concatenate([key, query], axis=0), key)
        lowers.append(jnp.where(masks[c][0], both[:CHUNK] * beta[rows[c], h : h + 1], 0.0))
        scores.append(jnp.where(masks[c][1], both[CHUNK:], 0.0).astype(BF16))
    solved = unit_inverses(lowers)
    parts = []
    for (c, h), inverse, score in zip(items, solved, scores):
        key = k[h][0][rows[c]]
        value = act[rows[c], 2 * hid + h * HEAD_DIM : 2 * hid + (h + 1) * HEAD_DIM]
        b = beta[rows[c], h : h + 1]
        enter, leave = aux[rows[c], 3:4], aux[rows[c], 4:5]
        inverse = inverse.astype(BF16)
        wu = mul(inverse, jnp.concatenate([key * b, value * b], axis=1))
        ew, u = wu[:, :HEAD_DIM] * enter, wu[:, HEAD_DIM:]
        phi_b = t_mul(key * leave, jnp.concatenate([ew, u], axis=1))
        parts.append((ew, u, phi_b[:, :HEAD_DIM].astype(BF16), phi_b[:, HEAD_DIM:]))
        t_ref[c, h] = inverse
        p_ref[c, h] = score
        ew_ref[c, h] = ew.astype(BF16)
        phi_ref[c, h] = parts[-1][2]
    for h in range(heads):
        s = state[h]
        for c in range(GROUP):
            low = s.astype(BF16)
            s_ref[c, h] = low
            _, _, phi, b_term = parts[c * heads + h]
            keep = aux[(c + 1) * CHUNK - 1 : (c + 1) * CHUNK, 3:4]
            s = s * keep - mul(phi, low) + b_term
        state[h] = s
    gain = gain_ref[...]
    for (c, h), (ew, u, _, _), score in zip(items, parts, scores):
        enter = aux[rows[c], 3:4]
        from_state = mul(jnp.concatenate([ew, q[h][0][rows[c]] * enter], axis=0), s_ref[c, h])
        d = (u - from_state[:CHUNK]).astype(BF16)
        d_ref[c, h] = d
        o = from_state[CHUNK:] + mul(score, d)
        cols = slice(h * HEAD_DIM, (h + 1) * HEAD_DIM)
        o_ref[rows[c], cols] = o
        normed = o * lax.rsqrt(jnp.mean(o * o, axis=-1, keepdims=True) + 1e-5) * gain
        gate = pre_ref[rows[c], 3 * hid + h * HEAD_DIM : 3 * hid + (h + 1) * HEAD_DIM]
        mixed_ref[rows[c], cols] = (normed * (gate * jax.nn.sigmoid(gate))).astype(BF16)


def mixer_bwd_kernel(
    hg_ref, wout_ref, pre_ref, halo_ref, aux_ref, docrow_ref, conv_ref, gain_ref,
    o_ref, t_ref, phi_ref, s_ref, p_ref, d_ref, ew_ref,
    dpre_ref, dconv_ref, dgain_ref,
    ext, later, dstate,
):
    heads = o_ref.shape[1] // HEAD_DIM
    hid = heads * HEAD_DIM

    @pl.when(pl.program_id(0) == 0)
    def _():
        later[STEP:, :] = jnp.zeros((PAD, 3 * hid), F32)
        dstate[...] = jnp.zeros_like(dstate)
        dconv_ref[...] = jnp.zeros_like(dconv_ref)
        dgain_ref[...] = jnp.zeros_like(dgain_ref)

    mixed_grad = dot(hg_ref[...], wout_ref[...], ((1,), (0,))).astype(BF16).astype(F32)
    aux = aux_ref[...]
    conv = conv_ref[...]
    pre = pre_ref[:, : 3 * hid]
    ext[0:PAD, :] = halo_ref[:, : 3 * hid]
    ext[PAD:, :] = pre
    lin = conv_parts(pre, ext, conv, aux)
    sig = jax.nn.sigmoid(lin)
    act = lin * sig
    dsilu = sig * (1.0 + lin * (1.0 - sig))
    scale = HEAD_DIM**-0.5
    q = unit_rows(act[:, :hid], 1.0)
    k = unit_rows(act[:, hid : 2 * hid], 1.0)
    beta = jax.nn.sigmoid(pre_ref[:, 4 * hid : 4 * hid + 8])
    masks = chunk_masks(aux, docrow_ref[0])
    gain = gain_ref[...]

    items = [(c, h) for c in range(GROUP) for h in range(heads)]
    rows = [slice(c * CHUNK, (c + 1) * CHUNK) for c in range(GROUP)]
    cols = [slice(h * HEAD_DIM, (h + 1) * HEAD_DIM) for h in range(heads)]

    d_out, d_gain = [], jnp.zeros((1, HEAD_DIM), F32)
    for h in range(heads):
        o = o_ref[:, cols[h]]
        inv = lax.rsqrt(jnp.mean(o * o, axis=-1, keepdims=True) + 1e-5)
        unit = o * inv
        gate = pre_ref[:, 3 * hid + h * HEAD_DIM : 3 * hid + (h + 1) * HEAD_DIM]
        s = jax.nn.sigmoid(gate)
        dm = mixed_grad[:, cols[h]]
        dpre_ref[:, 3 * hid + h * HEAD_DIM : 3 * hid + (h + 1) * HEAD_DIM] = (
            dm * unit * gain * (s * (1.0 + gate * (1.0 - s)))
        ).astype(BF16)
        dn = dm * (gate * s)
        d_gain = d_gain + jnp.sum(dn * unit, axis=0, keepdims=True)
        du = dn * gain
        d_out.append(inv * (du - unit * jnp.mean(du * unit, axis=-1, keepdims=True)))
    dgain_ref[...] += d_gain

    first = []
    for c, h in items:
        enter = aux[rows[c], 3:4]
        do = d_out[h][rows[c]].astype(BF16)
        eq = (q[h][0][rows[c]] * (enter * scale)).astype(BF16)
        x = t_mul(p_ref[c, h], do)
        c_term = t_mul(
            jnp.concatenate([eq, -ew_ref[c, h]], axis=0),
            jnp.concatenate([do, x.astype(BF16)], axis=0),
        )
        first.append((do, x, c_term))
    after = {}
    for h in range(heads):
        ds = dstate[h]
        for c in reversed(range(GROUP)):
            low = ds.astype(BF16)
            after[c, h] = low
            keep = aux[(c + 1) * CHUNK - 1 : (c + 1) * CHUNK, 3:4]
            ds = ds * keep - t_mul(phi_ref[c, h], low) + first[c * heads + h][2]
        dstate[h] = ds
    db_cols = []
    grads = {}
    for (c, h), (do, x, _) in zip(items, first):
        enter, leave = aux[rows[c], 3:4], aux[rows[c], 4:5]
        b = beta[rows[c], h : h + 1]
        key, query = k[h][0][rows[c]], q[h][0][rows[c]] * scale
        value = act[rows[c], 2 * hid + h * HEAD_DIM : 2 * hid + (h + 1) * HEAD_DIM]
        ds = after[c, h]
        d, s = d_ref[c, h], s_ref[c, h]
        dr = t_mul(t_ref[c, h], x + mul(key * leave, ds))
        stacked = jnp.concatenate([do, dr.astype(BF16)], axis=0)
        with_d = mul_t(stacked, d)
        with_s = mul_t(stacked, s) * jnp.concatenate([enter, enter], axis=0)
        dp = jnp.where(masks[c][1], with_d[:CHUNK], 0.0)
        da = jnp.where(masks[c][0], -with_d[CHUNK:], 0.0)
        pair = jnp.concatenate([dp, da], axis=0).astype(BF16)
        with_k = mul(pair, key)
        dq = with_s[:CHUNK] + with_k[:CHUNK]
        row_k = with_k[CHUNK:] - with_s[CHUNK:]
        dk = b * row_k + t_mul(pair, jnp.concatenate([query, key * b], axis=0))
        dk = dk + mul_t(d, ds) * leave
        db = jnp.sum(dr * value + key * row_k, axis=-1, keepdims=True)
        grads[c, h] = (dq * scale, dk, dr * b, db * b * (1.0 - b))
    for h in range(heads):
        whole = [jnp.concatenate([grads[c, h][i] for c in range(GROUP)], axis=0) for i in range(4)]
        for i, unit in ((0, q[h]), (1, k[h])):
            y, inv = unit
            grad = inv * (whole[i] - y * jnp.sum(y * whole[i], axis=-1, keepdims=True))
            at = slice(i * hid + h * HEAD_DIM, i * hid + (h + 1) * HEAD_DIM)
            later[0:STEP, at] = grad * dsilu[:, at]
        at = slice(2 * hid + h * HEAD_DIM, 2 * hid + (h + 1) * HEAD_DIM)
        later[0:STEP, at] = whole[2] * dsilu[:, at]
        db_cols.append(whole[3])
    lane = lax.broadcasted_iota(jnp.int32, (STEP, HEAD_DIM), 1)
    tail = jnp.zeros((STEP, HEAD_DIM), F32)
    for h in range(heads):
        tail = jnp.where(lane == h, db_cols[h], tail)
    dpre_ref[:, 4 * hid :] = tail.astype(BF16)
    dlin = later[0:STEP, :]
    dpre = dlin * conv[3:4, :]
    taps = [jnp.sum(dlin * pre, axis=0, keepdims=True)]
    for offset in range(1, 4):
        ahead = later[offset : offset + STEP, :]
        dpre = dpre + ahead * aux[:, 4 + offset : 5 + offset] * conv[3 - offset : 4 - offset, :]
        behind = ext[PAD - offset : PAD - offset + STEP, :] * aux[:, offset - 1 : offset]
        taps.append(jnp.sum(dlin * behind, axis=0, keepdims=True))
    dpre_ref[:, : 3 * hid] = dpre.astype(BF16)
    for offset in range(4):
        dconv_ref[3 - offset : 4 - offset, :] += taps[offset]
    later[STEP:, :] = later[0:PAD, :]


def mixer_fwd(x_rows, weights, aux, docrow, conv, gain):
    length, width = x_rows.shape[0], weights.shape[1]
    hid = conv.shape[1] // 3
    heads, chunks = hid // HEAD_DIM, length // CHUNK
    rows = lambda n: pl.BlockSpec((STEP, n), lambda i: (i, 0))
    whole = lambda a: pl.BlockSpec(a.shape, lambda i: (0,) * a.ndim)
    square = pl.BlockSpec((GROUP, heads, CHUNK, HEAD_DIM), lambda i: (i, 0, 0, 0))
    squares = jax.ShapeDtypeStruct((chunks, heads, CHUNK, HEAD_DIM), BF16)
    return pl.pallas_call(
        mixer_fwd_kernel,
        grid=(length // STEP,),
        in_specs=[
            rows(x_rows.shape[1]), whole(weights), rows(aux.shape[1]),
            pl.BlockSpec((1, GROUP, CHUNK), lambda i: (i, 0, 0)), whole(conv), whole(gain),
        ],
        out_specs=[rows(width), rows(hid), rows(hid)] + [square] * 6,
        out_shape=[
            jax.ShapeDtypeStruct((length, width), F32),
            jax.ShapeDtypeStruct((length, hid), BF16),
            jax.ShapeDtypeStruct((length, hid), F32),
        ]
        + [squares] * 6,
        scratch_shapes=[
            pltpu.VMEM((PAD + STEP, 3 * hid), F32),
            pltpu.VMEM((heads, HEAD_DIM, HEAD_DIM), F32),
        ],
        compiler_params=pltpu.CompilerParams(vmem_limit_bytes=VMEM_LIMIT),
        name="mixer_fwd",
    )(x_rows, weights, aux, docrow, conv, gain)


def mixer_bwd(hg_rows, out_t, aux, docrow, conv, gain, saved):
    pre, o, t, phi, s, p, d, ew = saved
    length, width = pre.shape
    hid = conv.shape[1] // 3
    heads, steps = hid // HEAD_DIM, length // STEP
    last = steps - 1
    rows = lambda n: pl.BlockSpec((STEP, n), lambda i: (last - i, 0))
    whole = lambda a: pl.BlockSpec(a.shape, lambda i: (0,) * a.ndim)
    square = pl.BlockSpec((GROUP, heads, CHUNK, HEAD_DIM), lambda i: (last - i, 0, 0, 0))
    halo = pl.BlockSpec(
        (PAD, width), lambda i: (jnp.maximum((last - i) * (STEP // PAD) - 1, 0), 0)
    )
    return pl.pallas_call(
        mixer_bwd_kernel,
        grid=(steps,),
        in_specs=[
            rows(hg_rows.shape[1]), whole(out_t), rows(width), halo, rows(aux.shape[1]),
            pl.BlockSpec((1, GROUP, CHUNK), lambda i: (last - i, 0, 0)), whole(conv), whole(gain),
            rows(hid),
        ]
        + [square] * 6,
        out_specs=[
            rows(width),
            pl.BlockSpec((4, 3 * hid), lambda i: (0, 0)),
            pl.BlockSpec((1, HEAD_DIM), lambda i: (0, 0)),
        ],
        out_shape=[
            jax.ShapeDtypeStruct((length, width), BF16),
            jax.ShapeDtypeStruct((4, 3 * hid), F32),
            jax.ShapeDtypeStruct((1, HEAD_DIM), F32),
        ],
        scratch_shapes=[
            pltpu.VMEM((PAD + STEP, 3 * hid), F32),
            pltpu.VMEM((STEP + PAD, 3 * hid), F32),
            pltpu.VMEM((heads, HEAD_DIM, HEAD_DIM), F32),
        ],
        compiler_params=pltpu.CompilerParams(vmem_limit_bytes=VMEM_LIMIT),
        name="mixer_bwd",
    )(hg_rows, out_t, pre, pre, aux, docrow, conv, gain, o, t, phi, s, p, d, ew)


def doc_tables(lengths, length):
    count = lengths.shape[0]
    index = jnp.arange(count)
    ends = jnp.sum(jnp.where(index[None, :] <= index[:, None], lengths[None, :], 0), axis=1)
    position = jnp.arange(length, dtype=jnp.int32)
    doc = jnp.sum((position[:, None] >= ends[None, :]).astype(jnp.int32), axis=1)
    no_doc = lambda n: jnp.full((n,), -1, jnp.int32)
    before = [jnp.concatenate([no_doc(o), doc[:-o]]) == doc for o in (1, 2, 3)]
    after = [jnp.concatenate([doc[o:], no_doc(o)]) == doc for o in (1, 2, 3)]
    blocks = doc.reshape(-1, CHUNK)
    ending = blocks[:, -1:]
    prior = jnp.concatenate([no_doc(1)[:, None], ending[:-1]], axis=0)
    enter = (blocks == prior).reshape(-1)
    leave = (blocks == ending).reshape(-1)
    columns = before + [enter, leave] + after + [doc]
    aux = jnp.stack([c.astype(F32) for c in columns], axis=1)
    return aux, doc.astype(F32).reshape(-1, GROUP, CHUNK)


def low(values):
    return values.astype(BF16)


def inverse_rms(values):
    return lax.rsqrt(jnp.mean(values * values, axis=-1, keepdims=True) + 1e-6)


def norm_back(grad, values, inverse, gain):
    scaled = grad * gain
    mean = jnp.mean(scaled * values, axis=-1, keepdims=True)
    into = inverse * scaled - values * (inverse * inverse * inverse) * mean
    return into, jnp.sum(grad * values * inverse, axis=0)


def gather_rows(values):
    return lax.all_gather(values, "head", axis=0, tiled=True)


def scatter_rows(values):
    return lax.psum_scatter(low(values), "head", scatter_dimension=0, tiled=True).astype(F32)


def on_device(
    tokens,
    lengths,
    attn_gain,
    w_query,
    w_key,
    w_value,
    w_beta,
    w_gate_out,
    conv_weight,
    head_gain,
    w_out,
    mlp_gain,
    w_mlp_gate,
    w_mlp_up,
    w_down,
    cotangent,
):
    hid, heads, ff = w_query.shape[1], w_beta.shape[1], w_mlp_gate.shape[1]
    beta_wide = jnp.pad(w_beta, ((0, 0), (0, HEAD_DIM - heads)))
    mine = jnp.concatenate([w_query, w_key, w_value, w_gate_out, beta_wide, w_out.T], axis=1)
    first_set = lax.all_gather(mine, "dp", axis=0, tiled=True)
    mine = jnp.concatenate([w_mlp_gate, w_mlp_up, w_down.T], axis=1)
    second_set = lax.all_gather(mine, "dp", axis=0, tiled=True)
    mix_width = 4 * hid + HEAD_DIM
    w_mix, out_t = first_set[:, :mix_width], first_set[:, mix_width:]
    w_ff, down_t = second_set[:, : 2 * ff], second_set[:, 2 * ff :]

    x = tokens.astype(F32)
    x_inv = inverse_rms(x)
    normed_rows = gather_rows(low(x * x_inv * attn_gain))
    length = normed_rows.shape[0]
    aux, docrow = doc_tables(lengths[0], length)
    conv = jnp.swapaxes(conv_weight.astype(F32), 0, 1).reshape(conv_weight.shape[1], 3 * hid)
    gain = head_gain[None, :]
    pre, mixed, *saved = mixer_fwd(normed_rows, w_mix, aux, docrow, conv, gain)
    attention = scatter_rows(dot(mixed, out_t, ((1,), (1,))))
    hidden = x + attention
    h_inv = inverse_rms(hidden)
    second_rows = gather_rows(low(hidden * h_inv * mlp_gain))
    both = dot(second_rows, w_ff, ((1,), (0,)))
    gate, up = both[:, :ff], both[:, ff:]
    sig = jax.nn.sigmoid(gate)
    activated = gate * sig
    middle = low(activated * up)
    output = low(hidden + scatter_rows(dot(middle, down_t, ((1,), (1,)))))

    cot_rows = gather_rows(cotangent)
    middle_grad = low(dot(cot_rows, down_t, ((1,), (0,)))).astype(F32)
    up_grad = low(middle_grad * activated)
    gate_grad = low(middle_grad * up * sig * (1.0 + gate * (1.0 - sig)))
    ff_grad = jnp.concatenate([gate_grad, up_grad], axis=1)
    outer = lambda left, right: dot(left, right, ((0,), (0,)))
    second_grad = low(scatter_rows(dot(ff_grad, w_ff, ((1,), (1,))))).astype(F32)
    mlp_terms = jnp.concatenate(
        [low(outer(second_rows, ff_grad)), low(outer(cot_rows, middle))], axis=1
    )
    mlp_reduced = lax.psum_scatter(mlp_terms, "dp", scatter_dimension=0, tiled=True).astype(F32)
    from_mlp, mlp_gain_grad = norm_back(second_grad, hidden, h_inv, mlp_gain)
    hidden_grad = cotangent.astype(F32) + from_mlp
    hg_rows = gather_rows(low(hidden_grad))
    dpre, conv_part, head_gain_grad = mixer_bwd(
        hg_rows, out_t, aux, docrow, conv, gain, (pre, *saved)
    )
    normed_grad = low(scatter_rows(dot(dpre, w_mix, ((1,), (1,))))).astype(F32)
    mix_terms = jnp.concatenate(
        [low(outer(normed_rows, dpre)), low(outer(hg_rows, mixed))], axis=1
    )
    mix_reduced = lax.psum_scatter(mix_terms, "dp", scatter_dimension=0, tiled=True).astype(F32)
    from_mixer, attn_gain_grad = norm_back(normed_grad, x, x_inv, attn_gain)
    input_grad = hidden_grad + from_mixer

    taps = conv_part.shape[0]
    conv_local = jnp.swapaxes(conv_part.reshape(taps, 3, hid), 0, 1)
    start = lax.axis_index("head") * hid
    conv_full = jnp.zeros((3, taps, hid * lax.axis_size("head")), F32)
    conv_full = lax.dynamic_update_slice(conv_full, conv_local, (0, 0, start))
    summed = lax.psum((attn_gain_grad, mlp_gain_grad, head_gain_grad[0], conv_full), ("dp", "head"))
    conv_grad = lax.dynamic_slice_in_dim(summed[3], start, hid, 2)
    part = lambda i: mix_reduced[:, i * hid : (i + 1) * hid]
    return (
        output,
        input_grad,
        summed[0],
        part(0),
        part(1),
        part(2),
        mix_reduced[:, 4 * hid : 4 * hid + heads],
        part(3),
        conv_grad,
        summed[2],
        mix_reduced[:, mix_width:].T,
        summed[1],
        mlp_reduced[:, :ff],
        mlp_reduced[:, ff : 2 * ff],
        mlp_reduced[:, 2 * ff :].T,
    )


def solution(mesh):
    rows = P(("dp", "head"), None)
    in_specs = (
        rows,
        P("dp", None),
        P(),
        P("dp", "head"),
        P("dp", "head"),
        P("dp", "head"),
        P("dp", "head"),
        P("dp", "head"),
        P(None, None, "head"),
        P(),
        P("head", "dp"),
        P(),
        P("dp", "head"),
        P("dp", "head"),
        P("head", "dp"),
        rows,
    )
    out_specs = (
        rows,
        rows,
        P(),
        P("dp", "head"),
        P("dp", "head"),
        P("dp", "head"),
        P("dp", "head"),
        P("dp", "head"),
        P(None, None, "head"),
        P(),
        P("head", "dp"),
        P(),
        P("dp", "head"),
        P("dp", "head"),
        P("head", "dp"),
    )
    return jax.shard_map(
        on_device, mesh=mesh, in_specs=in_specs, out_specs=out_specs, check_vma=False
    )
```

```python
from functools import partial

import jax
import jax.numpy as jnp
from jax import lax
from jax.experimental import pallas as pl
from jax.experimental.pallas import tpu as pltpu
from jax.sharding import PartitionSpec as P

HEAD_DIM = 128
CHUNK = 128
GROUP = 4
STEP = CHUNK * GROUP
PAD = 8
F32 = jnp.float32
BF16 = jnp.bfloat16
VMEM_LIMIT = 56 * 1024 * 1024
SOLVE_PASSES = 1


def dot(left, right, dims):
    return lax.dot_general(left, right, (dims, ((), ())), preferred_element_type=F32)


def mul(left, right):
    return dot(left.astype(BF16), right.astype(BF16), ((1,), (0,)))


def mul_t(left, right):
    return dot(left.astype(BF16), right.astype(BF16), ((1,), (1,)))


def t_mul(left, right):
    return dot(left.astype(BF16), right.astype(BF16), ((0,), (0,)))


def mul_split(left, right):
    lead_l = left.astype(BF16)
    rest_l = (left - lead_l.astype(F32)).astype(BF16)
    lead_r = right.astype(BF16)
    rest_r = (right - lead_r.astype(F32)).astype(BF16)
    dims = ((1,), (0,))
    return dot(lead_l, lead_r, dims) + (dot(rest_l, lead_r, dims) + dot(lead_l, rest_r, dims))


solve_mul = mul if SOLVE_PASSES == 1 else mul_split


def unit_inverses(lowers):
    row = lax.broadcasted_iota(jnp.int32, (CHUNK, CHUNK), 0)
    col = lax.broadcasted_iota(jnp.int32, (CHUNK, CHUNK), 1)
    eye = (row == col).astype(F32)
    level = lambda bit: jnp.logical_and(
        (row >> (bit + 1)) == (col >> (bit + 1)), (row >> bit) > (col >> bit)
    )
    first = level(0)
    solved = [eye - jnp.where(first, a, 0.0) for a in lowers]
    for bit in range(1, CHUNK.bit_length() - 1):
        mask = level(bit)
        right = [solve_mul(jnp.where(mask, a, 0.0), t) for a, t in zip(lowers, solved)]
        solved = [t - solve_mul(t, r) for t, r in zip(solved, right)]
    return solved


def conv_parts(pre, ext, conv, aux):
    summed = pre * conv[3:4, :]
    for offset in range(1, 4):
        shifted = ext[PAD - offset : PAD - offset + STEP, :]
        summed = summed + shifted * aux[:, offset - 1 : offset] * conv[3 - offset : 4 - offset, :]
    return summed


def unit_rows(act, scale):
    out = []
    for h in range(act.shape[1] // HEAD_DIM):
        part = act[:, h * HEAD_DIM : (h + 1) * HEAD_DIM]
        inv = lax.rsqrt(jnp.sum(part * part, axis=-1, keepdims=True) + 1e-6)
        out.append((part * inv * scale, inv))
    return out


def chunk_masks(aux, docrow):
    row = lax.broadcasted_iota(jnp.int32, (CHUNK, CHUNK), 0)
    col = lax.broadcasted_iota(jnp.int32, (CHUNK, CHUNK), 1)
    made = []
    for c in range(GROUP):
        same = aux[c * CHUNK : (c + 1) * CHUNK, 8:9] == docrow[c : c + 1, :]
        made.append((jnp.logical_and(same, row > col), jnp.logical_and(same, row >= col)))
    return made


def mixer_fwd_kernel(
    x_ref, w_ref, aux_ref, docrow_ref, conv_ref, gain_ref,
    pre_ref, mixed_ref, o_ref, t_ref, phi_ref, s_ref, p_ref, d_ref, ew_ref,
    ext, state,
):
    heads = mixed_ref.shape[1] // HEAD_DIM
    hid = heads * HEAD_DIM

    @pl.when(pl.program_id(0) == 0)
    def _():
        ext[0:PAD, :] = jnp.zeros((PAD, 3 * hid), F32)
        state[...] = jnp.zeros_like(state)

    pre_ref[...] = dot(x_ref[...], w_ref[:, hid:], ((1,), (0,)))
    aux = aux_ref[...]
    conv = conv_ref[...]
    pre = pre_ref[:, : 3 * hid]
    ext[PAD:, :] = pre
    act = conv_parts(pre, ext, conv, aux)
    act = act * jax.nn.sigmoid(act)
    ext[0:PAD, :] = ext[STEP:, :]
    q = unit_rows(act[:, :hid], HEAD_DIM**-0.5)
    k = unit_rows(act[:, hid : 2 * hid], 1.0)
    beta = jax.nn.sigmoid(pre_ref[:, 4 * hid : 4 * hid + 8])
    masks = chunk_masks(aux, docrow_ref[0])

    items = [(c, h) for c in range(GROUP) for h in range(heads)]
    rows = [slice(c * CHUNK, (c + 1) * CHUNK) for c in range(GROUP)]
    lowers, scores = [], []
    for c, h in items:
        key, query = k[h][0][rows[c]], q[h][0][rows[c]]
        both = mul_t(jnp.concatenate([key, query], axis=0), key)
        lowers.append(jnp.where(masks[c][0], both[:CHUNK] * beta[rows[c], h : h + 1], 0.0))
        scores.append(jnp.where(masks[c][1], both[CHUNK:], 0.0).astype(BF16))
    solved = unit_inverses(lowers)
    parts = []
    for (c, h), inverse, score in zip(items, solved, scores):
        key = k[h][0][rows[c]]
        value = act[rows[c], 2 * hid + h * HEAD_DIM : 2 * hid + (h + 1) * HEAD_DIM]
        b = beta[rows[c], h : h + 1]
        enter, leave = aux[rows[c], 3:4], aux[rows[c], 4:5]
        inverse = inverse.astype(BF16)
        wu = mul(inverse, jnp.concatenate([key * b, value * b], axis=1))
        ew, u = wu[:, :HEAD_DIM] * enter, wu[:, HEAD_DIM:]
        phi_b = t_mul(key * leave, jnp.concatenate([ew, u], axis=1))
        parts.append((ew, u, phi_b[:, :HEAD_DIM].astype(BF16), phi_b[:, HEAD_DIM:]))
        t_ref[c, h] = inverse
        p_ref[c, h] = score
        ew_ref[c, h] = ew.astype(BF16)
        phi_ref[c, h] = parts[-1][2]
    for h in range(heads):
        s = state[h]
        for c in range(GROUP):
            low = s.astype(BF16)
            s_ref[c, h] = low
            _, _, phi, b_term = parts[c * heads + h]
            keep = aux[(c + 1) * CHUNK - 1 : (c + 1) * CHUNK, 3:4]
            s = s * keep - mul(phi, low) + b_term
        state[h] = s
    gain = gain_ref[...]
    for (c, h), (ew, u, _, _), score in zip(items, parts, scores):
        enter = aux[rows[c], 3:4]
        from_state = mul(jnp.concatenate([ew, q[h][0][rows[c]] * enter], axis=0), s_ref[c, h])
        d = (u - from_state[:CHUNK]).astype(BF16)
        d_ref[c, h] = d
        o = from_state[CHUNK:] + mul(score, d)
        cols = slice(h * HEAD_DIM, (h + 1) * HEAD_DIM)
        o_ref[rows[c], cols] = o
        normed = o * lax.rsqrt(jnp.mean(o * o, axis=-1, keepdims=True) + 1e-5) * gain
        gate = pre_ref[rows[c], 3 * hid + h * HEAD_DIM : 3 * hid + (h + 1) * HEAD_DIM]
        mixed_ref[rows[c], cols] = (normed * (gate * jax.nn.sigmoid(gate))).astype(BF16)


def mixer_bwd_kernel(
    hg_ref, wout_ref, pre_ref, halo_ref, aux_ref, docrow_ref, conv_ref, gain_ref,
    o_ref, t_ref, phi_ref, s_ref, p_ref, d_ref, ew_ref,
    dpre_ref, dconv_ref, dgain_ref,
    ext, later, dstate,
):
    heads = o_ref.shape[1] // HEAD_DIM
    hid = heads * HEAD_DIM

    @pl.when(pl.program_id(0) == 0)
    def _():
        later[STEP:, :] = jnp.zeros((PAD, 3 * hid), F32)
        dstate[...] = jnp.zeros_like(dstate)
        dconv_ref[...] = jnp.zeros_like(dconv_ref)
        dgain_ref[...] = jnp.zeros_like(dgain_ref)

    mixed_grad = dot(hg_ref[...], wout_ref[...], ((1,), (0,))).astype(BF16).astype(F32)
    aux = aux_ref[...]
    conv = conv_ref[...]
    pre = pre_ref[:, : 3 * hid]
    ext[0:PAD, :] = halo_ref[:, : 3 * hid]
    ext[PAD:, :] = pre
    lin = conv_parts(pre, ext, conv, aux)
    sig = jax.nn.sigmoid(lin)
    act = lin * sig
    dsilu = sig * (1.0 + lin * (1.0 - sig))
    scale = HEAD_DIM**-0.5
    q = unit_rows(act[:, :hid], 1.0)
    k = unit_rows(act[:, hid : 2 * hid], 1.0)
    beta = jax.nn.sigmoid(pre_ref[:, 4 * hid : 4 * hid + 8])
    masks = chunk_masks(aux, docrow_ref[0])
    gain = gain_ref[...]

    items = [(c, h) for c in range(GROUP) for h in range(heads)]
    rows = [slice(c * CHUNK, (c + 1) * CHUNK) for c in range(GROUP)]
    cols = [slice(h * HEAD_DIM, (h + 1) * HEAD_DIM) for h in range(heads)]

    d_out, d_gain = [], jnp.zeros((1, HEAD_DIM), F32)
    for h in range(heads):
        o = o_ref[:, cols[h]]
        inv = lax.rsqrt(jnp.mean(o * o, axis=-1, keepdims=True) + 1e-5)
        unit = o * inv
        gate = pre_ref[:, 3 * hid + h * HEAD_DIM : 3 * hid + (h + 1) * HEAD_DIM]
        s = jax.nn.sigmoid(gate)
        dm = mixed_grad[:, cols[h]]
        dpre_ref[:, 3 * hid + h * HEAD_DIM : 3 * hid + (h + 1) * HEAD_DIM] = (
            dm * unit * gain * (s * (1.0 + gate * (1.0 - s)))
        ).astype(BF16)
        dn = dm * (gate * s)
        d_gain = d_gain + jnp.sum(dn * unit, axis=0, keepdims=True)
        du = dn * gain
        d_out.append(inv * (du - unit * jnp.mean(du * unit, axis=-1, keepdims=True)))
    dgain_ref[...] += d_gain

    first = []
    for c, h in items:
        enter = aux[rows[c], 3:4]
        do = d_out[h][rows[c]].astype(BF16)
        eq = (q[h][0][rows[c]] * (enter * scale)).astype(BF16)
        x = t_mul(p_ref[c, h], do)
        c_term = t_mul(
            jnp.concatenate([eq, -ew_ref[c, h]], axis=0),
            jnp.concatenate([do, x.astype(BF16)], axis=0),
        )
        first.append((do, x, c_term))
    after = {}
    for h in range(heads):
        ds = dstate[h]
        for c in reversed(range(GROUP)):
            low = ds.astype(BF16)
            after[c, h] = low
            keep = aux[(c + 1) * CHUNK - 1 : (c + 1) * CHUNK, 3:4]
            ds = ds * keep - t_mul(phi_ref[c, h], low) + first[c * heads + h][2]
        dstate[h] = ds
    db_cols = []
    grads = {}
    for (c, h), (do, x, _) in zip(items, first):
        enter, leave = aux[rows[c], 3:4], aux[rows[c], 4:5]
        b = beta[rows[c], h : h + 1]
        key, query = k[h][0][rows[c]], q[h][0][rows[c]] * scale
        value = act[rows[c], 2 * hid + h * HEAD_DIM : 2 * hid + (h + 1) * HEAD_DIM]
        ds = after[c, h]
        d, s = d_ref[c, h], s_ref[c, h]
        dr = t_mul(t_ref[c, h], x + mul(key * leave, ds))
        stacked = jnp.concatenate([do, dr.astype(BF16)], axis=0)
        with_d = mul_t(stacked, d)
        with_s = mul_t(stacked, s) * jnp.concatenate([enter, enter], axis=0)
        dp = jnp.where(masks[c][1], with_d[:CHUNK], 0.0)
        da = jnp.where(masks[c][0], -with_d[CHUNK:], 0.0)
        pair = jnp.concatenate([dp, da], axis=0).astype(BF16)
        with_k = mul(pair, key)
        dq = with_s[:CHUNK] + with_k[:CHUNK]
        row_k = with_k[CHUNK:] - with_s[CHUNK:]
        dk = b * row_k + t_mul(pair, jnp.concatenate([query, key * b], axis=0))
        dk = dk + mul_t(d, ds) * leave
        db = jnp.sum(dr * value + key * row_k, axis=-1, keepdims=True)
        grads[c, h] = (dq * scale, dk, dr * b, db * b * (1.0 - b))
    for h in range(heads):
        whole = [jnp.concatenate([grads[c, h][i] for c in range(GROUP)], axis=0) for i in range(4)]
        for i, unit in ((0, q[h]), (1, k[h])):
            y, inv = unit
            grad = inv * (whole[i] - y * jnp.sum(y * whole[i], axis=-1, keepdims=True))
            at = slice(i * hid + h * HEAD_DIM, i * hid + (h + 1) * HEAD_DIM)
            later[0:STEP, at] = grad * dsilu[:, at]
        at = slice(2 * hid + h * HEAD_DIM, 2 * hid + (h + 1) * HEAD_DIM)
        later[0:STEP, at] = whole[2] * dsilu[:, at]
        db_cols.append(whole[3])
    lane = lax.broadcasted_iota(jnp.int32, (STEP, HEAD_DIM), 1)
    tail = jnp.zeros((STEP, HEAD_DIM), F32)
    for h in range(heads):
        tail = jnp.where(lane == h, db_cols[h], tail)
    dpre_ref[:, 4 * hid :] = tail.astype(BF16)
    dlin = later[0:STEP, :]
    dpre = dlin * conv[3:4, :]
    taps = [jnp.sum(dlin * pre, axis=0, keepdims=True)]
    for offset in range(1, 4):
        ahead = later[offset : offset + STEP, :]
        dpre = dpre + ahead * aux[:, 4 + offset : 5 + offset] * conv[3 - offset : 4 - offset, :]
        behind = ext[PAD - offset : PAD - offset + STEP, :] * aux[:, offset - 1 : offset]
        taps.append(jnp.sum(dlin * behind, axis=0, keepdims=True))
    dpre_ref[:, : 3 * hid] = dpre.astype(BF16)
    for offset in range(4):
        dconv_ref[3 - offset : 4 - offset, :] += taps[offset]
    later[STEP:, :] = later[0:PAD, :]


def mixer_fwd(x_rows, weights, aux, docrow, conv, gain):
    hid = conv.shape[1] // 3
    length, width = x_rows.shape[0], weights.shape[1] - hid
    heads, chunks = hid // HEAD_DIM, length // CHUNK
    rows = lambda n: pl.BlockSpec((STEP, n), lambda i: (i, 0))
    whole = lambda a: pl.BlockSpec(a.shape, lambda i: (0,) * a.ndim)
    square = pl.BlockSpec((GROUP, heads, CHUNK, HEAD_DIM), lambda i: (i, 0, 0, 0))
    squares = jax.ShapeDtypeStruct((chunks, heads, CHUNK, HEAD_DIM), BF16)
    return pl.pallas_call(
        mixer_fwd_kernel,
        grid=(length // STEP,),
        in_specs=[
            rows(x_rows.shape[1]), whole(weights), rows(aux.shape[1]),
            pl.BlockSpec((1, GROUP, CHUNK), lambda i: (i, 0, 0)), whole(conv), whole(gain),
        ],
        out_specs=[rows(width), rows(hid), rows(hid)] + [square] * 6,
        out_shape=[
            jax.ShapeDtypeStruct((length, width), F32),
            jax.ShapeDtypeStruct((length, hid), BF16),
            jax.ShapeDtypeStruct((length, hid), F32),
        ]
        + [squares] * 6,
        scratch_shapes=[
            pltpu.VMEM((PAD + STEP, 3 * hid), F32),
            pltpu.VMEM((heads, HEAD_DIM, HEAD_DIM), F32),
        ],
        compiler_params=pltpu.CompilerParams(vmem_limit_bytes=VMEM_LIMIT),
        name="mixer_fwd",
    )(x_rows, weights, aux, docrow, conv, gain)


def mixer_bwd(hg_rows, weights, aux, docrow, conv, gain, saved):
    pre, o, t, phi, s, p, d, ew = saved
    length, width = pre.shape
    hid = conv.shape[1] // 3
    heads, steps = hid // HEAD_DIM, length // STEP
    last = steps - 1
    rows = lambda n: pl.BlockSpec((STEP, n), lambda i: (last - i, 0))
    whole = lambda a: pl.BlockSpec(a.shape, lambda i: (0,) * a.ndim)
    square = pl.BlockSpec((GROUP, heads, CHUNK, HEAD_DIM), lambda i: (last - i, 0, 0, 0))
    halo = pl.BlockSpec(
        (PAD, width), lambda i: (jnp.maximum((last - i) * (STEP // PAD) - 1, 0), 0)
    )
    return pl.pallas_call(
        mixer_bwd_kernel,
        grid=(steps,),
        in_specs=[
            rows(hg_rows.shape[1]), pl.BlockSpec((weights.shape[0], hid), lambda i: (0, 0)), rows(width), halo, rows(aux.shape[1]),
            pl.BlockSpec((1, GROUP, CHUNK), lambda i: (last - i, 0, 0)), whole(conv), whole(gain),
            rows(hid),
        ]
        + [square] * 6,
        out_specs=[
            rows(width),
            pl.BlockSpec((4, 3 * hid), lambda i: (0, 0)),
            pl.BlockSpec((1, HEAD_DIM), lambda i: (0, 0)),
        ],
        out_shape=[
            jax.ShapeDtypeStruct((length, width), BF16),
            jax.ShapeDtypeStruct((4, 3 * hid), F32),
            jax.ShapeDtypeStruct((1, HEAD_DIM), F32),
        ],
        scratch_shapes=[
            pltpu.VMEM((PAD + STEP, 3 * hid), F32),
            pltpu.VMEM((STEP + PAD, 3 * hid), F32),
            pltpu.VMEM((heads, HEAD_DIM, HEAD_DIM), F32),
        ],
        compiler_params=pltpu.CompilerParams(vmem_limit_bytes=VMEM_LIMIT),
        name="mixer_bwd",
    )(hg_rows, weights, pre, pre, aux, docrow, conv, gain, o, t, phi, s, p, d, ew)


MESH = pl.DeviceIdType.MESH


def remote(src, dst, sent, landed, axis, to):
    return pltpu.make_async_remote_copy(
        src_ref=src, dst_ref=dst, send_sem=sent, recv_sem=landed,
        device_id={axis: to}, device_id_type=MESH,
    )


def shard_line(lines, own, out, sems):
    right_s, left_s, over_s, landed, local = sems
    me = lax.axis_index("dp")
    spot, side = me // 2, me % 2
    slot = lambda place: 2 * place + side
    across = me + 1 - 2 * side

    def hop(step, where):
        return (spot - step, me + 2, right_s) if where == 0 else (spot + step, me - 2, left_s)

    def going(step, where):
        place, to, sent = hop(step, where)
        src = out.at[slot(place)] if not isinstance(step, int) or step else own
        return remote(src, out.at[slot(place)], sent.at[step], landed.at[slot(place)], "dp", to)

    def goes(step, where):
        if where == 0:
            return jnp.logical_and(spot - step >= 0, spot + 1 < lines)
        return jnp.logical_and(spot + step < lines, spot >= 1)

    def over(place):
        return remote(out.at[slot(place)], out.at[slot(place)], over_s.at[place], landed.at[slot(place)], "dp", across)

    def first():
        pltpu.make_async_copy(own, out.at[me], local).start()
        remote(own, out.at[me], over_s.at[spot], landed.at[me], "dp", across).start()
        for where in (0, 1):
            pl.when(goes(0, where))(lambda where=where: going(0, where).start())

    def arrive(step, place):
        @pl.when(jnp.logical_and(place >= 0, place < lines))
        def _():
            over(place).wait_recv()
            over(place).start()

    def hop_step(step):
        for where in (0, 1):
            place = spot - step - 1 if where == 0 else spot + step + 1
            arrive(step, place)
            if isinstance(step, int) and step + 1 >= lines - 1:
                continue
            pl.when(jnp.logical_and(goes(step + 1, where), step + 1 < lines - 1))(
                lambda where=where: going(step + 1, where).start()
            )

    def last():
        pltpu.make_async_copy(own, out.at[me], local).wait()

        @pl.loop(0, lines)
        def _(place):
            there = 2 * place + 1 - side
            remote(out.at[there], out.at[there], over_s.at[place], landed.at[there], "dp", across).wait_recv()
            over(place).wait_send()

        @pl.loop(0, lines - 1)
        def _(step):
            for where in (0, 1):
                pl.when(goes(step, where))(lambda where=where: going(step, where).wait_send())

    return first, hop_step, last


def greet(lines, count):
    barrier = pltpu.get_barrier_semaphore()
    me = lax.axis_index("dp")
    spot, across = me // 2, me + 1 - 2 * (me % 2)

    def tell(axis, to):
        pl.semaphore_signal(barrier, 1, device_id={axis: to}, device_id_type=MESH)

    tell("dp", across)
    pl.when(spot >= 1)(lambda: tell("dp", me - 2))
    pl.when(spot + 1 < lines)(lambda: tell("dp", me + 2))
    head = lax.axis_index("head")
    tell("head", head + 1 - 2 * (head % 2))
    for f in range(1, count // 2):
        tell("head", lax.rem(head + 2 * f, count))
    beside = jnp.minimum(spot, 1) + jnp.minimum(lines - 1 - spot, 1)
    pl.semaphore_wait(barrier, 1 + count // 2 + beside)


def start_kernel(lines, count, parts, tok_ref, gain_ref, w_ref, rows_ref, wall_ref, mine,
                 right_s, left_s, over_s, landed, local, far_s, pair_s, fwd_s, got, keep_s):
    greet(lines, count)
    first, hop_step, last = shard_line(lines, w_ref, wall_ref, (right_s, left_s, over_s, landed, local.at[0]))
    first()
    me = lax.axis_index("head")
    pair = me + 1 - 2 * (me % 2)
    fars = [lax.rem(me + 2 * f, count) for f in range(1, count // 2)]
    size = tok_ref.shape[0] // parts
    span = lambda p: pl.ds(p * size, size)

    def block(owner, p):
        return rows_ref.at[owner, span(p)]

    for p in range(parts):
        x = tok_ref[p * size : (p + 1) * size, :].astype(F32)
        inv = lax.rsqrt(jnp.mean(x * x, axis=-1, keepdims=True) + 1e-6)
        mine[p * size : (p + 1) * size, :] = (x * inv * gain_ref[...]).astype(BF16)
        for f, far in enumerate(fars):
            remote(mine.at[span(p)], block(me, p), far_s.at[f, p], got.at[me, p], "head", far).start()
        remote(mine.at[span(p)], block(me, p), pair_s.at[p], got.at[me, p], "head", pair).start()
        pltpu.make_async_copy(mine.at[span(p)], block(me, p), keep_s.at[p]).start()

    def pass_on(p):
        for f, far in enumerate(fars):
            moved = remote(block(far, p), block(far, p), fwd_s.at[f, p], got.at[far, p], "head", pair)
            moved.wait_recv()
            moved.start()

    for i in range(parts):
        pass_on(i)
        if i < lines - 1:
            hop_step(i)
    if lines - 1 > parts:
        pl.loop(parts, lines - 1)(hop_step)
    last()
    for p in range(parts):
        remote(mine.at[span(p)], block(pair, p), pair_s.at[p], got.at[pair, p], "head", pair).wait()
        pltpu.make_async_copy(mine.at[span(p)], block(me, p), keep_s.at[p]).wait()
        for f, far in enumerate(fars):
            remote(mine.at[span(p)], block(me, p), far_s.at[f, p], got.at[me, p], "head", far).wait_send()
            there = lax.rem(pair + 2 * (f + 1), count)
            remote(block(far, p), block(there, p), fwd_s.at[f, p], got.at[there, p], "head", pair).wait()


def start(tokens, gain, mine, n_dp, n_head, parts=4):
    rows, width = tokens.shape
    lines, far = n_dp // 2, n_head // 2 - 1
    dma = lambda *shape: pltpu.SemaphoreType.DMA(shape)
    anywhere = pl.BlockSpec(memory_space=pl.ANY)
    vmem = pl.BlockSpec(memory_space=pltpu.VMEM)
    return pl.pallas_call(
        partial(start_kernel, lines, n_head, parts),
        out_shape=[jax.ShapeDtypeStruct((n_head, rows, width), BF16),
                   jax.ShapeDtypeStruct((n_dp, *mine.shape), BF16)],
        in_specs=[vmem, vmem, anywhere],
        out_specs=[anywhere, anywhere],
        scratch_shapes=[
            pltpu.VMEM((rows, width), BF16),
            dma(lines), dma(lines), dma(lines), dma(n_dp), dma(1),
            dma(far, parts), dma(parts), dma(far, parts), dma(n_head, parts), dma(parts),
        ],
        compiler_params=pltpu.CompilerParams(vmem_limit_bytes=VMEM_LIMIT, has_side_effects=True, collective_id=0),
        name="start",
    )(tokens, gain, mine)


class HeadScatter:
    def __init__(self, count, parts, refs):
        self.count, self.parts = count, parts
        (self.out, self.near, self.onward, self.far, self.own,
         self.out_s, self.near_r, self.onward_s, self.far_r) = refs
        self.me = lax.axis_index("head")
        self.side, self.place = self.me % 2, self.me // 2
        self.pair = self.me + 1 - 2 * self.side
        self.size = self.own.shape[0] // parts

    @staticmethod
    def scratch(count, parts, rows, width):
        size, half = rows // parts, count // 2
        return [
            pltpu.VMEM((2, 2, half, size, width), BF16),
            pltpu.VMEM((parts, half, size, width), BF16),
            pltpu.VMEM((2, half - 1, size, width), BF16),
            pltpu.VMEM((parts, half - 1, size, width), BF16),
            pltpu.VMEM((rows, width), F32),
            pltpu.SemaphoreType.DMA((2,)),
            pltpu.SemaphoreType.DMA((parts,)),
            pltpu.SemaphoreType.DMA((2, half - 1)),
            pltpu.SemaphoreType.DMA((parts, half - 1)),
        ]

    def _near(self, p):
        slot = p % 2
        return remote(self.out.at[slot, 1 - self.side], self.near.at[p], self.out_s.at[slot], self.near_r.at[p], "head", self.pair)

    def _far(self, p, f):
        slot = p % 2
        to = lax.rem(self.me + 2 * (f + 1), self.count)
        return remote(self.onward.at[slot, f], self.far.at[p, f], self.onward_s.at[slot, f], self.far_r.at[p, f], "head", to)

    def offer(self, p, total):
        if p >= 2:
            self._near(p - 2).wait_send()
        for owner in range(self.count):
            self.out[p % 2, owner % 2, owner // 2] = total[owner * self.size : (owner + 1) * self.size].astype(BF16)
        self._near(p).start()

    def turn(self, p):
        slot, half = p % 2, self.count // 2
        self._near(p).wait_recv()
        both = lambda i: self.out[slot, self.side, i].astype(F32) + self.near[p, i].astype(F32)
        for f in range(half - 1):
            if p >= 2:
                self._far(p - 2, f).wait_send()
            self.onward[slot, f] = both(lax.rem(self.place + f + 1, half)).astype(BF16)
            self._far(p, f).start()
        self.own[p * self.size : (p + 1) * self.size, :] = both(self.place)

    def take(self, p):
        total = self.own[p * self.size : (p + 1) * self.size, :]
        for f in range(self.count // 2 - 1):
            self._far(p, f).wait_recv()
            total = total + self.far[p, f].astype(F32)
        return total

    def close(self):
        for p in range(max(self.parts - 2, 0), self.parts):
            self._near(p).wait_send()
            for f in range(self.count // 2 - 1):
                self._far(p, f).wait_send()


class DpScatter:
    def __init__(self, lines, terms, refs):
        self.lines, self.terms = lines, terms
        self.cross, self.going, self.coming, self.cross_s, self.cross_r, self.go_s, self.come_r = refs
        self.me = lax.axis_index("dp")
        self.spot, self.side = self.me // 2, self.me % 2
        self.across = self.me + 1 - 2 * self.side

    @staticmethod
    def scratch(lines, rows, width):
        return [
            pltpu.VMEM((lines, rows, width), BF16),
            pltpu.VMEM((2, lines, rows, width), BF16),
            pltpu.VMEM((2, lines, rows, width), BF16),
            pltpu.SemaphoreType.DMA((lines,)),
            pltpu.SemaphoreType.DMA((lines,)),
            pltpu.SemaphoreType.DMA((2, lines)),
            pltpu.SemaphoreType.DMA((2, lines)),
        ]

    def _cross(self, place):
        return remote(self.terms.at[2 * place + 1 - self.side], self.cross.at[place], self.cross_s.at[place], self.cross_r.at[place], "dp", self.across)

    def _line(self, way, dest):
        to = self.me + 2 if way == 0 else self.me - 2
        return remote(self.going.at[way, dest], self.coming.at[way, dest], self.go_s.at[way, dest], self.come_r.at[way, dest], "dp", to)

    def offer(self, place):
        self._cross(place).start()

    def _both(self, place):
        return self.terms[2 * place + self.side].astype(F32) + self.cross[place].astype(F32)

    def _passes(self, way, dest):
        return dest > self.spot if way == 0 else dest < self.spot

    def _fed(self, way):
        return self.spot >= 1 if way == 0 else self.spot + 1 < self.lines

    def step(self, d):
        for way in (0, 1):
            dest = self.lines - 1 - d if way == 0 else d

            @pl.when(self._passes(way, dest))
            def _(way=way, dest=dest):
                self._cross(dest).wait_recv()
                self.going[way, dest] = self._both(dest).astype(BF16)

                @pl.when(self._fed(way))
                def _():
                    self._line(way, dest).wait_recv()
                    self.going[way, dest] = (
                        self.going[way, dest].astype(F32) + self.coming[way, dest].astype(F32)
                    ).astype(BF16)

                self._line(way, dest).start()

    def finish(self, out_ref):
        self._cross(self.spot).wait_recv()
        out_ref[...] = self._both(self.spot)
        for way in (0, 1):
            @pl.when(self._fed(way))
            def _(way=way):
                self._line(way, self.spot).wait_recv()
                out_ref[...] += self.coming[way, self.spot].astype(F32)

    def close(self):
        @pl.loop(0, self.lines)
        def _(place):
            self._cross(place).wait_send()
            for way in (0, 1):
                pl.when(self._passes(way, place))(lambda way=way: self._line(way, place).wait_send())


class SmallSum:
    def __init__(self, n_dp, count, shared, refs):
        self.n_dp, self.count, self.shared = n_dp, count, shared
        self.mine, self.theirs, self.half, self.halves, self.a_s, self.a_r, self.b_s, self.b_r = refs
        self.dp, self.head = lax.axis_index("dp"), lax.axis_index("head")

    @staticmethod
    def scratch(n_dp, count, rows, shared):
        return [
            pltpu.VMEM((rows, 128), F32),
            pltpu.VMEM((n_dp, rows, 128), F32),
            pltpu.VMEM((shared, 128), F32),
            pltpu.VMEM((count, shared, 128), F32),
            pltpu.SemaphoreType.DMA((n_dp,)),
            pltpu.SemaphoreType.DMA((n_dp,)),
            pltpu.SemaphoreType.DMA((count,)),
            pltpu.SemaphoreType.DMA((count,)),
        ]

    def _a(self, hop):
        to = lax.rem(self.dp + hop, self.n_dp)
        return remote(self.mine, self.theirs.at[self.dp], self.a_s.at[hop], self.a_r.at[self.dp], "dp", to)

    def _b(self, hop):
        to = lax.rem(self.head + hop, self.count)
        return remote(self.half, self.halves.at[self.head], self.b_s.at[hop], self.b_r.at[self.head], "head", to)

    def run(self, out_ref):
        self.theirs[self.dp] = self.mine[...]

        @pl.loop(1, self.n_dp)
        def _(hop):
            self._a(hop).start()

        @pl.loop(1, self.n_dp)
        def _(hop):
            sender = lax.rem(self.dp + self.n_dp - hop, self.n_dp)
            remote(self.mine, self.theirs.at[sender], self.a_s.at[hop], self.a_r.at[sender], "dp", sender).wait_recv()

        total = self.theirs[0]
        for i in range(1, self.n_dp):
            total = total + self.theirs[i]
        out_ref[...] = total
        self.half[...] = total[: self.shared]
        self.halves[self.head] = total[: self.shared]
        for hop in range(1, self.count):
            self._b(hop).start()
        for hop in range(1, self.count):
            sender = lax.rem(self.head + self.count - hop, self.count)
            remote(self.half, self.halves.at[sender], self.b_s.at[hop], self.b_r.at[sender], "head", sender).wait_recv()
        total = self.halves[0]
        for i in range(1, self.count):
            total = total + self.halves[i]
        out_ref[: self.shared, :] = total

        @pl.loop(1, self.n_dp)
        def _(hop):
            self._a(hop).wait_send()

        for hop in range(1, self.count):
            self._b(hop).wait_send()


def greet_all(n_dp, count):
    barrier = pltpu.get_barrier_semaphore()
    dp, head = lax.axis_index("dp"), lax.axis_index("head")

    @pl.loop(1, n_dp)
    def _(hop):
        pl.semaphore_signal(barrier, 1, device_id={"dp": lax.rem(dp + hop, n_dp)}, device_id_type=MESH)

    for hop in range(1, count):
        pl.semaphore_signal(barrier, 1, device_id={"head": lax.rem(head + hop, count)}, device_id_type=MESH)
    pl.semaphore_wait(barrier, n_dp + count - 2)


def end_kernel(n_dp, count, parts, shared,
               dpre_ref, w_ref, normed_ref, hg_ref, mixed_ref, tok_ref, gain_ref, grad_ref, small_ref,
               in_ref, mix_ref, sum_ref, *scratch):
    scratch = list(scratch)
    take = lambda n: [scratch.pop(0) for _ in range(n)]
    head_refs, dp_refs, small_refs = take(9), take(7), take(8)
    terms, dpre, w, normed, hg, mixed, loads = scratch
    rows, width = tok_ref.shape
    block = terms.shape[1]
    hid = mixed.shape[1]
    greet_all(n_dp, count)
    moves = [pltpu.make_async_copy(s, d, loads.at[i]) for i, (s, d) in enumerate(
        ((dpre_ref, dpre), (w_ref.at[:, hid:], w), (normed_ref, normed), (mixed_ref, mixed), (hg_ref, hg)))]
    for m in moves:
        m.start()
    heads = HeadScatter(count, parts, head_refs)
    line = DpScatter(n_dp // 2, terms, dp_refs)
    small = SmallSum(n_dp, count, shared, small_refs)
    size = rows // parts

    def offer(p):
        part = jnp.concatenate([dpre[o * rows + p * size : o * rows + (p + 1) * size, :] for o in range(count)], axis=0)
        heads.offer(p, dot(part, w[...], ((1,), (1,))))

    tiles = width // 256
    per = 256 // block

    def outer(t):
        cols = slice(t * 256, (t + 1) * 256)
        left = dot(normed[:, cols], dpre[...], ((0,), (0,))).astype(BF16)
        right = dot(hg[:, cols], mixed[...], ((0,), (0,))).astype(BF16)
        for b in range(per):
            terms[t * per + b, :, :hid] = right[b * block : (b + 1) * block]
            terms[t * per + b, :, hid:] = left[b * block : (b + 1) * block]
        for place in range(t * per // 2, (t + 1) * per // 2):
            line.offer(place)

    order = [t // 2 if t % 2 else tiles - 1 - t // 2 for t in range(tiles)]
    moves[0].wait()
    moves[1].wait()
    offer(0)
    for m in moves[2:]:
        m.wait()
    for i in range(max(tiles, parts)):
        if i < tiles:
            outer(order[i])
        if i < parts:
            heads.turn(i)
        if i + 1 < parts:
            offer(i + 1)
    small.mine[...] = small_ref[...]
    gain_total = jnp.zeros((1, width), F32)
    gain = gain_ref[...]

    def finish(p):
        at = slice(p * size, (p + 1) * size)
        normed_grad = heads.take(p).astype(BF16).astype(F32)
        x = tok_ref[at, :].astype(F32)
        inv = lax.rsqrt(jnp.mean(x * x, axis=-1, keepdims=True) + 1e-6)
        scaled = normed_grad * gain
        mean = jnp.mean(scaled * x, axis=-1, keepdims=True)
        in_ref[at, :] = grad_ref[at, :] + inv * scaled - x * (inv * inv * inv * mean)
        return jnp.sum(normed_grad * x * inv, axis=0, keepdims=True)

    lines = n_dp // 2
    for i in range(parts):
        gain_total = gain_total + finish(i)
        if i < lines - 1:
            line.step(i)
    if lines - 1 > parts:
        pl.loop(parts, lines - 1)(line.step)
    for i in range(width // 128):
        small.mine[i : i + 1, :] = gain_total[:, i * 128 : (i + 1) * 128]
    line.finish(mix_ref)
    small.run(sum_ref)
    heads.close()
    line.close()


def end(dpre, weights, normed_rows, hg_rows, mixed, tokens, gain, hidden_grad, small, n_dp, count, shared, parts=4):
    rows, width = tokens.shape
    block = width // n_dp
    wide = weights.shape[1]
    anywhere = pl.BlockSpec(memory_space=pl.ANY)
    vmem = pl.BlockSpec(memory_space=pltpu.VMEM)
    like = lambda a: pltpu.VMEM(a.shape, a.dtype)
    return pl.pallas_call(
        partial(end_kernel, n_dp, count, parts, shared),
        out_shape=[
            jax.ShapeDtypeStruct((rows, width), F32),
            jax.ShapeDtypeStruct((block, wide), F32),
            jax.ShapeDtypeStruct(small.shape, F32),
        ],
        in_specs=[anywhere] * 5 + [vmem] * 4,
        out_specs=[vmem] * 3,
        scratch_shapes=HeadScatter.scratch(count, parts, rows, width)
        + DpScatter.scratch(n_dp // 2, block, wide)
        + SmallSum.scratch(n_dp, count, small.shape[0], shared)
        + [pltpu.VMEM((n_dp, block, wide), BF16), like(dpre), pltpu.VMEM((width, dpre.shape[1]), BF16), like(normed_rows), like(hg_rows), like(mixed),
           pltpu.SemaphoreType.DMA((5,))],
        compiler_params=pltpu.CompilerParams(vmem_limit_bytes=VMEM_LIMIT, has_side_effects=True, collective_id=1),
        name="end",
    )(dpre, weights, normed_rows, hg_rows, mixed, tokens, gain, hidden_grad, small)


def doc_tables(lengths, length):
    count = lengths.shape[0]
    index = jnp.arange(count)
    ends = jnp.sum(jnp.where(index[None, :] <= index[:, None], lengths[None, :], 0), axis=1)
    position = jnp.arange(length, dtype=jnp.int32)
    doc = jnp.sum((position[:, None] >= ends[None, :]).astype(jnp.int32), axis=1)
    no_doc = lambda n: jnp.full((n,), -1, jnp.int32)
    before = [jnp.concatenate([no_doc(o), doc[:-o]]) == doc for o in (1, 2, 3)]
    after = [jnp.concatenate([doc[o:], no_doc(o)]) == doc for o in (1, 2, 3)]
    blocks = doc.reshape(-1, CHUNK)
    ending = blocks[:, -1:]
    prior = jnp.concatenate([no_doc(1)[:, None], ending[:-1]], axis=0)
    enter = (blocks == prior).reshape(-1)
    leave = (blocks == ending).reshape(-1)
    columns = before + [enter, leave] + after + [doc]
    aux = jnp.stack([c.astype(F32) for c in columns], axis=1)
    return aux, doc.astype(F32).reshape(-1, GROUP, CHUNK)


def low(values):
    return values.astype(BF16)


def inverse_rms(values):
    return lax.rsqrt(jnp.mean(values * values, axis=-1, keepdims=True) + 1e-6)


def norm_back(grad, values, inverse, gain):
    scaled = grad * gain
    mean = jnp.mean(scaled * values, axis=-1, keepdims=True)
    into = inverse * scaled - values * (inverse * inverse * inverse) * mean
    return into, jnp.sum(grad * values * inverse, axis=0)


def gather_rows(values):
    return lax.all_gather(values, "head", axis=0, tiled=True)


def scatter_rows(values):
    return lax.psum_scatter(low(values), "head", scatter_dimension=0, tiled=True).astype(F32)


def on_device(
    tokens,
    lengths,
    attn_gain,
    w_query,
    w_key,
    w_value,
    w_beta,
    w_gate_out,
    conv_weight,
    head_gain,
    w_out,
    mlp_gain,
    w_mlp_gate,
    w_mlp_up,
    w_down,
    cotangent,
):
    hid, heads, ff = w_query.shape[1], w_beta.shape[1], w_mlp_gate.shape[1]
    beta_wide = jnp.pad(w_beta, ((0, 0), (0, HEAD_DIM - heads)))
    mine = jnp.concatenate([w_out.T, w_query, w_key, w_value, w_gate_out, beta_wide], axis=1)
    n_dp, n_head = lax.axis_size("dp"), lax.axis_size("head")
    normed_rows, first_set = start(tokens, attn_gain[None, :], mine, n_dp, n_head)
    normed_rows = normed_rows.reshape(-1, normed_rows.shape[2])
    first_set = first_set.reshape(-1, first_set.shape[2])
    mine = jnp.concatenate([w_mlp_gate, w_mlp_up, w_down.T], axis=1)
    second_set = lax.all_gather(mine, "dp", axis=0, tiled=True)
    out_t = first_set[:, :hid]
    w_ff, down_t = second_set[:, : 2 * ff], second_set[:, 2 * ff :]

    x = tokens.astype(F32)
    length = normed_rows.shape[0]
    aux, docrow = doc_tables(lengths[0], length)
    conv = jnp.swapaxes(conv_weight.astype(F32), 0, 1).reshape(conv_weight.shape[1], 3 * hid)
    gain = head_gain[None, :]
    pre, mixed, *saved = mixer_fwd(normed_rows, first_set, aux, docrow, conv, gain)
    attention = scatter_rows(dot(mixed, out_t, ((1,), (1,))))
    hidden = x + attention
    h_inv = inverse_rms(hidden)
    second_rows = gather_rows(low(hidden * h_inv * mlp_gain))
    both = dot(second_rows, w_ff, ((1,), (0,)))
    gate, up = both[:, :ff], both[:, ff:]
    sig = jax.nn.sigmoid(gate)
    activated = gate * sig
    middle = low(activated * up)
    output = low(hidden + scatter_rows(dot(middle, down_t, ((1,), (1,)))))

    cot_rows = gather_rows(cotangent)
    middle_grad = low(dot(cot_rows, down_t, ((1,), (0,)))).astype(F32)
    up_grad = low(middle_grad * activated)
    gate_grad = low(middle_grad * up * sig * (1.0 + gate * (1.0 - sig)))
    ff_grad = jnp.concatenate([gate_grad, up_grad], axis=1)
    outer = lambda left, right: dot(left, right, ((0,), (0,)))
    second_grad = low(scatter_rows(dot(ff_grad, w_ff, ((1,), (1,))))).astype(F32)
    mlp_terms = jnp.concatenate(
        [low(outer(second_rows, ff_grad)), low(outer(cot_rows, middle))], axis=1
    )
    mlp_reduced = lax.psum_scatter(mlp_terms, "dp", scatter_dimension=0, tiled=True).astype(F32)
    from_mlp, mlp_gain_grad = norm_back(second_grad, hidden, h_inv, mlp_gain)
    hidden_grad = cotangent.astype(F32) + from_mlp
    hg_rows = gather_rows(low(hidden_grad))
    dpre, conv_part, head_gain_grad = mixer_bwd(
        hg_rows, first_set, aux, docrow, conv, gain, (pre, *saved)
    )
    taps = conv_part.shape[0]
    shared = 2 * (x.shape[1] // 128) + 8
    small = jnp.concatenate(
        [
            jnp.zeros((x.shape[1] // 128, 128), F32),
            mlp_gain_grad.reshape(-1, 128),
            jnp.pad(head_gain_grad, ((0, 7), (0, 0))),
            conv_part.reshape(-1, 128),
        ]
    )
    input_grad, mix_reduced, summed = end(
        dpre, first_set, normed_rows, hg_rows, mixed, tokens, attn_gain[None, :], hidden_grad, small,
        n_dp, n_head, shared,
    )
    gains = summed[: shared - 8].reshape(2, -1)
    conv_grad = jnp.swapaxes(summed[shared:].reshape(taps, 3, hid), 0, 1)
    part = lambda i: mix_reduced[:, (i + 1) * hid : (i + 2) * hid]
    return (
        output,
        input_grad,
        gains[0],
        part(0),
        part(1),
        part(2),
        mix_reduced[:, 5 * hid : 5 * hid + heads],
        part(3),
        conv_grad,
        summed[shared - 8],
        mix_reduced[:, :hid].T,
        gains[1],
        mlp_reduced[:, :ff],
        mlp_reduced[:, ff : 2 * ff],
        mlp_reduced[:, 2 * ff :].T,
    )


def solution(mesh):
    rows = P(("dp", "head"), None)
    in_specs = (
        rows,
        P("dp", None),
        P(),
        P("dp", "head"),
        P("dp", "head"),
        P("dp", "head"),
        P("dp", "head"),
        P("dp", "head"),
        P(None, None, "head"),
        P(),
        P("head", "dp"),
        P(),
        P("dp", "head"),
        P("dp", "head"),
        P("head", "dp"),
        rows,
    )
    out_specs = (
        rows,
        rows,
        P(),
        P("dp", "head"),
        P("dp", "head"),
        P("dp", "head"),
        P("dp", "head"),
        P("dp", "head"),
        P(None, None, "head"),
        P(),
        P("head", "dp"),
        P(),
        P("dp", "head"),
        P("dp", "head"),
        P("head", "dp"),
    )
    return jax.shard_map(
        on_device, mesh=mesh, in_specs=in_specs, out_specs=out_specs, check_vma=False
    )
```

```python
from functools import partial

import jax
import jax.numpy as jnp
from jax import lax
from jax.experimental import pallas as pl
from jax.experimental.pallas import tpu as pltpu
from jax.sharding import PartitionSpec as P

HEAD_DIM = 128
CHUNK = 128
GROUP = 4
STEP = CHUNK * GROUP
PAD = 8
F32 = jnp.float32
BF16 = jnp.bfloat16
VMEM_LIMIT = 56 * 1024 * 1024


def dot(left, right, dims):
    return lax.dot_general(left, right, (dims, ((), ())), preferred_element_type=F32)


def mul(left, right):
    return dot(left.astype(BF16), right.astype(BF16), ((1,), (0,)))


def mul_t(left, right):
    return dot(left.astype(BF16), right.astype(BF16), ((1,), (1,)))


def t_mul(left, right):
    return dot(left.astype(BF16), right.astype(BF16), ((0,), (0,)))


def unit_inverses(lowers):
    row = lax.broadcasted_iota(jnp.int32, (CHUNK, CHUNK), 0)
    col = lax.broadcasted_iota(jnp.int32, (CHUNK, CHUNK), 1)
    eye = (row == col).astype(F32)
    level = lambda bit: jnp.logical_and(
        (row >> (bit + 1)) == (col >> (bit + 1)), (row >> bit) > (col >> bit)
    )
    first = level(0)
    solved = [eye - jnp.where(first, a, 0.0) for a in lowers]
    for bit in range(1, CHUNK.bit_length() - 1):
        mask = level(bit)
        right = [mul(jnp.where(mask, a, 0.0), t) for a, t in zip(lowers, solved)]
        solved = [t - mul(t, r) for t, r in zip(solved, right)]
    return solved


def conv_parts(pre, ext, conv, aux):
    summed = pre * conv[3:4, :]
    for offset in range(1, 4):
        shifted = ext[PAD - offset : PAD - offset + STEP, :]
        summed = summed + shifted * aux[:, offset - 1 : offset] * conv[3 - offset : 4 - offset, :]
    return summed


def unit_rows(act, scale):
    out = []
    for h in range(act.shape[1] // HEAD_DIM):
        part = act[:, h * HEAD_DIM : (h + 1) * HEAD_DIM]
        inv = lax.rsqrt(jnp.sum(part * part, axis=-1, keepdims=True) + 1e-6)
        out.append((part * inv * scale, inv))
    return out


def chunk_masks(aux, docrow):
    row = lax.broadcasted_iota(jnp.int32, (CHUNK, CHUNK), 0)
    col = lax.broadcasted_iota(jnp.int32, (CHUNK, CHUNK), 1)
    made = []
    for c in range(GROUP):
        same = aux[c * CHUNK : (c + 1) * CHUNK, 8:9] == docrow[c : c + 1, :]
        made.append((jnp.logical_and(same, row > col), jnp.logical_and(same, row >= col)))
    return made


def mixer_fwd_kernel(
    x_ref, w_ref, aux_ref, docrow_ref, conv_ref, gain_ref,
    pre_ref, mixed_ref, o_ref, t_ref, phi_ref, s_ref, p_ref, d_ref, ew_ref,
    ext, state,
):
    heads = mixed_ref.shape[1] // HEAD_DIM
    hid = heads * HEAD_DIM

    @pl.when(pl.program_id(0) == 0)
    def _():
        ext[0:PAD, :] = jnp.zeros((PAD, 3 * hid), F32)
        state[...] = jnp.zeros_like(state)

    pre_ref[...] = dot(x_ref[...], w_ref[:, hid:], ((1,), (0,)))
    aux = aux_ref[...]
    conv = conv_ref[...]
    pre = pre_ref[:, : 3 * hid]
    ext[PAD:, :] = pre
    act = conv_parts(pre, ext, conv, aux)
    act = act * jax.nn.sigmoid(act)
    ext[0:PAD, :] = ext[STEP:, :]
    q = unit_rows(act[:, :hid], HEAD_DIM**-0.5)
    k = unit_rows(act[:, hid : 2 * hid], 1.0)
    beta = jax.nn.sigmoid(pre_ref[:, 4 * hid : 4 * hid + 8])
    masks = chunk_masks(aux, docrow_ref[0])

    items = [(c, h) for c in range(GROUP) for h in range(heads)]
    rows = [slice(c * CHUNK, (c + 1) * CHUNK) for c in range(GROUP)]
    lowers, scores = [], []
    for c, h in items:
        key, query = k[h][0][rows[c]], q[h][0][rows[c]]
        both = mul_t(jnp.concatenate([key, query], axis=0), key)
        lowers.append(jnp.where(masks[c][0], both[:CHUNK] * beta[rows[c], h : h + 1], 0.0))
        scores.append(jnp.where(masks[c][1], both[CHUNK:], 0.0).astype(BF16))
    solved = unit_inverses(lowers)
    parts = []
    for (c, h), inverse, score in zip(items, solved, scores):
        key = k[h][0][rows[c]]
        value = act[rows[c], 2 * hid + h * HEAD_DIM : 2 * hid + (h + 1) * HEAD_DIM]
        b = beta[rows[c], h : h + 1]
        enter, leave = aux[rows[c], 3:4], aux[rows[c], 4:5]
        inverse = inverse.astype(BF16)
        wu = mul(inverse, jnp.concatenate([key * b, value * b], axis=1))
        ew, u = wu[:, :HEAD_DIM] * enter, wu[:, HEAD_DIM:]
        phi_b = t_mul(key * leave, jnp.concatenate([ew, u], axis=1))
        parts.append((ew, u, phi_b[:, :HEAD_DIM].astype(BF16), phi_b[:, HEAD_DIM:]))
        t_ref[c, h] = inverse
        p_ref[c, h] = score
        ew_ref[c, h] = ew.astype(BF16)
        phi_ref[c, h] = parts[-1][2]
    for h in range(heads):
        s = state[h]
        for c in range(GROUP):
            low = s.astype(BF16)
            s_ref[c, h] = low
            _, _, phi, b_term = parts[c * heads + h]
            keep = aux[(c + 1) * CHUNK - 1 : (c + 1) * CHUNK, 3:4]
            s = s * keep - mul(phi, low) + b_term
        state[h] = s
    gain = gain_ref[...]
    for (c, h), (ew, u, _, _), score in zip(items, parts, scores):
        enter = aux[rows[c], 3:4]
        from_state = mul(jnp.concatenate([ew, q[h][0][rows[c]] * enter], axis=0), s_ref[c, h])
        d = (u - from_state[:CHUNK]).astype(BF16)
        d_ref[c, h] = d
        o = from_state[CHUNK:] + mul(score, d)
        cols = slice(h * HEAD_DIM, (h + 1) * HEAD_DIM)
        o_ref[rows[c], cols] = o
        normed = o * lax.rsqrt(jnp.mean(o * o, axis=-1, keepdims=True) + 1e-5) * gain
        gate = pre_ref[rows[c], 3 * hid + h * HEAD_DIM : 3 * hid + (h + 1) * HEAD_DIM]
        mixed_ref[rows[c], cols] = (normed * (gate * jax.nn.sigmoid(gate))).astype(BF16)


def mixer_bwd_kernel(
    hg_ref, wout_ref, pre_ref, halo_ref, aux_ref, docrow_ref, conv_ref, gain_ref,
    o_ref, t_ref, phi_ref, s_ref, p_ref, d_ref, ew_ref,
    dpre_ref, dconv_ref, dgain_ref,
    ext, later, dstate,
):
    heads = o_ref.shape[1] // HEAD_DIM
    hid = heads * HEAD_DIM

    @pl.when(pl.program_id(0) == 0)
    def _():
        later[STEP:, :] = jnp.zeros((PAD, 3 * hid), F32)
        dstate[...] = jnp.zeros_like(dstate)
        dconv_ref[...] = jnp.zeros_like(dconv_ref)
        dgain_ref[...] = jnp.zeros_like(dgain_ref)

    mixed_grad = dot(hg_ref[...], wout_ref[...], ((1,), (0,))).astype(BF16).astype(F32)
    aux = aux_ref[...]
    conv = conv_ref[...]
    pre = pre_ref[:, : 3 * hid]
    ext[0:PAD, :] = halo_ref[:, : 3 * hid]
    ext[PAD:, :] = pre
    lin = conv_parts(pre, ext, conv, aux)
    sig = jax.nn.sigmoid(lin)
    act = lin * sig
    dsilu = sig * (1.0 + lin * (1.0 - sig))
    scale = HEAD_DIM**-0.5
    q = unit_rows(act[:, :hid], 1.0)
    k = unit_rows(act[:, hid : 2 * hid], 1.0)
    beta = jax.nn.sigmoid(pre_ref[:, 4 * hid : 4 * hid + 8])
    masks = chunk_masks(aux, docrow_ref[0])
    gain = gain_ref[...]

    items = [(c, h) for c in range(GROUP) for h in range(heads)]
    rows = [slice(c * CHUNK, (c + 1) * CHUNK) for c in range(GROUP)]
    cols = [slice(h * HEAD_DIM, (h + 1) * HEAD_DIM) for h in range(heads)]

    d_out, d_gain = [], jnp.zeros((1, HEAD_DIM), F32)
    for h in range(heads):
        o = o_ref[:, cols[h]]
        inv = lax.rsqrt(jnp.mean(o * o, axis=-1, keepdims=True) + 1e-5)
        unit = o * inv
        gate = pre_ref[:, 3 * hid + h * HEAD_DIM : 3 * hid + (h + 1) * HEAD_DIM]
        s = jax.nn.sigmoid(gate)
        dm = mixed_grad[:, cols[h]]
        dpre_ref[:, 3 * hid + h * HEAD_DIM : 3 * hid + (h + 1) * HEAD_DIM] = (
            dm * unit * gain * (s * (1.0 + gate * (1.0 - s)))
        ).astype(BF16)
        dn = dm * (gate * s)
        d_gain = d_gain + jnp.sum(dn * unit, axis=0, keepdims=True)
        du = dn * gain
        d_out.append(inv * (du - unit * jnp.mean(du * unit, axis=-1, keepdims=True)))
    dgain_ref[...] += d_gain

    first = []
    for c, h in items:
        enter = aux[rows[c], 3:4]
        do = d_out[h][rows[c]].astype(BF16)
        eq = (q[h][0][rows[c]] * (enter * scale)).astype(BF16)
        x = t_mul(p_ref[c, h], do)
        c_term = t_mul(
            jnp.concatenate([eq, -ew_ref[c, h]], axis=0),
            jnp.concatenate([do, x.astype(BF16)], axis=0),
        )
        first.append((do, x, c_term))
    after = {}
    for h in range(heads):
        ds = dstate[h]
        for c in reversed(range(GROUP)):
            low = ds.astype(BF16)
            after[c, h] = low
            keep = aux[(c + 1) * CHUNK - 1 : (c + 1) * CHUNK, 3:4]
            ds = ds * keep - t_mul(phi_ref[c, h], low) + first[c * heads + h][2]
        dstate[h] = ds
    db_cols = []
    grads = {}
    for (c, h), (do, x, _) in zip(items, first):
        enter, leave = aux[rows[c], 3:4], aux[rows[c], 4:5]
        b = beta[rows[c], h : h + 1]
        key, query = k[h][0][rows[c]], q[h][0][rows[c]] * scale
        value = act[rows[c], 2 * hid + h * HEAD_DIM : 2 * hid + (h + 1) * HEAD_DIM]
        ds = after[c, h]
        d, s = d_ref[c, h], s_ref[c, h]
        dr = t_mul(t_ref[c, h], x + mul(key * leave, ds))
        stacked = jnp.concatenate([do, dr.astype(BF16)], axis=0)
        with_d = mul_t(stacked, d)
        with_s = mul_t(stacked, s) * jnp.concatenate([enter, enter], axis=0)
        dp = jnp.where(masks[c][1], with_d[:CHUNK], 0.0)
        da = jnp.where(masks[c][0], -with_d[CHUNK:], 0.0)
        pair = jnp.concatenate([dp, da], axis=0).astype(BF16)
        with_k = mul(pair, key)
        dq = with_s[:CHUNK] + with_k[:CHUNK]
        row_k = with_k[CHUNK:] - with_s[CHUNK:]
        dk = b * row_k + t_mul(pair, jnp.concatenate([query, key * b], axis=0))
        dk = dk + mul_t(d, ds) * leave
        db = jnp.sum(dr * value + key * row_k, axis=-1, keepdims=True)
        grads[c, h] = (dq * scale, dk, dr * b, db * b * (1.0 - b))
    for h in range(heads):
        whole = [jnp.concatenate([grads[c, h][i] for c in range(GROUP)], axis=0) for i in range(4)]
        for i, unit in ((0, q[h]), (1, k[h])):
            y, inv = unit
            grad = inv * (whole[i] - y * jnp.sum(y * whole[i], axis=-1, keepdims=True))
            at = slice(i * hid + h * HEAD_DIM, i * hid + (h + 1) * HEAD_DIM)
            later[0:STEP, at] = grad * dsilu[:, at]
        at = slice(2 * hid + h * HEAD_DIM, 2 * hid + (h + 1) * HEAD_DIM)
        later[0:STEP, at] = whole[2] * dsilu[:, at]
        db_cols.append(whole[3])
    lane = lax.broadcasted_iota(jnp.int32, (STEP, HEAD_DIM), 1)
    tail = jnp.zeros((STEP, HEAD_DIM), F32)
    for h in range(heads):
        tail = jnp.where(lane == h, db_cols[h], tail)
    dpre_ref[:, 4 * hid :] = tail.astype(BF16)
    dlin = later[0:STEP, :]
    dpre = dlin * conv[3:4, :]
    taps = [jnp.sum(dlin * pre, axis=0, keepdims=True)]
    for offset in range(1, 4):
        ahead = later[offset : offset + STEP, :]
        dpre = dpre + ahead * aux[:, 4 + offset : 5 + offset] * conv[3 - offset : 4 - offset, :]
        behind = ext[PAD - offset : PAD - offset + STEP, :] * aux[:, offset - 1 : offset]
        taps.append(jnp.sum(dlin * behind, axis=0, keepdims=True))
    dpre_ref[:, : 3 * hid] = dpre.astype(BF16)
    for offset in range(4):
        dconv_ref[3 - offset : 4 - offset, :] += taps[offset]
    later[STEP:, :] = later[0:PAD, :]


def mixer_fwd(x_rows, weights, aux, docrow, conv, gain):
    hid = conv.shape[1] // 3
    length, width = x_rows.shape[0], weights.shape[1] - hid
    heads, chunks = hid // HEAD_DIM, length // CHUNK
    rows = lambda n: pl.BlockSpec((STEP, n), lambda i: (i, 0))
    whole = lambda a: pl.BlockSpec(a.shape, lambda i: (0,) * a.ndim)
    square = pl.BlockSpec((GROUP, heads, CHUNK, HEAD_DIM), lambda i: (i, 0, 0, 0))
    squares = jax.ShapeDtypeStruct((chunks, heads, CHUNK, HEAD_DIM), BF16)
    return pl.pallas_call(
        mixer_fwd_kernel,
        grid=(length // STEP,),
        in_specs=[
            rows(x_rows.shape[1]), whole(weights), rows(aux.shape[1]),
            pl.BlockSpec((1, GROUP, CHUNK), lambda i: (i, 0, 0)), whole(conv), whole(gain),
        ],
        out_specs=[rows(width), rows(hid), rows(hid)] + [square] * 6,
        out_shape=[
            jax.ShapeDtypeStruct((length, width), F32),
            jax.ShapeDtypeStruct((length, hid), BF16),
            jax.ShapeDtypeStruct((length, hid), F32),
        ]
        + [squares] * 6,
        scratch_shapes=[
            pltpu.VMEM((PAD + STEP, 3 * hid), F32),
            pltpu.VMEM((heads, HEAD_DIM, HEAD_DIM), F32),
        ],
        compiler_params=pltpu.CompilerParams(vmem_limit_bytes=VMEM_LIMIT),
        name="mixer_fwd",
    )(x_rows, weights, aux, docrow, conv, gain)


def mixer_bwd(hg_rows, weights, aux, docrow, conv, gain, saved):
    pre, o, t, phi, s, p, d, ew = saved
    length, width = pre.shape
    hid = conv.shape[1] // 3
    heads, steps = hid // HEAD_DIM, length // STEP
    last = steps - 1
    rows = lambda n: pl.BlockSpec((STEP, n), lambda i: (last - i, 0))
    whole = lambda a: pl.BlockSpec(a.shape, lambda i: (0,) * a.ndim)
    square = pl.BlockSpec((GROUP, heads, CHUNK, HEAD_DIM), lambda i: (last - i, 0, 0, 0))
    halo = pl.BlockSpec(
        (PAD, width), lambda i: (jnp.maximum((last - i) * (STEP // PAD) - 1, 0), 0)
    )
    return pl.pallas_call(
        mixer_bwd_kernel,
        grid=(steps,),
        in_specs=[
            rows(hg_rows.shape[1]), pl.BlockSpec((weights.shape[0], hid), lambda i: (0, 0)), rows(width), halo, rows(aux.shape[1]),
            pl.BlockSpec((1, GROUP, CHUNK), lambda i: (last - i, 0, 0)), whole(conv), whole(gain),
            rows(hid),
        ]
        + [square] * 6,
        out_specs=[
            rows(width),
            pl.BlockSpec((4, 3 * hid), lambda i: (0, 0)),
            pl.BlockSpec((1, HEAD_DIM), lambda i: (0, 0)),
        ],
        out_shape=[
            jax.ShapeDtypeStruct((length, width), BF16),
            jax.ShapeDtypeStruct((4, 3 * hid), F32),
            jax.ShapeDtypeStruct((1, HEAD_DIM), F32),
        ],
        scratch_shapes=[
            pltpu.VMEM((PAD + STEP, 3 * hid), F32),
            pltpu.VMEM((STEP + PAD, 3 * hid), F32),
            pltpu.VMEM((heads, HEAD_DIM, HEAD_DIM), F32),
        ],
        compiler_params=pltpu.CompilerParams(vmem_limit_bytes=VMEM_LIMIT),
        name="mixer_bwd",
    )(hg_rows, weights, pre, pre, aux, docrow, conv, gain, o, t, phi, s, p, d, ew)


MESH = pl.DeviceIdType.MESH


def remote(src, dst, sent, landed, axis, to):
    return pltpu.make_async_remote_copy(
        src_ref=src, dst_ref=dst, send_sem=sent, recv_sem=landed,
        device_id={axis: to}, device_id_type=MESH,
    )


def shard_line(lines, own, out, sems):
    right_s, left_s, over_s, landed, local = sems
    me = lax.axis_index("dp")
    spot, side = me // 2, me % 2
    slot = lambda place: 2 * place + side
    across = me + 1 - 2 * side

    def hop(step, where):
        return (spot - step, me + 2, right_s) if where == 0 else (spot + step, me - 2, left_s)

    def going(step, where):
        place, to, sent = hop(step, where)
        src = out.at[slot(place)] if not isinstance(step, int) or step else own
        return remote(src, out.at[slot(place)], sent.at[step], landed.at[slot(place)], "dp", to)

    def goes(step, where):
        if where == 0:
            return jnp.logical_and(spot - step >= 0, spot + 1 < lines)
        return jnp.logical_and(spot + step < lines, spot >= 1)

    def over(place):
        return remote(out.at[slot(place)], out.at[slot(place)], over_s.at[place], landed.at[slot(place)], "dp", across)

    def first():
        pltpu.make_async_copy(own, out.at[me], local).start()
        remote(own, out.at[me], over_s.at[spot], landed.at[me], "dp", across).start()
        for where in (0, 1):
            pl.when(goes(0, where))(lambda where=where: going(0, where).start())

    def arrive(step, place):
        @pl.when(jnp.logical_and(place >= 0, place < lines))
        def _():
            over(place).wait_recv()
            over(place).start()

    def hop_step(step):
        for where in (0, 1):
            place = spot - step - 1 if where == 0 else spot + step + 1
            arrive(step, place)
            if isinstance(step, int) and step + 1 >= lines - 1:
                continue
            pl.when(jnp.logical_and(goes(step + 1, where), step + 1 < lines - 1))(
                lambda where=where: going(step + 1, where).start()
            )

    def last():
        pltpu.make_async_copy(own, out.at[me], local).wait()

        @pl.loop(0, lines)
        def _(place):
            there = 2 * place + 1 - side
            remote(out.at[there], out.at[there], over_s.at[place], landed.at[there], "dp", across).wait_recv()
            over(place).wait_send()

        @pl.loop(0, lines - 1)
        def _(step):
            for where in (0, 1):
                pl.when(goes(step, where))(lambda where=where: going(step, where).wait_send())

    return first, hop_step, last


def greet(lines, count):
    barrier = pltpu.get_barrier_semaphore()
    me = lax.axis_index("dp")
    spot, across = me // 2, me + 1 - 2 * (me % 2)

    def tell(axis, to):
        pl.semaphore_signal(barrier, 1, device_id={axis: to}, device_id_type=MESH)

    tell("dp", across)
    pl.when(spot >= 1)(lambda: tell("dp", me - 2))
    pl.when(spot + 1 < lines)(lambda: tell("dp", me + 2))
    head = lax.axis_index("head")
    tell("head", head + 1 - 2 * (head % 2))
    for f in range(1, count // 2):
        tell("head", lax.rem(head + 2 * f, count))
    beside = jnp.minimum(spot, 1) + jnp.minimum(lines - 1 - spot, 1)
    pl.semaphore_wait(barrier, 1 + count // 2 + beside)


def start_kernel(lines, count, parts, tok_ref, gain_ref, w_ref, rows_ref, wall_ref, mine,
                 right_s, left_s, over_s, landed, local, far_s, pair_s, fwd_s, got, keep_s):
    greet(lines, count)
    first, hop_step, last = shard_line(lines, w_ref, wall_ref, (right_s, left_s, over_s, landed, local.at[0]))
    first()
    me = lax.axis_index("head")
    pair = me + 1 - 2 * (me % 2)
    fars = [lax.rem(me + 2 * f, count) for f in range(1, count // 2)]
    size = tok_ref.shape[0] // parts
    span = lambda p: pl.ds(p * size, size)

    def block(owner, p):
        return rows_ref.at[owner, span(p)]

    for p in range(parts):
        x = tok_ref[p * size : (p + 1) * size, :].astype(F32)
        inv = lax.rsqrt(jnp.mean(x * x, axis=-1, keepdims=True) + 1e-6)
        mine[p * size : (p + 1) * size, :] = (x * inv * gain_ref[...]).astype(BF16)
        for f, far in enumerate(fars):
            remote(mine.at[span(p)], block(me, p), far_s.at[f, p], got.at[me, p], "head", far).start()
        remote(mine.at[span(p)], block(me, p), pair_s.at[p], got.at[me, p], "head", pair).start()
        pltpu.make_async_copy(mine.at[span(p)], block(me, p), keep_s.at[p]).start()

    def pass_on(p):
        for f, far in enumerate(fars):
            moved = remote(block(far, p), block(far, p), fwd_s.at[f, p], got.at[far, p], "head", pair)
            moved.wait_recv()
            moved.start()

    for i in range(parts):
        pass_on(i)
        if i < lines - 1:
            hop_step(i)
    if lines - 1 > parts:
        pl.loop(parts, lines - 1)(hop_step)
    last()
    for p in range(parts):
        remote(mine.at[span(p)], block(pair, p), pair_s.at[p], got.at[pair, p], "head", pair).wait()
        pltpu.make_async_copy(mine.at[span(p)], block(me, p), keep_s.at[p]).wait()
        for f, far in enumerate(fars):
            remote(mine.at[span(p)], block(me, p), far_s.at[f, p], got.at[me, p], "head", far).wait_send()
            there = lax.rem(pair + 2 * (f + 1), count)
            remote(block(far, p), block(there, p), fwd_s.at[f, p], got.at[there, p], "head", pair).wait()


def start(tokens, gain, mine, n_dp, n_head, parts=4):
    rows, width = tokens.shape
    lines, far = n_dp // 2, n_head // 2 - 1
    dma = lambda *shape: pltpu.SemaphoreType.DMA(shape)
    anywhere = pl.BlockSpec(memory_space=pl.ANY)
    vmem = pl.BlockSpec(memory_space=pltpu.VMEM)
    return pl.pallas_call(
        partial(start_kernel, lines, n_head, parts),
        out_shape=[jax.ShapeDtypeStruct((n_head, rows, width), BF16),
                   jax.ShapeDtypeStruct((n_dp, *mine.shape), BF16)],
        in_specs=[vmem, vmem, anywhere],
        out_specs=[anywhere, anywhere],
        scratch_shapes=[
            pltpu.VMEM((rows, width), BF16),
            dma(lines), dma(lines), dma(lines), dma(n_dp), dma(1),
            dma(far, parts), dma(parts), dma(far, parts), dma(n_head, parts), dma(parts),
        ],
        compiler_params=pltpu.CompilerParams(vmem_limit_bytes=VMEM_LIMIT, has_side_effects=True, collective_id=0),
        name="start",
    )(tokens, gain, mine)


def when(condition):
    return pl.when(condition) if not isinstance(condition, bool) else (lambda f: f() if condition else None)


class HeadScatter:
    def __init__(self, count, refs):
        self.count = count
        (self.out, self.near, self.onward, self.far, self.own,
         self.out_s, self.near_r, self.onward_s, self.far_r) = refs
        self.me = lax.axis_index("head")
        self.side, self.place = self.me % 2, self.me // 2
        self.pair = self.me + 1 - 2 * self.side
        self.parts, self.depth, self.size = self.near.shape[0], self.own.shape[0], self.own.shape[1]

    @staticmethod
    def scratch(count, parts, size, width, depth):
        half = count // 2
        return [
            pltpu.VMEM((2, 2, half, size, width), BF16),
            pltpu.VMEM((parts, half, size, width), BF16),
            pltpu.VMEM((2, half - 1, size, width), BF16),
            pltpu.VMEM((parts, half - 1, size, width), BF16),
            pltpu.VMEM((depth, size, width), F32),
            pltpu.SemaphoreType.DMA((2,)),
            pltpu.SemaphoreType.DMA((parts,)),
            pltpu.SemaphoreType.DMA((2, half - 1)),
            pltpu.SemaphoreType.DMA((parts, half - 1)),
        ]

    def _near(self, p):
        slot = p % 2
        return remote(self.out.at[slot, 1 - self.side], self.near.at[p], self.out_s.at[slot], self.near_r.at[p], "head", self.pair)

    def _far(self, p, f):
        slot = p % 2
        to = lax.rem(self.me + 2 * (f + 1), self.count)
        return remote(self.onward.at[slot, f], self.far.at[p, f], self.onward_s.at[slot, f], self.far_r.at[p, f], "head", to)

    def offer(self, p, total):
        when(p >= 2)(lambda: self._near(p - 2).wait_send())
        for owner in range(self.count):
            self.out[p % 2, owner % 2, owner // 2] = total[owner * self.size : (owner + 1) * self.size].astype(BF16)
        self._near(p).start()

    def turn(self, p):
        slot, half = p % 2, self.count // 2
        self._near(p).wait_recv()
        both = lambda i: self.out[slot, self.side, i].astype(F32) + self.near[p, i].astype(F32)
        for f in range(half - 1):
            when(p >= 2)(lambda f=f: self._far(p - 2, f).wait_send())
            self.onward[slot, f] = both(lax.rem(self.place + f + 1, half)).astype(BF16)
            self._far(p, f).start()
        self.own[p % self.depth] = both(self.place)

    def take(self, p):
        total = self.own[p % self.depth]
        for f in range(self.count // 2 - 1):
            self._far(p, f).wait_recv()
            total = total + self.far[p, f].astype(F32)
        return total

    def close(self):
        for p in range(max(self.parts - 2, 0), self.parts):
            self._near(p).wait_send()
            for f in range(self.count // 2 - 1):
                self._far(p, f).wait_send()


class HeadGather:
    def __init__(self, count, parts, own, block, refs):
        self.count, self.parts, self.own, self.block = count, parts, own, block
        self.far_s, self.pair_s, self.fwd_s, self.got = refs
        self.me = lax.axis_index("head")
        self.pair = self.me + 1 - 2 * (self.me % 2)

    @staticmethod
    def scratch(count, parts):
        far = count // 2 - 1
        return [pltpu.SemaphoreType.DMA(s) for s in ((far, parts), (parts,), (far, parts), (count, parts))]

    def _fars(self, base):
        return [(f, lax.rem(base + 2 * (f + 1), self.count)) for f in range(self.count // 2 - 1)]

    def _far(self, p, f, far):
        return remote(self.own(p), self.block(self.me, p), self.far_s.at[f, p], self.got.at[self.me, p], "head", far)

    def _pair(self, p):
        return remote(self.own(p), self.block(self.me, p), self.pair_s.at[p], self.got.at[self.me, p], "head", self.pair)

    def _on(self, p, f, owner):
        return remote(self.block(owner, p), self.block(owner, p), self.fwd_s.at[f, p], self.got.at[owner, p], "head", self.pair)

    def send(self, p):
        for f, far in self._fars(self.me):
            self._far(p, f, far).start()
        self._pair(p).start()

    def pass_on(self, p):
        for f, far in self._fars(self.me):
            self._on(p, f, far).wait_recv()
            self._on(p, f, far).start()

    def arrive(self, p):
        remote(self.own(p), self.block(self.pair, p), self.pair_s.at[p], self.got.at[self.pair, p], "head", self.pair).wait_recv()
        for f, far in self._fars(self.pair):
            self._on(p, f, far).wait_recv()

    def sent(self, p):
        self._pair(p).wait_send()
        for f, far in self._fars(self.me):
            self._far(p, f, far).wait_send()
            self._on(p, f, far).wait_send()


def greet_head(count):
    barrier = pltpu.get_barrier_semaphore()
    me = lax.axis_index("head")
    for to in [me + 1 - 2 * (me % 2)] + [lax.rem(me + 2 * f, count) for f in range(1, count // 2)]:
        pl.semaphore_signal(barrier, 1, device_id={"head": to}, device_id_type=MESH)
    pl.semaphore_wait(barrier, count // 2)


def mid_kernel(count, parts, mixed_ref, weights_ref, tok_ref, gain_ref, cot_ref, ff_ref,
               out_ref, grad_ref, hg_ref, gain_grad_ref, terms_ref, *scratch):
    scratch = list(scratch)
    take = lambda n: [scratch.pop(0) for _ in range(n)]
    att_refs, down_refs, back_refs = take(9), take(9), take(9)
    second_sems, hg_sems = take(4), take(4)
    out_t, second, hidden, hg_own, total, loads, keep_s = scratch
    size, width = tok_ref.shape[1:]
    ff = ff_ref.shape[1] // 3
    me = lax.axis_index("head")
    load = pltpu.make_async_copy(weights_ref.at[:, : out_t.shape[1]], out_t, loads.at[0])
    load.start()
    greet_head(count)
    att, down, back = (HeadScatter(count, r) for r in (att_refs, down_refs, back_refs))
    here = lambda owner, p: second.at[p, owner]
    seconds = HeadGather(count, parts, lambda p: here(me, p), here, second_sems)
    there = lambda owner, p: hg_ref.at[owner, p]
    hgs = HeadGather(count, parts, lambda p: hg_own.at[p], there, hg_sems)
    keep = lambda p: pltpu.make_async_copy(hg_own.at[p], there(me, p), keep_s.at[p])
    total[...] = jnp.zeros_like(total)
    gain_grad_ref[...] = jnp.zeros_like(gain_grad_ref)
    load.wait()

    def within(p, stage):
        pl.when(jnp.logical_and(p >= 0, p < parts))(lambda: stage(p))

    def attend(p):
        rows = mixed_ref[:, p].reshape(count * size, mixed_ref.shape[3])
        att.offer(p, dot(rows, out_t[...], ((1,), (1,))))

    def norm(p):
        rows = tok_ref[p].astype(F32) + att.take(p)
        hidden[p] = rows
        inv = lax.rsqrt(jnp.mean(rows * rows, axis=-1, keepdims=True) + 1e-6)
        second[p, me] = (rows * inv * gain_ref[...]).astype(BF16)
        seconds.send(p)

    def feed(p):
        seconds.arrive(p)
        rows = second[p].reshape(count * size, width)
        both = dot(rows, ff_ref[:, : 2 * ff], ((1,), (0,)))
        gate, up = both[:, :ff], both[:, ff:]
        sig = jax.nn.sigmoid(gate)
        act = gate * sig
        middle = (act * up).astype(BF16)
        down.offer(p, dot(middle, ff_ref[:, 2 * ff :], ((1,), (1,))))
        cot = cot_ref[:, p].reshape(count * size, width)
        grad = dot(cot, ff_ref[:, 2 * ff :], ((1,), (0,))).astype(BF16).astype(F32)
        pair = jnp.concatenate(
            [(grad * up * sig * (1.0 + gate * (1.0 - sig))).astype(BF16), (grad * act).astype(BF16)], axis=1
        )
        back.offer(p, dot(pair, ff_ref[:, : 2 * ff], ((1,), (1,))))
        total[:, : 2 * ff] += dot(rows, pair, ((0,), (0,)))
        total[:, 2 * ff :] += dot(cot, middle, ((0,), (0,)))

    def turn(p):
        down.turn(p)
        back.turn(p)

    def finish(p):
        rows = hidden[p]
        out_ref[p] = (rows + down.take(p)).astype(BF16)
        second_grad = back.take(p).astype(BF16).astype(F32)
        inv = lax.rsqrt(jnp.mean(rows * rows, axis=-1, keepdims=True) + 1e-6)
        scaled = second_grad * gain_ref[...]
        mean = jnp.mean(scaled * rows, axis=-1, keepdims=True)
        grad = cot_ref[me, p].astype(F32) + inv * scaled - rows * (inv * inv * inv * mean)
        grad_ref[p] = grad
        gain_grad_ref[...] += jnp.sum(second_grad * rows * inv, axis=0, keepdims=True)
        hg_own[p] = grad.astype(BF16)
        hgs.send(p)
        keep(p).start()

    @pl.loop(0, parts + 4)
    def _(step):
        i = step - 1
        within(i + 1, attend)
        within(i, norm)
        within(i + 1, att.turn)
        within(i - 1, feed)
        within(i, seconds.pass_on)
        within(i - 1, turn)
        within(i - 2, finish)
        within(i - 3, hgs.pass_on)

    terms_ref[...] = total[...].astype(BF16)

    @pl.loop(0, parts)
    def _(p):
        hgs.arrive(p)
        keep(p).wait()
        hgs.sent(p)
        seconds.sent(p)

    for s in (att, down, back):
        s.close()


def mid(mixed, weights, tokens, gain, cot_rows, ff_set, count, parts=8):
    rows, width = tokens.shape
    size, hid = rows // parts, mixed.shape[1]
    anywhere = pl.BlockSpec(memory_space=pl.ANY)
    vmem = pl.BlockSpec(memory_space=pltpu.VMEM)
    scatter = HeadScatter.scratch(count, parts, size, width, 2)
    out, grad, hg, gain_grad, terms = pl.pallas_call(
        partial(mid_kernel, count, parts),
        out_shape=[
            jax.ShapeDtypeStruct((parts, size, width), BF16),
            jax.ShapeDtypeStruct((parts, size, width), F32),
            jax.ShapeDtypeStruct((count, parts, size, width), BF16),
            jax.ShapeDtypeStruct((1, width), F32),
            jax.ShapeDtypeStruct(ff_set.shape, BF16),
        ],
        in_specs=[vmem, anywhere] + [vmem] * 4,
        out_specs=[vmem, vmem, anywhere, vmem, vmem],
        scratch_shapes=scatter * 3
        + HeadGather.scratch(count, parts) * 2
        + [
            pltpu.VMEM((width, hid), BF16),
            pltpu.VMEM((parts, count, size, width), BF16),
            pltpu.VMEM((parts, size, width), F32),
            pltpu.VMEM((parts, size, width), BF16),
            pltpu.VMEM(ff_set.shape, F32),
            pltpu.SemaphoreType.DMA((1,)),
            pltpu.SemaphoreType.DMA((parts,)),
        ],
        compiler_params=pltpu.CompilerParams(vmem_limit_bytes=61 * 1024 * 1024, has_side_effects=True, collective_id=2),
        name="mid",
    )(
        mixed.reshape(count, parts, size, hid), weights, tokens.reshape(parts, size, width), gain,
        cot_rows.reshape(count, parts, size, width), ff_set,
    )
    return out.reshape(rows, width), grad.reshape(rows, width), hg.reshape(-1, width), gain_grad, terms


class DpScatter:
    def __init__(self, lines, terms, refs):
        self.lines, self.terms = lines, terms
        self.cross, self.going, self.coming, self.cross_s, self.cross_r, self.go_s, self.come_r = refs
        self.me = lax.axis_index("dp")
        self.spot, self.side = self.me // 2, self.me % 2
        self.across = self.me + 1 - 2 * self.side

    @staticmethod
    def scratch(lines, rows, width):
        return [
            pltpu.VMEM((lines, rows, width), BF16),
            pltpu.VMEM((2, lines, rows, width), BF16),
            pltpu.VMEM((2, lines, rows, width), BF16),
            pltpu.SemaphoreType.DMA((lines,)),
            pltpu.SemaphoreType.DMA((lines,)),
            pltpu.SemaphoreType.DMA((2, lines)),
            pltpu.SemaphoreType.DMA((2, lines)),
        ]

    def _cross(self, place):
        return remote(self.terms.at[2 * place + 1 - self.side], self.cross.at[place], self.cross_s.at[place], self.cross_r.at[place], "dp", self.across)

    def _line(self, way, dest):
        to = self.me + 2 if way == 0 else self.me - 2
        return remote(self.going.at[way, dest], self.coming.at[way, dest], self.go_s.at[way, dest], self.come_r.at[way, dest], "dp", to)

    def offer(self, place):
        self._cross(place).start()

    def _both(self, place):
        return self.terms[2 * place + self.side].astype(F32) + self.cross[place].astype(F32)

    def _passes(self, way, dest):
        return dest > self.spot if way == 0 else dest < self.spot

    def _fed(self, way):
        return self.spot >= 1 if way == 0 else self.spot + 1 < self.lines

    def step(self, d):
        for way in (0, 1):
            dest = self.lines - 1 - d if way == 0 else d

            @pl.when(self._passes(way, dest))
            def _(way=way, dest=dest):
                self._cross(dest).wait_recv()
                self.going[way, dest] = self._both(dest).astype(BF16)

                @pl.when(self._fed(way))
                def _():
                    self._line(way, dest).wait_recv()
                    self.going[way, dest] = (
                        self.going[way, dest].astype(F32) + self.coming[way, dest].astype(F32)
                    ).astype(BF16)

                self._line(way, dest).start()

    def finish(self, out_ref):
        self._cross(self.spot).wait_recv()
        out_ref[...] = self._both(self.spot)
        for way in (0, 1):
            @pl.when(self._fed(way))
            def _(way=way):
                self._line(way, self.spot).wait_recv()
                out_ref[...] += self.coming[way, self.spot].astype(F32)

    def close(self):
        @pl.loop(0, self.lines)
        def _(place):
            self._cross(place).wait_send()
            for way in (0, 1):
                pl.when(self._passes(way, place))(lambda way=way: self._line(way, place).wait_send())


class SmallSum:
    def __init__(self, n_dp, count, shared, refs):
        self.n_dp, self.count, self.shared = n_dp, count, shared
        self.mine, self.theirs, self.half, self.halves, self.a_s, self.a_r, self.b_s, self.b_r = refs
        self.dp, self.head = lax.axis_index("dp"), lax.axis_index("head")

    @staticmethod
    def scratch(n_dp, count, rows, shared):
        return [
            pltpu.VMEM((rows, 128), F32),
            pltpu.VMEM((n_dp, rows, 128), F32),
            pltpu.VMEM((shared, 128), F32),
            pltpu.VMEM((count, shared, 128), F32),
            pltpu.SemaphoreType.DMA((n_dp,)),
            pltpu.SemaphoreType.DMA((n_dp,)),
            pltpu.SemaphoreType.DMA((count,)),
            pltpu.SemaphoreType.DMA((count,)),
        ]

    def _a(self, hop):
        to = lax.rem(self.dp + hop, self.n_dp)
        return remote(self.mine, self.theirs.at[self.dp], self.a_s.at[hop], self.a_r.at[self.dp], "dp", to)

    def _b(self, hop):
        to = lax.rem(self.head + hop, self.count)
        return remote(self.half, self.halves.at[self.head], self.b_s.at[hop], self.b_r.at[self.head], "head", to)

    def run(self, out_ref):
        self.theirs[self.dp] = self.mine[...]

        @pl.loop(1, self.n_dp)
        def _(hop):
            self._a(hop).start()

        @pl.loop(1, self.n_dp)
        def _(hop):
            sender = lax.rem(self.dp + self.n_dp - hop, self.n_dp)
            remote(self.mine, self.theirs.at[sender], self.a_s.at[hop], self.a_r.at[sender], "dp", sender).wait_recv()

        total = self.theirs[0]
        for i in range(1, self.n_dp):
            total = total + self.theirs[i]
        out_ref[...] = total
        self.half[...] = total[: self.shared]
        self.halves[self.head] = total[: self.shared]
        for hop in range(1, self.count):
            self._b(hop).start()
        for hop in range(1, self.count):
            sender = lax.rem(self.head + self.count - hop, self.count)
            remote(self.half, self.halves.at[sender], self.b_s.at[hop], self.b_r.at[sender], "head", sender).wait_recv()
        total = self.halves[0]
        for i in range(1, self.count):
            total = total + self.halves[i]
        out_ref[: self.shared, :] = total

        @pl.loop(1, self.n_dp)
        def _(hop):
            self._a(hop).wait_send()

        for hop in range(1, self.count):
            self._b(hop).wait_send()


def greet_all(n_dp, count):
    barrier = pltpu.get_barrier_semaphore()
    dp, head = lax.axis_index("dp"), lax.axis_index("head")

    @pl.loop(1, n_dp)
    def _(hop):
        pl.semaphore_signal(barrier, 1, device_id={"dp": lax.rem(dp + hop, n_dp)}, device_id_type=MESH)

    for hop in range(1, count):
        pl.semaphore_signal(barrier, 1, device_id={"head": lax.rem(head + hop, count)}, device_id_type=MESH)
    pl.semaphore_wait(barrier, n_dp + count - 2)


def end_kernel(n_dp, count, parts, shared,
               dpre_ref, w_ref, normed_ref, hg_ref, mixed_ref, tok_ref, gain_ref, grad_ref, small_ref,
               in_ref, mix_ref, sum_ref, *scratch):
    scratch = list(scratch)
    take = lambda n: [scratch.pop(0) for _ in range(n)]
    head_refs, dp_refs, small_refs = take(9), take(7), take(8)
    terms, dpre, w, normed, hg, mixed, loads = scratch
    rows, width = tok_ref.shape
    block = terms.shape[1]
    hid = mixed.shape[1]
    greet_all(n_dp, count)
    moves = [pltpu.make_async_copy(s, d, loads.at[i]) for i, (s, d) in enumerate(
        ((dpre_ref, dpre), (w_ref.at[:, hid:], w), (normed_ref, normed), (mixed_ref, mixed), (hg_ref, hg)))]
    for m in moves:
        m.start()
    heads = HeadScatter(count, head_refs)
    line = DpScatter(n_dp // 2, terms, dp_refs)
    small = SmallSum(n_dp, count, shared, small_refs)
    size = rows // parts

    def offer(p):
        part = jnp.concatenate([dpre[o * rows + p * size : o * rows + (p + 1) * size, :] for o in range(count)], axis=0)
        heads.offer(p, dot(part, w[...], ((1,), (1,))))

    tiles = width // 256
    per = 256 // block

    def outer(t):
        cols = slice(t * 256, (t + 1) * 256)
        left = dot(normed[:, cols], dpre[...], ((0,), (0,))).astype(BF16)
        right = dot(hg[:, cols], mixed[...], ((0,), (0,))).astype(BF16)
        for b in range(per):
            terms[t * per + b, :, :hid] = right[b * block : (b + 1) * block]
            terms[t * per + b, :, hid:] = left[b * block : (b + 1) * block]
        for place in range(t * per // 2, (t + 1) * per // 2):
            line.offer(place)

    order = [t // 2 if t % 2 else tiles - 1 - t // 2 for t in range(tiles)]
    moves[0].wait()
    moves[1].wait()
    offer(0)
    for m in moves[2:]:
        m.wait()
    for i in range(max(tiles, parts)):
        if i < tiles:
            outer(order[i])
        if i < parts:
            heads.turn(i)
        if i + 1 < parts:
            offer(i + 1)
    small.mine[...] = small_ref[...]
    gain_total = jnp.zeros((1, width), F32)
    gain = gain_ref[...]

    def finish(p):
        at = slice(p * size, (p + 1) * size)
        normed_grad = heads.take(p).astype(BF16).astype(F32)
        x = tok_ref[at, :].astype(F32)
        inv = lax.rsqrt(jnp.mean(x * x, axis=-1, keepdims=True) + 1e-6)
        scaled = normed_grad * gain
        mean = jnp.mean(scaled * x, axis=-1, keepdims=True)
        in_ref[at, :] = grad_ref[at, :] + inv * scaled - x * (inv * inv * inv * mean)
        return jnp.sum(normed_grad * x * inv, axis=0, keepdims=True)

    lines = n_dp // 2
    for i in range(parts):
        gain_total = gain_total + finish(i)
        if i < lines - 1:
            line.step(i)
    if lines - 1 > parts:
        pl.loop(parts, lines - 1)(line.step)
    for i in range(width // 128):
        small.mine[i : i + 1, :] = gain_total[:, i * 128 : (i + 1) * 128]
    line.finish(mix_ref)
    small.run(sum_ref)
    heads.close()
    line.close()


def end(dpre, weights, normed_rows, hg_rows, mixed, tokens, gain, hidden_grad, small, n_dp, count, shared, parts=4):
    rows, width = tokens.shape
    block = width // n_dp
    wide = weights.shape[1]
    anywhere = pl.BlockSpec(memory_space=pl.ANY)
    vmem = pl.BlockSpec(memory_space=pltpu.VMEM)
    like = lambda a: pltpu.VMEM(a.shape, a.dtype)
    return pl.pallas_call(
        partial(end_kernel, n_dp, count, parts, shared),
        out_shape=[
            jax.ShapeDtypeStruct((rows, width), F32),
            jax.ShapeDtypeStruct((block, wide), F32),
            jax.ShapeDtypeStruct(small.shape, F32),
        ],
        in_specs=[anywhere] * 5 + [vmem] * 4,
        out_specs=[vmem] * 3,
        scratch_shapes=HeadScatter.scratch(count, parts, rows // parts, width, parts)
        + DpScatter.scratch(n_dp // 2, block, wide)
        + SmallSum.scratch(n_dp, count, small.shape[0], shared)
        + [pltpu.VMEM((n_dp, block, wide), BF16), like(dpre), pltpu.VMEM((width, dpre.shape[1]), BF16), like(normed_rows), like(hg_rows), like(mixed),
           pltpu.SemaphoreType.DMA((5,))],
        compiler_params=pltpu.CompilerParams(vmem_limit_bytes=VMEM_LIMIT, has_side_effects=True, collective_id=1),
        name="end",
    )(dpre, weights, normed_rows, hg_rows, mixed, tokens, gain, hidden_grad, small)


def doc_tables(lengths, length):
    count = lengths.shape[0]
    index = jnp.arange(count)
    ends = jnp.sum(jnp.where(index[None, :] <= index[:, None], lengths[None, :], 0), axis=1)
    position = jnp.arange(length, dtype=jnp.int32)
    doc = jnp.sum((position[:, None] >= ends[None, :]).astype(jnp.int32), axis=1)
    no_doc = lambda n: jnp.full((n,), -1, jnp.int32)
    before = [jnp.concatenate([no_doc(o), doc[:-o]]) == doc for o in (1, 2, 3)]
    after = [jnp.concatenate([doc[o:], no_doc(o)]) == doc for o in (1, 2, 3)]
    blocks = doc.reshape(-1, CHUNK)
    ending = blocks[:, -1:]
    prior = jnp.concatenate([no_doc(1)[:, None], ending[:-1]], axis=0)
    enter = (blocks == prior).reshape(-1)
    leave = (blocks == ending).reshape(-1)
    columns = before + [enter, leave] + after + [doc]
    aux = jnp.stack([c.astype(F32) for c in columns], axis=1)
    return aux, doc.astype(F32).reshape(-1, GROUP, CHUNK)


def on_device(
    tokens,
    lengths,
    attn_gain,
    w_query,
    w_key,
    w_value,
    w_beta,
    w_gate_out,
    conv_weight,
    head_gain,
    w_out,
    mlp_gain,
    w_mlp_gate,
    w_mlp_up,
    w_down,
    cotangent,
):
    hid, heads, ff = w_query.shape[1], w_beta.shape[1], w_mlp_gate.shape[1]
    n_dp, n_head = lax.axis_size("dp"), lax.axis_size("head")
    beta_wide = jnp.pad(w_beta, ((0, 0), (0, HEAD_DIM - heads)))
    mine = jnp.concatenate([w_out.T, w_query, w_key, w_value, w_gate_out, beta_wide], axis=1)
    normed_rows, first_set = start(tokens, attn_gain[None, :], mine, n_dp, n_head)
    normed_rows = normed_rows.reshape(-1, normed_rows.shape[2])
    first_set = first_set.reshape(-1, first_set.shape[2])
    wide = -(-ff // 256) * 256
    mine = jnp.concatenate(
        [jnp.pad(w, ((0, 0), (0, wide - ff))) for w in (w_mlp_gate, w_mlp_up, w_down.T)], axis=1
    )
    ff_set = lax.all_gather(mine, "dp", axis=0, tiled=True)
    cot_rows = lax.all_gather(cotangent, "head", axis=0, tiled=True)

    length = normed_rows.shape[0]
    aux, docrow = doc_tables(lengths[0], length)
    conv = jnp.swapaxes(conv_weight.astype(F32), 0, 1).reshape(conv_weight.shape[1], 3 * hid)
    gain = head_gain[None, :]
    pre, mixed, *saved = mixer_fwd(normed_rows, first_set, aux, docrow, conv, gain)
    output, hidden_grad, hg_rows, mlp_gain_grad, mlp_terms = mid(
        mixed, first_set, tokens, mlp_gain[None, :], cot_rows, ff_set, n_head
    )
    mlp_reduced = lax.psum_scatter(mlp_terms, "dp", scatter_dimension=0, tiled=True).astype(F32)
    dpre, conv_part, head_gain_grad = mixer_bwd(
        hg_rows, first_set, aux, docrow, conv, gain, (pre, *saved)
    )
    taps = conv_part.shape[0]
    shared = 2 * (tokens.shape[1] // 128) + 8
    small = jnp.concatenate(
        [
            jnp.zeros((tokens.shape[1] // 128, 128), F32),
            mlp_gain_grad.reshape(-1, 128),
            jnp.pad(head_gain_grad, ((0, 7), (0, 0))),
            conv_part.reshape(-1, 128),
        ]
    )
    input_grad, mix_reduced, summed = end(
        dpre, first_set, normed_rows, hg_rows, mixed, tokens, attn_gain[None, :], hidden_grad, small,
        n_dp, n_head, shared,
    )
    gains = summed[: shared - 8].reshape(2, -1)
    conv_grad = jnp.swapaxes(summed[shared:].reshape(taps, 3, hid), 0, 1)
    part = lambda i: mix_reduced[:, (i + 1) * hid : (i + 2) * hid]
    return (
        output,
        input_grad,
        gains[0],
        part(0),
        part(1),
        part(2),
        mix_reduced[:, 5 * hid : 5 * hid + heads],
        part(3),
        conv_grad,
        summed[shared - 8],
        mix_reduced[:, :hid].T,
        gains[1],
        mlp_reduced[:, :ff],
        mlp_reduced[:, wide : wide + ff],
        mlp_reduced[:, 2 * wide : 2 * wide + ff].T,
    )


def solution(mesh):
    rows = P(("dp", "head"), None)
    in_specs = (
        rows,
        P("dp", None),
        P(),
        P("dp", "head"),
        P("dp", "head"),
        P("dp", "head"),
        P("dp", "head"),
        P("dp", "head"),
        P(None, None, "head"),
        P(),
        P("head", "dp"),
        P(),
        P("dp", "head"),
        P("dp", "head"),
        P("head", "dp"),
        rows,
    )
    out_specs = (
        rows,
        rows,
        P(),
        P("dp", "head"),
        P("dp", "head"),
        P("dp", "head"),
        P("dp", "head"),
        P("dp", "head"),
        P(None, None, "head"),
        P(),
        P("head", "dp"),
        P(),
        P("dp", "head"),
        P("dp", "head"),
        P("head", "dp"),
    )
    return jax.shard_map(
        on_device, mesh=mesh, in_specs=in_specs, out_specs=out_specs, check_vma=False
    )
```

```python
from functools import partial

import jax
import jax.numpy as jnp
from jax import lax
from jax.experimental import pallas as pl
from jax.experimental.pallas import tpu as pltpu
from jax.sharding import PartitionSpec as P

HEAD_DIM = 128
CHUNK = 128
GROUP = 4
STEP = CHUNK * GROUP
PAD = 8
F32 = jnp.float32
BF16 = jnp.bfloat16
VMEM_LIMIT = 56 * 1024 * 1024


def dot(left, right, dims):
    return lax.dot_general(left, right, (dims, ((), ())), preferred_element_type=F32)


def mul(left, right):
    return dot(left.astype(BF16), right.astype(BF16), ((1,), (0,)))


def mul_t(left, right):
    return dot(left.astype(BF16), right.astype(BF16), ((1,), (1,)))


def t_mul(left, right):
    return dot(left.astype(BF16), right.astype(BF16), ((0,), (0,)))


def unit_inverses(lowers):
    row = lax.broadcasted_iota(jnp.int32, (CHUNK, CHUNK), 0)
    col = lax.broadcasted_iota(jnp.int32, (CHUNK, CHUNK), 1)
    eye = (row == col).astype(F32)
    level = lambda bit: jnp.logical_and(
        (row >> (bit + 1)) == (col >> (bit + 1)), (row >> bit) > (col >> bit)
    )
    first = level(0)
    solved = [eye - jnp.where(first, a, 0.0) for a in lowers]
    for bit in range(1, CHUNK.bit_length() - 1):
        mask = level(bit)
        right = [mul(jnp.where(mask, a, 0.0), t) for a, t in zip(lowers, solved)]
        solved = [t - mul(t, r) for t, r in zip(solved, right)]
    return solved


def conv_parts(pre, ext, conv, aux):
    summed = pre * conv[3:4, :]
    for offset in range(1, 4):
        shifted = ext[PAD - offset : PAD - offset + STEP, :]
        summed = summed + shifted * aux[:, offset - 1 : offset] * conv[3 - offset : 4 - offset, :]
    return summed


def unit_rows(act, scale):
    out = []
    for h in range(act.shape[1] // HEAD_DIM):
        part = act[:, h * HEAD_DIM : (h + 1) * HEAD_DIM]
        inv = lax.rsqrt(jnp.sum(part * part, axis=-1, keepdims=True) + 1e-6)
        out.append((part * inv * scale, inv))
    return out


def chunk_masks(aux, docrow):
    row = lax.broadcasted_iota(jnp.int32, (CHUNK, CHUNK), 0)
    col = lax.broadcasted_iota(jnp.int32, (CHUNK, CHUNK), 1)
    made = []
    for c in range(GROUP):
        same = aux[c * CHUNK : (c + 1) * CHUNK, 8:9] == docrow[c : c + 1, :]
        made.append((jnp.logical_and(same, row > col), jnp.logical_and(same, row >= col)))
    return made


def mixer_fwd_kernel(
    lines, count,
    x_ref, w_ref, aux_ref, docrow_ref, conv_ref, gain_ref, cot_ref, ff_ref,
    pre_ref, mixed_ref, o_ref, t_ref, phi_ref, s_ref, p_ref, d_ref, ew_ref, cot_rows, ff_rows,
    ext, state, right_s, left_s, over_s, landed, local, *cot_sems,
):
    heads = mixed_ref.shape[1] // HEAD_DIM
    hid = heads * HEAD_DIM
    grid_step, last_step = pl.program_id(0), pl.num_programs(0) - 1
    first, hop_step, last = shard_line(lines, ff_ref, ff_rows, (right_s, left_s, over_s, landed, local.at[0]))
    cot_parts = cot_sems[1].shape[0]
    size = cot_ref.shape[0] // cot_parts
    part = lambda p: pl.ds(p * size, size)
    me = lax.axis_index("head")
    cots = HeadGather(
        count, cot_parts, lambda p: cot_ref.at[part(p)], lambda owner, p: cot_rows.at[owner, part(p)], cot_sems
    )
    held = pltpu.make_async_copy(cot_ref, cot_rows.at[me], local.at[1])

    @pl.when(grid_step == 0)
    def _():
        greet(lines, count)
        first()
        held.start()
        for p in range(cot_parts):
            cots.send(p)

    @pl.when(grid_step == 2)
    def _():
        hop_step(0)
        cots.pass_on(0)

    @pl.when(pl.program_id(0) == 0)
    def _():
        ext[0:PAD, :] = jnp.zeros((PAD, 3 * hid), F32)
        state[...] = jnp.zeros_like(state)

    pre_ref[...] = dot(x_ref[...], w_ref[:, hid:], ((1,), (0,)))
    aux = aux_ref[...]
    conv = conv_ref[...]
    pre = pre_ref[:, : 3 * hid]
    ext[PAD:, :] = pre
    act = conv_parts(pre, ext, conv, aux)
    act = act * jax.nn.sigmoid(act)
    ext[0:PAD, :] = ext[STEP:, :]
    q = unit_rows(act[:, :hid], HEAD_DIM**-0.5)
    k = unit_rows(act[:, hid : 2 * hid], 1.0)
    beta = jax.nn.sigmoid(pre_ref[:, 4 * hid : 4 * hid + 8])
    masks = chunk_masks(aux, docrow_ref[0])

    items = [(c, h) for c in range(GROUP) for h in range(heads)]
    rows = [slice(c * CHUNK, (c + 1) * CHUNK) for c in range(GROUP)]
    lowers, scores = [], []
    for c, h in items:
        key, query = k[h][0][rows[c]], q[h][0][rows[c]]
        both = mul_t(jnp.concatenate([key, query], axis=0), key)
        lowers.append(jnp.where(masks[c][0], both[:CHUNK] * beta[rows[c], h : h + 1], 0.0))
        scores.append(jnp.where(masks[c][1], both[CHUNK:], 0.0).astype(BF16))
    solved = unit_inverses(lowers)
    parts = []
    for (c, h), inverse, score in zip(items, solved, scores):
        key = k[h][0][rows[c]]
        value = act[rows[c], 2 * hid + h * HEAD_DIM : 2 * hid + (h + 1) * HEAD_DIM]
        b = beta[rows[c], h : h + 1]
        enter, leave = aux[rows[c], 3:4], aux[rows[c], 4:5]
        inverse = inverse.astype(BF16)
        wu = mul(inverse, jnp.concatenate([key * b, value * b], axis=1))
        ew, u = wu[:, :HEAD_DIM] * enter, wu[:, HEAD_DIM:]
        phi_b = t_mul(key * leave, jnp.concatenate([ew, u], axis=1))
        parts.append((ew, u, phi_b[:, :HEAD_DIM].astype(BF16), phi_b[:, HEAD_DIM:]))
        t_ref[c, h] = inverse
        p_ref[c, h] = score
        ew_ref[c, h] = ew.astype(BF16)
        phi_ref[c, h] = parts[-1][2]
    for h in range(heads):
        s = state[h]
        for c in range(GROUP):
            low = s.astype(BF16)
            s_ref[c, h] = low
            _, _, phi, b_term = parts[c * heads + h]
            keep = aux[(c + 1) * CHUNK - 1 : (c + 1) * CHUNK, 3:4]
            s = s * keep - mul(phi, low) + b_term
        state[h] = s
    gain = gain_ref[...]
    for (c, h), (ew, u, _, _), score in zip(items, parts, scores):
        enter = aux[rows[c], 3:4]
        from_state = mul(jnp.concatenate([ew, q[h][0][rows[c]] * enter], axis=0), s_ref[c, h])
        d = (u - from_state[:CHUNK]).astype(BF16)
        d_ref[c, h] = d
        o = from_state[CHUNK:] + mul(score, d)
        cols = slice(h * HEAD_DIM, (h + 1) * HEAD_DIM)
        o_ref[rows[c], cols] = o
        normed = o * lax.rsqrt(jnp.mean(o * o, axis=-1, keepdims=True) + 1e-5) * gain
        gate = pre_ref[rows[c], 3 * hid + h * HEAD_DIM : 3 * hid + (h + 1) * HEAD_DIM]
        mixed_ref[rows[c], cols] = (normed * (gate * jax.nn.sigmoid(gate))).astype(BF16)

    @pl.when(grid_step == last_step)
    def _():
        for p in range(1, cot_parts):
            cots.pass_on(p)
        pl.loop(1, lines - 1)(hop_step)
        held.wait()
        for p in range(cot_parts):
            cots.arrive(p)
            cots.sent(p)
        last()


def mixer_bwd_kernel(
    lines, steps,
    hg_ref, wout_ref, pre_ref, halo_ref, aux_ref, docrow_ref, conv_ref, gain_ref,
    o_ref, t_ref, phi_ref, s_ref, p_ref, d_ref, ew_ref, terms_ref,
    dpre_ref, dconv_ref, dgain_ref, sum_ref,
    ext, later, dstate, own, own_s, *dp_refs,
):
    heads = o_ref.shape[1] // HEAD_DIM
    hid = heads * HEAD_DIM
    grid_step = pl.program_id(0)
    side = lax.axis_index("dp") % 2
    line = DpScatter(lines, lambda j: terms_ref.at[j], lambda place: own.at[place], dp_refs, True)
    fetch = lambda place: pltpu.make_async_copy(terms_ref.at[2 * place + side], own.at[place], own_s.at[place])

    @pl.when(grid_step == 0)
    def _():
        greet_line(lines)
        for place in range(lines):
            fetch(place).start()
        for k in range(line.pieces):
            for d in range((lines + 1) // 2):
                for place in sorted({lines - 1 - d, d}, reverse=True):
                    line.offer(place, k)
        for place in range(lines):
            fetch(place).wait()

    per_step = 5
    base = 5

    def point(i):
        n = grid_step * per_step + i - base
        line.point(n)

    point(0)

    @pl.when(pl.program_id(0) == 0)
    def _():
        later[STEP:, :] = jnp.zeros((PAD, 3 * hid), F32)
        dstate[...] = jnp.zeros_like(dstate)
        dconv_ref[...] = jnp.zeros_like(dconv_ref)
        dgain_ref[...] = jnp.zeros_like(dgain_ref)

    mixed_grad = dot(hg_ref[...], wout_ref[...], ((1,), (0,))).astype(BF16).astype(F32)
    aux = aux_ref[...]
    conv = conv_ref[...]
    pre = pre_ref[:, : 3 * hid]
    ext[0:PAD, :] = halo_ref[:, : 3 * hid]
    ext[PAD:, :] = pre
    lin = conv_parts(pre, ext, conv, aux)
    sig = jax.nn.sigmoid(lin)
    act = lin * sig
    dsilu = sig * (1.0 + lin * (1.0 - sig))
    scale = HEAD_DIM**-0.5
    q = unit_rows(act[:, :hid], 1.0)
    k = unit_rows(act[:, hid : 2 * hid], 1.0)
    beta = jax.nn.sigmoid(pre_ref[:, 4 * hid : 4 * hid + 8])
    masks = chunk_masks(aux, docrow_ref[0])
    gain = gain_ref[...]

    items = [(c, h) for c in range(GROUP) for h in range(heads)]
    rows = [slice(c * CHUNK, (c + 1) * CHUNK) for c in range(GROUP)]
    cols = [slice(h * HEAD_DIM, (h + 1) * HEAD_DIM) for h in range(heads)]

    d_out, d_gain = [], jnp.zeros((1, HEAD_DIM), F32)
    for h in range(heads):
        o = o_ref[:, cols[h]]
        inv = lax.rsqrt(jnp.mean(o * o, axis=-1, keepdims=True) + 1e-5)
        unit = o * inv
        gate = pre_ref[:, 3 * hid + h * HEAD_DIM : 3 * hid + (h + 1) * HEAD_DIM]
        s = jax.nn.sigmoid(gate)
        dm = mixed_grad[:, cols[h]]
        dpre_ref[:, 3 * hid + h * HEAD_DIM : 3 * hid + (h + 1) * HEAD_DIM] = (
            dm * unit * gain * (s * (1.0 + gate * (1.0 - s)))
        ).astype(BF16)
        dn = dm * (gate * s)
        d_gain = d_gain + jnp.sum(dn * unit, axis=0, keepdims=True)
        du = dn * gain
        d_out.append(inv * (du - unit * jnp.mean(du * unit, axis=-1, keepdims=True)))
    dgain_ref[...] += d_gain
    point(1)

    first = []
    for c, h in items:
        enter = aux[rows[c], 3:4]
        do = d_out[h][rows[c]].astype(BF16)
        eq = (q[h][0][rows[c]] * (enter * scale)).astype(BF16)
        x = t_mul(p_ref[c, h], do)
        c_term = t_mul(
            jnp.concatenate([eq, -ew_ref[c, h]], axis=0),
            jnp.concatenate([do, x.astype(BF16)], axis=0),
        )
        first.append((do, x, c_term))
    point(2)
    after = {}
    for h in range(heads):
        ds = dstate[h]
        for c in reversed(range(GROUP)):
            low = ds.astype(BF16)
            after[c, h] = low
            keep = aux[(c + 1) * CHUNK - 1 : (c + 1) * CHUNK, 3:4]
            ds = ds * keep - t_mul(phi_ref[c, h], low) + first[c * heads + h][2]
        dstate[h] = ds
    db_cols = []
    grads = {}
    point(3)
    for (c, h), (do, x, _) in zip(items, first):
        enter, leave = aux[rows[c], 3:4], aux[rows[c], 4:5]
        b = beta[rows[c], h : h + 1]
        key, query = k[h][0][rows[c]], q[h][0][rows[c]] * scale
        value = act[rows[c], 2 * hid + h * HEAD_DIM : 2 * hid + (h + 1) * HEAD_DIM]
        ds = after[c, h]
        d, s = d_ref[c, h], s_ref[c, h]
        dr = t_mul(t_ref[c, h], x + mul(key * leave, ds))
        stacked = jnp.concatenate([do, dr.astype(BF16)], axis=0)
        with_d = mul_t(stacked, d)
        with_s = mul_t(stacked, s) * jnp.concatenate([enter, enter], axis=0)
        dp = jnp.where(masks[c][1], with_d[:CHUNK], 0.0)
        da = jnp.where(masks[c][0], -with_d[CHUNK:], 0.0)
        pair = jnp.concatenate([dp, da], axis=0).astype(BF16)
        with_k = mul(pair, key)
        dq = with_s[:CHUNK] + with_k[:CHUNK]
        row_k = with_k[CHUNK:] - with_s[CHUNK:]
        dk = b * row_k + t_mul(pair, jnp.concatenate([query, key * b], axis=0))
        dk = dk + mul_t(d, ds) * leave
        db = jnp.sum(dr * value + key * row_k, axis=-1, keepdims=True)
        grads[c, h] = (dq * scale, dk, dr * b, db * b * (1.0 - b))
    point(4)
    for h in range(heads):
        whole = [jnp.concatenate([grads[c, h][i] for c in range(GROUP)], axis=0) for i in range(4)]
        for i, unit in ((0, q[h]), (1, k[h])):
            y, inv = unit
            grad = inv * (whole[i] - y * jnp.sum(y * whole[i], axis=-1, keepdims=True))
            at = slice(i * hid + h * HEAD_DIM, i * hid + (h + 1) * HEAD_DIM)
            later[0:STEP, at] = grad * dsilu[:, at]
        at = slice(2 * hid + h * HEAD_DIM, 2 * hid + (h + 1) * HEAD_DIM)
        later[0:STEP, at] = whole[2] * dsilu[:, at]
        db_cols.append(whole[3])
    lane = lax.broadcasted_iota(jnp.int32, (STEP, HEAD_DIM), 1)
    tail = jnp.zeros((STEP, HEAD_DIM), F32)
    for h in range(heads):
        tail = jnp.where(lane == h, db_cols[h], tail)
    dpre_ref[:, 4 * hid :] = tail.astype(BF16)
    dlin = later[0:STEP, :]
    dpre = dlin * conv[3:4, :]
    taps = [jnp.sum(dlin * pre, axis=0, keepdims=True)]
    for offset in range(1, 4):
        ahead = later[offset : offset + STEP, :]
        dpre = dpre + ahead * aux[:, 4 + offset : 5 + offset] * conv[3 - offset : 4 - offset, :]
        behind = ext[PAD - offset : PAD - offset + STEP, :] * aux[:, offset - 1 : offset]
        taps.append(jnp.sum(dlin * behind, axis=0, keepdims=True))
    dpre_ref[:, : 3 * hid] = dpre.astype(BF16)
    for offset in range(4):
        dconv_ref[3 - offset : 4 - offset, :] += taps[offset]
    later[STEP:, :] = later[0:PAD, :]

    @pl.when(grid_step == steps - 1)
    def _():
        pl.loop(max(steps * per_step - base, 0), line.points)(line.point)
        line.finish(sum_ref)
        line.close()


def mixer_fwd(x_rows, weights, aux, docrow, conv, gain, cotangent, ff_mine, n_dp, count, parts=2):
    hid = conv.shape[1] // 3
    length, width = x_rows.shape[0], weights.shape[1] - hid
    heads, chunks = hid // HEAD_DIM, length // CHUNK
    lines, dma = n_dp // 2, lambda *shape: pltpu.SemaphoreType.DMA(shape)
    anywhere = pl.BlockSpec(memory_space=pl.ANY)
    rows = lambda n: pl.BlockSpec((STEP, n), lambda i: (i, 0))
    whole = lambda a: pl.BlockSpec(a.shape, lambda i: (0,) * a.ndim)
    square = pl.BlockSpec((GROUP, heads, CHUNK, HEAD_DIM), lambda i: (i, 0, 0, 0))
    squares = jax.ShapeDtypeStruct((chunks, heads, CHUNK, HEAD_DIM), BF16)
    return pl.pallas_call(
        partial(mixer_fwd_kernel, lines, count),
        grid=(length // STEP,),
        in_specs=[
            rows(x_rows.shape[1]), whole(weights), rows(aux.shape[1]),
            pl.BlockSpec((1, GROUP, CHUNK), lambda i: (i, 0, 0)), whole(conv), whole(gain),
            anywhere, anywhere,
        ],
        out_specs=[rows(width), rows(hid), rows(hid)] + [square] * 6 + [anywhere] * 2,
        out_shape=[
            jax.ShapeDtypeStruct((length, width), F32),
            jax.ShapeDtypeStruct((length, hid), BF16),
            jax.ShapeDtypeStruct((length, hid), F32),
        ]
        + [squares] * 6
        + [
            jax.ShapeDtypeStruct((count, *cotangent.shape), BF16),
            jax.ShapeDtypeStruct((n_dp, *ff_mine.shape), BF16),
        ],
        scratch_shapes=[
            pltpu.VMEM((PAD + STEP, 3 * hid), F32),
            pltpu.VMEM((heads, HEAD_DIM, HEAD_DIM), F32),
            dma(lines), dma(lines), dma(lines), dma(n_dp), dma(2),
        ]
        + HeadGather.scratch(count, parts),
        compiler_params=pltpu.CompilerParams(vmem_limit_bytes=VMEM_LIMIT, has_side_effects=True, collective_id=3),
        name="mixer_fwd",
    )(x_rows, weights, aux, docrow, conv, gain, cotangent, ff_mine)


def mixer_bwd(hg_rows, weights, aux, docrow, conv, gain, saved, terms):
    pre, o, t, phi, s, p, d, ew = saved
    length, width = pre.shape
    hid = conv.shape[1] // 3
    heads, steps = hid // HEAD_DIM, length // STEP
    last = steps - 1
    n_dp, block, wide = terms.shape
    lines = n_dp // 2
    rows = lambda n: pl.BlockSpec((STEP, n), lambda i: (last - i, 0))
    whole = lambda a: pl.BlockSpec(a.shape, lambda i: (0,) * a.ndim)
    square = pl.BlockSpec((GROUP, heads, CHUNK, HEAD_DIM), lambda i: (last - i, 0, 0, 0))
    halo = pl.BlockSpec(
        (PAD, width), lambda i: (jnp.maximum((last - i) * (STEP // PAD) - 1, 0), 0)
    )
    return pl.pallas_call(
        partial(mixer_bwd_kernel, lines, steps),
        grid=(steps,),
        in_specs=[
            rows(hg_rows.shape[1]), pl.BlockSpec((weights.shape[0], hid), lambda i: (0, 0)), rows(width), halo, rows(aux.shape[1]),
            pl.BlockSpec((1, GROUP, CHUNK), lambda i: (last - i, 0, 0)), whole(conv), whole(gain),
            rows(hid),
        ]
        + [square] * 6
        + [pl.BlockSpec(memory_space=pl.ANY)],
        out_specs=[
            rows(width),
            pl.BlockSpec((4, 3 * hid), lambda i: (0, 0)),
            pl.BlockSpec((1, HEAD_DIM), lambda i: (0, 0)),
            pl.BlockSpec((block, wide), lambda i: (0, 0)),
        ],
        out_shape=[
            jax.ShapeDtypeStruct((length, width), BF16),
            jax.ShapeDtypeStruct((4, 3 * hid), F32),
            jax.ShapeDtypeStruct((1, HEAD_DIM), F32),
            jax.ShapeDtypeStruct((block, wide), F32),
        ],
        scratch_shapes=[
            pltpu.VMEM((PAD + STEP, 3 * hid), F32),
            pltpu.VMEM((STEP + PAD, 3 * hid), F32),
            pltpu.VMEM((heads, HEAD_DIM, HEAD_DIM), F32),
            pltpu.VMEM((lines, block, wide), BF16),
            pltpu.SemaphoreType.DMA((lines,)),
        ]
        + DpScatter.scratch(lines, block, wide),
        compiler_params=pltpu.CompilerParams(vmem_limit_bytes=VMEM_LIMIT, has_side_effects=True, collective_id=4),
        name="mixer_bwd",
    )(hg_rows, weights, pre, pre, aux, docrow, conv, gain, o, t, phi, s, p, d, ew, terms)


MESH = pl.DeviceIdType.MESH


def remote(src, dst, sent, landed, axis, to):
    return pltpu.make_async_remote_copy(
        src_ref=src, dst_ref=dst, send_sem=sent, recv_sem=landed,
        device_id={axis: to}, device_id_type=MESH,
    )


def shard_line(lines, own, out, sems):
    right_s, left_s, over_s, landed, local = sems
    me = lax.axis_index("dp")
    spot, side = me // 2, me % 2
    slot = lambda place: 2 * place + side
    across = me + 1 - 2 * side

    def hop(step, where):
        return (spot - step, me + 2, right_s) if where == 0 else (spot + step, me - 2, left_s)

    def going(step, where):
        place, to, sent = hop(step, where)
        src = out.at[slot(place)] if not isinstance(step, int) or step else own
        return remote(src, out.at[slot(place)], sent.at[step], landed.at[slot(place)], "dp", to)

    def goes(step, where):
        if where == 0:
            return jnp.logical_and(spot - step >= 0, spot + 1 < lines)
        return jnp.logical_and(spot + step < lines, spot >= 1)

    def over(place):
        return remote(out.at[slot(place)], out.at[slot(place)], over_s.at[place], landed.at[slot(place)], "dp", across)

    def first():
        pltpu.make_async_copy(own, out.at[me], local).start()
        remote(own, out.at[me], over_s.at[spot], landed.at[me], "dp", across).start()
        for where in (0, 1):
            pl.when(goes(0, where))(lambda where=where: going(0, where).start())

    def arrive(step, place):
        @pl.when(jnp.logical_and(place >= 0, place < lines))
        def _():
            over(place).wait_recv()
            over(place).start()

    def hop_step(step):
        for where in (0, 1):
            place = spot - step - 1 if where == 0 else spot + step + 1
            arrive(step, place)
            if isinstance(step, int) and step + 1 >= lines - 1:
                continue
            pl.when(jnp.logical_and(goes(step + 1, where), step + 1 < lines - 1))(
                lambda where=where: going(step + 1, where).start()
            )

    def last():
        pltpu.make_async_copy(own, out.at[me], local).wait()

        @pl.loop(0, lines)
        def _(place):
            there = 2 * place + 1 - side
            remote(out.at[there], out.at[there], over_s.at[place], landed.at[there], "dp", across).wait_recv()
            over(place).wait_send()

        @pl.loop(0, lines - 1)
        def _(step):
            for where in (0, 1):
                pl.when(goes(step, where))(lambda where=where: going(step, where).wait_send())

    return first, hop_step, last


def greet(lines, count):
    barrier = pltpu.get_barrier_semaphore()
    me = lax.axis_index("dp")
    spot, across = me // 2, me + 1 - 2 * (me % 2)

    def tell(axis, to):
        pl.semaphore_signal(barrier, 1, device_id={axis: to}, device_id_type=MESH)

    tell("dp", across)
    pl.when(spot >= 1)(lambda: tell("dp", me - 2))
    pl.when(spot + 1 < lines)(lambda: tell("dp", me + 2))
    head = lax.axis_index("head")
    tell("head", head + 1 - 2 * (head % 2))
    for f in range(1, count // 2):
        tell("head", lax.rem(head + 2 * f, count))
    beside = jnp.minimum(spot, 1) + jnp.minimum(lines - 1 - spot, 1)
    pl.semaphore_wait(barrier, 1 + count // 2 + beside)


def greet_line(lines):
    barrier = pltpu.get_barrier_semaphore()
    me = lax.axis_index("dp")
    spot = me // 2

    def tell(to):
        pl.semaphore_signal(barrier, 1, device_id={"dp": to}, device_id_type=MESH)

    tell(me + 1 - 2 * (me % 2))
    pl.when(spot >= 1)(lambda: tell(me - 2))
    pl.when(spot + 1 < lines)(lambda: tell(me + 2))
    pl.semaphore_wait(barrier, 1 + jnp.minimum(spot, 1) + jnp.minimum(lines - 1 - spot, 1))


def start_kernel(lines, count, parts, tok_ref, gain_ref, w_ref, rows_ref, wall_ref, mine,
                 right_s, left_s, over_s, landed, local, far_s, pair_s, fwd_s, got, keep_s):
    greet(lines, count)
    first, hop_step, last = shard_line(lines, w_ref, wall_ref, (right_s, left_s, over_s, landed, local.at[0]))
    first()
    me = lax.axis_index("head")
    pair = me + 1 - 2 * (me % 2)
    fars = [lax.rem(me + 2 * f, count) for f in range(1, count // 2)]
    size = tok_ref.shape[0] // parts
    span = lambda p: pl.ds(p * size, size)

    def block(owner, p):
        return rows_ref.at[owner, span(p)]

    for p in range(parts):
        x = tok_ref[p * size : (p + 1) * size, :].astype(F32)
        inv = lax.rsqrt(jnp.mean(x * x, axis=-1, keepdims=True) + 1e-6)
        mine[p * size : (p + 1) * size, :] = (x * inv * gain_ref[...]).astype(BF16)
        for f, far in enumerate(fars):
            remote(mine.at[span(p)], block(me, p), far_s.at[f, p], got.at[me, p], "head", far).start()
        remote(mine.at[span(p)], block(me, p), pair_s.at[p], got.at[me, p], "head", pair).start()
        pltpu.make_async_copy(mine.at[span(p)], block(me, p), keep_s.at[p]).start()

    def pass_on(p):
        for f, far in enumerate(fars):
            moved = remote(block(far, p), block(far, p), fwd_s.at[f, p], got.at[far, p], "head", pair)
            moved.wait_recv()
            moved.start()

    for i in range(parts):
        pass_on(i)
        if i < lines - 1:
            hop_step(i)
    if lines - 1 > parts:
        pl.loop(parts, lines - 1)(hop_step)
    last()
    for p in range(parts):
        remote(mine.at[span(p)], block(pair, p), pair_s.at[p], got.at[pair, p], "head", pair).wait()
        pltpu.make_async_copy(mine.at[span(p)], block(me, p), keep_s.at[p]).wait()
        for f, far in enumerate(fars):
            remote(mine.at[span(p)], block(me, p), far_s.at[f, p], got.at[me, p], "head", far).wait_send()
            there = lax.rem(pair + 2 * (f + 1), count)
            remote(block(far, p), block(there, p), fwd_s.at[f, p], got.at[there, p], "head", pair).wait()


def start(tokens, gain, mine, n_dp, n_head, parts=4):
    rows, width = tokens.shape
    lines, far = n_dp // 2, n_head // 2 - 1
    dma = lambda *shape: pltpu.SemaphoreType.DMA(shape)
    anywhere = pl.BlockSpec(memory_space=pl.ANY)
    vmem = pl.BlockSpec(memory_space=pltpu.VMEM)
    return pl.pallas_call(
        partial(start_kernel, lines, n_head, parts),
        out_shape=[jax.ShapeDtypeStruct((n_head, rows, width), BF16),
                   jax.ShapeDtypeStruct((n_dp, *mine.shape), BF16)],
        in_specs=[vmem, vmem, anywhere],
        out_specs=[anywhere, anywhere],
        scratch_shapes=[
            pltpu.VMEM((rows, width), BF16),
            dma(lines), dma(lines), dma(lines), dma(n_dp), dma(1),
            dma(far, parts), dma(parts), dma(far, parts), dma(n_head, parts), dma(parts),
        ],
        compiler_params=pltpu.CompilerParams(vmem_limit_bytes=VMEM_LIMIT, has_side_effects=True, collective_id=0),
        name="start",
    )(tokens, gain, mine)


def when(condition):
    return pl.when(condition) if not isinstance(condition, bool) else (lambda f: f() if condition else None)


class HeadScatter:
    def __init__(self, count, refs):
        self.count = count
        (self.out, self.near, self.onward, self.far, self.own,
         self.out_s, self.near_r, self.onward_s, self.far_r) = refs
        self.me = lax.axis_index("head")
        self.side, self.place = self.me % 2, self.me // 2
        self.pair = self.me + 1 - 2 * self.side
        self.parts, self.depth, self.size = self.near.shape[0], self.own.shape[0], self.own.shape[1]

    @staticmethod
    def scratch(count, parts, size, width, depth):
        half = count // 2
        return [
            pltpu.VMEM((2, 2, half, size, width), BF16),
            pltpu.VMEM((parts, half, size, width), BF16),
            pltpu.VMEM((2, half - 1, size, width), BF16),
            pltpu.VMEM((parts, half - 1, size, width), BF16),
            pltpu.VMEM((depth, size, width), F32),
            pltpu.SemaphoreType.DMA((2,)),
            pltpu.SemaphoreType.DMA((parts,)),
            pltpu.SemaphoreType.DMA((2, half - 1)),
            pltpu.SemaphoreType.DMA((parts, half - 1)),
        ]

    def _near(self, p):
        slot = p % 2
        return remote(self.out.at[slot, 1 - self.side], self.near.at[p], self.out_s.at[slot], self.near_r.at[p], "head", self.pair)

    def _far(self, p, f):
        slot = p % 2
        to = lax.rem(self.me + 2 * (f + 1), self.count)
        return remote(self.onward.at[slot, f], self.far.at[p, f], self.onward_s.at[slot, f], self.far_r.at[p, f], "head", to)

    def offer(self, p, total):
        when(p >= 2)(lambda: self._near(p - 2).wait_send())
        for owner in range(self.count):
            self.out[p % 2, owner % 2, owner // 2] = total[owner * self.size : (owner + 1) * self.size].astype(BF16)
        self._near(p).start()

    def turn(self, p):
        slot, half = p % 2, self.count // 2
        self._near(p).wait_recv()
        both = lambda i: self.out[slot, self.side, i].astype(F32) + self.near[p, i].astype(F32)
        for f in range(half - 1):
            when(p >= 2)(lambda f=f: self._far(p - 2, f).wait_send())
            self.onward[slot, f] = both(lax.rem(self.place + f + 1, half)).astype(BF16)
            self._far(p, f).start()
        self.own[p % self.depth] = both(self.place)

    def take(self, p):
        total = self.own[p % self.depth]
        for f in range(self.count // 2 - 1):
            self._far(p, f).wait_recv()
            total = total + self.far[p, f].astype(F32)
        return total

    def close(self):
        for p in range(max(self.parts - 2, 0), self.parts):
            self._near(p).wait_send()
            for f in range(self.count // 2 - 1):
                self._far(p, f).wait_send()


class HeadGather:
    def __init__(self, count, parts, own, block, refs):
        self.count, self.parts, self.own, self.block = count, parts, own, block
        self.far_s, self.pair_s, self.fwd_s, self.got = refs
        self.me = lax.axis_index("head")
        self.pair = self.me + 1 - 2 * (self.me % 2)

    @staticmethod
    def scratch(count, parts):
        far = count // 2 - 1
        return [pltpu.SemaphoreType.DMA(s) for s in ((far, parts), (parts,), (far, parts), (count, parts))]

    def _fars(self, base):
        return [(f, lax.rem(base + 2 * (f + 1), self.count)) for f in range(self.count // 2 - 1)]

    def _far(self, p, f, far):
        return remote(self.own(p), self.block(self.me, p), self.far_s.at[f, p], self.got.at[self.me, p], "head", far)

    def _pair(self, p):
        return remote(self.own(p), self.block(self.me, p), self.pair_s.at[p], self.got.at[self.me, p], "head", self.pair)

    def _on(self, p, f, owner):
        return remote(self.block(owner, p), self.block(owner, p), self.fwd_s.at[f, p], self.got.at[owner, p], "head", self.pair)

    def send(self, p):
        for f, far in self._fars(self.me):
            self._far(p, f, far).start()
        self._pair(p).start()

    def pass_on(self, p):
        for f, far in self._fars(self.me):
            self._on(p, f, far).wait_recv()
            self._on(p, f, far).start()

    def arrive(self, p):
        remote(self.own(p), self.block(self.pair, p), self.pair_s.at[p], self.got.at[self.pair, p], "head", self.pair).wait_recv()
        for f, far in self._fars(self.pair):
            self._on(p, f, far).wait_recv()

    def sent(self, p):
        self._pair(p).wait_send()
        for f, far in self._fars(self.me):
            self._far(p, f, far).wait_send()
            self._on(p, f, far).wait_send()


def greet_head(count):
    barrier = pltpu.get_barrier_semaphore()
    me = lax.axis_index("head")
    for to in [me + 1 - 2 * (me % 2)] + [lax.rem(me + 2 * f, count) for f in range(1, count // 2)]:
        pl.semaphore_signal(barrier, 1, device_id={"head": to}, device_id_type=MESH)
    pl.semaphore_wait(barrier, count // 2)


def mid_kernel(count, parts, mixed_ref, weights_ref, tok_ref, gain_ref, cot_ref, ff_ref,
               out_ref, grad_ref, hg_ref, gain_grad_ref, terms_ref, *scratch):
    scratch = list(scratch)
    take = lambda n: [scratch.pop(0) for _ in range(n)]
    att_refs, down_refs, back_refs = take(9), take(9), take(9)
    second_sems, hg_sems = take(4), take(4)
    out_t, second, hidden, hg_own, total, loads, keep_s = scratch
    size, width = tok_ref.shape[1:]
    ff = ff_ref.shape[1] // 3
    me = lax.axis_index("head")
    load = pltpu.make_async_copy(weights_ref.at[:, : out_t.shape[1]], out_t, loads.at[0])
    load.start()
    greet_head(count)
    att, down, back = (HeadScatter(count, r) for r in (att_refs, down_refs, back_refs))
    here = lambda owner, p: second.at[p, owner]
    seconds = HeadGather(count, parts, lambda p: here(me, p), here, second_sems)
    there = lambda owner, p: hg_ref.at[owner, p]
    hgs = HeadGather(count, parts, lambda p: hg_own.at[p], there, hg_sems)
    keep = lambda p: pltpu.make_async_copy(hg_own.at[p], there(me, p), keep_s.at[p])
    total[...] = jnp.zeros_like(total)
    gain_grad_ref[...] = jnp.zeros_like(gain_grad_ref)
    load.wait()

    def within(p, stage):
        pl.when(jnp.logical_and(p >= 0, p < parts))(lambda: stage(p))

    def attend(p):
        rows = mixed_ref[:, p].reshape(count * size, mixed_ref.shape[3])
        att.offer(p, dot(rows, out_t[...], ((1,), (1,))))

    def norm(p):
        rows = tok_ref[p].astype(F32) + att.take(p)
        hidden[p] = rows
        inv = lax.rsqrt(jnp.mean(rows * rows, axis=-1, keepdims=True) + 1e-6)
        second[p, me] = (rows * inv * gain_ref[...]).astype(BF16)
        seconds.send(p)

    def feed(p):
        seconds.arrive(p)
        rows = second[p].reshape(count * size, width)
        both = dot(rows, ff_ref[:, : 2 * ff], ((1,), (0,)))
        gate, up = both[:, :ff], both[:, ff:]
        sig = jax.nn.sigmoid(gate)
        act = gate * sig
        middle = (act * up).astype(BF16)
        down.offer(p, dot(middle, ff_ref[:, 2 * ff :], ((1,), (1,))))
        cot = cot_ref[:, p].reshape(count * size, width)
        grad = dot(cot, ff_ref[:, 2 * ff :], ((1,), (0,))).astype(BF16).astype(F32)
        pair = jnp.concatenate(
            [(grad * up * sig * (1.0 + gate * (1.0 - sig))).astype(BF16), (grad * act).astype(BF16)], axis=1
        )
        back.offer(p, dot(pair, ff_ref[:, : 2 * ff], ((1,), (1,))))
        total[:, : 2 * ff] += dot(rows, pair, ((0,), (0,)))
        total[:, 2 * ff :] += dot(cot, middle, ((0,), (0,)))

    def turn(p):
        down.turn(p)
        back.turn(p)

    def finish(p):
        rows = hidden[p]
        out_ref[p] = (rows + down.take(p)).astype(BF16)
        second_grad = back.take(p).astype(BF16).astype(F32)
        inv = lax.rsqrt(jnp.mean(rows * rows, axis=-1, keepdims=True) + 1e-6)
        scaled = second_grad * gain_ref[...]
        mean = jnp.mean(scaled * rows, axis=-1, keepdims=True)
        grad = cot_ref[me, p].astype(F32) + inv * scaled - rows * (inv * inv * inv * mean)
        grad_ref[p] = grad
        gain_grad_ref[...] += jnp.sum(second_grad * rows * inv, axis=0, keepdims=True)
        hg_own[p] = grad.astype(BF16)
        hgs.send(p)
        keep(p).start()

    @pl.loop(0, parts + 4)
    def _(step):
        i = step - 1
        within(i + 1, attend)
        within(i, norm)
        within(i + 1, att.turn)
        within(i - 1, feed)
        within(i, seconds.pass_on)
        within(i - 1, turn)
        within(i - 2, finish)
        within(i - 3, hgs.pass_on)

    terms_ref[...] = total[...].astype(BF16)

    @pl.loop(0, parts)
    def _(p):
        hgs.arrive(p)
        keep(p).wait()
        hgs.sent(p)
        seconds.sent(p)

    for s in (att, down, back):
        s.close()


def mid(mixed, weights, tokens, gain, cot_rows, ff_set, count, parts=8):
    rows, width = tokens.shape
    size, hid = rows // parts, mixed.shape[1]
    anywhere = pl.BlockSpec(memory_space=pl.ANY)
    vmem = pl.BlockSpec(memory_space=pltpu.VMEM)
    scatter = HeadScatter.scratch(count, parts, size, width, 2)
    out, grad, hg, gain_grad, terms = pl.pallas_call(
        partial(mid_kernel, count, parts),
        out_shape=[
            jax.ShapeDtypeStruct((parts, size, width), BF16),
            jax.ShapeDtypeStruct((parts, size, width), F32),
            jax.ShapeDtypeStruct((count, parts, size, width), BF16),
            jax.ShapeDtypeStruct((1, width), F32),
            jax.ShapeDtypeStruct(ff_set.shape, BF16),
        ],
        in_specs=[vmem, anywhere] + [vmem] * 4,
        out_specs=[vmem, vmem, anywhere, vmem, vmem],
        scratch_shapes=scatter * 3
        + HeadGather.scratch(count, parts) * 2
        + [
            pltpu.VMEM((width, hid), BF16),
            pltpu.VMEM((parts, count, size, width), BF16),
            pltpu.VMEM((parts, size, width), F32),
            pltpu.VMEM((parts, size, width), BF16),
            pltpu.VMEM(ff_set.shape, F32),
            pltpu.SemaphoreType.DMA((1,)),
            pltpu.SemaphoreType.DMA((parts,)),
        ],
        compiler_params=pltpu.CompilerParams(vmem_limit_bytes=61 * 1024 * 1024, has_side_effects=True, collective_id=2),
        name="mid",
    )(
        mixed.reshape(count, parts, size, hid), weights, tokens.reshape(parts, size, width), gain,
        cot_rows.reshape(count, parts, size, width), ff_set,
    )
    return out.reshape(rows, width), grad.reshape(rows, width), hg.reshape(-1, width), gain_grad, terms


class DpScatter:
    LAG = 2

    def __init__(self, lines, terms, own, refs, by_piece):
        self.lines, self.terms, self.own, self.by_piece = lines, terms, own, by_piece
        self.cross, self.going, self.coming, self.cross_s, self.cross_r, self.go_s, self.come_r = refs
        self.pieces = self.cross_s.shape[1]
        self.size = self.cross.shape[1] // self.pieces
        self.me = lax.axis_index("dp")
        self.spot, self.side = self.me // 2, self.me % 2
        self.across = self.me + 1 - 2 * self.side
        self.items = (lines - 1) * self.pieces
        self.points = self.items + (lines - 1) * self.LAG

    @staticmethod
    def scratch(lines, rows, width):
        pieces = max(1, rows // 32)
        wide = lambda *lead: pltpu.VMEM((*lead, rows, width), BF16)
        sems = lambda *shape: pltpu.SemaphoreType.DMA((*shape, pieces))
        return [
            wide(lines), wide(2, lines), wide(2, lines),
            sems(lines), sems(lines), sems(2, lines), sems(2, lines),
        ]

    def _at(self, k):
        return pl.ds(pl.multiple_of(k * self.size, self.size), self.size)

    def _cross(self, place, k):
        at = self._at(k)
        src = self.terms(2 * place + 1 - self.side).at[at]
        return remote(src, self.cross.at[place, at], self.cross_s.at[place, k], self.cross_r.at[place, k], "dp", self.across)

    def _line(self, way, dest, k):
        to = self.me + 2 if way == 0 else self.me - 2
        at = self._at(k)
        return remote(self.going.at[way, dest, at], self.coming.at[way, dest, at], self.go_s.at[way, dest, k], self.come_r.at[way, dest, k], "dp", to)

    def offer(self, place, k):
        self._cross(place, k).start()

    def _both(self, place, k):
        return self.own(place)[self._at(k), :].astype(F32) + self.cross[place, self._at(k), :].astype(F32)

    def _passes(self, way, dest):
        return dest > self.spot if way == 0 else dest < self.spot

    def _fed(self, way):
        return self.spot >= 1 if way == 0 else self.spot + 1 < self.lines

    def point(self, n):
        for way in (0, 1):
            away = self.spot if way == 0 else self.lines - 1 - self.spot
            item = n - away * self.LAG
            safe = jnp.clip(item, 0, self.items - 1)
            if self.by_piece:
                k, d = safe // (self.lines - 1), safe % (self.lines - 1)
            else:
                d, k = safe // self.pieces, safe % self.pieces
            dest = self.lines - 1 - d if way == 0 else d
            live = jnp.logical_and(item >= 0, item < self.items)

            @pl.when(jnp.logical_and(live, self._passes(way, dest)))
            def _(way=way, dest=dest, k=k):
                at = self._at(k)
                self._cross(dest, k).wait_recv()

                @pl.when(self._fed(way))
                def _():
                    self._line(way, dest, k).wait_recv()
                    self.going[way, dest, at, :] = (self._both(dest, k) + self.coming[way, dest, at, :].astype(F32)).astype(BF16)

                @pl.when(jnp.logical_not(self._fed(way)))
                def _():
                    self.going[way, dest, at, :] = self._both(dest, k).astype(BF16)

                self._line(way, dest, k).start()

    def finish(self, out_ref):
        for k in range(self.pieces):
            at = slice(k * self.size, (k + 1) * self.size)
            self._cross(self.spot, k).wait_recv()
            out_ref[at, :] = self._both(self.spot, k)
            for way in (0, 1):
                @pl.when(self._fed(way))
                def _(way=way, k=k, at=at):
                    self._line(way, self.spot, k).wait_recv()
                    out_ref[at, :] += self.coming[way, self.spot, at, :].astype(F32)

    def close(self):
        @pl.loop(0, self.lines * self.pieces)
        def _(i):
            place, k = i // self.pieces, i % self.pieces
            self._cross(place, k).wait_send()
            for way in (0, 1):
                pl.when(self._passes(way, place))(lambda way=way: self._line(way, place, k).wait_send())


class SmallSum:
    def __init__(self, n_dp, count, shared, refs):
        self.n_dp, self.count, self.shared = n_dp, count, shared
        self.mine, self.theirs, self.half, self.halves, self.a_s, self.a_r, self.b_s, self.b_r = refs
        self.dp, self.head = lax.axis_index("dp"), lax.axis_index("head")

    @staticmethod
    def scratch(n_dp, count, rows, shared):
        return [
            pltpu.VMEM((rows, 128), F32),
            pltpu.VMEM((n_dp, rows, 128), F32),
            pltpu.VMEM((shared, 128), F32),
            pltpu.VMEM((count, shared, 128), F32),
            pltpu.SemaphoreType.DMA((n_dp,)),
            pltpu.SemaphoreType.DMA((n_dp,)),
            pltpu.SemaphoreType.DMA((count,)),
            pltpu.SemaphoreType.DMA((count,)),
        ]

    def _a(self, hop):
        to = lax.rem(self.dp + hop, self.n_dp)
        return remote(self.mine, self.theirs.at[self.dp], self.a_s.at[hop], self.a_r.at[self.dp], "dp", to)

    def _b(self, hop):
        to = lax.rem(self.head + hop, self.count)
        return remote(self.half, self.halves.at[self.head], self.b_s.at[hop], self.b_r.at[self.head], "head", to)

    def start(self):
        self.theirs[self.dp] = self.mine[...]

        @pl.loop(1, self.n_dp)
        def _(hop):
            self._a(hop).start()

    def turn(self, out_ref):
        @pl.loop(1, self.n_dp)
        def _(hop):
            sender = lax.rem(self.dp + self.n_dp - hop, self.n_dp)
            remote(self.mine, self.theirs.at[sender], self.a_s.at[hop], self.a_r.at[sender], "dp", sender).wait_recv()

        total = self.theirs[0]
        for i in range(1, self.n_dp):
            total = total + self.theirs[i]
        out_ref[...] = total
        self.half[...] = total[: self.shared]
        self.halves[self.head] = total[: self.shared]
        for hop in range(1, self.count):
            self._b(hop).start()

    def finish(self, out_ref):
        for hop in range(1, self.count):
            sender = lax.rem(self.head + self.count - hop, self.count)
            remote(self.half, self.halves.at[sender], self.b_s.at[hop], self.b_r.at[sender], "head", sender).wait_recv()
        total = self.halves[0]
        for i in range(1, self.count):
            total = total + self.halves[i]
        out_ref[: self.shared, :] = total

        @pl.loop(1, self.n_dp)
        def _(hop):
            self._a(hop).wait_send()

        for hop in range(1, self.count):
            self._b(hop).wait_send()


def greet_all(n_dp, count):
    barrier = pltpu.get_barrier_semaphore()
    dp, head = lax.axis_index("dp"), lax.axis_index("head")

    @pl.loop(1, n_dp)
    def _(hop):
        pl.semaphore_signal(barrier, 1, device_id={"dp": lax.rem(dp + hop, n_dp)}, device_id_type=MESH)

    for hop in range(1, count):
        pl.semaphore_signal(barrier, 1, device_id={"head": lax.rem(head + hop, count)}, device_id_type=MESH)
    pl.semaphore_wait(barrier, n_dp + count - 2)


def end_kernel(n_dp, count, parts, shared,
               dpre_ref, w_ref, normed_ref, hg_ref, mixed_ref, tok_ref, gain_ref, grad_ref, small_ref,
               in_ref, mix_ref, sum_ref, *scratch):
    scratch = list(scratch)
    take = lambda n: [scratch.pop(0) for _ in range(n)]
    head_refs, dp_refs, small_refs = take(9), take(7), take(8)
    terms, dpre, w, normed, hg, mixed, loads = scratch
    rows, width = tok_ref.shape
    block = terms.shape[1]
    hid = mixed.shape[1]
    greet_all(n_dp, count)
    moves = [pltpu.make_async_copy(s, d, loads.at[i]) for i, (s, d) in enumerate(
        ((dpre_ref, dpre), (w_ref.at[:, hid:], w), (normed_ref, normed), (mixed_ref, mixed), (hg_ref, hg)))]
    for m in moves:
        m.start()
    heads = HeadScatter(count, head_refs)
    lines = n_dp // 2
    side = lax.axis_index("dp") % 2
    line = DpScatter(lines, lambda j: terms.at[j], lambda place: terms.at[2 * place + side], dp_refs, False)
    small = SmallSum(n_dp, count, shared, small_refs)
    size = rows // parts

    def offer(p):
        part = jnp.concatenate([dpre[o * rows + p * size : o * rows + (p + 1) * size, :] for o in range(count)], axis=0)
        heads.offer(p, dot(part, w[...], ((1,), (1,))))

    tiles = width // 256
    per = 256 // block

    def outer(t):
        cols = slice(t * 256, (t + 1) * 256)
        left = dot(normed[:, cols], dpre[...], ((0,), (0,))).astype(BF16)
        right = dot(hg[:, cols], mixed[...], ((0,), (0,))).astype(BF16)
        for b in range(per):
            terms[t * per + b, :, :hid] = right[b * block : (b + 1) * block]
            terms[t * per + b, :, hid:] = left[b * block : (b + 1) * block]
        for place in range(t * per // 2, (t + 1) * per // 2):
            for k in range(line.pieces):
                line.offer(place, k)

    order = [t // 2 if t % 2 else tiles - 1 - t // 2 for t in range(tiles)]
    moves[0].wait()
    moves[1].wait()
    offer(0)
    for m in moves[2:]:
        m.wait()
    for i in range(max(tiles, parts)):
        if i < tiles:
            outer(order[i])
        if i < parts:
            heads.turn(i)
        if i + 1 < parts:
            offer(i + 1)
    small.mine[...] = small_ref[...]
    gain_total = jnp.zeros((1, width), F32)
    gain = gain_ref[...]

    def finish(p):
        at = slice(p * size, (p + 1) * size)
        normed_grad = heads.take(p).astype(BF16).astype(F32)
        x = tok_ref[at, :].astype(F32)
        inv = lax.rsqrt(jnp.mean(x * x, axis=-1, keepdims=True) + 1e-6)
        scaled = normed_grad * gain
        mean = jnp.mean(scaled * x, axis=-1, keepdims=True)
        in_ref[at, :] = grad_ref[at, :] + inv * scaled - x * (inv * inv * inv * mean)
        return jnp.sum(normed_grad * x * inv, axis=0, keepdims=True)

    done = 0
    for i in range(parts):
        for n in range(2):
            if done < line.points:
                line.point(done)
                done += 1
        gain_total = gain_total + finish(i)
    for i in range(width // 128):
        small.mine[i : i + 1, :] = gain_total[:, i * 128 : (i + 1) * 128]
    small.start()
    half = (done + line.points) // 2
    pl.loop(done, half)(line.point)
    small.turn(sum_ref)
    pl.loop(half, line.points)(line.point)
    line.finish(mix_ref)
    small.finish(sum_ref)
    heads.close()
    line.close()


def end(dpre, weights, normed_rows, hg_rows, mixed, tokens, gain, hidden_grad, small, n_dp, count, shared, parts=4):
    rows, width = tokens.shape
    block = width // n_dp
    wide = weights.shape[1]
    anywhere = pl.BlockSpec(memory_space=pl.ANY)
    vmem = pl.BlockSpec(memory_space=pltpu.VMEM)
    like = lambda a: pltpu.VMEM(a.shape, a.dtype)
    return pl.pallas_call(
        partial(end_kernel, n_dp, count, parts, shared),
        out_shape=[
            jax.ShapeDtypeStruct((rows, width), F32),
            jax.ShapeDtypeStruct((block, wide), F32),
            jax.ShapeDtypeStruct(small.shape, F32),
        ],
        in_specs=[anywhere] * 5 + [vmem] * 4,
        out_specs=[vmem] * 3,
        scratch_shapes=HeadScatter.scratch(count, parts, rows // parts, width, parts)
        + DpScatter.scratch(n_dp // 2, block, wide)
        + SmallSum.scratch(n_dp, count, small.shape[0], shared)
        + [pltpu.VMEM((n_dp, block, wide), BF16), like(dpre), pltpu.VMEM((width, dpre.shape[1]), BF16), like(normed_rows), like(hg_rows), like(mixed),
           pltpu.SemaphoreType.DMA((5,))],
        compiler_params=pltpu.CompilerParams(vmem_limit_bytes=VMEM_LIMIT, has_side_effects=True, collective_id=1),
        name="end",
    )(dpre, weights, normed_rows, hg_rows, mixed, tokens, gain, hidden_grad, small)


def doc_tables(lengths, length):
    count = lengths.shape[0]
    index = jnp.arange(count)
    ends = jnp.sum(jnp.where(index[None, :] <= index[:, None], lengths[None, :], 0), axis=1)
    position = jnp.arange(length, dtype=jnp.int32)
    doc = jnp.sum((position[:, None] >= ends[None, :]).astype(jnp.int32), axis=1)
    no_doc = lambda n: jnp.full((n,), -1, jnp.int32)
    before = [jnp.concatenate([no_doc(o), doc[:-o]]) == doc for o in (1, 2, 3)]
    after = [jnp.concatenate([doc[o:], no_doc(o)]) == doc for o in (1, 2, 3)]
    blocks = doc.reshape(-1, CHUNK)
    ending = blocks[:, -1:]
    prior = jnp.concatenate([no_doc(1)[:, None], ending[:-1]], axis=0)
    enter = (blocks == prior).reshape(-1)
    leave = (blocks == ending).reshape(-1)
    columns = before + [enter, leave] + after + [doc]
    aux = jnp.stack([c.astype(F32) for c in columns], axis=1)
    return aux, doc.astype(F32).reshape(-1, GROUP, CHUNK)


def on_device(
    tokens,
    lengths,
    attn_gain,
    w_query,
    w_key,
    w_value,
    w_beta,
    w_gate_out,
    conv_weight,
    head_gain,
    w_out,
    mlp_gain,
    w_mlp_gate,
    w_mlp_up,
    w_down,
    cotangent,
):
    hid, heads, ff = w_query.shape[1], w_beta.shape[1], w_mlp_gate.shape[1]
    n_dp, n_head = lax.axis_size("dp"), lax.axis_size("head")
    beta_wide = jnp.pad(w_beta, ((0, 0), (0, HEAD_DIM - heads)))
    mine = jnp.concatenate([w_out.T, w_query, w_key, w_value, w_gate_out, beta_wide], axis=1)
    normed_rows, first_set = start(tokens, attn_gain[None, :], mine, n_dp, n_head)
    normed_rows = normed_rows.reshape(-1, normed_rows.shape[2])
    first_set = first_set.reshape(-1, first_set.shape[2])
    wide = -(-ff // 256) * 256
    mine = jnp.concatenate(
        [jnp.pad(w, ((0, 0), (0, wide - ff))) for w in (w_mlp_gate, w_mlp_up, w_down.T)], axis=1
    )

    length = normed_rows.shape[0]
    aux, docrow = doc_tables(lengths[0], length)
    conv = jnp.swapaxes(conv_weight.astype(F32), 0, 1).reshape(conv_weight.shape[1], 3 * hid)
    gain = head_gain[None, :]
    pre, mixed, *saved, cot_rows, ff_set = mixer_fwd(
        normed_rows, first_set, aux, docrow, conv, gain, cotangent, mine, n_dp, n_head
    )
    ff_set = ff_set.reshape(-1, ff_set.shape[2])
    output, hidden_grad, hg_rows, mlp_gain_grad, mlp_terms = mid(
        mixed, first_set, tokens, mlp_gain[None, :], cot_rows, ff_set, n_head
    )
    dpre, conv_part, head_gain_grad, mlp_reduced = mixer_bwd(
        hg_rows, first_set, aux, docrow, conv, gain, (pre, *saved),
        mlp_terms.reshape(n_dp, -1, mlp_terms.shape[1]),
    )
    taps = conv_part.shape[0]
    shared = 2 * (tokens.shape[1] // 128) + 8
    small = jnp.concatenate(
        [
            jnp.zeros((tokens.shape[1] // 128, 128), F32),
            mlp_gain_grad.reshape(-1, 128),
            jnp.pad(head_gain_grad, ((0, 7), (0, 0))),
            conv_part.reshape(-1, 128),
        ]
    )
    input_grad, mix_reduced, summed = end(
        dpre, first_set, normed_rows, hg_rows, mixed, tokens, attn_gain[None, :], hidden_grad, small,
        n_dp, n_head, shared,
    )
    gains = summed[: shared - 8].reshape(2, -1)
    conv_grad = jnp.swapaxes(summed[shared:].reshape(taps, 3, hid), 0, 1)
    part = lambda i: mix_reduced[:, (i + 1) * hid : (i + 2) * hid]
    return (
        output,
        input_grad,
        gains[0],
        part(0),
        part(1),
        part(2),
        mix_reduced[:, 5 * hid : 5 * hid + heads],
        part(3),
        conv_grad,
        summed[shared - 8],
        mix_reduced[:, :hid].T,
        gains[1],
        mlp_reduced[:, :ff],
        mlp_reduced[:, wide : wide + ff],
        mlp_reduced[:, 2 * wide : 2 * wide + ff].T,
    )


def solution(mesh):
    rows = P(("dp", "head"), None)
    in_specs = (
        rows,
        P("dp", None),
        P(),
        P("dp", "head"),
        P("dp", "head"),
        P("dp", "head"),
        P("dp", "head"),
        P("dp", "head"),
        P(None, None, "head"),
        P(),
        P("head", "dp"),
        P(),
        P("dp", "head"),
        P("dp", "head"),
        P("head", "dp"),
        rows,
    )
    out_specs = (
        rows,
        rows,
        P(),
        P("dp", "head"),
        P("dp", "head"),
        P("dp", "head"),
        P("dp", "head"),
        P("dp", "head"),
        P(None, None, "head"),
        P(),
        P("head", "dp"),
        P(),
        P("dp", "head"),
        P("dp", "head"),
        P("head", "dp"),
    )
    return jax.shard_map(
        on_device, mesh=mesh, in_specs=in_specs, out_specs=out_specs, check_vma=False
    )
```

```python
from functools import partial

import jax
import jax.numpy as jnp
from jax import lax
from jax.experimental import pallas as pl
from jax.experimental.pallas import tpu as pltpu
from jax.sharding import PartitionSpec as P

HEAD_DIM = 128
CHUNK = 128
GROUP = 4
STEP = CHUNK * GROUP
PAD = 8
F32 = jnp.float32
BF16 = jnp.bfloat16
COT_PARTS = 2
VMEM_LIMIT = 56 * 1024 * 1024


def dot(left, right, dims):
    return lax.dot_general(left, right, (dims, ((), ())), preferred_element_type=F32)


def mul(left, right):
    return dot(left.astype(BF16), right.astype(BF16), ((1,), (0,)))


def mul_t(left, right):
    return dot(left.astype(BF16), right.astype(BF16), ((1,), (1,)))


def t_mul(left, right):
    return dot(left.astype(BF16), right.astype(BF16), ((0,), (0,)))


def unit_inverses(lowers):
    row = lax.broadcasted_iota(jnp.int32, (CHUNK, CHUNK), 0)
    col = lax.broadcasted_iota(jnp.int32, (CHUNK, CHUNK), 1)
    eye = (row == col).astype(F32)
    level = lambda bit: jnp.logical_and(
        (row >> (bit + 1)) == (col >> (bit + 1)), (row >> bit) > (col >> bit)
    )
    first = level(0)
    solved = [eye - jnp.where(first, a, 0.0) for a in lowers]
    for bit in range(1, CHUNK.bit_length() - 1):
        mask = level(bit)
        right = [mul(jnp.where(mask, a, 0.0), t) for a, t in zip(lowers, solved)]
        solved = [t - mul(t, r) for t, r in zip(solved, right)]
    return solved


def conv_parts(pre, ext, conv, aux):
    summed = pre * conv[3:4, :]
    for offset in range(1, 4):
        shifted = ext[PAD - offset : PAD - offset + STEP, :]
        summed = summed + shifted * aux[:, offset - 1 : offset] * conv[3 - offset : 4 - offset, :]
    return summed


def unit_rows(act, scale):
    out = []
    for h in range(act.shape[1] // HEAD_DIM):
        part = act[:, h * HEAD_DIM : (h + 1) * HEAD_DIM]
        inv = lax.rsqrt(jnp.sum(part * part, axis=-1, keepdims=True) + 1e-6)
        out.append((part * inv * scale, inv))
    return out


def chunk_masks(aux, docrow):
    row = lax.broadcasted_iota(jnp.int32, (CHUNK, CHUNK), 0)
    col = lax.broadcasted_iota(jnp.int32, (CHUNK, CHUNK), 1)
    made = []
    for c in range(GROUP):
        same = aux[c * CHUNK : (c + 1) * CHUNK, 8:9] == docrow[c : c + 1, :]
        made.append((jnp.logical_and(same, row > col), jnp.logical_and(same, row >= col)))
    return made


def mixer_fwd_kernel(
    lines, count,
    x_ref, w_ref, aux_ref, docrow_ref, conv_ref, gain_ref, cot_ref, ff_ref,
    pre_ref, mixed_ref, o_ref, t_ref, phi_ref, s_ref, p_ref, d_ref, ew_ref, att_ref, cot_rows, ff_rows,
    ext, state, terms, near, far_terms, near_s, near_r, far_s, far_r, right_s, left_s, over_s, landed, local, *cot_sems,
):
    heads = mixed_ref.shape[1] // HEAD_DIM
    hid = heads * HEAD_DIM
    grid_step, last_step = pl.program_id(0), pl.num_programs(0) - 1
    first, hop_step, arrived, last = shard_line(lines, ff_ref, ff_rows, (right_s, left_s, over_s, landed, local.at[0]))
    cots, held = cot_gather(count, cot_ref, cot_rows, cot_sems, local.at[1])
    cot_parts = cots.parts

    attend = OwnerScatter(count, att_ref, (terms, near, far_terms, near_s, near_r, far_s, far_r))

    @pl.when(grid_step == 0)
    def _():
        greet(lines, count)
        first()
        held.start()
        for p in range(cot_parts):
            cots.send(p)

    @pl.when(grid_step == 2)
    def _():
        hop_step(0)
        cots.pass_on(0)

    @pl.when(pl.program_id(0) == 0)
    def _():
        ext[0:PAD, :] = jnp.zeros((PAD, 3 * hid), F32)
        state[...] = jnp.zeros_like(state)

    pre_ref[...] = dot(x_ref[...], w_ref[:, hid:], ((1,), (0,)))
    pl.when(grid_step >= 1)(lambda: attend.settle(grid_step - 1))
    aux = aux_ref[...]
    conv = conv_ref[...]
    pre = pre_ref[:, : 3 * hid]
    ext[PAD:, :] = pre
    act = conv_parts(pre, ext, conv, aux)
    act = act * jax.nn.sigmoid(act)
    ext[0:PAD, :] = ext[STEP:, :]
    q = unit_rows(act[:, :hid], HEAD_DIM**-0.5)
    k = unit_rows(act[:, hid : 2 * hid], 1.0)
    beta = jax.nn.sigmoid(pre_ref[:, 4 * hid : 4 * hid + 8])
    masks = chunk_masks(aux, docrow_ref[0])

    items = [(c, h) for c in range(GROUP) for h in range(heads)]
    rows = [slice(c * CHUNK, (c + 1) * CHUNK) for c in range(GROUP)]
    lowers, scores = [], []
    for c, h in items:
        key, query = k[h][0][rows[c]], q[h][0][rows[c]]
        both = mul_t(jnp.concatenate([key, query], axis=0), key)
        lowers.append(jnp.where(masks[c][0], both[:CHUNK] * beta[rows[c], h : h + 1], 0.0))
        scores.append(jnp.where(masks[c][1], both[CHUNK:], 0.0).astype(BF16))
    solved = unit_inverses(lowers)
    parts = []
    for (c, h), inverse, score in zip(items, solved, scores):
        key = k[h][0][rows[c]]
        value = act[rows[c], 2 * hid + h * HEAD_DIM : 2 * hid + (h + 1) * HEAD_DIM]
        b = beta[rows[c], h : h + 1]
        enter, leave = aux[rows[c], 3:4], aux[rows[c], 4:5]
        inverse = inverse.astype(BF16)
        wu = mul(inverse, jnp.concatenate([key * b, value * b], axis=1))
        ew, u = wu[:, :HEAD_DIM] * enter, wu[:, HEAD_DIM:]
        phi_b = t_mul(key * leave, jnp.concatenate([ew, u], axis=1))
        parts.append((ew, u, phi_b[:, :HEAD_DIM].astype(BF16), phi_b[:, HEAD_DIM:]))
        t_ref[c, h] = inverse
        p_ref[c, h] = score
        ew_ref[c, h] = ew.astype(BF16)
        phi_ref[c, h] = parts[-1][2]
    for h in range(heads):
        s = state[h]
        for c in range(GROUP):
            low = s.astype(BF16)
            s_ref[c, h] = low
            _, _, phi, b_term = parts[c * heads + h]
            keep = aux[(c + 1) * CHUNK - 1 : (c + 1) * CHUNK, 3:4]
            s = s * keep - mul(phi, low) + b_term
        state[h] = s
    gain = gain_ref[...]
    for (c, h), (ew, u, _, _), score in zip(items, parts, scores):
        enter = aux[rows[c], 3:4]
        from_state = mul(jnp.concatenate([ew, q[h][0][rows[c]] * enter], axis=0), s_ref[c, h])
        d = (u - from_state[:CHUNK]).astype(BF16)
        d_ref[c, h] = d
        o = from_state[CHUNK:] + mul(score, d)
        cols = slice(h * HEAD_DIM, (h + 1) * HEAD_DIM)
        o_ref[rows[c], cols] = o
        normed = o * lax.rsqrt(jnp.mean(o * o, axis=-1, keepdims=True) + 1e-5) * gain
        gate = pre_ref[rows[c], 3 * hid + h * HEAD_DIM : 3 * hid + (h + 1) * HEAD_DIM]
        mixed_ref[rows[c], cols] = (normed * (gate * jax.nn.sigmoid(gate))).astype(BF16)

    attend.offer(grid_step, dot(mixed_ref[...], w_ref[:, :hid], ((1,), (1,))))

    @pl.when(grid_step == last_step)
    def _():
        attend.settle(grid_step)
        for p in range(1, cot_parts):
            cots.pass_on(p)
        pl.loop(1, lines - 1)(hop_step)
        held.wait()
        for p in range(cot_parts):
            cots.arrive(p)
            cots.sent(p)
        arrived()
        attend.finish()
        last()


def mixer_bwd_kernel(
    lines, steps,
    hg_ref, wout_ref, pre_ref, halo_ref, aux_ref, docrow_ref, conv_ref, gain_ref,
    o_ref, t_ref, phi_ref, s_ref, p_ref, d_ref, ew_ref, terms_ref,
    dpre_ref, dconv_ref, dgain_ref, sum_ref,
    ext, later, dstate, own, own_s, *dp_refs,
):
    heads = o_ref.shape[1] // HEAD_DIM
    hid = heads * HEAD_DIM
    grid_step = pl.program_id(0)
    side = lax.axis_index("dp") % 2
    order = lambda n: (n // lines, outside_in(lines, n % lines))
    line = LineScatter(lines, lambda j: terms_ref.at[j], lambda place: own.at[place], dp_refs, order)
    fetch = lambda place: pltpu.make_async_copy(terms_ref.at[2 * place + side], own.at[place], own_s.at[place])

    @pl.when(grid_step == 0)
    def _():
        greet_line(lines)
        for place in range(lines):
            fetch(place).start()
        line.offer_all()
        for place in range(lines):
            fetch(place).wait()

    per_step = 5
    base = 3

    def point(i):
        n = grid_step * per_step + i - base
        line.point(n)

    point(0)

    @pl.when(pl.program_id(0) == 0)
    def _():
        later[STEP:, :] = jnp.zeros((PAD, 3 * hid), F32)
        dstate[...] = jnp.zeros_like(dstate)
        dconv_ref[...] = jnp.zeros_like(dconv_ref)
        dgain_ref[...] = jnp.zeros_like(dgain_ref)

    mixed_grad = dot(hg_ref[...], wout_ref[...], ((1,), (0,))).astype(BF16).astype(F32)
    aux = aux_ref[...]
    conv = conv_ref[...]
    pre = pre_ref[:, : 3 * hid]
    ext[0:PAD, :] = halo_ref[:, : 3 * hid]
    ext[PAD:, :] = pre
    lin = conv_parts(pre, ext, conv, aux)
    sig = jax.nn.sigmoid(lin)
    act = lin * sig
    dsilu = sig * (1.0 + lin * (1.0 - sig))
    scale = HEAD_DIM**-0.5
    q = unit_rows(act[:, :hid], 1.0)
    k = unit_rows(act[:, hid : 2 * hid], 1.0)
    beta = jax.nn.sigmoid(pre_ref[:, 4 * hid : 4 * hid + 8])
    masks = chunk_masks(aux, docrow_ref[0])
    gain = gain_ref[...]

    items = [(c, h) for c in range(GROUP) for h in range(heads)]
    rows = [slice(c * CHUNK, (c + 1) * CHUNK) for c in range(GROUP)]
    cols = [slice(h * HEAD_DIM, (h + 1) * HEAD_DIM) for h in range(heads)]

    d_out, d_gain = [], jnp.zeros((1, HEAD_DIM), F32)
    for h in range(heads):
        o = o_ref[:, cols[h]]
        inv = lax.rsqrt(jnp.mean(o * o, axis=-1, keepdims=True) + 1e-5)
        unit = o * inv
        gate = pre_ref[:, 3 * hid + h * HEAD_DIM : 3 * hid + (h + 1) * HEAD_DIM]
        s = jax.nn.sigmoid(gate)
        dm = mixed_grad[:, cols[h]]
        dpre_ref[:, 3 * hid + h * HEAD_DIM : 3 * hid + (h + 1) * HEAD_DIM] = (
            dm * unit * gain * (s * (1.0 + gate * (1.0 - s)))
        ).astype(BF16)
        dn = dm * (gate * s)
        d_gain = d_gain + jnp.sum(dn * unit, axis=0, keepdims=True)
        du = dn * gain
        d_out.append(inv * (du - unit * jnp.mean(du * unit, axis=-1, keepdims=True)))
    dgain_ref[...] += d_gain
    point(1)

    first = []
    for c, h in items:
        enter = aux[rows[c], 3:4]
        do = d_out[h][rows[c]].astype(BF16)
        eq = (q[h][0][rows[c]] * (enter * scale)).astype(BF16)
        x = t_mul(p_ref[c, h], do)
        c_term = t_mul(
            jnp.concatenate([eq, -ew_ref[c, h]], axis=0),
            jnp.concatenate([do, x.astype(BF16)], axis=0),
        )
        first.append((do, x, c_term))
    point(2)
    after = {}
    for h in range(heads):
        ds = dstate[h]
        for c in reversed(range(GROUP)):
            low = ds.astype(BF16)
            after[c, h] = low
            keep = aux[(c + 1) * CHUNK - 1 : (c + 1) * CHUNK, 3:4]
            ds = ds * keep - t_mul(phi_ref[c, h], low) + first[c * heads + h][2]
        dstate[h] = ds
    db_cols = []
    grads = {}
    point(3)
    for (c, h), (do, x, _) in zip(items, first):
        enter, leave = aux[rows[c], 3:4], aux[rows[c], 4:5]
        b = beta[rows[c], h : h + 1]
        key, query = k[h][0][rows[c]], q[h][0][rows[c]] * scale
        value = act[rows[c], 2 * hid + h * HEAD_DIM : 2 * hid + (h + 1) * HEAD_DIM]
        ds = after[c, h]
        d, s = d_ref[c, h], s_ref[c, h]
        dr = t_mul(t_ref[c, h], x + mul(key * leave, ds))
        stacked = jnp.concatenate([do, dr.astype(BF16)], axis=0)
        with_d = mul_t(stacked, d)
        with_s = mul_t(stacked, s) * jnp.concatenate([enter, enter], axis=0)
        dp = jnp.where(masks[c][1], with_d[:CHUNK], 0.0)
        da = jnp.where(masks[c][0], -with_d[CHUNK:], 0.0)
        pair = jnp.concatenate([dp, da], axis=0).astype(BF16)
        with_k = mul(pair, key)
        dq = with_s[:CHUNK] + with_k[:CHUNK]
        row_k = with_k[CHUNK:] - with_s[CHUNK:]
        dk = b * row_k + t_mul(pair, jnp.concatenate([query, key * b], axis=0))
        dk = dk + mul_t(d, ds) * leave
        db = jnp.sum(dr * value + key * row_k, axis=-1, keepdims=True)
        grads[c, h] = (dq * scale, dk, dr * b, db * b * (1.0 - b))
    point(4)
    for h in range(heads):
        whole = [jnp.concatenate([grads[c, h][i] for c in range(GROUP)], axis=0) for i in range(4)]
        for i, unit in ((0, q[h]), (1, k[h])):
            y, inv = unit
            grad = inv * (whole[i] - y * jnp.sum(y * whole[i], axis=-1, keepdims=True))
            at = slice(i * hid + h * HEAD_DIM, i * hid + (h + 1) * HEAD_DIM)
            later[0:STEP, at] = grad * dsilu[:, at]
        at = slice(2 * hid + h * HEAD_DIM, 2 * hid + (h + 1) * HEAD_DIM)
        later[0:STEP, at] = whole[2] * dsilu[:, at]
        db_cols.append(whole[3])
    lane = lax.broadcasted_iota(jnp.int32, (STEP, HEAD_DIM), 1)
    tail = jnp.zeros((STEP, HEAD_DIM), F32)
    for h in range(heads):
        tail = jnp.where(lane == h, db_cols[h], tail)
    dpre_ref[:, 4 * hid :] = tail.astype(BF16)
    dlin = later[0:STEP, :]
    dpre = dlin * conv[3:4, :]
    taps = [jnp.sum(dlin * pre, axis=0, keepdims=True)]
    for offset in range(1, 4):
        ahead = later[offset : offset + STEP, :]
        dpre = dpre + ahead * aux[:, 4 + offset : 5 + offset] * conv[3 - offset : 4 - offset, :]
        behind = ext[PAD - offset : PAD - offset + STEP, :] * aux[:, offset - 1 : offset]
        taps.append(jnp.sum(dlin * behind, axis=0, keepdims=True))
    dpre_ref[:, : 3 * hid] = dpre.astype(BF16)
    for offset in range(4):
        dconv_ref[3 - offset : 4 - offset, :] += taps[offset]
    later[STEP:, :] = later[0:PAD, :]

    @pl.when(grid_step == steps - 1)
    def _():
        pl.loop(max(steps * per_step - base, 0), line.points)(line.point)
        line.finish(sum_ref)
        line.close()


def mixer_fwd(x_rows, weights, aux, docrow, conv, gain, cotangent, ff_mine, n_dp, count):
    hid = conv.shape[1] // 3
    length, width = x_rows.shape[0], weights.shape[1] - hid
    heads, chunks = hid // HEAD_DIM, length // CHUNK
    lines, dma = n_dp // 2, lambda *shape: pltpu.SemaphoreType.DMA(shape)
    anywhere = pl.BlockSpec(memory_space=pl.ANY)
    rows = lambda n: pl.BlockSpec((STEP, n), lambda i: (i, 0))
    whole = lambda a: pl.BlockSpec(a.shape, lambda i: (0,) * a.ndim)
    square = pl.BlockSpec((GROUP, heads, CHUNK, HEAD_DIM), lambda i: (i, 0, 0, 0))
    squares = jax.ShapeDtypeStruct((chunks, heads, CHUNK, HEAD_DIM), BF16)
    return pl.pallas_call(
        partial(mixer_fwd_kernel, lines, count),
        grid=(length // STEP,),
        in_specs=[
            rows(x_rows.shape[1]), whole(weights), rows(aux.shape[1]),
            pl.BlockSpec((1, GROUP, CHUNK), lambda i: (i, 0, 0)), whole(conv), whole(gain),
            whole(cotangent), whole(ff_mine),
        ],
        out_specs=[rows(width), rows(hid), rows(hid)]
        + [square] * 6
        + [pl.BlockSpec((STEP, x_rows.shape[1]), lambda i: (0, 0))]
        + [anywhere] * 2,
        out_shape=[
            jax.ShapeDtypeStruct((length, width), F32),
            jax.ShapeDtypeStruct((length, hid), BF16),
            jax.ShapeDtypeStruct((length, hid), F32),
        ]
        + [squares] * 6
        + [
            jax.ShapeDtypeStruct((STEP, x_rows.shape[1]), F32),
            jax.ShapeDtypeStruct((count, *cotangent.shape), BF16),
            jax.ShapeDtypeStruct((n_dp, *ff_mine.shape), BF16),
        ],
        scratch_shapes=[
            pltpu.VMEM((PAD + STEP, 3 * hid), F32),
            pltpu.VMEM((heads, HEAD_DIM, HEAD_DIM), F32),
        ]
        + OwnerScatter.scratch(count, STEP, x_rows.shape[1])
        + [
            dma(lines), dma(lines), dma(lines), dma(n_dp), dma(2),
        ]
        + HeadGather.scratch(count, COT_PARTS),
        compiler_params=pltpu.CompilerParams(vmem_limit_bytes=VMEM_LIMIT, has_side_effects=True, collective_id=3),
        name="mixer_fwd",
    )(x_rows, weights, aux, docrow, conv, gain, cotangent, ff_mine)


def mixer_bwd(hg_rows, weights, aux, docrow, conv, gain, saved, terms):
    pre, o, t, phi, s, p, d, ew = saved
    length, width = pre.shape
    hid = conv.shape[1] // 3
    heads, steps = hid // HEAD_DIM, length // STEP
    last = steps - 1
    n_dp, block, wide = terms.shape
    lines = n_dp // 2
    rows = lambda n: pl.BlockSpec((STEP, n), lambda i: (last - i, 0))
    whole = lambda a: pl.BlockSpec(a.shape, lambda i: (0,) * a.ndim)
    square = pl.BlockSpec((GROUP, heads, CHUNK, HEAD_DIM), lambda i: (last - i, 0, 0, 0))
    halo = pl.BlockSpec(
        (PAD, width), lambda i: (jnp.maximum((last - i) * (STEP // PAD) - 1, 0), 0)
    )
    return pl.pallas_call(
        partial(mixer_bwd_kernel, lines, steps),
        grid=(steps,),
        in_specs=[
            rows(hg_rows.shape[1]), pl.BlockSpec((weights.shape[0], hid), lambda i: (0, 0)), rows(width), halo, rows(aux.shape[1]),
            pl.BlockSpec((1, GROUP, CHUNK), lambda i: (last - i, 0, 0)), whole(conv), whole(gain),
            rows(hid),
        ]
        + [square] * 6
        + [pl.BlockSpec(memory_space=pl.ANY)],
        out_specs=[
            rows(width),
            pl.BlockSpec((4, 3 * hid), lambda i: (0, 0)),
            pl.BlockSpec((1, HEAD_DIM), lambda i: (0, 0)),
            pl.BlockSpec((block, wide), lambda i: (0, 0)),
        ],
        out_shape=[
            jax.ShapeDtypeStruct((length, width), BF16),
            jax.ShapeDtypeStruct((4, 3 * hid), F32),
            jax.ShapeDtypeStruct((1, HEAD_DIM), F32),
            jax.ShapeDtypeStruct((block, wide), F32),
        ],
        scratch_shapes=[
            pltpu.VMEM((PAD + STEP, 3 * hid), F32),
            pltpu.VMEM((STEP + PAD, 3 * hid), F32),
            pltpu.VMEM((heads, HEAD_DIM, HEAD_DIM), F32),
            pltpu.VMEM((lines, block, wide), BF16),
            pltpu.SemaphoreType.DMA((lines,)),
        ]
        + LineScatter.scratch(lines, block, wide),
        compiler_params=pltpu.CompilerParams(vmem_limit_bytes=VMEM_LIMIT, has_side_effects=True, collective_id=4),
        name="mixer_bwd",
    )(hg_rows, weights, pre, pre, aux, docrow, conv, gain, o, t, phi, s, p, d, ew, terms)


MESH = pl.DeviceIdType.MESH


def remote(src, dst, sent, landed, axis, to):
    return pltpu.make_async_remote_copy(
        src_ref=src, dst_ref=dst, send_sem=sent, recv_sem=landed,
        device_id={axis: to}, device_id_type=MESH,
    )


def shard_line(lines, own, out, sems):
    right_s, left_s, over_s, landed, local = sems
    me = lax.axis_index("dp")
    spot, side = me // 2, me % 2
    slot = lambda place: 2 * place + side
    across = me + 1 - 2 * side

    def hop(step, where):
        return (spot - step, me + 2, right_s) if where == 0 else (spot + step, me - 2, left_s)

    def going(step, where):
        place, to, sent = hop(step, where)
        src = out.at[slot(place)] if not isinstance(step, int) or step else own
        return remote(src, out.at[slot(place)], sent.at[step], landed.at[slot(place)], "dp", to)

    def goes(step, where):
        if where == 0:
            return jnp.logical_and(spot - step >= 0, spot + 1 < lines)
        return jnp.logical_and(spot + step < lines, spot >= 1)

    def over(place):
        return remote(out.at[slot(place)], out.at[slot(place)], over_s.at[place], landed.at[slot(place)], "dp", across)

    def first():
        pltpu.make_async_copy(own, out.at[me], local).start()
        remote(own, out.at[me], over_s.at[spot], landed.at[me], "dp", across).start()
        for where in (0, 1):
            pl.when(goes(0, where))(lambda where=where: going(0, where).start())

    def arrive(step, place):
        @pl.when(jnp.logical_and(place >= 0, place < lines))
        def _():
            over(place).wait_recv()
            over(place).start()

    def hop_step(step):
        for where in (0, 1):
            place = spot - step - 1 if where == 0 else spot + step + 1
            arrive(step, place)
            if isinstance(step, int) and step + 1 >= lines - 1:
                continue
            pl.when(jnp.logical_and(goes(step + 1, where), step + 1 < lines - 1))(
                lambda where=where: going(step + 1, where).start()
            )

    def arrived():
        pltpu.make_async_copy(own, out.at[me], local).wait()

        @pl.loop(0, lines)
        def _(place):
            there = 2 * place + 1 - side
            remote(out.at[there], out.at[there], over_s.at[place], landed.at[there], "dp", across).wait_recv()

    def last():
        pl.loop(0, lines)(lambda place: over(place).wait_send())

        @pl.loop(0, lines - 1)
        def _(step):
            for where in (0, 1):
                pl.when(goes(step, where))(lambda where=where: going(step, where).wait_send())

    return first, hop_step, arrived, last


def greet(lines, count):
    barrier = pltpu.get_barrier_semaphore()
    me = lax.axis_index("dp")
    spot, across = me // 2, me + 1 - 2 * (me % 2)

    def tell(axis, to):
        pl.semaphore_signal(barrier, 1, device_id={axis: to}, device_id_type=MESH)

    tell("dp", across)
    pl.when(spot >= 1)(lambda: tell("dp", me - 2))
    pl.when(spot + 1 < lines)(lambda: tell("dp", me + 2))
    head = lax.axis_index("head")
    tell("head", head + 1 - 2 * (head % 2))
    for f in range(1, count // 2):
        tell("head", lax.rem(head + 2 * f, count))
    beside = jnp.minimum(spot, 1) + jnp.minimum(lines - 1 - spot, 1)
    pl.semaphore_wait(barrier, 1 + count // 2 + beside)


def greet_line(lines):
    barrier = pltpu.get_barrier_semaphore()
    me = lax.axis_index("dp")

    def tell(to):
        pl.semaphore_signal(barrier, 1, device_id={"dp": to}, device_id_type=MESH)

    tell(me + 1 - 2 * (me % 2))
    pl.loop(1, lines)(lambda hop: tell(lax.rem(me + 2 * hop, 2 * lines)))
    pl.semaphore_wait(barrier, lines)


def cot_gather(count, cot_ref, cot_rows, sems, held_s):
    parts = sems[1].shape[0]
    size = cot_ref.shape[0] // parts
    at = lambda p: pl.ds(p * size, size)
    me = lax.axis_index("head")
    cots = HeadGather(count, parts, lambda p: cot_ref.at[at(p)], lambda owner, p: cot_rows.at[owner, at(p)], sems)
    return cots, pltpu.make_async_copy(cot_ref, cot_rows.at[me], held_s)


def start_kernel(lines, count, parts, tok_ref, gain_ref, out_w, *refs):
    *in_ws, cot_ref, rows_ref, wall_ref, cot_rows, mine, w_ref = refs[:11]
    start_body(
        lines, count, parts, tok_ref, gain_ref, out_w, in_ws, cot_ref, rows_ref, wall_ref, cot_rows, mine, w_ref, *refs[11:]
    )


def start_body(lines, count, parts, tok_ref, gain_ref, out_w, in_ws, cot_ref, rows_ref, wall_ref, cot_rows, mine, w_ref,
               right_s, left_s, over_s, landed, local, far_s, pair_s, fwd_s, got, keep_s, *cot_sems):
    first, hop_step, arrived, last = shard_line(lines, w_ref, wall_ref, (right_s, left_s, over_s, landed, local.at[0]))
    at = out_w.shape[0]
    w_ref[:, :at] = out_w[...].T
    for w in in_ws:
        w_ref[:, at : at + w.shape[1]] = w[...]
        at += w.shape[1]
    greet(lines, count)
    first()
    me = lax.axis_index("head")
    pair = me + 1 - 2 * (me % 2)
    fars = [lax.rem(me + 2 * f, count) for f in range(1, count // 2)]
    size = tok_ref.shape[0] // parts
    span = lambda p: pl.ds(p * size, size)

    def block(owner, p):
        return rows_ref.at[owner, span(p)]

    for p in range(parts):
        x = tok_ref[p * size : (p + 1) * size, :].astype(F32)
        inv = lax.rsqrt(jnp.mean(x * x, axis=-1, keepdims=True) + 1e-6)
        mine[p * size : (p + 1) * size, :] = (x * inv * gain_ref[...]).astype(BF16)
        for f, far in enumerate(fars):
            remote(mine.at[span(p)], block(me, p), far_s.at[f, p], got.at[me, p], "head", far).start()
        remote(mine.at[span(p)], block(me, p), pair_s.at[p], got.at[me, p], "head", pair).start()
        pltpu.make_async_copy(mine.at[span(p)], block(me, p), keep_s.at[p]).start()

    cots, held = cot_gather(count, cot_ref, cot_rows, cot_sems, local.at[1])
    held.start()
    for p in range(cots.parts):
        cots.send(p)

    def pass_on(p):
        for f, far in enumerate(fars):
            moved = remote(block(far, p), block(far, p), fwd_s.at[f, p], got.at[far, p], "head", pair)
            moved.wait_recv()
            moved.start()

    for i in range(parts):
        pass_on(i)
        if i < lines - 1:
            hop_step(i)
    if lines - 1 > parts:
        pl.loop(parts, lines - 1)(hop_step)
    for p in range(cots.parts):
        cots.pass_on(p)
    arrived()
    last()
    held.wait()
    for p in range(cots.parts):
        cots.arrive(p)
        cots.sent(p)
    for p in range(parts):
        remote(mine.at[span(p)], block(pair, p), pair_s.at[p], got.at[pair, p], "head", pair).wait()
        pltpu.make_async_copy(mine.at[span(p)], block(me, p), keep_s.at[p]).wait()
        for f, far in enumerate(fars):
            remote(mine.at[span(p)], block(me, p), far_s.at[f, p], got.at[me, p], "head", far).wait_send()
            there = lax.rem(pair + 2 * (f + 1), count)
            remote(block(far, p), block(there, p), fwd_s.at[f, p], got.at[there, p], "head", pair).wait()


def start(tokens, gain, w_out, in_ws, cot, n_dp, n_head, parts=4):
    rows, width = tokens.shape
    shard = (in_ws[0].shape[0], w_out.shape[0] + sum(w.shape[1] for w in in_ws))
    lines, far = n_dp // 2, n_head // 2 - 1
    dma = lambda *shape: pltpu.SemaphoreType.DMA(shape)
    anywhere = pl.BlockSpec(memory_space=pl.ANY)
    vmem = pl.BlockSpec(memory_space=pltpu.VMEM)
    return pl.pallas_call(
        partial(start_kernel, lines, n_head, parts),
        out_shape=[jax.ShapeDtypeStruct((n_head, rows, width), BF16),
                   jax.ShapeDtypeStruct((n_dp, *shard), BF16),
                   jax.ShapeDtypeStruct((n_head, *cot.shape), BF16)],
        in_specs=[vmem] * (4 + len(in_ws)),
        out_specs=[anywhere] * 3,
        scratch_shapes=[
            pltpu.VMEM((rows, width), BF16),
            pltpu.VMEM(shard, BF16),
            dma(lines), dma(lines), dma(lines), dma(n_dp), dma(2),
            dma(far, parts), dma(parts), dma(far, parts), dma(n_head, parts), dma(parts),
        ]
        + HeadGather.scratch(n_head, COT_PARTS),
        compiler_params=pltpu.CompilerParams(vmem_limit_bytes=VMEM_LIMIT, has_side_effects=True, collective_id=0),
        name="start",
    )(tokens, gain, w_out, *in_ws, cot)


def when(condition):
    return pl.when(condition) if not isinstance(condition, bool) else (lambda f: f() if condition else None)


class HeadScatter:
    def __init__(self, count, refs):
        self.count = count
        (self.out, self.near, self.onward, self.far, self.own,
         self.out_s, self.near_r, self.onward_s, self.far_r) = refs
        self.me = lax.axis_index("head")
        self.side, self.place = self.me % 2, self.me // 2
        self.pair = self.me + 1 - 2 * self.side
        self.parts, self.depth, self.size = self.near.shape[0], self.own.shape[0], self.own.shape[1]

    @staticmethod
    def scratch(count, parts, size, width, depth):
        half = count // 2
        return [
            pltpu.VMEM((2, 2, half, size, width), BF16),
            pltpu.VMEM((parts, half, size, width), BF16),
            pltpu.VMEM((2, half - 1, size, width), BF16),
            pltpu.VMEM((parts, half - 1, size, width), BF16),
            pltpu.VMEM((depth, size, width), F32),
            pltpu.SemaphoreType.DMA((2,)),
            pltpu.SemaphoreType.DMA((parts,)),
            pltpu.SemaphoreType.DMA((2, half - 1)),
            pltpu.SemaphoreType.DMA((parts, half - 1)),
        ]

    def _near(self, p):
        slot = p % 2
        return remote(self.out.at[slot, 1 - self.side], self.near.at[p], self.out_s.at[slot], self.near_r.at[p], "head", self.pair)

    def _far(self, p, f):
        slot = p % 2
        to = lax.rem(self.me + 2 * (f + 1), self.count)
        return remote(self.onward.at[slot, f], self.far.at[p, f], self.onward_s.at[slot, f], self.far_r.at[p, f], "head", to)

    def offer(self, p, total):
        when(p >= 2)(lambda: self._near(p - 2).wait_send())
        for owner in range(self.count):
            self.out[p % 2, owner % 2, owner // 2] = total[owner * self.size : (owner + 1) * self.size].astype(BF16)
        self._near(p).start()

    def turn(self, p):
        slot, half = p % 2, self.count // 2
        self._near(p).wait_recv()
        both = lambda i: self.out[slot, self.side, i].astype(F32) + self.near[p, i].astype(F32)
        for f in range(half - 1):
            when(p >= 2)(lambda f=f: self._far(p - 2, f).wait_send())
            self.onward[slot, f] = both(lax.rem(self.place + f + 1, half)).astype(BF16)
            self._far(p, f).start()
        self.own[p % self.depth] = both(self.place)

    def take(self, p):
        total = self.own[p % self.depth]
        for f in range(self.count // 2 - 1):
            self._far(p, f).wait_recv()
            total = total + self.far[p, f].astype(F32)
        return total

    def close(self):
        for p in range(max(self.parts - 2, 0), self.parts):
            self._near(p).wait_send()
            for f in range(self.count // 2 - 1):
                self._far(p, f).wait_send()


class OwnerScatter:
    def __init__(self, count, out_ref, refs):
        self.count, self.out_ref = count, out_ref
        self.terms, self.near, self.far, self.near_s, self.near_r, self.far_s, self.far_r = refs
        self.me = lax.axis_index("head")
        self.side = self.me % 2
        self.pair = self.me + 1 - 2 * self.side

    @staticmethod
    def scratch(count, rows, width):
        half = count // 2
        sems = lambda n: pltpu.SemaphoreType.DMA((n,))
        return [
            pltpu.VMEM((count, rows, width), BF16),
            pltpu.VMEM((half, rows, width), BF16),
            pltpu.VMEM((half - 1, rows, width), BF16),
            sems(half), sems(half), sems(count), sems(half - 1),
        ]

    def _near(self, owner):
        at = owner // 2
        return remote(self.terms.at[owner], self.near.at[at], self.near_s.at[at], self.near_r.at[at], "head", self.pair)

    def _far(self, owner):
        at = lax.rem(self.me - owner + self.count, self.count) // 2 - 1
        return remote(self.terms.at[owner], self.far.at[at], self.far_s.at[owner], self.far_r.at[at], "head", owner)

    def _mine(self, owner):
        return owner % 2 == self.side

    def offer(self, owner, total):
        self.terms[owner] = total.astype(BF16)
        pl.when(jnp.logical_not(self._mine(owner)))(lambda: self._near(owner).start())

    def settle(self, owner):
        @pl.when(self._mine(owner))
        def _():
            self._near(owner).wait_recv()
            both = self.terms[owner].astype(F32) + self.near[owner // 2].astype(F32)

            @pl.when(owner == self.me)
            def _():
                self.out_ref[...] = both

            @pl.when(owner != self.me)
            def _():
                self.terms[owner] = both.astype(BF16)
                self._far(owner).start()

    def finish(self):
        for f in range(self.count // 2 - 1):
            sender = lax.rem(self.me + 2 * (f + 1), self.count)
            remote(self.terms.at[0], self.far.at[f], self.far_s.at[0], self.far_r.at[f], "head", sender).wait_recv()
            self.out_ref[...] += self.far[f].astype(F32)

        @pl.loop(0, self.count)
        def _(owner):
            pl.when(jnp.logical_not(self._mine(owner)))(lambda: self._near(owner).wait_send())
            pl.when(jnp.logical_and(self._mine(owner), owner != self.me))(lambda: self._far(owner).wait_send())


class HeadGather:
    def __init__(self, count, parts, own, block, refs):
        self.count, self.parts, self.own, self.block = count, parts, own, block
        self.far_s, self.pair_s, self.fwd_s, self.got = refs
        self.me = lax.axis_index("head")
        self.pair = self.me + 1 - 2 * (self.me % 2)

    @staticmethod
    def scratch(count, parts):
        far = count // 2 - 1
        return [pltpu.SemaphoreType.DMA(s) for s in ((far, parts), (parts,), (far, parts), (count, parts))]

    def _fars(self, base):
        return [(f, lax.rem(base + 2 * (f + 1), self.count)) for f in range(self.count // 2 - 1)]

    def _far(self, p, f, far):
        return remote(self.own(p), self.block(self.me, p), self.far_s.at[f, p], self.got.at[self.me, p], "head", far)

    def _pair(self, p):
        return remote(self.own(p), self.block(self.me, p), self.pair_s.at[p], self.got.at[self.me, p], "head", self.pair)

    def _on(self, p, f, owner):
        return remote(self.block(owner, p), self.block(owner, p), self.fwd_s.at[f, p], self.got.at[owner, p], "head", self.pair)

    def send(self, p):
        for f, far in self._fars(self.me):
            self._far(p, f, far).start()
        self._pair(p).start()

    def pass_on(self, p):
        for f, far in self._fars(self.me):
            self._on(p, f, far).wait_recv()
            self._on(p, f, far).start()

    def arrive(self, p):
        remote(self.own(p), self.block(self.pair, p), self.pair_s.at[p], self.got.at[self.pair, p], "head", self.pair).wait_recv()
        for f, far in self._fars(self.pair):
            self._on(p, f, far).wait_recv()

    def sent(self, p):
        self._pair(p).wait_send()
        for f, far in self._fars(self.me):
            self._far(p, f, far).wait_send()
            self._on(p, f, far).wait_send()


LEAD = 4


def mid_kernel(lines, count, parts, att_ref, tok_ref, gain_ref, cot_early, cot_late, ff_ref, down_mine,
               out_ref, grad_ref, hg_ref, gain_grad_ref, terms_ref, down_terms_ref, *scratch):
    scratch = list(scratch)
    take = lambda n: [scratch.pop(0) for _ in range(n)]
    down_refs, back_refs = take(9), take(9)
    second_sems, hg_sems = take(4), take(4)
    cot_ref, second, hidden, hg_own, total, loads, keep_s, down_all, right_s, left_s, over_s, landed = scratch
    size, width = tok_ref.shape[1:]
    ff = ff_ref.shape[1] // 2
    me = lax.axis_index("head")
    greet(lines, count)
    first, hop_step, arrived, last = shard_line(
        lines, down_mine, down_all, (right_s, left_s, over_s, landed, loads.at[1])
    )
    first()
    half = parts // 2
    loading = [
        pltpu.make_async_copy(src, cot_ref.at[:, at : at + half], loads.at[i])
        for i, (src, at) in ((0, (cot_early, 0)), (2, (cot_late, half)))
    ]
    for m in loading:
        m.start()
    down_w = lambda: down_all[...].reshape(-1, ff)
    down, back = (HeadScatter(count, r) for r in (down_refs, back_refs))
    here = lambda owner, p: second.at[p, owner]
    seconds = HeadGather(count, parts, lambda p: here(me, p), here, second_sems)
    there = lambda owner, p: hg_ref.at[owner, p]
    hgs = HeadGather(count, parts, lambda p: hg_own.at[p], there, hg_sems)
    keep = lambda p: pltpu.make_async_copy(hg_own.at[p], there(me, p), keep_s.at[p])
    total[...] = jnp.zeros_like(total)
    gain_grad_ref[...] = jnp.zeros_like(gain_grad_ref)

    def within(p, stage):
        pl.when(jnp.logical_and(p >= 0, p < parts))(lambda: stage(p))

    def norm(p):
        rows = tok_ref[p].astype(F32) + att_ref[p]
        hidden[p] = rows
        inv = lax.rsqrt(jnp.mean(rows * rows, axis=-1, keepdims=True) + 1e-6)
        second[p, me] = (rows * inv * gain_ref[...]).astype(BF16)
        seconds.send(p)

    def feed(p):
        seconds.arrive(p)
        rows = second[p].reshape(count * size, width)
        both = dot(rows, ff_ref[...], ((1,), (0,)))
        gate, up = both[:, :ff], both[:, ff:]
        sig = jax.nn.sigmoid(gate)
        act = gate * sig
        middle = (act * up).astype(BF16)

        @pl.when(p == 0)
        def _():
            hop_step(0)
            pl.loop(1, lines - 1)(hop_step)
            arrived()

        down.offer(p, dot(middle, down_w(), ((1,), (1,))))
        cot = cot_ref[:, p].reshape(count * size, width)
        grad = dot(cot, down_w(), ((1,), (0,))).astype(BF16).astype(F32)
        pair = jnp.concatenate(
            [(grad * up * sig * (1.0 + gate * (1.0 - sig))).astype(BF16), (grad * act).astype(BF16)], axis=1
        )
        back.offer(p, dot(pair, ff_ref[...], ((1,), (1,))))
        total[:, : 2 * ff] += dot(rows, pair, ((0,), (0,)))
        total[:, 2 * ff :] += dot(cot, middle, ((0,), (0,)))

    def turn(p):
        down.turn(p)
        back.turn(p)

    def finish(p):
        rows = hidden[p]
        out_ref[p] = (rows + down.take(p)).astype(BF16)
        second_grad = back.take(p).astype(BF16).astype(F32)
        inv = lax.rsqrt(jnp.mean(rows * rows, axis=-1, keepdims=True) + 1e-6)
        scaled = second_grad * gain_ref[...]
        mean = jnp.mean(scaled * rows, axis=-1, keepdims=True)
        grad = cot_ref[me, p].astype(F32) + inv * scaled - rows * (inv * inv * inv * mean)
        grad_ref[p] = grad
        gain_grad_ref[...] += jnp.sum(second_grad * rows * inv, axis=0, keepdims=True)
        hg_own[p] = grad.astype(BF16)
        hgs.send(p)
        keep(p).start()

    for p in range(LEAD):
        norm(p)
    for m in loading:
        m.wait()

    @pl.loop(0, parts + 2)
    def _(step):
        within(step + LEAD, norm)
        within(step, seconds.pass_on)
        within(step, feed)
        within(step, turn)
        within(step - 1, finish)
        within(step - 2, hgs.pass_on)

    terms_ref[...] = total[:, : 2 * ff].astype(BF16)
    down_terms_ref[...] = total[:, 2 * ff :].astype(BF16)

    @pl.loop(0, parts)
    def _(p):
        hgs.arrive(p)
        keep(p).wait()
        hgs.sent(p)
        seconds.sent(p)

    for s in (down, back):
        s.close()
    last()


def mid(attention, tokens, gain, cot_early, cot_late, ff_set, down_mine, n_dp, count, parts=8):
    rows, width = tokens.shape
    lines, ff = n_dp // 2, down_mine.shape[1]
    dma = lambda *shape: pltpu.SemaphoreType.DMA(shape)
    size = rows // parts
    anywhere = pl.BlockSpec(memory_space=pl.ANY)
    vmem = pl.BlockSpec(memory_space=pltpu.VMEM)
    scatter = HeadScatter.scratch(count, parts, size, width, 2)
    out, grad, hg, gain_grad, terms, down_terms = pl.pallas_call(
        partial(mid_kernel, lines, count, parts),
        out_shape=[
            jax.ShapeDtypeStruct((parts, size, width), BF16),
            jax.ShapeDtypeStruct((parts, size, width), F32),
            jax.ShapeDtypeStruct((count, parts, size, width), BF16),
            jax.ShapeDtypeStruct((1, width), F32),
            jax.ShapeDtypeStruct((width, 2 * ff), BF16),
            jax.ShapeDtypeStruct((width, ff), BF16),
        ],
        in_specs=[vmem] * 3 + [anywhere] * 2 + [vmem] * 2,
        out_specs=[vmem, vmem, anywhere, vmem, vmem, vmem],
        scratch_shapes=scatter * 2
        + HeadGather.scratch(count, parts) * 2
        + [
            pltpu.VMEM((count, parts, size, width), BF16),
            pltpu.VMEM((parts, count, size, width), BF16),
            pltpu.VMEM((parts, size, width), F32),
            pltpu.VMEM((parts, size, width), BF16),
            pltpu.VMEM((width, 3 * ff), F32),
            dma(3),
            dma(parts),
            pltpu.VMEM((n_dp, *down_mine.shape), BF16),
            dma(lines), dma(lines), dma(lines), dma(n_dp),
        ],
        compiler_params=pltpu.CompilerParams(vmem_limit_bytes=61 * 1024 * 1024, has_side_effects=True, collective_id=2),
        name="mid",
    )(
        attention.reshape(parts, size, width), tokens.reshape(parts, size, width), gain,
        *(c.reshape(count, parts // 2, size, width) for c in (cot_early, cot_late)), ff_set, down_mine,
    )
    return out.reshape(rows, width), grad.reshape(rows, width), hg.reshape(-1, width), gain_grad, terms, down_terms


class ChainScatter:
    LAG = 2

    def __init__(self, lines, terms, own, refs, by_piece):
        self.lines, self.terms, self.own, self.by_piece = lines, terms, own, by_piece
        self.cross, self.going, self.coming, self.cross_s, self.cross_r, self.go_s, self.come_r = refs
        self.pieces = self.cross_s.shape[1]
        self.size = self.cross.shape[1] // self.pieces
        self.me = lax.axis_index("dp")
        self.spot, self.side = self.me // 2, self.me % 2
        self.across = self.me + 1 - 2 * self.side
        self.items = (lines - 1) * self.pieces
        self.points = self.items + (lines - 1) * self.LAG

    @staticmethod
    def scratch(lines, rows, width):
        pieces = max(1, rows // 32)
        wide = lambda *lead: pltpu.VMEM((*lead, rows, width), BF16)
        sems = lambda *shape: pltpu.SemaphoreType.DMA((*shape, pieces))
        return [
            wide(lines), wide(2, lines), wide(2, lines),
            sems(lines), sems(lines), sems(2, lines), sems(2, lines),
        ]

    def _at(self, k):
        return pl.ds(pl.multiple_of(k * self.size, self.size), self.size)

    def _cross(self, place, k):
        at = self._at(k)
        src = self.terms(2 * place + 1 - self.side).at[at]
        return remote(src, self.cross.at[place, at], self.cross_s.at[place, k], self.cross_r.at[place, k], "dp", self.across)

    def _line(self, way, dest, k):
        to = self.me + 2 if way == 0 else self.me - 2
        at = self._at(k)
        return remote(self.going.at[way, dest, at], self.coming.at[way, dest, at], self.go_s.at[way, dest, k], self.come_r.at[way, dest, k], "dp", to)

    def offer(self, place, k):
        self._cross(place, k).start()

    def offer_all(self):
        for k in range(self.pieces):
            for d in range((self.lines + 1) // 2):
                for place in sorted({self.lines - 1 - d, d}, reverse=True):
                    self.offer(place, k)

    def _both(self, place, k):
        return self.own(place)[self._at(k), :].astype(F32) + self.cross[place, self._at(k), :].astype(F32)

    def _passes(self, way, dest):
        return dest > self.spot if way == 0 else dest < self.spot

    def _fed(self, way):
        return self.spot >= 1 if way == 0 else self.spot + 1 < self.lines

    def point(self, n):
        for way in (0, 1):
            away = self.spot if way == 0 else self.lines - 1 - self.spot
            item = n - away * self.LAG
            safe = jnp.clip(item, 0, self.items - 1)
            if self.by_piece:
                k, d = safe // (self.lines - 1), safe % (self.lines - 1)
            else:
                d, k = safe // self.pieces, safe % self.pieces
            dest = self.lines - 1 - d if way == 0 else d
            live = jnp.logical_and(item >= 0, item < self.items)

            @pl.when(jnp.logical_and(live, self._passes(way, dest)))
            def _(way=way, dest=dest, k=k):
                at = self._at(k)
                self._cross(dest, k).wait_recv()

                @pl.when(self._fed(way))
                def _():
                    self._line(way, dest, k).wait_recv()
                    self.going[way, dest, at, :] = (self._both(dest, k) + self.coming[way, dest, at, :].astype(F32)).astype(BF16)

                @pl.when(jnp.logical_not(self._fed(way)))
                def _():
                    self.going[way, dest, at, :] = self._both(dest, k).astype(BF16)

                self._line(way, dest, k).start()

    def finish(self, out_ref):
        for k in range(self.pieces):
            at = slice(k * self.size, (k + 1) * self.size)
            self._cross(self.spot, k).wait_recv()
            out_ref[at, :] = self._both(self.spot, k)
            for way in (0, 1):
                @pl.when(self._fed(way))
                def _(way=way, k=k, at=at):
                    self._line(way, self.spot, k).wait_recv()
                    out_ref[at, :] += self.coming[way, self.spot, at, :].astype(F32)

    def close(self):
        @pl.loop(0, self.lines * self.pieces)
        def _(i):
            place, k = i // self.pieces, i % self.pieces
            self._cross(place, k).wait_send()
            for way in (0, 1):
                pl.when(self._passes(way, place))(lambda way=way: self._line(way, place, k).wait_send())


class LineScatter:
    def __init__(self, lines, terms, own, refs, order):
        self.lines, self.terms, self.own, self.order = lines, terms, own, order
        self.cross, self.going, self.coming, self.cross_s, self.cross_r, self.go_s, self.come_r = refs
        self.pieces = self.cross_s.shape[1]
        self.size = self.cross.shape[1] // self.pieces
        self.me = lax.axis_index("dp")
        self.spot, self.side = self.me // 2, self.me % 2
        self.across = self.me + 1 - 2 * self.side
        self.points = lines * self.pieces

    @staticmethod
    def scratch(lines, rows, width):
        pieces = max(1, rows // 32)
        wide = pltpu.VMEM((lines, rows, width), BF16)
        sems = pltpu.SemaphoreType.DMA((lines, pieces))
        return [wide, wide, wide, sems, sems, sems, sems]

    def _at(self, k):
        return pl.ds(pl.multiple_of(k * self.size, self.size), self.size)

    def _cross(self, place, k):
        at = self._at(k)
        src = self.terms(2 * place + 1 - self.side).at[at]
        return remote(src, self.cross.at[place, at], self.cross_s.at[place, k], self.cross_r.at[place, k], "dp", self.across)

    def _on(self, sender, dest, k):
        at = self._at(k)
        return remote(self.going.at[dest, at], self.coming.at[sender, at], self.go_s.at[dest, k], self.come_r.at[sender, k], "dp", 2 * dest + self.side)

    def offer(self, place, k):
        self._cross(place, k).start()

    def offer_all(self):
        @pl.loop(0, self.points)
        def _(n):
            k, place = self.order(n)
            self.offer(place, k)

    def _both(self, place, k):
        return self.own(place)[self._at(k), :].astype(F32) + self.cross[place, self._at(k), :].astype(F32)

    def point(self, n):
        k, dest = self.order(jnp.clip(n, 0, self.points - 1))

        @pl.when(jnp.logical_and(jnp.logical_and(n >= 0, n < self.points), dest != self.spot))
        def _():
            self._cross(dest, k).wait_recv()
            self.going[dest, self._at(k), :] = self._both(dest, k).astype(BF16)
            self._on(self.spot, dest, k).start()

    def finish(self, out_ref):
        for k in range(self.pieces):
            at = slice(k * self.size, (k + 1) * self.size)
            self._cross(self.spot, k).wait_recv()
            out_ref[at, :] = self._both(self.spot, k)

            @pl.loop(1, self.lines)
            def _(hop, k=k, at=at):
                sender = lax.rem(self.spot + hop, self.lines)
                self._on(sender, self.spot, k).wait_recv()
                out_ref[at, :] += self.coming[sender, at, :].astype(F32)

    def close(self):
        @pl.loop(0, self.points)
        def _(i):
            place, k = i // self.pieces, i % self.pieces
            self._cross(place, k).wait_send()
            pl.when(place != self.spot)(lambda: self._on(self.spot, place, k).wait_send())


def outside_in(lines, i):
    return jnp.where(i % 2 == 0, lines - 1 - i // 2, i // 2)


class SmallSum:
    def __init__(self, n_dp, count, shared, refs):
        self.n_dp, self.count, self.shared = n_dp, count, shared
        self.mine, self.theirs, self.half, self.halves, self.a_s, self.a_r, self.b_s, self.b_r = refs
        self.dp, self.head = lax.axis_index("dp"), lax.axis_index("head")

    @staticmethod
    def scratch(n_dp, count, rows, shared):
        return [
            pltpu.VMEM((rows, 128), F32),
            pltpu.VMEM((n_dp, rows, 128), F32),
            pltpu.VMEM((shared, 128), F32),
            pltpu.VMEM((count, shared, 128), F32),
            pltpu.SemaphoreType.DMA((n_dp,)),
            pltpu.SemaphoreType.DMA((n_dp,)),
            pltpu.SemaphoreType.DMA((count,)),
            pltpu.SemaphoreType.DMA((count,)),
        ]

    def _a(self, hop):
        to = lax.rem(self.dp + hop, self.n_dp)
        return remote(self.mine, self.theirs.at[self.dp], self.a_s.at[hop], self.a_r.at[self.dp], "dp", to)

    def _b(self, hop):
        to = lax.rem(self.head + hop, self.count)
        return remote(self.half, self.halves.at[self.head], self.b_s.at[hop], self.b_r.at[self.head], "head", to)

    def start(self):
        self.theirs[self.dp] = self.mine[...]

        @pl.loop(1, self.n_dp)
        def _(hop):
            self._a(hop).start()

    def turn(self, out_ref):
        @pl.loop(1, self.n_dp)
        def _(hop):
            sender = lax.rem(self.dp + self.n_dp - hop, self.n_dp)
            remote(self.mine, self.theirs.at[sender], self.a_s.at[hop], self.a_r.at[sender], "dp", sender).wait_recv()

        total = self.theirs[0]
        for i in range(1, self.n_dp):
            total = total + self.theirs[i]
        out_ref[...] = total
        self.half[...] = total[: self.shared]
        self.halves[self.head] = total[: self.shared]
        for hop in range(1, self.count):
            self._b(hop).start()

    def finish(self, out_ref):
        for hop in range(1, self.count):
            sender = lax.rem(self.head + self.count - hop, self.count)
            remote(self.half, self.halves.at[sender], self.b_s.at[hop], self.b_r.at[sender], "head", sender).wait_recv()
        total = self.halves[0]
        for i in range(1, self.count):
            total = total + self.halves[i]
        out_ref[: self.shared, :] = total

        @pl.loop(1, self.n_dp)
        def _(hop):
            self._a(hop).wait_send()

        for hop in range(1, self.count):
            self._b(hop).wait_send()


def greet_all(n_dp, count):
    barrier = pltpu.get_barrier_semaphore()
    dp, head = lax.axis_index("dp"), lax.axis_index("head")

    @pl.loop(1, n_dp)
    def _(hop):
        pl.semaphore_signal(barrier, 1, device_id={"dp": lax.rem(dp + hop, n_dp)}, device_id_type=MESH)

    for hop in range(1, count):
        pl.semaphore_signal(barrier, 1, device_id={"head": lax.rem(head + hop, count)}, device_id_type=MESH)
    pl.semaphore_wait(barrier, n_dp + count - 2)


def end_kernel(n_dp, count, parts, shared,
               dpre_ref, w_ref, normed_ref, hg_ref, mixed_ref, down_ref, tok_ref, gain_ref, grad_ref, small_ref,
               in_ref, mix_ref, sum_ref, down_sum_ref, *scratch):
    scratch = list(scratch)
    take = lambda n: [scratch.pop(0) for _ in range(n)]
    head_refs, dp_refs, down_refs, small_refs = take(9), take(7), take(7), take(8)
    terms, dpre, w, normed, hg, mixed, down_own, loads, down_s = scratch
    rows, width = tok_ref.shape
    block = terms.shape[1]
    hid = mixed.shape[1]
    greet_all(n_dp, count)
    lines = n_dp // 2
    side = lax.axis_index("dp") % 2
    down = ChainScatter(lines, lambda j: down_ref.at[j], lambda place: down_own.at[place], down_refs, True)
    fetch = lambda place: pltpu.make_async_copy(down_ref.at[2 * place + side], down_own.at[place], down_s.at[place])
    moves = [pltpu.make_async_copy(s, d, loads.at[i]) for i, (s, d) in enumerate(
        ((dpre_ref, dpre), (w_ref.at[:, hid:], w), (normed_ref, normed), (mixed_ref, mixed), (hg_ref, hg)))]
    for m in moves:
        m.start()
    down.offer_all()
    for place in range(lines):
        fetch(place).start()
    heads = HeadScatter(count, head_refs)
    line = ChainScatter(lines, lambda j: terms.at[j], lambda place: terms.at[2 * place + side], dp_refs, False)
    small = SmallSum(n_dp, count, shared, small_refs)
    size = rows // parts

    def offer(p):
        part = jnp.concatenate([dpre[o * rows + p * size : o * rows + (p + 1) * size, :] for o in range(count)], axis=0)
        heads.offer(p, dot(part, w[...], ((1,), (1,))))

    tiles = width // 256
    per = 256 // block

    def outer(t):
        cols = slice(t * 256, (t + 1) * 256)
        left = dot(normed[:, cols], dpre[...], ((0,), (0,))).astype(BF16)
        right = dot(hg[:, cols], mixed[...], ((0,), (0,))).astype(BF16)
        for b in range(per):
            terms[t * per + b, :, :hid] = right[b * block : (b + 1) * block]
            terms[t * per + b, :, hid:] = left[b * block : (b + 1) * block]
        for place in range(t * per // 2, (t + 1) * per // 2):
            for k in range(line.pieces):
                line.offer(place, k)

    order = [t // 2 if t % 2 else tiles - 1 - t // 2 for t in range(tiles)]
    moves[0].wait()
    moves[1].wait()
    offer(0)
    for m in moves[2:]:
        m.wait()
    for place in range(lines):
        fetch(place).wait()
    down_done = 0
    for i in range(max(tiles, parts)):
        if i < tiles:
            outer(order[i])
        if i < parts:
            heads.turn(i)
        if i + 1 < parts:
            offer(i + 1)
        for n in range(4):
            if down_done < down.points:
                down.point(down_done)
                down_done += 1
    pl.loop(down_done, down.points)(down.point)
    small.mine[...] = small_ref[...]
    gain_total = jnp.zeros((1, width), F32)
    gain = gain_ref[...]

    def finish(p):
        at = slice(p * size, (p + 1) * size)
        normed_grad = heads.take(p).astype(BF16).astype(F32)
        x = tok_ref[at, :].astype(F32)
        inv = lax.rsqrt(jnp.mean(x * x, axis=-1, keepdims=True) + 1e-6)
        scaled = normed_grad * gain
        mean = jnp.mean(scaled * x, axis=-1, keepdims=True)
        in_ref[at, :] = grad_ref[at, :] + inv * scaled - x * (inv * inv * inv * mean)
        return jnp.sum(normed_grad * x * inv, axis=0, keepdims=True)

    done = 0
    for i in range(parts):
        for n in range(2):
            if done < line.points:
                line.point(done)
                done += 1
        gain_total = gain_total + finish(i)
    for i in range(width // 128):
        small.mine[i : i + 1, :] = gain_total[:, i * 128 : (i + 1) * 128]
    small.start()
    half = (done + line.points) // 2
    pl.loop(done, half)(line.point)
    small.turn(sum_ref)
    pl.loop(half, line.points)(line.point)
    line.finish(mix_ref)
    down.finish(down_sum_ref)
    small.finish(sum_ref)
    down.close()
    heads.close()
    line.close()


def end(dpre, weights, normed_rows, hg_rows, mixed, down_terms, tokens, gain, hidden_grad, small, n_dp, count, shared, parts=4):
    rows, width = tokens.shape
    block = width // n_dp
    wide = weights.shape[1]
    anywhere = pl.BlockSpec(memory_space=pl.ANY)
    vmem = pl.BlockSpec(memory_space=pltpu.VMEM)
    like = lambda a: pltpu.VMEM(a.shape, a.dtype)
    return pl.pallas_call(
        partial(end_kernel, n_dp, count, parts, shared),
        out_shape=[
            jax.ShapeDtypeStruct((rows, width), F32),
            jax.ShapeDtypeStruct((block, wide), F32),
            jax.ShapeDtypeStruct(small.shape, F32),
            jax.ShapeDtypeStruct(down_terms.shape[1:], F32),
        ],
        in_specs=[anywhere] * 6 + [vmem] * 4,
        out_specs=[vmem] * 4,
        scratch_shapes=HeadScatter.scratch(count, parts, rows // parts, width, parts)
        + ChainScatter.scratch(n_dp // 2, block, wide)
        + ChainScatter.scratch(n_dp // 2, block, down_terms.shape[2])
        + SmallSum.scratch(n_dp, count, small.shape[0], shared)
        + [pltpu.VMEM((n_dp, block, wide), BF16), like(dpre), pltpu.VMEM((width, dpre.shape[1]), BF16), like(normed_rows), like(hg_rows), like(mixed),
           pltpu.VMEM((n_dp // 2, *down_terms.shape[1:]), BF16),
           pltpu.SemaphoreType.DMA((5,)), pltpu.SemaphoreType.DMA((n_dp // 2,))],
        compiler_params=pltpu.CompilerParams(vmem_limit_bytes=VMEM_LIMIT, has_side_effects=True, collective_id=1),
        name="end",
    )(dpre, weights, normed_rows, hg_rows, mixed, down_terms, tokens, gain, hidden_grad, small)


def spread_kernel(out_ref, in_ref, mix_ref, ff_ref, down_ref, out_to, in_to, *results):
    to_out, *mixes, beta, ff_gate, ff_up, ff_down = results
    hid, heads, ff = to_out.shape[0], beta.shape[0], ff_gate.shape[0]
    wide = down_ref.shape[1]
    out_to[...] = out_ref[...]
    in_to[...] = in_ref[...]
    to_out[...] = mix_ref[:, :hid].T
    for i, r in enumerate(mixes):
        r[...] = mix_ref[:, (i + 1) * hid : (i + 2) * hid]
    beta[...] = mix_ref[:, 5 * hid :].T[:heads]
    ff_gate[...] = ff_ref[:, :wide].T[:ff]
    ff_up[...] = ff_ref[:, wide:].T[:ff]
    ff_down[...] = down_ref[...].T[:ff]


def spread(output, input_grad, mix, ff_sum, down_sum, hid, heads, ff):
    block = mix.shape[0]
    vmem = pl.BlockSpec(memory_space=pltpu.VMEM)
    shapes = [(hid, block)] + [(block, hid)] * 4 + [(heads, block)] + [(ff, block)] * 3
    return pl.pallas_call(
        spread_kernel,
        out_shape=[jax.ShapeDtypeStruct(a.shape, a.dtype) for a in (output, input_grad)]
        + [jax.ShapeDtypeStruct(s, F32) for s in shapes],
        in_specs=[vmem] * 5,
        out_specs=[vmem] * (2 + len(shapes)),
        compiler_params=pltpu.CompilerParams(vmem_limit_bytes=VMEM_LIMIT),
        name="spread",
    )(output, input_grad, mix, ff_sum, down_sum)


def doc_tables(lengths, length):
    count = lengths.shape[0]
    index = jnp.arange(count)
    ends = jnp.sum(jnp.where(index[None, :] <= index[:, None], lengths[None, :], 0), axis=1)
    position = jnp.arange(length, dtype=jnp.int32)
    doc = jnp.sum((position[:, None] >= ends[None, :]).astype(jnp.int32), axis=1)
    no_doc = lambda n: jnp.full((n,), -1, jnp.int32)
    before = [jnp.concatenate([no_doc(o), doc[:-o]]) == doc for o in (1, 2, 3)]
    after = [jnp.concatenate([doc[o:], no_doc(o)]) == doc for o in (1, 2, 3)]
    blocks = doc.reshape(-1, CHUNK)
    ending = blocks[:, -1:]
    prior = jnp.concatenate([no_doc(1)[:, None], ending[:-1]], axis=0)
    enter = (blocks == prior).reshape(-1)
    leave = (blocks == ending).reshape(-1)
    columns = before + [enter, leave] + after + [doc]
    aux = jnp.stack([c.astype(F32) for c in columns], axis=1)
    return aux, doc.astype(F32).reshape(-1, GROUP, CHUNK)


def on_device(
    tokens,
    lengths,
    attn_gain,
    w_query,
    w_key,
    w_value,
    w_beta,
    w_gate_out,
    conv_weight,
    head_gain,
    w_out,
    mlp_gain,
    w_mlp_gate,
    w_mlp_up,
    w_down,
    cotangent,
):
    hid, heads, ff = w_query.shape[1], w_beta.shape[1], w_mlp_gate.shape[1]
    n_dp, n_head = lax.axis_size("dp"), lax.axis_size("head")
    beta_wide = jnp.pad(w_beta, ((0, 0), (0, HEAD_DIM - heads)))
    in_ws = [w_query, w_key, w_value, w_gate_out, beta_wide]
    half = cotangent.shape[0] // 2
    normed_rows, first_set, cot_early = start(
        tokens, attn_gain[None, :], w_out, in_ws, cotangent[:half], n_dp, n_head
    )
    normed_rows = normed_rows.reshape(-1, normed_rows.shape[2])
    first_set = first_set.reshape(-1, first_set.shape[2])
    wide = -(-ff // 256) * 256
    padded = lambda w: jnp.pad(w, ((0, 0), (0, wide - ff)))
    mine = jnp.concatenate([padded(w_mlp_gate), padded(w_mlp_up)], axis=1)

    length = normed_rows.shape[0]
    aux, docrow = doc_tables(lengths[0], length)
    conv = jnp.swapaxes(conv_weight.astype(F32), 0, 1).reshape(conv_weight.shape[1], 3 * hid)
    gain = head_gain[None, :]
    pre, mixed, *saved, attention, cot_late, ff_set = mixer_fwd(
        normed_rows, first_set, aux, docrow, conv, gain, cotangent[half:], mine, n_dp, n_head
    )
    ff_set = ff_set.reshape(-1, ff_set.shape[2])
    output, hidden_grad, hg_rows, mlp_gain_grad, mlp_terms, down_terms = mid(
        attention, tokens, mlp_gain[None, :], cot_early, cot_late, ff_set, padded(w_down.T), n_dp, n_head
    )
    dpre, conv_part, head_gain_grad, mlp_reduced = mixer_bwd(
        hg_rows, first_set, aux, docrow, conv, gain, (pre, *saved),
        mlp_terms.reshape(n_dp, -1, mlp_terms.shape[1]),
    )
    taps = conv_part.shape[0]
    shared = 2 * (tokens.shape[1] // 128) + 8
    small = jnp.concatenate(
        [
            jnp.zeros((tokens.shape[1] // 128, 128), F32),
            mlp_gain_grad.reshape(-1, 128),
            jnp.pad(head_gain_grad, ((0, 7), (0, 0))),
            conv_part.reshape(-1, 128),
        ]
    )
    input_grad, mix_reduced, summed, down_reduced = end(
        dpre, first_set, normed_rows, hg_rows, mixed, down_terms.reshape(n_dp, -1, wide), tokens, attn_gain[None, :], hidden_grad, small,
        n_dp, n_head, shared,
    )
    gains = summed[: shared - 8].reshape(2, -1)
    conv_grad = jnp.swapaxes(summed[shared:].reshape(taps, 3, hid), 0, 1)
    spread_out = spread(output, input_grad, mix_reduced, mlp_reduced, down_reduced, hid, heads, ff)
    output, input_grad, to_out, query, key, value, gate, beta, ff_gate, ff_up, ff_down = spread_out
    return (
        output,
        input_grad,
        gains[0],
        query,
        key,
        value,
        beta.T,
        gate,
        conv_grad,
        summed[shared - 8],
        to_out,
        gains[1],
        ff_gate.T,
        ff_up.T,
        ff_down,
    )


def solution(mesh):
    rows = P(("dp", "head"), None)
    in_specs = (
        rows,
        P("dp", None),
        P(),
        P("dp", "head"),
        P("dp", "head"),
        P("dp", "head"),
        P("dp", "head"),
        P("dp", "head"),
        P(None, None, "head"),
        P(),
        P("head", "dp"),
        P(),
        P("dp", "head"),
        P("dp", "head"),
        P("head", "dp"),
        rows,
    )
    out_specs = (
        rows,
        rows,
        P(),
        P("dp", "head"),
        P("dp", "head"),
        P("dp", "head"),
        P("dp", "head"),
        P("dp", "head"),
        P(None, None, "head"),
        P(),
        P("head", "dp"),
        P(),
        P("dp", "head"),
        P("dp", "head"),
        P("head", "dp"),
    )
    return jax.shard_map(
        on_device, mesh=mesh, in_specs=in_specs, out_specs=out_specs, check_vma=False
    )
```

```python
from functools import partial

import jax
import jax.numpy as jnp
from jax import lax
from jax.experimental import pallas as pl
from jax.experimental.pallas import tpu as pltpu
from jax.sharding import PartitionSpec as P

HEAD_DIM = 128
CHUNK = 128
GROUP = 4
STEP = CHUNK * GROUP
PAD = 8
F32 = jnp.float32
BF16 = jnp.bfloat16
COT_PARTS = 2
VMEM_LIMIT = 56 * 1024 * 1024


def dot(left, right, dims):
    return lax.dot_general(left, right, (dims, ((), ())), preferred_element_type=F32)


def mul(left, right):
    return dot(left.astype(BF16), right.astype(BF16), ((1,), (0,)))


def mul_t(left, right):
    return dot(left.astype(BF16), right.astype(BF16), ((1,), (1,)))


def t_mul(left, right):
    return dot(left.astype(BF16), right.astype(BF16), ((0,), (0,)))


def unit_inverses(lowers):
    row = lax.broadcasted_iota(jnp.int32, (CHUNK, CHUNK), 0)
    col = lax.broadcasted_iota(jnp.int32, (CHUNK, CHUNK), 1)
    eye = (row == col).astype(F32)
    level = lambda bit: jnp.logical_and(
        (row >> (bit + 1)) == (col >> (bit + 1)), (row >> bit) > (col >> bit)
    )
    first = level(0)
    solved = [eye - jnp.where(first, a, 0.0) for a in lowers]
    for bit in range(1, CHUNK.bit_length() - 1):
        mask = level(bit)
        right = [mul(jnp.where(mask, a, 0.0), t) for a, t in zip(lowers, solved)]
        solved = [t - mul(t, r) for t, r in zip(solved, right)]
    return solved


def conv_parts(pre, ext, conv, aux):
    summed = pre * conv[3:4, :]
    for offset in range(1, 4):
        shifted = ext[PAD - offset : PAD - offset + STEP, :]
        summed = summed + shifted * aux[:, offset - 1 : offset] * conv[3 - offset : 4 - offset, :]
    return summed


def unit_rows(act, scale):
    out = []
    for h in range(act.shape[1] // HEAD_DIM):
        part = act[:, h * HEAD_DIM : (h + 1) * HEAD_DIM]
        inv = lax.rsqrt(jnp.sum(part * part, axis=-1, keepdims=True) + 1e-6)
        out.append((part * inv * scale, inv))
    return out


def chunk_masks(aux, docrow):
    row = lax.broadcasted_iota(jnp.int32, (CHUNK, CHUNK), 0)
    col = lax.broadcasted_iota(jnp.int32, (CHUNK, CHUNK), 1)
    made = []
    for c in range(GROUP):
        same = aux[c * CHUNK : (c + 1) * CHUNK, 8:9] == docrow[c : c + 1, :]
        made.append((jnp.logical_and(same, row > col), jnp.logical_and(same, row >= col)))
    return made


def mixer_fwd_kernel(
    lines, count,
    x_ref, w_ref, aux_ref, docrow_ref, conv_ref, gain_ref, cot_ref, ff_ref,
    pre_ref, mixed_ref, o_ref, t_ref, phi_ref, s_ref, p_ref, d_ref, ew_ref, att_ref, cot_rows, ff_rows,
    ext, state, terms, near, far_terms, near_s, near_r, far_s, far_r, right_s, left_s, over_s, landed, local, *cot_sems,
):
    heads = mixed_ref.shape[1] // HEAD_DIM
    hid = heads * HEAD_DIM
    grid_step, last_step = pl.program_id(0), pl.num_programs(0) - 1
    first, hop_step, arrived, last = shard_line(lines, ff_ref, ff_rows, (right_s, left_s, over_s, landed, local.at[0]))
    cots, held = cot_gather(count, cot_ref, cot_rows, cot_sems, local.at[1])
    cot_parts = cots.parts

    attend = OwnerScatter(count, att_ref, (terms, near, far_terms, near_s, near_r, far_s, far_r))

    @pl.when(grid_step == 0)
    def _():
        greet(lines, count)
        first()
        held.start()
        for p in range(cot_parts):
            cots.send(p)

    @pl.when(grid_step == 2)
    def _():
        hop_step(0)
        cots.pass_on(0)

    @pl.when(pl.program_id(0) == 0)
    def _():
        ext[0:PAD, :] = jnp.zeros((PAD, 3 * hid), F32)
        state[...] = jnp.zeros_like(state)

    pre_ref[...] = dot(x_ref[...], w_ref[:, hid:], ((1,), (0,)))
    pl.when(grid_step >= 1)(lambda: attend.settle(grid_step - 1))
    aux = aux_ref[...]
    conv = conv_ref[...]
    pre = pre_ref[:, : 3 * hid]
    ext[PAD:, :] = pre
    act = conv_parts(pre, ext, conv, aux)
    act = act * jax.nn.sigmoid(act)
    ext[0:PAD, :] = ext[STEP:, :]
    q = unit_rows(act[:, :hid], HEAD_DIM**-0.5)
    k = unit_rows(act[:, hid : 2 * hid], 1.0)
    beta = jax.nn.sigmoid(pre_ref[:, 4 * hid : 4 * hid + 8])
    masks = chunk_masks(aux, docrow_ref[0])

    items = [(c, h) for c in range(GROUP) for h in range(heads)]
    rows = [slice(c * CHUNK, (c + 1) * CHUNK) for c in range(GROUP)]
    lowers, scores = [], []
    for c, h in items:
        key, query = k[h][0][rows[c]], q[h][0][rows[c]]
        both = mul_t(jnp.concatenate([key, query], axis=0), key)
        lowers.append(jnp.where(masks[c][0], both[:CHUNK] * beta[rows[c], h : h + 1], 0.0))
        scores.append(jnp.where(masks[c][1], both[CHUNK:], 0.0).astype(BF16))
    solved = unit_inverses(lowers)
    parts = []
    for (c, h), inverse, score in zip(items, solved, scores):
        key = k[h][0][rows[c]]
        value = act[rows[c], 2 * hid + h * HEAD_DIM : 2 * hid + (h + 1) * HEAD_DIM]
        b = beta[rows[c], h : h + 1]
        enter, leave = aux[rows[c], 3:4], aux[rows[c], 4:5]
        inverse = inverse.astype(BF16)
        wu = mul(inverse, jnp.concatenate([key * b, value * b], axis=1))
        ew, u = wu[:, :HEAD_DIM] * enter, wu[:, HEAD_DIM:]
        phi_b = t_mul(key * leave, jnp.concatenate([ew, u], axis=1))
        parts.append((ew, u, phi_b[:, :HEAD_DIM].astype(BF16), phi_b[:, HEAD_DIM:]))
        t_ref[c, h] = inverse
        p_ref[c, h] = score
        ew_ref[c, h] = ew.astype(BF16)
        phi_ref[c, h] = parts[-1][2]
    for h in range(heads):
        s = state[h]
        for c in range(GROUP):
            low = s.astype(BF16)
            s_ref[c, h] = low
            _, _, phi, b_term = parts[c * heads + h]
            keep = aux[(c + 1) * CHUNK - 1 : (c + 1) * CHUNK, 3:4]
            s = s * keep - mul(phi, low) + b_term
        state[h] = s
    gain = gain_ref[...]
    for (c, h), (ew, u, _, _), score in zip(items, parts, scores):
        enter = aux[rows[c], 3:4]
        from_state = mul(jnp.concatenate([ew, q[h][0][rows[c]] * enter], axis=0), s_ref[c, h])
        d = (u - from_state[:CHUNK]).astype(BF16)
        d_ref[c, h] = d
        o = from_state[CHUNK:] + mul(score, d)
        cols = slice(h * HEAD_DIM, (h + 1) * HEAD_DIM)
        o_ref[rows[c], cols] = o
        normed = o * lax.rsqrt(jnp.mean(o * o, axis=-1, keepdims=True) + 1e-5) * gain
        gate = pre_ref[rows[c], 3 * hid + h * HEAD_DIM : 3 * hid + (h + 1) * HEAD_DIM]
        mixed_ref[rows[c], cols] = (normed * (gate * jax.nn.sigmoid(gate))).astype(BF16)

    attend.offer(grid_step, dot(mixed_ref[...], w_ref[:, :hid], ((1,), (1,))))

    @pl.when(grid_step == last_step)
    def _():
        attend.settle(grid_step)
        for p in range(1, cot_parts):
            cots.pass_on(p)
        pl.loop(1, lines - 1)(hop_step)
        held.wait()
        for p in range(cot_parts):
            cots.arrive(p)
            cots.sent(p)
        arrived()
        attend.finish()
        last()


def mixer_bwd_kernel(
    lines, steps,
    hg_ref, wout_ref, pre_ref, halo_ref, aux_ref, docrow_ref, conv_ref, gain_ref,
    o_ref, t_ref, phi_ref, s_ref, p_ref, d_ref, ew_ref, terms_ref,
    dpre_ref, dconv_ref, dgain_ref, sum_ref,
    ext, later, dstate, own, own_s, *dp_refs,
):
    heads = o_ref.shape[1] // HEAD_DIM
    hid = heads * HEAD_DIM
    grid_step = pl.program_id(0)
    side = lax.axis_index("dp") % 2
    order = lambda n: (n // lines, outside_in(lines, n % lines))
    line = LineScatter(lines, lambda j: terms_ref.at[j], lambda place: own.at[place], dp_refs, order)
    fetch = lambda place: pltpu.make_async_copy(terms_ref.at[2 * place + side], own.at[place], own_s.at[place])

    @pl.when(grid_step == 0)
    def _():
        greet_line(lines)
        for place in range(lines):
            fetch(place).start()
        line.offer_all()
        for place in range(lines):
            fetch(place).wait()

    per_step = 5
    base = 3

    def point(i):
        n = grid_step * per_step + i - base
        line.point(n)

    point(0)

    @pl.when(pl.program_id(0) == 0)
    def _():
        later[STEP:, :] = jnp.zeros((PAD, 3 * hid), F32)
        dstate[...] = jnp.zeros_like(dstate)
        dconv_ref[...] = jnp.zeros_like(dconv_ref)
        dgain_ref[...] = jnp.zeros_like(dgain_ref)

    mixed_grad = dot(hg_ref[...], wout_ref[...], ((1,), (0,))).astype(BF16).astype(F32)
    aux = aux_ref[...]
    conv = conv_ref[...]
    pre = pre_ref[:, : 3 * hid]
    ext[0:PAD, :] = halo_ref[:, : 3 * hid]
    ext[PAD:, :] = pre
    lin = conv_parts(pre, ext, conv, aux)
    sig = jax.nn.sigmoid(lin)
    act = lin * sig
    dsilu = sig * (1.0 + lin * (1.0 - sig))
    scale = HEAD_DIM**-0.5
    q = unit_rows(act[:, :hid], 1.0)
    k = unit_rows(act[:, hid : 2 * hid], 1.0)
    beta = jax.nn.sigmoid(pre_ref[:, 4 * hid : 4 * hid + 8])
    masks = chunk_masks(aux, docrow_ref[0])
    gain = gain_ref[...]

    items = [(c, h) for c in range(GROUP) for h in range(heads)]
    rows = [slice(c * CHUNK, (c + 1) * CHUNK) for c in range(GROUP)]
    cols = [slice(h * HEAD_DIM, (h + 1) * HEAD_DIM) for h in range(heads)]

    d_out, d_gain = [], jnp.zeros((1, HEAD_DIM), F32)
    for h in range(heads):
        o = o_ref[:, cols[h]]
        inv = lax.rsqrt(jnp.mean(o * o, axis=-1, keepdims=True) + 1e-5)
        unit = o * inv
        gate = pre_ref[:, 3 * hid + h * HEAD_DIM : 3 * hid + (h + 1) * HEAD_DIM]
        s = jax.nn.sigmoid(gate)
        dm = mixed_grad[:, cols[h]]
        dpre_ref[:, 3 * hid + h * HEAD_DIM : 3 * hid + (h + 1) * HEAD_DIM] = (
            dm * unit * gain * (s * (1.0 + gate * (1.0 - s)))
        ).astype(BF16)
        dn = dm * (gate * s)
        d_gain = d_gain + jnp.sum(dn * unit, axis=0, keepdims=True)
        du = dn * gain
        d_out.append(inv * (du - unit * jnp.mean(du * unit, axis=-1, keepdims=True)))
    dgain_ref[...] += d_gain
    point(1)

    first = []
    for c, h in items:
        enter = aux[rows[c], 3:4]
        do = d_out[h][rows[c]].astype(BF16)
        eq = (q[h][0][rows[c]] * (enter * scale)).astype(BF16)
        x = t_mul(p_ref[c, h], do)
        c_term = t_mul(
            jnp.concatenate([eq, -ew_ref[c, h]], axis=0),
            jnp.concatenate([do, x.astype(BF16)], axis=0),
        )
        first.append((do, x, c_term))
    point(2)
    after = {}
    for h in range(heads):
        ds = dstate[h]
        for c in reversed(range(GROUP)):
            low = ds.astype(BF16)
            after[c, h] = low
            keep = aux[(c + 1) * CHUNK - 1 : (c + 1) * CHUNK, 3:4]
            ds = ds * keep - t_mul(phi_ref[c, h], low) + first[c * heads + h][2]
        dstate[h] = ds
    db_cols = []
    grads = {}
    point(3)
    for (c, h), (do, x, _) in zip(items, first):
        enter, leave = aux[rows[c], 3:4], aux[rows[c], 4:5]
        b = beta[rows[c], h : h + 1]
        key, query = k[h][0][rows[c]], q[h][0][rows[c]] * scale
        value = act[rows[c], 2 * hid + h * HEAD_DIM : 2 * hid + (h + 1) * HEAD_DIM]
        ds = after[c, h]
        d, s = d_ref[c, h], s_ref[c, h]
        dr = t_mul(t_ref[c, h], x + mul(key * leave, ds))
        stacked = jnp.concatenate([do, dr.astype(BF16)], axis=0)
        with_d = mul_t(stacked, d)
        with_s = mul_t(stacked, s) * jnp.concatenate([enter, enter], axis=0)
        dp = jnp.where(masks[c][1], with_d[:CHUNK], 0.0)
        da = jnp.where(masks[c][0], -with_d[CHUNK:], 0.0)
        pair = jnp.concatenate([dp, da], axis=0).astype(BF16)
        with_k = mul(pair, key)
        dq = with_s[:CHUNK] + with_k[:CHUNK]
        row_k = with_k[CHUNK:] - with_s[CHUNK:]
        dk = b * row_k + t_mul(pair, jnp.concatenate([query, key * b], axis=0))
        dk = dk + mul_t(d, ds) * leave
        db = jnp.sum(dr * value + key * row_k, axis=-1, keepdims=True)
        grads[c, h] = (dq * scale, dk, dr * b, db * b * (1.0 - b))
    point(4)
    for h in range(heads):
        whole = [jnp.concatenate([grads[c, h][i] for c in range(GROUP)], axis=0) for i in range(4)]
        for i, unit in ((0, q[h]), (1, k[h])):
            y, inv = unit
            grad = inv * (whole[i] - y * jnp.sum(y * whole[i], axis=-1, keepdims=True))
            at = slice(i * hid + h * HEAD_DIM, i * hid + (h + 1) * HEAD_DIM)
            later[0:STEP, at] = grad * dsilu[:, at]
        at = slice(2 * hid + h * HEAD_DIM, 2 * hid + (h + 1) * HEAD_DIM)
        later[0:STEP, at] = whole[2] * dsilu[:, at]
        db_cols.append(whole[3])
    lane = lax.broadcasted_iota(jnp.int32, (STEP, HEAD_DIM), 1)
    tail = jnp.zeros((STEP, HEAD_DIM), F32)
    for h in range(heads):
        tail = jnp.where(lane == h, db_cols[h], tail)
    dpre_ref[:, 4 * hid :] = tail.astype(BF16)
    dlin = later[0:STEP, :]
    dpre = dlin * conv[3:4, :]
    taps = [jnp.sum(dlin * pre, axis=0, keepdims=True)]
    for offset in range(1, 4):
        ahead = later[offset : offset + STEP, :]
        dpre = dpre + ahead * aux[:, 4 + offset : 5 + offset] * conv[3 - offset : 4 - offset, :]
        behind = ext[PAD - offset : PAD - offset + STEP, :] * aux[:, offset - 1 : offset]
        taps.append(jnp.sum(dlin * behind, axis=0, keepdims=True))
    dpre_ref[:, : 3 * hid] = dpre.astype(BF16)
    for offset in range(4):
        dconv_ref[3 - offset : 4 - offset, :] += taps[offset]
    later[STEP:, :] = later[0:PAD, :]

    @pl.when(grid_step == steps - 1)
    def _():
        pl.loop(max(steps * per_step - base, 0), line.points)(line.point)
        line.finish(sum_ref)
        line.close()


def mixer_fwd(x_rows, weights, aux, docrow, conv, gain, cotangent, ff_mine, n_dp, count):
    hid = conv.shape[1] // 3
    length, width = x_rows.shape[0], weights.shape[1] - hid
    heads, chunks = hid // HEAD_DIM, length // CHUNK
    lines, dma = n_dp // 2, lambda *shape: pltpu.SemaphoreType.DMA(shape)
    anywhere = pl.BlockSpec(memory_space=pl.ANY)
    rows = lambda n: pl.BlockSpec((STEP, n), lambda i: (i, 0))
    whole = lambda a: pl.BlockSpec(a.shape, lambda i: (0,) * a.ndim)
    square = pl.BlockSpec((GROUP, heads, CHUNK, HEAD_DIM), lambda i: (i, 0, 0, 0))
    squares = jax.ShapeDtypeStruct((chunks, heads, CHUNK, HEAD_DIM), BF16)
    return pl.pallas_call(
        partial(mixer_fwd_kernel, lines, count),
        grid=(length // STEP,),
        in_specs=[
            rows(x_rows.shape[1]), whole(weights), rows(aux.shape[1]),
            pl.BlockSpec((1, GROUP, CHUNK), lambda i: (i, 0, 0)), whole(conv), whole(gain),
            whole(cotangent), whole(ff_mine),
        ],
        out_specs=[rows(width), rows(hid), rows(hid)]
        + [square] * 6
        + [pl.BlockSpec((STEP, x_rows.shape[1]), lambda i: (0, 0))]
        + [anywhere] * 2,
        out_shape=[
            jax.ShapeDtypeStruct((length, width), F32),
            jax.ShapeDtypeStruct((length, hid), BF16),
            jax.ShapeDtypeStruct((length, hid), F32),
        ]
        + [squares] * 6
        + [
            jax.ShapeDtypeStruct((STEP, x_rows.shape[1]), F32),
            jax.ShapeDtypeStruct((count, *cotangent.shape), BF16),
            jax.ShapeDtypeStruct((n_dp, *ff_mine.shape), BF16),
        ],
        scratch_shapes=[
            pltpu.VMEM((PAD + STEP, 3 * hid), F32),
            pltpu.VMEM((heads, HEAD_DIM, HEAD_DIM), F32),
        ]
        + OwnerScatter.scratch(count, STEP, x_rows.shape[1])
        + [
            dma(lines), dma(lines), dma(lines), dma(n_dp), dma(2),
        ]
        + HeadGather.scratch(count, COT_PARTS),
        compiler_params=pltpu.CompilerParams(vmem_limit_bytes=VMEM_LIMIT, has_side_effects=True, collective_id=3),
        name="mixer_fwd",
    )(x_rows, weights, aux, docrow, conv, gain, cotangent, ff_mine)


def mixer_bwd(hg_rows, weights, aux, docrow, conv, gain, saved, terms):
    pre, o, t, phi, s, p, d, ew = saved
    length, width = pre.shape
    hid = conv.shape[1] // 3
    heads, steps = hid // HEAD_DIM, length // STEP
    last = steps - 1
    n_dp, block, wide = terms.shape
    lines = n_dp // 2
    rows = lambda n: pl.BlockSpec((STEP, n), lambda i: (last - i, 0))
    whole = lambda a: pl.BlockSpec(a.shape, lambda i: (0,) * a.ndim)
    square = pl.BlockSpec((GROUP, heads, CHUNK, HEAD_DIM), lambda i: (last - i, 0, 0, 0))
    halo = pl.BlockSpec(
        (PAD, width), lambda i: (jnp.maximum((last - i) * (STEP // PAD) - 1, 0), 0)
    )
    return pl.pallas_call(
        partial(mixer_bwd_kernel, lines, steps),
        grid=(steps,),
        in_specs=[
            rows(hg_rows.shape[1]), pl.BlockSpec((weights.shape[0], hid), lambda i: (0, 0)), rows(width), halo, rows(aux.shape[1]),
            pl.BlockSpec((1, GROUP, CHUNK), lambda i: (last - i, 0, 0)), whole(conv), whole(gain),
            rows(hid),
        ]
        + [square] * 6
        + [pl.BlockSpec(memory_space=pl.ANY)],
        out_specs=[
            rows(width),
            pl.BlockSpec((4, 3 * hid), lambda i: (0, 0)),
            pl.BlockSpec((1, HEAD_DIM), lambda i: (0, 0)),
            pl.BlockSpec((block, wide), lambda i: (0, 0)),
        ],
        out_shape=[
            jax.ShapeDtypeStruct((length, width), BF16),
            jax.ShapeDtypeStruct((4, 3 * hid), F32),
            jax.ShapeDtypeStruct((1, HEAD_DIM), F32),
            jax.ShapeDtypeStruct((block, wide), F32),
        ],
        scratch_shapes=[
            pltpu.VMEM((PAD + STEP, 3 * hid), F32),
            pltpu.VMEM((STEP + PAD, 3 * hid), F32),
            pltpu.VMEM((heads, HEAD_DIM, HEAD_DIM), F32),
            pltpu.VMEM((lines, block, wide), BF16),
            pltpu.SemaphoreType.DMA((lines,)),
        ]
        + LineScatter.scratch(lines, block, wide),
        compiler_params=pltpu.CompilerParams(vmem_limit_bytes=VMEM_LIMIT, has_side_effects=True, collective_id=4),
        name="mixer_bwd",
    )(hg_rows, weights, pre, pre, aux, docrow, conv, gain, o, t, phi, s, p, d, ew, terms)


MESH = pl.DeviceIdType.MESH


def remote(src, dst, sent, landed, axis, to):
    return pltpu.make_async_remote_copy(
        src_ref=src, dst_ref=dst, send_sem=sent, recv_sem=landed,
        device_id={axis: to}, device_id_type=MESH,
    )


def shard_line(lines, own, out, sems):
    right_s, left_s, over_s, landed, local = sems
    me = lax.axis_index("dp")
    spot, side = me // 2, me % 2
    slot = lambda place: 2 * place + side
    across = me + 1 - 2 * side

    def hop(step, where):
        return (spot - step, me + 2, right_s) if where == 0 else (spot + step, me - 2, left_s)

    def going(step, where):
        place, to, sent = hop(step, where)
        src = out.at[slot(place)] if not isinstance(step, int) or step else own
        return remote(src, out.at[slot(place)], sent.at[step], landed.at[slot(place)], "dp", to)

    def goes(step, where):
        if where == 0:
            return jnp.logical_and(spot - step >= 0, spot + 1 < lines)
        return jnp.logical_and(spot + step < lines, spot >= 1)

    def over(place):
        return remote(out.at[slot(place)], out.at[slot(place)], over_s.at[place], landed.at[slot(place)], "dp", across)

    def first():
        pltpu.make_async_copy(own, out.at[me], local).start()
        remote(own, out.at[me], over_s.at[spot], landed.at[me], "dp", across).start()
        for where in (0, 1):
            pl.when(goes(0, where))(lambda where=where: going(0, where).start())

    def arrive(step, place):
        @pl.when(jnp.logical_and(place >= 0, place < lines))
        def _():
            over(place).wait_recv()
            over(place).start()

    def hop_step(step):
        for where in (0, 1):
            place = spot - step - 1 if where == 0 else spot + step + 1
            arrive(step, place)
            if isinstance(step, int) and step + 1 >= lines - 1:
                continue
            pl.when(jnp.logical_and(goes(step + 1, where), step + 1 < lines - 1))(
                lambda where=where: going(step + 1, where).start()
            )

    def arrived():
        pltpu.make_async_copy(own, out.at[me], local).wait()

        @pl.loop(0, lines)
        def _(place):
            there = 2 * place + 1 - side
            remote(out.at[there], out.at[there], over_s.at[place], landed.at[there], "dp", across).wait_recv()

    def last():
        pl.loop(0, lines)(lambda place: over(place).wait_send())

        @pl.loop(0, lines - 1)
        def _(step):
            for where in (0, 1):
                pl.when(goes(step, where))(lambda where=where: going(step, where).wait_send())

    return first, hop_step, arrived, last


def greet(lines, count):
    barrier = pltpu.get_barrier_semaphore()
    me = lax.axis_index("dp")
    spot, across = me // 2, me + 1 - 2 * (me % 2)

    def tell(axis, to):
        pl.semaphore_signal(barrier, 1, device_id={axis: to}, device_id_type=MESH)

    tell("dp", across)
    pl.when(spot >= 1)(lambda: tell("dp", me - 2))
    pl.when(spot + 1 < lines)(lambda: tell("dp", me + 2))
    head = lax.axis_index("head")
    tell("head", head + 1 - 2 * (head % 2))
    for f in range(1, count // 2):
        tell("head", lax.rem(head + 2 * f, count))
    beside = jnp.minimum(spot, 1) + jnp.minimum(lines - 1 - spot, 1)
    pl.semaphore_wait(barrier, 1 + count // 2 + beside)


def greet_line(lines):
    barrier = pltpu.get_barrier_semaphore()
    me = lax.axis_index("dp")

    def tell(to):
        pl.semaphore_signal(barrier, 1, device_id={"dp": to}, device_id_type=MESH)

    tell(me + 1 - 2 * (me % 2))
    pl.loop(1, lines)(lambda hop: tell(lax.rem(me + 2 * hop, 2 * lines)))
    pl.semaphore_wait(barrier, lines)


def cot_gather(count, cot_ref, cot_rows, sems, held_s):
    parts = sems[1].shape[0]
    size = cot_ref.shape[0] // parts
    at = lambda p: pl.ds(p * size, size)
    me = lax.axis_index("head")
    cots = HeadGather(count, parts, lambda p: cot_ref.at[at(p)], lambda owner, p: cot_rows.at[owner, at(p)], sems)
    return cots, pltpu.make_async_copy(cot_ref, cot_rows.at[me], held_s)


def start_kernel(lines, count, parts, tok_ref, gain_ref, out_w, *refs):
    *in_ws, cot_ref, rows_ref, wall_ref, cot_rows, mine, w_ref = refs[:11]
    start_body(
        lines, count, parts, tok_ref, gain_ref, out_w, in_ws, cot_ref, rows_ref, wall_ref, cot_rows, mine, w_ref, *refs[11:]
    )


def start_body(lines, count, parts, tok_ref, gain_ref, out_w, in_ws, cot_ref, rows_ref, wall_ref, cot_rows, mine, w_ref,
               right_s, left_s, over_s, landed, local, far_s, pair_s, fwd_s, got, keep_s, *cot_sems):
    first, hop_step, arrived, last = shard_line(lines, w_ref, wall_ref, (right_s, left_s, over_s, landed, local.at[0]))
    at = out_w.shape[0]
    w_ref[:, :at] = out_w[...].T
    for w in in_ws:
        w_ref[:, at : at + w.shape[1]] = w[...]
        at += w.shape[1]
    greet(lines, count)
    first()
    me = lax.axis_index("head")
    pair = me + 1 - 2 * (me % 2)
    fars = [lax.rem(me + 2 * f, count) for f in range(1, count // 2)]
    size = tok_ref.shape[0] // parts
    span = lambda p: pl.ds(p * size, size)

    def block(owner, p):
        return rows_ref.at[owner, span(p)]

    for p in range(parts):
        x = tok_ref[p * size : (p + 1) * size, :].astype(F32)
        inv = lax.rsqrt(jnp.mean(x * x, axis=-1, keepdims=True) + 1e-6)
        mine[p * size : (p + 1) * size, :] = (x * inv * gain_ref[...]).astype(BF16)
        for f, far in enumerate(fars):
            remote(mine.at[span(p)], block(me, p), far_s.at[f, p], got.at[me, p], "head", far).start()
        remote(mine.at[span(p)], block(me, p), pair_s.at[p], got.at[me, p], "head", pair).start()
        pltpu.make_async_copy(mine.at[span(p)], block(me, p), keep_s.at[p]).start()

    cots, held = cot_gather(count, cot_ref, cot_rows, cot_sems, local.at[1])
    held.start()
    for p in range(cots.parts):
        cots.send(p)

    def pass_on(p):
        for f, far in enumerate(fars):
            moved = remote(block(far, p), block(far, p), fwd_s.at[f, p], got.at[far, p], "head", pair)
            moved.wait_recv()
            moved.start()

    for i in range(parts):
        pass_on(i)
        if i < lines - 1:
            hop_step(i)
    if lines - 1 > parts:
        pl.loop(parts, lines - 1)(hop_step)
    for p in range(cots.parts):
        cots.pass_on(p)
    arrived()
    last()
    held.wait()
    for p in range(cots.parts):
        cots.arrive(p)
        cots.sent(p)
    for p in range(parts):
        remote(mine.at[span(p)], block(pair, p), pair_s.at[p], got.at[pair, p], "head", pair).wait()
        pltpu.make_async_copy(mine.at[span(p)], block(me, p), keep_s.at[p]).wait()
        for f, far in enumerate(fars):
            remote(mine.at[span(p)], block(me, p), far_s.at[f, p], got.at[me, p], "head", far).wait_send()
            there = lax.rem(pair + 2 * (f + 1), count)
            remote(block(far, p), block(there, p), fwd_s.at[f, p], got.at[there, p], "head", pair).wait()


def start(tokens, gain, w_out, in_ws, cot, n_dp, n_head, parts=4):
    rows, width = tokens.shape
    shard = (in_ws[0].shape[0], w_out.shape[0] + sum(w.shape[1] for w in in_ws))
    lines, far = n_dp // 2, n_head // 2 - 1
    dma = lambda *shape: pltpu.SemaphoreType.DMA(shape)
    anywhere = pl.BlockSpec(memory_space=pl.ANY)
    vmem = pl.BlockSpec(memory_space=pltpu.VMEM)
    return pl.pallas_call(
        partial(start_kernel, lines, n_head, parts),
        out_shape=[jax.ShapeDtypeStruct((n_head, rows, width), BF16),
                   jax.ShapeDtypeStruct((n_dp, *shard), BF16),
                   jax.ShapeDtypeStruct((n_head, *cot.shape), BF16)],
        in_specs=[vmem] * (4 + len(in_ws)),
        out_specs=[anywhere] * 3,
        scratch_shapes=[
            pltpu.VMEM((rows, width), BF16),
            pltpu.VMEM(shard, BF16),
            dma(lines), dma(lines), dma(lines), dma(n_dp), dma(2),
            dma(far, parts), dma(parts), dma(far, parts), dma(n_head, parts), dma(parts),
        ]
        + HeadGather.scratch(n_head, COT_PARTS),
        compiler_params=pltpu.CompilerParams(vmem_limit_bytes=VMEM_LIMIT, has_side_effects=True, collective_id=0),
        name="start",
    )(tokens, gain, w_out, *in_ws, cot)


def when(condition):
    return pl.when(condition) if not isinstance(condition, bool) else (lambda f: f() if condition else None)


class HeadScatter:
    def __init__(self, count, refs):
        self.count = count
        (self.out, self.near, self.onward, self.far, self.own,
         self.out_s, self.near_r, self.onward_s, self.far_r) = refs
        self.me = lax.axis_index("head")
        self.side, self.place = self.me % 2, self.me // 2
        self.pair = self.me + 1 - 2 * self.side
        self.parts, self.depth, self.size = self.near.shape[0], self.own.shape[0], self.own.shape[1]

    @staticmethod
    def scratch(count, parts, size, width, depth):
        half = count // 2
        return [
            pltpu.VMEM((2, 2, half, size, width), BF16),
            pltpu.VMEM((parts, half, size, width), BF16),
            pltpu.VMEM((2, half - 1, size, width), BF16),
            pltpu.VMEM((parts, half - 1, size, width), BF16),
            pltpu.VMEM((depth, size, width), F32),
            pltpu.SemaphoreType.DMA((2,)),
            pltpu.SemaphoreType.DMA((parts,)),
            pltpu.SemaphoreType.DMA((2, half - 1)),
            pltpu.SemaphoreType.DMA((parts, half - 1)),
        ]

    def _near(self, p):
        slot = p % 2
        return remote(self.out.at[slot, 1 - self.side], self.near.at[p], self.out_s.at[slot], self.near_r.at[p], "head", self.pair)

    def _far(self, p, f):
        slot = p % 2
        to = lax.rem(self.me + 2 * (f + 1), self.count)
        return remote(self.onward.at[slot, f], self.far.at[p, f], self.onward_s.at[slot, f], self.far_r.at[p, f], "head", to)

    def offer(self, p, total):
        when(p >= 2)(lambda: self._near(p - 2).wait_send())
        for owner in range(self.count):
            self.out[p % 2, owner % 2, owner // 2] = total[owner * self.size : (owner + 1) * self.size].astype(BF16)
        self._near(p).start()

    def turn(self, p):
        slot, half = p % 2, self.count // 2
        self._near(p).wait_recv()
        both = lambda i: self.out[slot, self.side, i].astype(F32) + self.near[p, i].astype(F32)
        for f in range(half - 1):
            when(p >= 2)(lambda f=f: self._far(p - 2, f).wait_send())
            self.onward[slot, f] = both(lax.rem(self.place + f + 1, half)).astype(BF16)
            self._far(p, f).start()
        self.own[p % self.depth] = both(self.place)

    def take(self, p):
        total = self.own[p % self.depth]
        for f in range(self.count // 2 - 1):
            self._far(p, f).wait_recv()
            total = total + self.far[p, f].astype(F32)
        return total

    def close(self):
        for p in range(max(self.parts - 2, 0), self.parts):
            self._near(p).wait_send()
            for f in range(self.count // 2 - 1):
                self._far(p, f).wait_send()


class OwnerScatter:
    def __init__(self, count, out_ref, refs):
        self.count, self.out_ref = count, out_ref
        self.terms, self.near, self.far, self.near_s, self.near_r, self.far_s, self.far_r = refs
        self.me = lax.axis_index("head")
        self.side = self.me % 2
        self.pair = self.me + 1 - 2 * self.side

    @staticmethod
    def scratch(count, rows, width):
        half = count // 2
        sems = lambda n: pltpu.SemaphoreType.DMA((n,))
        return [
            pltpu.VMEM((count, rows, width), BF16),
            pltpu.VMEM((half, rows, width), BF16),
            pltpu.VMEM((half - 1, rows, width), BF16),
            sems(half), sems(half), sems(count), sems(half - 1),
        ]

    def _near(self, owner):
        at = owner // 2
        return remote(self.terms.at[owner], self.near.at[at], self.near_s.at[at], self.near_r.at[at], "head", self.pair)

    def _far(self, owner):
        at = lax.rem(self.me - owner + self.count, self.count) // 2 - 1
        return remote(self.terms.at[owner], self.far.at[at], self.far_s.at[owner], self.far_r.at[at], "head", owner)

    def _mine(self, owner):
        return owner % 2 == self.side

    def offer(self, owner, total):
        self.terms[owner] = total.astype(BF16)
        pl.when(jnp.logical_not(self._mine(owner)))(lambda: self._near(owner).start())

    def settle(self, owner):
        @pl.when(self._mine(owner))
        def _():
            self._near(owner).wait_recv()
            both = self.terms[owner].astype(F32) + self.near[owner // 2].astype(F32)

            @pl.when(owner == self.me)
            def _():
                self.out_ref[...] = both

            @pl.when(owner != self.me)
            def _():
                self.terms[owner] = both.astype(BF16)
                self._far(owner).start()

    def finish(self):
        for f in range(self.count // 2 - 1):
            sender = lax.rem(self.me + 2 * (f + 1), self.count)
            remote(self.terms.at[0], self.far.at[f], self.far_s.at[0], self.far_r.at[f], "head", sender).wait_recv()
            self.out_ref[...] += self.far[f].astype(F32)

        @pl.loop(0, self.count)
        def _(owner):
            pl.when(jnp.logical_not(self._mine(owner)))(lambda: self._near(owner).wait_send())
            pl.when(jnp.logical_and(self._mine(owner), owner != self.me))(lambda: self._far(owner).wait_send())


class HeadGather:
    def __init__(self, count, parts, own, block, refs):
        self.count, self.parts, self.own, self.block = count, parts, own, block
        self.far_s, self.pair_s, self.fwd_s, self.got = refs
        self.me = lax.axis_index("head")
        self.pair = self.me + 1 - 2 * (self.me % 2)

    @staticmethod
    def scratch(count, parts):
        far = count // 2 - 1
        return [pltpu.SemaphoreType.DMA(s) for s in ((far, parts), (parts,), (far, parts), (count, parts))]

    def _fars(self, base):
        return [(f, lax.rem(base + 2 * (f + 1), self.count)) for f in range(self.count // 2 - 1)]

    def _far(self, p, f, far):
        return remote(self.own(p), self.block(self.me, p), self.far_s.at[f, p], self.got.at[self.me, p], "head", far)

    def _pair(self, p):
        return remote(self.own(p), self.block(self.me, p), self.pair_s.at[p], self.got.at[self.me, p], "head", self.pair)

    def _on(self, p, f, owner):
        return remote(self.block(owner, p), self.block(owner, p), self.fwd_s.at[f, p], self.got.at[owner, p], "head", self.pair)

    def send(self, p):
        for f, far in self._fars(self.me):
            self._far(p, f, far).start()
        self._pair(p).start()

    def pass_on(self, p):
        for f, far in self._fars(self.me):
            self._on(p, f, far).wait_recv()
            self._on(p, f, far).start()

    def arrive(self, p):
        remote(self.own(p), self.block(self.pair, p), self.pair_s.at[p], self.got.at[self.pair, p], "head", self.pair).wait_recv()
        for f, far in self._fars(self.pair):
            self._on(p, f, far).wait_recv()

    def sent(self, p):
        self._pair(p).wait_send()
        for f, far in self._fars(self.me):
            self._far(p, f, far).wait_send()
            self._on(p, f, far).wait_send()


LEAD = 8


def mid_kernel(lines, count, parts, att_ref, tok_ref, gain_ref, cot_early, cot_late, ff_ref, down_mine,
               out_ref, grad_ref, hg_ref, gain_grad_ref, terms_ref, down_terms_ref, *scratch):
    scratch = list(scratch)
    take = lambda n: [scratch.pop(0) for _ in range(n)]
    down_refs, back_refs = take(9), take(9)
    second_sems, hg_sems = take(4), take(4)
    cot_ref, second, hidden, hg_own, total, loads, keep_s, down_all, right_s, left_s, over_s, landed = scratch
    size, width = tok_ref.shape[1:]
    ff = ff_ref.shape[1] // 2
    me = lax.axis_index("head")
    greet(lines, count)
    first, hop_step, arrived, last = shard_line(
        lines, down_mine, down_all, (right_s, left_s, over_s, landed, loads.at[1])
    )
    first()
    half = parts // 2
    loading = [
        pltpu.make_async_copy(src, cot_ref.at[:, at : at + half], loads.at[i])
        for i, (src, at) in ((0, (cot_early, 0)), (2, (cot_late, half)))
    ]
    for m in loading:
        m.start()
    down_w = lambda: down_all[...].reshape(-1, ff)
    down, back = (HeadScatter(count, r) for r in (down_refs, back_refs))
    here = lambda owner, p: second.at[p, owner]
    seconds = HeadGather(count, parts, lambda p: here(me, p), here, second_sems)
    there = lambda owner, p: hg_ref.at[owner, p]
    hgs = HeadGather(count, parts, lambda p: hg_own.at[p], there, hg_sems)
    keep = lambda p: pltpu.make_async_copy(hg_own.at[p], there(me, p), keep_s.at[p])
    total[...] = jnp.zeros_like(total)
    gain_grad_ref[...] = jnp.zeros_like(gain_grad_ref)

    def within(p, stage):
        pl.when(jnp.logical_and(p >= 0, p < parts))(lambda: stage(p))

    def norm(p):
        rows = tok_ref[p].astype(F32) + att_ref[p]
        hidden[p] = rows
        inv = lax.rsqrt(jnp.mean(rows * rows, axis=-1, keepdims=True) + 1e-6)
        second[p, me] = (rows * inv * gain_ref[...]).astype(BF16)
        seconds.send(p)

    def feed(p):
        seconds.arrive(p)
        rows = second[p].reshape(count * size, width)
        both = dot(rows, ff_ref[...], ((1,), (0,)))
        gate, up = both[:, :ff], both[:, ff:]
        sig = jax.nn.sigmoid(gate)
        act = gate * sig
        middle = (act * up).astype(BF16)

        @pl.when(p == 0)
        def _():
            hop_step(0)
            pl.loop(1, lines - 1)(hop_step)
            arrived()

        down.offer(p, dot(middle, down_w(), ((1,), (1,))))
        cot = cot_ref[:, p].reshape(count * size, width)
        grad = dot(cot, down_w(), ((1,), (0,))).astype(BF16).astype(F32)
        pair = jnp.concatenate(
            [(grad * up * sig * (1.0 + gate * (1.0 - sig))).astype(BF16), (grad * act).astype(BF16)], axis=1
        )
        back.offer(p, dot(pair, ff_ref[...], ((1,), (1,))))
        total[:, : 2 * ff] += dot(rows, pair, ((0,), (0,)))
        total[:, 2 * ff :] += dot(cot, middle, ((0,), (0,)))

    def turn(p):
        down.turn(p)
        back.turn(p)

    def finish(p):
        rows = hidden[p]
        out_ref[p] = (rows + down.take(p)).astype(BF16)
        second_grad = back.take(p).astype(BF16).astype(F32)
        inv = lax.rsqrt(jnp.mean(rows * rows, axis=-1, keepdims=True) + 1e-6)
        scaled = second_grad * gain_ref[...]
        mean = jnp.mean(scaled * rows, axis=-1, keepdims=True)
        grad = cot_ref[me, p].astype(F32) + inv * scaled - rows * (inv * inv * inv * mean)
        grad_ref[p] = grad
        gain_grad_ref[...] += jnp.sum(second_grad * rows * inv, axis=0, keepdims=True)
        hg_own[p] = grad.astype(BF16)
        hgs.send(p)
        keep(p).start()

    for p in range(LEAD):
        norm(p)
    for m in loading:
        m.wait()

    @pl.loop(0, parts + 2)
    def _(step):
        within(step + LEAD, norm)
        within(step, seconds.pass_on)
        within(step, feed)
        within(step, turn)
        within(step - 1, finish)
        within(step - 2, hgs.pass_on)

    terms_ref[...] = total[:, : 2 * ff].astype(BF16)
    down_terms_ref[...] = total[:, 2 * ff :].astype(BF16)

    @pl.loop(0, parts)
    def _(p):
        hgs.arrive(p)
        keep(p).wait()
        hgs.sent(p)
        seconds.sent(p)

    for s in (down, back):
        s.close()
    last()


def mid(attention, tokens, gain, cot_early, cot_late, ff_set, down_mine, n_dp, count, parts=8):
    rows, width = tokens.shape
    lines, ff = n_dp // 2, down_mine.shape[1]
    dma = lambda *shape: pltpu.SemaphoreType.DMA(shape)
    size = rows // parts
    anywhere = pl.BlockSpec(memory_space=pl.ANY)
    vmem = pl.BlockSpec(memory_space=pltpu.VMEM)
    scatter = HeadScatter.scratch(count, parts, size, width, 2)
    out, grad, hg, gain_grad, terms, down_terms = pl.pallas_call(
        partial(mid_kernel, lines, count, parts),
        out_shape=[
            jax.ShapeDtypeStruct((parts, size, width), BF16),
            jax.ShapeDtypeStruct((parts, size, width), F32),
            jax.ShapeDtypeStruct((count, parts, size, width), BF16),
            jax.ShapeDtypeStruct((1, width), F32),
            jax.ShapeDtypeStruct((width, 2 * ff), BF16),
            jax.ShapeDtypeStruct((width, ff), BF16),
        ],
        in_specs=[vmem] * 3 + [anywhere] * 2 + [vmem] * 2,
        out_specs=[vmem, vmem, anywhere, vmem, vmem, vmem],
        scratch_shapes=scatter * 2
        + HeadGather.scratch(count, parts) * 2
        + [
            pltpu.VMEM((count, parts, size, width), BF16),
            pltpu.VMEM((parts, count, size, width), BF16),
            pltpu.VMEM((parts, size, width), F32),
            pltpu.VMEM((parts, size, width), BF16),
            pltpu.VMEM((width, 3 * ff), F32),
            dma(3),
            dma(parts),
            pltpu.VMEM((n_dp, *down_mine.shape), BF16),
            dma(lines), dma(lines), dma(lines), dma(n_dp),
        ],
        compiler_params=pltpu.CompilerParams(vmem_limit_bytes=61 * 1024 * 1024, has_side_effects=True, collective_id=2),
        name="mid",
    )(
        attention.reshape(parts, size, width), tokens.reshape(parts, size, width), gain,
        *(c.reshape(count, parts // 2, size, width) for c in (cot_early, cot_late)), ff_set, down_mine,
    )
    return out.reshape(rows, width), grad.reshape(rows, width), hg.reshape(-1, width), gain_grad, terms, down_terms


class ChainScatter:
    LAG = 2

    def __init__(self, lines, terms, own, refs, by_piece):
        self.lines, self.terms, self.own, self.by_piece = lines, terms, own, by_piece
        self.cross, self.going, self.coming, self.cross_s, self.cross_r, self.go_s, self.come_r = refs
        self.pieces = self.cross_s.shape[1]
        self.size = self.cross.shape[1] // self.pieces
        self.me = lax.axis_index("dp")
        self.spot, self.side = self.me // 2, self.me % 2
        self.across = self.me + 1 - 2 * self.side
        self.items = (lines - 1) * self.pieces
        self.points = self.items + (lines - 1) * self.LAG

    @staticmethod
    def scratch(lines, rows, width):
        pieces = max(1, rows // 32)
        wide = lambda *lead: pltpu.VMEM((*lead, rows, width), BF16)
        sems = lambda *shape: pltpu.SemaphoreType.DMA((*shape, pieces))
        return [
            wide(lines), wide(2, lines), wide(2, lines),
            sems(lines), sems(lines), sems(2, lines), sems(2, lines),
        ]

    def _at(self, k):
        return pl.ds(pl.multiple_of(k * self.size, self.size), self.size)

    def _cross(self, place, k):
        at = self._at(k)
        src = self.terms(2 * place + 1 - self.side).at[at]
        return remote(src, self.cross.at[place, at], self.cross_s.at[place, k], self.cross_r.at[place, k], "dp", self.across)

    def _line(self, way, dest, k):
        to = self.me + 2 if way == 0 else self.me - 2
        at = self._at(k)
        return remote(self.going.at[way, dest, at], self.coming.at[way, dest, at], self.go_s.at[way, dest, k], self.come_r.at[way, dest, k], "dp", to)

    def offer(self, place, k):
        self._cross(place, k).start()

    def offer_all(self):
        for k in range(self.pieces):
            for d in range((self.lines + 1) // 2):
                for place in sorted({self.lines - 1 - d, d}, reverse=True):
                    self.offer(place, k)

    def _both(self, place, k):
        return self.own(place)[self._at(k), :].astype(F32) + self.cross[place, self._at(k), :].astype(F32)

    def _passes(self, way, dest):
        return dest > self.spot if way == 0 else dest < self.spot

    def _fed(self, way):
        return self.spot >= 1 if way == 0 else self.spot + 1 < self.lines

    def point(self, n):
        for way in (0, 1):
            away = self.spot if way == 0 else self.lines - 1 - self.spot
            item = n - away * self.LAG
            safe = jnp.clip(item, 0, self.items - 1)
            if self.by_piece:
                k, d = safe // (self.lines - 1), safe % (self.lines - 1)
            else:
                d, k = safe // self.pieces, safe % self.pieces
            dest = self.lines - 1 - d if way == 0 else d
            live = jnp.logical_and(item >= 0, item < self.items)

            @pl.when(jnp.logical_and(live, self._passes(way, dest)))
            def _(way=way, dest=dest, k=k):
                at = self._at(k)
                self._cross(dest, k).wait_recv()

                @pl.when(self._fed(way))
                def _():
                    self._line(way, dest, k).wait_recv()
                    self.going[way, dest, at, :] = (self._both(dest, k) + self.coming[way, dest, at, :].astype(F32)).astype(BF16)

                @pl.when(jnp.logical_not(self._fed(way)))
                def _():
                    self.going[way, dest, at, :] = self._both(dest, k).astype(BF16)

                self._line(way, dest, k).start()

    def finish(self, out_ref):
        for k in range(self.pieces):
            at = slice(k * self.size, (k + 1) * self.size)
            self._cross(self.spot, k).wait_recv()
            out_ref[at, :] = self._both(self.spot, k)
            for way in (0, 1):
                @pl.when(self._fed(way))
                def _(way=way, k=k, at=at):
                    self._line(way, self.spot, k).wait_recv()
                    out_ref[at, :] += self.coming[way, self.spot, at, :].astype(F32)

    def close(self):
        @pl.loop(0, self.lines * self.pieces)
        def _(i):
            place, k = i // self.pieces, i % self.pieces
            self._cross(place, k).wait_send()
            for way in (0, 1):
                pl.when(self._passes(way, place))(lambda way=way: self._line(way, place, k).wait_send())


class LineScatter:
    def __init__(self, lines, terms, own, refs, order):
        self.lines, self.terms, self.own, self.order = lines, terms, own, order
        self.cross, self.going, self.coming, self.cross_s, self.cross_r, self.go_s, self.come_r = refs
        self.pieces = self.cross_s.shape[1]
        self.size = self.cross.shape[1] // self.pieces
        self.me = lax.axis_index("dp")
        self.spot, self.side = self.me // 2, self.me % 2
        self.across = self.me + 1 - 2 * self.side
        self.points = lines * self.pieces

    @staticmethod
    def scratch(lines, rows, width):
        pieces = max(1, rows // 32)
        wide = pltpu.VMEM((lines, rows, width), BF16)
        sems = pltpu.SemaphoreType.DMA((lines, pieces))
        return [wide, wide, wide, sems, sems, sems, sems]

    def _at(self, k):
        return pl.ds(pl.multiple_of(k * self.size, self.size), self.size)

    def _cross(self, place, k):
        at = self._at(k)
        src = self.terms(2 * place + 1 - self.side).at[at]
        return remote(src, self.cross.at[place, at], self.cross_s.at[place, k], self.cross_r.at[place, k], "dp", self.across)

    def _on(self, sender, dest, k):
        at = self._at(k)
        return remote(self.going.at[dest, at], self.coming.at[sender, at], self.go_s.at[dest, k], self.come_r.at[sender, k], "dp", 2 * dest + self.side)

    def offer(self, place, k):
        self._cross(place, k).start()

    def offer_all(self):
        @pl.loop(0, self.points)
        def _(n):
            k, place = self.order(n)
            self.offer(place, k)

    def _both(self, place, k):
        return self.own(place)[self._at(k), :].astype(F32) + self.cross[place, self._at(k), :].astype(F32)

    def point(self, n):
        k, dest = self.order(jnp.clip(n, 0, self.points - 1))

        @pl.when(jnp.logical_and(jnp.logical_and(n >= 0, n < self.points), dest != self.spot))
        def _():
            self._cross(dest, k).wait_recv()
            self.going[dest, self._at(k), :] = self._both(dest, k).astype(BF16)
            self._on(self.spot, dest, k).start()

    def finish(self, out_ref):
        for k in range(self.pieces):
            at = slice(k * self.size, (k + 1) * self.size)
            self._cross(self.spot, k).wait_recv()
            out_ref[at, :] = self._both(self.spot, k)

            @pl.loop(1, self.lines)
            def _(hop, k=k, at=at):
                sender = lax.rem(self.spot + hop, self.lines)
                self._on(sender, self.spot, k).wait_recv()
                out_ref[at, :] += self.coming[sender, at, :].astype(F32)

    def close(self):
        @pl.loop(0, self.points)
        def _(i):
            place, k = i // self.pieces, i % self.pieces
            self._cross(place, k).wait_send()
            pl.when(place != self.spot)(lambda: self._on(self.spot, place, k).wait_send())


def outside_in(lines, i):
    return jnp.where(i % 2 == 0, lines - 1 - i // 2, i // 2)


class SmallSum:
    def __init__(self, n_dp, count, shared, refs):
        self.n_dp, self.count, self.shared = n_dp, count, shared
        self.mine, self.theirs, self.half, self.halves, self.a_s, self.a_r, self.b_s, self.b_r = refs
        self.dp, self.head = lax.axis_index("dp"), lax.axis_index("head")

    @staticmethod
    def scratch(n_dp, count, rows, shared):
        return [
            pltpu.VMEM((rows, 128), F32),
            pltpu.VMEM((n_dp, rows, 128), F32),
            pltpu.VMEM((shared, 128), F32),
            pltpu.VMEM((count, shared, 128), F32),
            pltpu.SemaphoreType.DMA((n_dp,)),
            pltpu.SemaphoreType.DMA((n_dp,)),
            pltpu.SemaphoreType.DMA((count,)),
            pltpu.SemaphoreType.DMA((count,)),
        ]

    def _a(self, hop):
        to = lax.rem(self.dp + hop, self.n_dp)
        return remote(self.mine, self.theirs.at[self.dp], self.a_s.at[hop], self.a_r.at[self.dp], "dp", to)

    def _b(self, hop):
        to = lax.rem(self.head + hop, self.count)
        return remote(self.half, self.halves.at[self.head], self.b_s.at[hop], self.b_r.at[self.head], "head", to)

    def start(self):
        self.theirs[self.dp] = self.mine[...]

        @pl.loop(1, self.n_dp)
        def _(hop):
            self._a(hop).start()

    def turn(self, out_ref):
        @pl.loop(1, self.n_dp)
        def _(hop):
            sender = lax.rem(self.dp + self.n_dp - hop, self.n_dp)
            remote(self.mine, self.theirs.at[sender], self.a_s.at[hop], self.a_r.at[sender], "dp", sender).wait_recv()

        total = self.theirs[0]
        for i in range(1, self.n_dp):
            total = total + self.theirs[i]
        out_ref[...] = total
        self.half[...] = total[: self.shared]
        self.halves[self.head] = total[: self.shared]
        for hop in range(1, self.count):
            self._b(hop).start()

    def finish(self, out_ref):
        for hop in range(1, self.count):
            sender = lax.rem(self.head + self.count - hop, self.count)
            remote(self.half, self.halves.at[sender], self.b_s.at[hop], self.b_r.at[sender], "head", sender).wait_recv()
        total = self.halves[0]
        for i in range(1, self.count):
            total = total + self.halves[i]
        out_ref[: self.shared, :] = total

        @pl.loop(1, self.n_dp)
        def _(hop):
            self._a(hop).wait_send()

        for hop in range(1, self.count):
            self._b(hop).wait_send()


def greet_all(n_dp, count):
    barrier = pltpu.get_barrier_semaphore()
    dp, head = lax.axis_index("dp"), lax.axis_index("head")

    @pl.loop(1, n_dp)
    def _(hop):
        pl.semaphore_signal(barrier, 1, device_id={"dp": lax.rem(dp + hop, n_dp)}, device_id_type=MESH)

    for hop in range(1, count):
        pl.semaphore_signal(barrier, 1, device_id={"head": lax.rem(head + hop, count)}, device_id_type=MESH)
    pl.semaphore_wait(barrier, n_dp + count - 2)


def end_kernel(n_dp, count, parts, shared,
               dpre_ref, w_ref, normed_ref, hg_ref, mixed_ref, down_ref, tok_ref, gain_ref, grad_ref, small_ref,
               in_ref, mix_ref, sum_ref, down_sum_ref, *scratch):
    scratch = list(scratch)
    take = lambda n: [scratch.pop(0) for _ in range(n)]
    head_refs, dp_refs, down_refs, small_refs = take(9), take(7), take(7), take(8)
    terms, dpre, w, normed, hg, mixed, down_own, loads, down_s = scratch
    rows, width = tok_ref.shape
    block = terms.shape[1]
    hid = mixed.shape[1]
    greet_all(n_dp, count)
    lines = n_dp // 2
    side = lax.axis_index("dp") % 2
    down = ChainScatter(lines, lambda j: down_ref.at[j], lambda place: down_own.at[place], down_refs, True)
    fetch = lambda place: pltpu.make_async_copy(down_ref.at[2 * place + side], down_own.at[place], down_s.at[place])
    moves = [pltpu.make_async_copy(s, d, loads.at[i]) for i, (s, d) in enumerate(
        ((dpre_ref, dpre), (w_ref.at[:, hid:], w), (normed_ref, normed), (mixed_ref, mixed), (hg_ref, hg)))]
    for m in moves:
        m.start()
    down.offer_all()
    for place in range(lines):
        fetch(place).start()
    heads = HeadScatter(count, head_refs)
    line = ChainScatter(lines, lambda j: terms.at[j], lambda place: terms.at[2 * place + side], dp_refs, False)
    small = SmallSum(n_dp, count, shared, small_refs)
    size = rows // parts

    def offer(p):
        part = jnp.concatenate([dpre[o * rows + p * size : o * rows + (p + 1) * size, :] for o in range(count)], axis=0)
        heads.offer(p, dot(part, w[...], ((1,), (1,))))

    tiles = width // 256
    per = 256 // block

    def outer(t):
        cols = slice(t * 256, (t + 1) * 256)
        left = dot(normed[:, cols], dpre[...], ((0,), (0,))).astype(BF16)
        right = dot(hg[:, cols], mixed[...], ((0,), (0,))).astype(BF16)
        for b in range(per):
            terms[t * per + b, :, :hid] = right[b * block : (b + 1) * block]
            terms[t * per + b, :, hid:] = left[b * block : (b + 1) * block]
        for place in range(t * per // 2, (t + 1) * per // 2):
            for k in range(line.pieces):
                line.offer(place, k)

    order = [t // 2 if t % 2 else tiles - 1 - t // 2 for t in range(tiles)]
    moves[0].wait()
    moves[1].wait()
    offer(0)
    for m in moves[2:]:
        m.wait()
    for place in range(lines):
        fetch(place).wait()
    down_done = 0
    for i in range(max(tiles, parts)):
        if i < tiles:
            outer(order[i])
        if i < parts:
            heads.turn(i)
        if i + 1 < parts:
            offer(i + 1)
        for n in range(4):
            if down_done < down.points:
                down.point(down_done)
                down_done += 1
    pl.loop(down_done, down.points)(down.point)
    small.mine[...] = small_ref[...]
    gain_total = jnp.zeros((1, width), F32)
    gain = gain_ref[...]

    def finish(p):
        at = slice(p * size, (p + 1) * size)
        normed_grad = heads.take(p).astype(BF16).astype(F32)
        x = tok_ref[at, :].astype(F32)
        inv = lax.rsqrt(jnp.mean(x * x, axis=-1, keepdims=True) + 1e-6)
        scaled = normed_grad * gain
        mean = jnp.mean(scaled * x, axis=-1, keepdims=True)
        in_ref[at, :] = grad_ref[at, :] + inv * scaled - x * (inv * inv * inv * mean)
        return jnp.sum(normed_grad * x * inv, axis=0, keepdims=True)

    done = 0
    for i in range(parts):
        for n in range(2):
            if done < line.points:
                line.point(done)
                done += 1
        gain_total = gain_total + finish(i)
    for i in range(width // 128):
        small.mine[i : i + 1, :] = gain_total[:, i * 128 : (i + 1) * 128]
    small.start()
    half = (done + line.points) // 2
    pl.loop(done, half)(line.point)
    small.turn(sum_ref)
    pl.loop(half, line.points)(line.point)
    line.finish(mix_ref)
    down.finish(down_sum_ref)
    small.finish(sum_ref)
    down.close()
    heads.close()
    line.close()


def end(dpre, weights, normed_rows, hg_rows, mixed, down_terms, tokens, gain, hidden_grad, small, n_dp, count, shared, parts=4):
    rows, width = tokens.shape
    block = width // n_dp
    wide = weights.shape[1]
    anywhere = pl.BlockSpec(memory_space=pl.ANY)
    vmem = pl.BlockSpec(memory_space=pltpu.VMEM)
    like = lambda a: pltpu.VMEM(a.shape, a.dtype)
    return pl.pallas_call(
        partial(end_kernel, n_dp, count, parts, shared),
        out_shape=[
            jax.ShapeDtypeStruct((rows, width), F32),
            jax.ShapeDtypeStruct((block, wide), F32),
            jax.ShapeDtypeStruct(small.shape, F32),
            jax.ShapeDtypeStruct(down_terms.shape[1:], F32),
        ],
        in_specs=[anywhere] * 6 + [vmem] * 4,
        out_specs=[vmem] * 4,
        scratch_shapes=HeadScatter.scratch(count, parts, rows // parts, width, parts)
        + ChainScatter.scratch(n_dp // 2, block, wide)
        + ChainScatter.scratch(n_dp // 2, block, down_terms.shape[2])
        + SmallSum.scratch(n_dp, count, small.shape[0], shared)
        + [pltpu.VMEM((n_dp, block, wide), BF16), like(dpre), pltpu.VMEM((width, dpre.shape[1]), BF16), like(normed_rows), like(hg_rows), like(mixed),
           pltpu.VMEM((n_dp // 2, *down_terms.shape[1:]), BF16),
           pltpu.SemaphoreType.DMA((5,)), pltpu.SemaphoreType.DMA((n_dp // 2,))],
        compiler_params=pltpu.CompilerParams(vmem_limit_bytes=VMEM_LIMIT, has_side_effects=True, collective_id=1),
        name="end",
    )(dpre, weights, normed_rows, hg_rows, mixed, down_terms, tokens, gain, hidden_grad, small)


def spread_kernel(out_ref, in_ref, mix_ref, ff_ref, down_ref, out_to, in_to, *results):
    to_out, *mixes, beta, ff_gate, ff_up, ff_down = results
    hid, heads, ff = to_out.shape[0], beta.shape[0], ff_gate.shape[0]
    wide = down_ref.shape[1]
    out_to[...] = out_ref[...]
    in_to[...] = in_ref[...]
    to_out[...] = mix_ref[:, :hid].T
    for i, r in enumerate(mixes):
        r[...] = mix_ref[:, (i + 1) * hid : (i + 2) * hid]
    beta[...] = mix_ref[:, 5 * hid :].T[:heads]
    ff_gate[...] = ff_ref[:, :wide].T[:ff]
    ff_up[...] = ff_ref[:, wide:].T[:ff]
    ff_down[...] = down_ref[...].T[:ff]


def spread(output, input_grad, mix, ff_sum, down_sum, hid, heads, ff):
    block = mix.shape[0]
    vmem = pl.BlockSpec(memory_space=pltpu.VMEM)
    shapes = [(hid, block)] + [(block, hid)] * 4 + [(heads, block)] + [(ff, block)] * 3
    return pl.pallas_call(
        spread_kernel,
        out_shape=[jax.ShapeDtypeStruct(a.shape, a.dtype) for a in (output, input_grad)]
        + [jax.ShapeDtypeStruct(s, F32) for s in shapes],
        in_specs=[vmem] * 5,
        out_specs=[vmem] * (2 + len(shapes)),
        compiler_params=pltpu.CompilerParams(vmem_limit_bytes=VMEM_LIMIT),
        name="spread",
    )(output, input_grad, mix, ff_sum, down_sum)


def doc_tables(lengths, length):
    count = lengths.shape[0]
    index = jnp.arange(count)
    ends = jnp.sum(jnp.where(index[None, :] <= index[:, None], lengths[None, :], 0), axis=1)
    position = jnp.arange(length, dtype=jnp.int32)
    doc = jnp.sum((position[:, None] >= ends[None, :]).astype(jnp.int32), axis=1)
    no_doc = lambda n: jnp.full((n,), -1, jnp.int32)
    before = [jnp.concatenate([no_doc(o), doc[:-o]]) == doc for o in (1, 2, 3)]
    after = [jnp.concatenate([doc[o:], no_doc(o)]) == doc for o in (1, 2, 3)]
    blocks = doc.reshape(-1, CHUNK)
    ending = blocks[:, -1:]
    prior = jnp.concatenate([no_doc(1)[:, None], ending[:-1]], axis=0)
    enter = (blocks == prior).reshape(-1)
    leave = (blocks == ending).reshape(-1)
    columns = before + [enter, leave] + after + [doc]
    aux = jnp.stack([c.astype(F32) for c in columns], axis=1)
    return aux, doc.astype(F32).reshape(-1, GROUP, CHUNK)


def on_device(
    tokens,
    lengths,
    attn_gain,
    w_query,
    w_key,
    w_value,
    w_beta,
    w_gate_out,
    conv_weight,
    head_gain,
    w_out,
    mlp_gain,
    w_mlp_gate,
    w_mlp_up,
    w_down,
    cotangent,
):
    hid, heads, ff = w_query.shape[1], w_beta.shape[1], w_mlp_gate.shape[1]
    n_dp, n_head = lax.axis_size("dp"), lax.axis_size("head")
    beta_wide = jnp.pad(w_beta, ((0, 0), (0, HEAD_DIM - heads)))
    in_ws = [w_query, w_key, w_value, w_gate_out, beta_wide]
    half = cotangent.shape[0] // 2
    normed_rows, first_set, cot_early = start(
        tokens, attn_gain[None, :], w_out, in_ws, cotangent[:half], n_dp, n_head
    )
    normed_rows = normed_rows.reshape(-1, normed_rows.shape[2])
    first_set = first_set.reshape(-1, first_set.shape[2])
    wide = -(-ff // 256) * 256
    padded = lambda w: jnp.pad(w, ((0, 0), (0, wide - ff)))
    mine = jnp.concatenate([padded(w_mlp_gate), padded(w_mlp_up)], axis=1)

    length = normed_rows.shape[0]
    aux, docrow = doc_tables(lengths[0], length)
    conv = jnp.swapaxes(conv_weight.astype(F32), 0, 1).reshape(conv_weight.shape[1], 3 * hid)
    gain = head_gain[None, :]
    pre, mixed, *saved, attention, cot_late, ff_set = mixer_fwd(
        normed_rows, first_set, aux, docrow, conv, gain, cotangent[half:], mine, n_dp, n_head
    )
    ff_set = ff_set.reshape(-1, ff_set.shape[2])
    output, hidden_grad, hg_rows, mlp_gain_grad, mlp_terms, down_terms = mid(
        attention, tokens, mlp_gain[None, :], cot_early, cot_late, ff_set, padded(w_down.T), n_dp, n_head
    )
    dpre, conv_part, head_gain_grad, mlp_reduced = mixer_bwd(
        hg_rows, first_set, aux, docrow, conv, gain, (pre, *saved),
        mlp_terms.reshape(n_dp, -1, mlp_terms.shape[1]),
    )
    taps = conv_part.shape[0]
    shared = 2 * (tokens.shape[1] // 128) + 8
    small = jnp.concatenate(
        [
            jnp.zeros((tokens.shape[1] // 128, 128), F32),
            mlp_gain_grad.reshape(-1, 128),
            jnp.pad(head_gain_grad, ((0, 7), (0, 0))),
            conv_part.reshape(-1, 128),
        ]
    )
    input_grad, mix_reduced, summed, down_reduced = end(
        dpre, first_set, normed_rows, hg_rows, mixed, down_terms.reshape(n_dp, -1, wide), tokens, attn_gain[None, :], hidden_grad, small,
        n_dp, n_head, shared,
    )
    gains = summed[: shared - 8].reshape(2, -1)
    conv_grad = jnp.swapaxes(summed[shared:].reshape(taps, 3, hid), 0, 1)
    spread_out = spread(output, input_grad, mix_reduced, mlp_reduced, down_reduced, hid, heads, ff)
    output, input_grad, to_out, query, key, value, gate, beta, ff_gate, ff_up, ff_down = spread_out
    return (
        output,
        input_grad,
        gains[0],
        query,
        key,
        value,
        beta.T,
        gate,
        conv_grad,
        summed[shared - 8],
        to_out,
        gains[1],
        ff_gate.T,
        ff_up.T,
        ff_down,
    )


def solution(mesh):
    rows = P(("dp", "head"), None)
    in_specs = (
        rows,
        P("dp", None),
        P(),
        P("dp", "head"),
        P("dp", "head"),
        P("dp", "head"),
        P("dp", "head"),
        P("dp", "head"),
        P(None, None, "head"),
        P(),
        P("head", "dp"),
        P(),
        P("dp", "head"),
        P("dp", "head"),
        P("head", "dp"),
        rows,
    )
    out_specs = (
        rows,
        rows,
        P(),
        P("dp", "head"),
        P("dp", "head"),
        P("dp", "head"),
        P("dp", "head"),
        P("dp", "head"),
        P(None, None, "head"),
        P(),
        P("head", "dp"),
        P(),
        P("dp", "head"),
        P("dp", "head"),
        P("head", "dp"),
    )
    return jax.shard_map(
        on_device, mesh=mesh, in_specs=in_specs, out_specs=out_specs, check_vma=False
    )
```

```python
from functools import partial

import jax
import jax.numpy as jnp
from jax import lax
from jax.experimental import pallas as pl
from jax.experimental.pallas import tpu as pltpu
from jax.sharding import PartitionSpec as P

HEAD_DIM = 128
CHUNK = 128
GROUP = 4
STEP = CHUNK * GROUP
PAD = 8
F32 = jnp.float32
BF16 = jnp.bfloat16
COT_PARTS = 2
HG_PARTS = 2
VMEM_LIMIT = 56 * 1024 * 1024


def dot(left, right, dims):
    return lax.dot_general(left, right, (dims, ((), ())), preferred_element_type=F32)


def mul(left, right):
    return dot(left.astype(BF16), right.astype(BF16), ((1,), (0,)))


def mul_t(left, right):
    return dot(left.astype(BF16), right.astype(BF16), ((1,), (1,)))


def t_mul(left, right):
    return dot(left.astype(BF16), right.astype(BF16), ((0,), (0,)))


def unit_inverses(lowers):
    row = lax.broadcasted_iota(jnp.int32, (CHUNK, CHUNK), 0)
    col = lax.broadcasted_iota(jnp.int32, (CHUNK, CHUNK), 1)
    eye = (row == col).astype(F32)
    level = lambda bit: jnp.logical_and(
        (row >> (bit + 1)) == (col >> (bit + 1)), (row >> bit) > (col >> bit)
    )
    first = level(0)
    solved = [eye - jnp.where(first, a, 0.0) for a in lowers]
    for bit in range(1, CHUNK.bit_length() - 1):
        mask = level(bit)
        right = [mul(jnp.where(mask, a, 0.0), t) for a, t in zip(lowers, solved)]
        solved = [t - mul(t, r) for t, r in zip(solved, right)]
    return solved


def conv_parts(pre, ext, conv, aux):
    summed = pre * conv[3:4, :]
    for offset in range(1, 4):
        shifted = ext[PAD - offset : PAD - offset + STEP, :]
        summed = summed + shifted * aux[:, offset - 1 : offset] * conv[3 - offset : 4 - offset, :]
    return summed


def unit_rows(act, scale):
    out = []
    for h in range(act.shape[1] // HEAD_DIM):
        part = act[:, h * HEAD_DIM : (h + 1) * HEAD_DIM]
        inv = lax.rsqrt(jnp.sum(part * part, axis=-1, keepdims=True) + 1e-6)
        out.append((part * inv * scale, inv))
    return out


def chunk_masks(aux, docrow):
    row = lax.broadcasted_iota(jnp.int32, (CHUNK, CHUNK), 0)
    col = lax.broadcasted_iota(jnp.int32, (CHUNK, CHUNK), 1)
    made = []
    for c in range(GROUP):
        same = aux[c * CHUNK : (c + 1) * CHUNK, 8:9] == docrow[c : c + 1, :]
        made.append((jnp.logical_and(same, row > col), jnp.logical_and(same, row >= col)))
    return made


def mixer_fwd_kernel(
    lines, count,
    x_ref, w_ref, aux_ref, docrow_ref, conv_ref, gain_ref, cot_ref, ff_ref,
    pre_ref, mixed_ref, o_ref, t_ref, phi_ref, s_ref, p_ref, d_ref, ew_ref, att_ref, cot_rows, ff_rows,
    ext, state, terms, near, far_terms, near_s, near_r, far_s, far_r, right_s, left_s, over_s, landed, local, *cot_sems,
):
    heads = mixed_ref.shape[1] // HEAD_DIM
    hid = heads * HEAD_DIM
    grid_step, last_step = pl.program_id(0), pl.num_programs(0) - 1
    first, hop_step, arrived, last = shard_line(lines, ff_ref, ff_rows, (right_s, left_s, over_s, landed, local.at[0]))
    cots, held = cot_gather(count, cot_ref, cot_rows, cot_sems, local.at[1])
    cot_parts = cots.parts

    attend = OwnerScatter(count, att_ref, (terms, near, far_terms, near_s, near_r, far_s, far_r))

    @pl.when(grid_step == 0)
    def _():
        greet(lines, count)
        first()
        held.start()
        for p in range(cot_parts):
            cots.send(p)

    @pl.when(grid_step == 2)
    def _():
        hop_step(0)
        cots.pass_on(0)

    @pl.when(pl.program_id(0) == 0)
    def _():
        ext[0:PAD, :] = jnp.zeros((PAD, 3 * hid), F32)
        state[...] = jnp.zeros_like(state)

    pre_ref[...] = dot(x_ref[...], w_ref[:, hid:], ((1,), (0,)))
    pl.when(grid_step >= 1)(lambda: attend.settle(grid_step - 1))
    aux = aux_ref[...]
    conv = conv_ref[...]
    pre = pre_ref[:, : 3 * hid]
    ext[PAD:, :] = pre
    act = conv_parts(pre, ext, conv, aux)
    act = act * jax.nn.sigmoid(act)
    ext[0:PAD, :] = ext[STEP:, :]
    q = unit_rows(act[:, :hid], HEAD_DIM**-0.5)
    k = unit_rows(act[:, hid : 2 * hid], 1.0)
    beta = jax.nn.sigmoid(pre_ref[:, 4 * hid : 4 * hid + 8])
    masks = chunk_masks(aux, docrow_ref[0])

    items = [(c, h) for c in range(GROUP) for h in range(heads)]
    rows = [slice(c * CHUNK, (c + 1) * CHUNK) for c in range(GROUP)]
    lowers, scores = [], []
    for c, h in items:
        key, query = k[h][0][rows[c]], q[h][0][rows[c]]
        both = mul_t(jnp.concatenate([key, query], axis=0), key)
        lowers.append(jnp.where(masks[c][0], both[:CHUNK] * beta[rows[c], h : h + 1], 0.0))
        scores.append(jnp.where(masks[c][1], both[CHUNK:], 0.0).astype(BF16))
    solved = unit_inverses(lowers)
    parts = []
    for (c, h), inverse, score in zip(items, solved, scores):
        key = k[h][0][rows[c]]
        value = act[rows[c], 2 * hid + h * HEAD_DIM : 2 * hid + (h + 1) * HEAD_DIM]
        b = beta[rows[c], h : h + 1]
        enter, leave = aux[rows[c], 3:4], aux[rows[c], 4:5]
        inverse = inverse.astype(BF16)
        wu = mul(inverse, jnp.concatenate([key * b, value * b], axis=1))
        ew, u = wu[:, :HEAD_DIM] * enter, wu[:, HEAD_DIM:]
        phi_b = t_mul(key * leave, jnp.concatenate([ew, u], axis=1))
        parts.append((ew, u, phi_b[:, :HEAD_DIM].astype(BF16), phi_b[:, HEAD_DIM:]))
        t_ref[c, h] = inverse
        p_ref[c, h] = score
        ew_ref[c, h] = ew.astype(BF16)
        phi_ref[c, h] = parts[-1][2]
    for h in range(heads):
        s = state[h]
        for c in range(GROUP):
            low = s.astype(BF16)
            s_ref[c, h] = low
            _, _, phi, b_term = parts[c * heads + h]
            keep = aux[(c + 1) * CHUNK - 1 : (c + 1) * CHUNK, 3:4]
            s = s * keep - mul(phi, low) + b_term
        state[h] = s
    gain = gain_ref[...]
    for (c, h), (ew, u, _, _), score in zip(items, parts, scores):
        enter = aux[rows[c], 3:4]
        from_state = mul(jnp.concatenate([ew, q[h][0][rows[c]] * enter], axis=0), s_ref[c, h])
        d = (u - from_state[:CHUNK]).astype(BF16)
        d_ref[c, h] = d
        o = from_state[CHUNK:] + mul(score, d)
        cols = slice(h * HEAD_DIM, (h + 1) * HEAD_DIM)
        o_ref[rows[c], cols] = o
        normed = o * lax.rsqrt(jnp.mean(o * o, axis=-1, keepdims=True) + 1e-5) * gain
        gate = pre_ref[rows[c], 3 * hid + h * HEAD_DIM : 3 * hid + (h + 1) * HEAD_DIM]
        mixed_ref[rows[c], cols] = (normed * (gate * jax.nn.sigmoid(gate))).astype(BF16)

    attend.offer(grid_step, dot(mixed_ref[...], w_ref[:, :hid], ((1,), (1,))))

    @pl.when(grid_step == last_step)
    def _():
        attend.settle(grid_step)
        for p in range(1, cot_parts):
            cots.pass_on(p)
        pl.loop(1, lines - 1)(hop_step)
        held.wait()
        for p in range(cot_parts):
            cots.arrive(p)
            cots.sent(p)
        arrived()
        attend.finish()
        last()


def mixer_bwd_kernel(
    lines, steps,
    hg_in, wout_ref, pre_ref, halo_ref, aux_ref, docrow_ref, conv_ref, gain_ref,
    o_ref, t_ref, phi_ref, s_ref, p_ref, d_ref, ew_ref, terms_ref,
    dpre_ref, dconv_ref, dgain_ref, sum_ref, hg_out,
    ext, later, dstate, own, own_s, hg_all, hg_s, *refs,
):
    heads = o_ref.shape[1] // HEAD_DIM
    hid = heads * HEAD_DIM
    grid_step = pl.program_id(0)
    side = lax.axis_index("dp") % 2
    dp_refs, hg_sems = refs[:7], refs[7:]
    me, final = lax.axis_index("head"), hg_all.shape[0] - 1
    hg_parts = hg_sems[1].shape[0]
    hg_size = hg_all.shape[1] // hg_parts
    hg_block = lambda owner, p: hg_all.at[owner, pl.ds(p * hg_size, hg_size)]
    hgs = HeadGather(
        final + 1, hg_parts, lambda p: hg_block(me, p), hg_block, hg_sems, lambda owner: owner != final
    )
    load = lambda owner, i: pltpu.make_async_copy(hg_in.at[owner], hg_all.at[owner], hg_s.at[i])
    order = lambda n: (n // lines, outside_in(lines, n % lines))
    line = LineScatter(lines, lambda j: terms_ref.at[j], lambda place: own.at[place], dp_refs, order)
    fetch = lambda place: pltpu.make_async_copy(terms_ref.at[2 * place + side], own.at[place], own_s.at[place])

    @pl.when(grid_step == 0)
    def _():
        load(final, 0).start()
        pl.when(me != final)(lambda: load(me, 1).start())
        greet_line(lines, final + 1)
        line.offer_all()
        pl.when(me != final)(lambda: load(me, 1).wait())
        for p in range(hg_parts):
            hgs.send(p)
        for place in range(lines):
            fetch(place).start()
        load(final, 0).wait()
        for place in range(lines):
            fetch(place).wait()

    per_step = 5
    base = 3

    def point(i):
        n = grid_step * per_step + i - base
        line.point(n)

    point(0)

    @pl.when(pl.program_id(0) == 0)
    def _():
        later[STEP:, :] = jnp.zeros((PAD, 3 * hid), F32)
        dstate[...] = jnp.zeros_like(dstate)
        dconv_ref[...] = jnp.zeros_like(dconv_ref)
        dgain_ref[...] = jnp.zeros_like(dgain_ref)

    @pl.when(grid_step >= 1)
    def _():
        for p in range(hg_parts):
            hgs.arrive(p, final - grid_step)

    hg_out[...] = hg_all[final - grid_step]
    mixed_grad = dot(hg_out[...], wout_ref[...], ((1,), (0,))).astype(BF16).astype(F32)
    aux = aux_ref[...]
    conv = conv_ref[...]
    pre = pre_ref[:, : 3 * hid]
    ext[0:PAD, :] = halo_ref[:, : 3 * hid]
    ext[PAD:, :] = pre
    lin = conv_parts(pre, ext, conv, aux)
    sig = jax.nn.sigmoid(lin)
    act = lin * sig
    dsilu = sig * (1.0 + lin * (1.0 - sig))
    scale = HEAD_DIM**-0.5
    q = unit_rows(act[:, :hid], 1.0)
    k = unit_rows(act[:, hid : 2 * hid], 1.0)
    beta = jax.nn.sigmoid(pre_ref[:, 4 * hid : 4 * hid + 8])
    masks = chunk_masks(aux, docrow_ref[0])
    gain = gain_ref[...]

    items = [(c, h) for c in range(GROUP) for h in range(heads)]
    rows = [slice(c * CHUNK, (c + 1) * CHUNK) for c in range(GROUP)]
    cols = [slice(h * HEAD_DIM, (h + 1) * HEAD_DIM) for h in range(heads)]

    d_out, d_gain = [], jnp.zeros((1, HEAD_DIM), F32)
    for h in range(heads):
        o = o_ref[:, cols[h]]
        inv = lax.rsqrt(jnp.mean(o * o, axis=-1, keepdims=True) + 1e-5)
        unit = o * inv
        gate = pre_ref[:, 3 * hid + h * HEAD_DIM : 3 * hid + (h + 1) * HEAD_DIM]
        s = jax.nn.sigmoid(gate)
        dm = mixed_grad[:, cols[h]]
        dpre_ref[:, 3 * hid + h * HEAD_DIM : 3 * hid + (h + 1) * HEAD_DIM] = (
            dm * unit * gain * (s * (1.0 + gate * (1.0 - s)))
        ).astype(BF16)
        dn = dm * (gate * s)
        d_gain = d_gain + jnp.sum(dn * unit, axis=0, keepdims=True)
        du = dn * gain
        d_out.append(inv * (du - unit * jnp.mean(du * unit, axis=-1, keepdims=True)))
    dgain_ref[...] += d_gain
    point(1)

    first = []
    for c, h in items:
        enter = aux[rows[c], 3:4]
        do = d_out[h][rows[c]].astype(BF16)
        eq = (q[h][0][rows[c]] * (enter * scale)).astype(BF16)
        x = t_mul(p_ref[c, h], do)
        c_term = t_mul(
            jnp.concatenate([eq, -ew_ref[c, h]], axis=0),
            jnp.concatenate([do, x.astype(BF16)], axis=0),
        )
        first.append((do, x, c_term))
    point(2)
    after = {}
    for h in range(heads):
        ds = dstate[h]
        for c in reversed(range(GROUP)):
            low = ds.astype(BF16)
            after[c, h] = low
            keep = aux[(c + 1) * CHUNK - 1 : (c + 1) * CHUNK, 3:4]
            ds = ds * keep - t_mul(phi_ref[c, h], low) + first[c * heads + h][2]
        dstate[h] = ds
    db_cols = []
    grads = {}
    point(3)
    for (c, h), (do, x, _) in zip(items, first):
        enter, leave = aux[rows[c], 3:4], aux[rows[c], 4:5]
        b = beta[rows[c], h : h + 1]
        key, query = k[h][0][rows[c]], q[h][0][rows[c]] * scale
        value = act[rows[c], 2 * hid + h * HEAD_DIM : 2 * hid + (h + 1) * HEAD_DIM]
        ds = after[c, h]
        d, s = d_ref[c, h], s_ref[c, h]
        dr = t_mul(t_ref[c, h], x + mul(key * leave, ds))
        stacked = jnp.concatenate([do, dr.astype(BF16)], axis=0)
        with_d = mul_t(stacked, d)
        with_s = mul_t(stacked, s) * jnp.concatenate([enter, enter], axis=0)
        dp = jnp.where(masks[c][1], with_d[:CHUNK], 0.0)
        da = jnp.where(masks[c][0], -with_d[CHUNK:], 0.0)
        pair = jnp.concatenate([dp, da], axis=0).astype(BF16)
        with_k = mul(pair, key)
        dq = with_s[:CHUNK] + with_k[:CHUNK]
        row_k = with_k[CHUNK:] - with_s[CHUNK:]
        dk = b * row_k + t_mul(pair, jnp.concatenate([query, key * b], axis=0))
        dk = dk + mul_t(d, ds) * leave
        db = jnp.sum(dr * value + key * row_k, axis=-1, keepdims=True)
        grads[c, h] = (dq * scale, dk, dr * b, db * b * (1.0 - b))
    point(4)
    for h in range(heads):
        whole = [jnp.concatenate([grads[c, h][i] for c in range(GROUP)], axis=0) for i in range(4)]
        for i, unit in ((0, q[h]), (1, k[h])):
            y, inv = unit
            grad = inv * (whole[i] - y * jnp.sum(y * whole[i], axis=-1, keepdims=True))
            at = slice(i * hid + h * HEAD_DIM, i * hid + (h + 1) * HEAD_DIM)
            later[0:STEP, at] = grad * dsilu[:, at]
        at = slice(2 * hid + h * HEAD_DIM, 2 * hid + (h + 1) * HEAD_DIM)
        later[0:STEP, at] = whole[2] * dsilu[:, at]
        db_cols.append(whole[3])
    lane = lax.broadcasted_iota(jnp.int32, (STEP, HEAD_DIM), 1)
    tail = jnp.zeros((STEP, HEAD_DIM), F32)
    for h in range(heads):
        tail = jnp.where(lane == h, db_cols[h], tail)
    dpre_ref[:, 4 * hid :] = tail.astype(BF16)
    dlin = later[0:STEP, :]
    dpre = dlin * conv[3:4, :]
    taps = [jnp.sum(dlin * pre, axis=0, keepdims=True)]
    for offset in range(1, 4):
        ahead = later[offset : offset + STEP, :]
        dpre = dpre + ahead * aux[:, 4 + offset : 5 + offset] * conv[3 - offset : 4 - offset, :]
        behind = ext[PAD - offset : PAD - offset + STEP, :] * aux[:, offset - 1 : offset]
        taps.append(jnp.sum(dlin * behind, axis=0, keepdims=True))
    dpre_ref[:, : 3 * hid] = dpre.astype(BF16)
    for offset in range(4):
        dconv_ref[3 - offset : 4 - offset, :] += taps[offset]
    later[STEP:, :] = later[0:PAD, :]

    @pl.when(grid_step < steps - 1)
    def _():
        for p in range(hg_parts):
            hgs.pass_on(p, final - 1 - grid_step)

    @pl.when(grid_step == steps - 1)
    def _():
        for p in range(hg_parts):
            hgs.sent(p)
        pl.loop(max(steps * per_step - base, 0), line.points)(line.point)
        line.finish(sum_ref)
        line.close()


def mixer_fwd(x_rows, weights, aux, docrow, conv, gain, cotangent, ff_mine, n_dp, count):
    hid = conv.shape[1] // 3
    length, width = x_rows.shape[0], weights.shape[1] - hid
    heads, chunks = hid // HEAD_DIM, length // CHUNK
    lines, dma = n_dp // 2, lambda *shape: pltpu.SemaphoreType.DMA(shape)
    anywhere = pl.BlockSpec(memory_space=pl.ANY)
    rows = lambda n: pl.BlockSpec((STEP, n), lambda i: (i, 0))
    whole = lambda a: pl.BlockSpec(a.shape, lambda i: (0,) * a.ndim)
    square = pl.BlockSpec((GROUP, heads, CHUNK, HEAD_DIM), lambda i: (i, 0, 0, 0))
    squares = jax.ShapeDtypeStruct((chunks, heads, CHUNK, HEAD_DIM), BF16)
    return pl.pallas_call(
        partial(mixer_fwd_kernel, lines, count),
        grid=(length // STEP,),
        in_specs=[
            rows(x_rows.shape[1]), whole(weights), rows(aux.shape[1]),
            pl.BlockSpec((1, GROUP, CHUNK), lambda i: (i, 0, 0)), whole(conv), whole(gain),
            whole(cotangent), whole(ff_mine),
        ],
        out_specs=[rows(width), rows(hid), rows(hid)]
        + [square] * 6
        + [pl.BlockSpec((STEP, x_rows.shape[1]), lambda i: (0, 0))]
        + [anywhere] * 2,
        out_shape=[
            jax.ShapeDtypeStruct((length, width), F32),
            jax.ShapeDtypeStruct((length, hid), BF16),
            jax.ShapeDtypeStruct((length, hid), F32),
        ]
        + [squares] * 6
        + [
            jax.ShapeDtypeStruct((STEP, x_rows.shape[1]), F32),
            jax.ShapeDtypeStruct((count, *cotangent.shape), BF16),
            jax.ShapeDtypeStruct((n_dp, *ff_mine.shape), BF16),
        ],
        scratch_shapes=[
            pltpu.VMEM((PAD + STEP, 3 * hid), F32),
            pltpu.VMEM((heads, HEAD_DIM, HEAD_DIM), F32),
        ]
        + OwnerScatter.scratch(count, STEP, x_rows.shape[1])
        + [
            dma(lines), dma(lines), dma(lines), dma(n_dp), dma(2),
        ]
        + HeadGather.scratch(count, COT_PARTS),
        compiler_params=pltpu.CompilerParams(vmem_limit_bytes=VMEM_LIMIT, has_side_effects=True, collective_id=3),
        name="mixer_fwd",
    )(x_rows, weights, aux, docrow, conv, gain, cotangent, ff_mine)


def mixer_bwd(hg_rows, weights, aux, docrow, conv, gain, saved, terms):
    pre, o, t, phi, s, p, d, ew = saved
    length, width = pre.shape
    hid = conv.shape[1] // 3
    heads, steps = hid // HEAD_DIM, length // STEP
    last = steps - 1
    n_dp, block, wide = terms.shape
    lines = n_dp // 2
    rows = lambda n: pl.BlockSpec((STEP, n), lambda i: (last - i, 0))
    whole = lambda a: pl.BlockSpec(a.shape, lambda i: (0,) * a.ndim)
    square = pl.BlockSpec((GROUP, heads, CHUNK, HEAD_DIM), lambda i: (last - i, 0, 0, 0))
    halo = pl.BlockSpec(
        (PAD, width), lambda i: (jnp.maximum((last - i) * (STEP // PAD) - 1, 0), 0)
    )
    return pl.pallas_call(
        partial(mixer_bwd_kernel, lines, steps),
        grid=(steps,),
        in_specs=[
            pl.BlockSpec(memory_space=pl.ANY), pl.BlockSpec((weights.shape[0], hid), lambda i: (0, 0)), rows(width), halo, rows(aux.shape[1]),
            pl.BlockSpec((1, GROUP, CHUNK), lambda i: (last - i, 0, 0)), whole(conv), whole(gain),
            rows(hid),
        ]
        + [square] * 6
        + [pl.BlockSpec(memory_space=pl.ANY)],
        out_specs=[
            rows(width),
            pl.BlockSpec((4, 3 * hid), lambda i: (0, 0)),
            pl.BlockSpec((1, HEAD_DIM), lambda i: (0, 0)),
            pl.BlockSpec((block, wide), lambda i: (0, 0)),
            rows(weights.shape[0]),
        ],
        out_shape=[
            jax.ShapeDtypeStruct((length, width), BF16),
            jax.ShapeDtypeStruct((4, 3 * hid), F32),
            jax.ShapeDtypeStruct((1, HEAD_DIM), F32),
            jax.ShapeDtypeStruct((block, wide), F32),
            jax.ShapeDtypeStruct((length, weights.shape[0]), BF16),
        ],
        scratch_shapes=[
            pltpu.VMEM((PAD + STEP, 3 * hid), F32),
            pltpu.VMEM((STEP + PAD, 3 * hid), F32),
            pltpu.VMEM((heads, HEAD_DIM, HEAD_DIM), F32),
            pltpu.VMEM((lines, block, wide), BF16),
            pltpu.SemaphoreType.DMA((lines,)),
            pltpu.VMEM(hg_rows.shape, BF16),
            pltpu.SemaphoreType.DMA((2,)),
        ]
        + LineScatter.scratch(lines, block, wide)
        + HeadGather.scratch(hg_rows.shape[0], HG_PARTS),
        compiler_params=pltpu.CompilerParams(vmem_limit_bytes=VMEM_LIMIT, has_side_effects=True, collective_id=4),
        name="mixer_bwd",
    )(hg_rows, weights, pre, pre, aux, docrow, conv, gain, o, t, phi, s, p, d, ew, terms)


MESH = pl.DeviceIdType.MESH


def remote(src, dst, sent, landed, axis, to):
    return pltpu.make_async_remote_copy(
        src_ref=src, dst_ref=dst, send_sem=sent, recv_sem=landed,
        device_id={axis: to}, device_id_type=MESH,
    )


def shard_line(lines, own, out, sems):
    right_s, left_s, over_s, landed, local = sems
    me = lax.axis_index("dp")
    spot, side = me // 2, me % 2
    slot = lambda place: 2 * place + side
    across = me + 1 - 2 * side

    def hop(step, where):
        return (spot - step, me + 2, right_s) if where == 0 else (spot + step, me - 2, left_s)

    def going(step, where):
        place, to, sent = hop(step, where)
        src = out.at[slot(place)] if not isinstance(step, int) or step else own
        return remote(src, out.at[slot(place)], sent.at[step], landed.at[slot(place)], "dp", to)

    def goes(step, where):
        if where == 0:
            return jnp.logical_and(spot - step >= 0, spot + 1 < lines)
        return jnp.logical_and(spot + step < lines, spot >= 1)

    def over(place):
        return remote(out.at[slot(place)], out.at[slot(place)], over_s.at[place], landed.at[slot(place)], "dp", across)

    def first():
        pltpu.make_async_copy(own, out.at[me], local).start()
        remote(own, out.at[me], over_s.at[spot], landed.at[me], "dp", across).start()
        for where in (0, 1):
            pl.when(goes(0, where))(lambda where=where: going(0, where).start())

    def arrive(step, place):
        @pl.when(jnp.logical_and(place >= 0, place < lines))
        def _():
            over(place).wait_recv()
            over(place).start()

    def hop_step(step):
        for where in (0, 1):
            place = spot - step - 1 if where == 0 else spot + step + 1
            arrive(step, place)
            if isinstance(step, int) and step + 1 >= lines - 1:
                continue
            pl.when(jnp.logical_and(goes(step + 1, where), step + 1 < lines - 1))(
                lambda where=where: going(step + 1, where).start()
            )

    def arrived():
        pltpu.make_async_copy(own, out.at[me], local).wait()

        @pl.loop(0, lines)
        def _(place):
            there = 2 * place + 1 - side
            remote(out.at[there], out.at[there], over_s.at[place], landed.at[there], "dp", across).wait_recv()

    def last():
        pl.loop(0, lines)(lambda place: over(place).wait_send())

        @pl.loop(0, lines - 1)
        def _(step):
            for where in (0, 1):
                pl.when(goes(step, where))(lambda where=where: going(step, where).wait_send())

    return first, hop_step, arrived, last


def greet(lines, count):
    barrier = pltpu.get_barrier_semaphore()
    me = lax.axis_index("dp")
    spot, across = me // 2, me + 1 - 2 * (me % 2)

    def tell(axis, to):
        pl.semaphore_signal(barrier, 1, device_id={axis: to}, device_id_type=MESH)

    tell("dp", across)
    pl.when(spot >= 1)(lambda: tell("dp", me - 2))
    pl.when(spot + 1 < lines)(lambda: tell("dp", me + 2))
    head = lax.axis_index("head")
    tell("head", head + 1 - 2 * (head % 2))
    for f in range(1, count // 2):
        tell("head", lax.rem(head + 2 * f, count))
    beside = jnp.minimum(spot, 1) + jnp.minimum(lines - 1 - spot, 1)
    pl.semaphore_wait(barrier, 1 + count // 2 + beside)


def greet_line(lines, count):
    barrier = pltpu.get_barrier_semaphore()
    head = lax.axis_index("head")
    for to in [head + 1 - 2 * (head % 2)] + [lax.rem(head + hop, count) for hop in range(2, count, 2)]:
        pl.semaphore_signal(barrier, 1, device_id={"head": to}, device_id_type=MESH)
    me = lax.axis_index("dp")

    def tell(to):
        pl.semaphore_signal(barrier, 1, device_id={"dp": to}, device_id_type=MESH)

    tell(me + 1 - 2 * (me % 2))
    pl.loop(1, lines)(lambda hop: tell(lax.rem(me + 2 * hop, 2 * lines)))
    pl.semaphore_wait(barrier, lines + count // 2)


def cot_gather(count, cot_ref, cot_rows, sems, held_s):
    parts = sems[1].shape[0]
    size = cot_ref.shape[0] // parts
    at = lambda p: pl.ds(p * size, size)
    me = lax.axis_index("head")
    cots = HeadGather(count, parts, lambda p: cot_ref.at[at(p)], lambda owner, p: cot_rows.at[owner, at(p)], sems)
    return cots, pltpu.make_async_copy(cot_ref, cot_rows.at[me], held_s)


def start_kernel(lines, count, parts, tok_ref, gain_ref, out_w, *refs):
    *in_ws, cot_ref, rows_ref, wall_ref, cot_rows, mine, w_ref = refs[:11]
    start_body(
        lines, count, parts, tok_ref, gain_ref, out_w, in_ws, cot_ref, rows_ref, wall_ref, cot_rows, mine, w_ref, *refs[11:]
    )


def start_body(lines, count, parts, tok_ref, gain_ref, out_w, in_ws, cot_ref, rows_ref, wall_ref, cot_rows, mine, w_ref,
               right_s, left_s, over_s, landed, local, far_s, pair_s, fwd_s, got, keep_s, *cot_sems):
    first, hop_step, arrived, last = shard_line(lines, w_ref, wall_ref, (right_s, left_s, over_s, landed, local.at[0]))
    at = out_w.shape[0]
    w_ref[:, :at] = out_w[...].T
    for w in in_ws:
        w_ref[:, at : at + w.shape[1]] = w[...]
        at += w.shape[1]
    greet(lines, count)
    first()
    me = lax.axis_index("head")
    pair = me + 1 - 2 * (me % 2)
    fars = [lax.rem(me + 2 * f, count) for f in range(1, count // 2)]
    size = tok_ref.shape[0] // parts
    span = lambda p: pl.ds(p * size, size)

    def block(owner, p):
        return rows_ref.at[owner, span(p)]

    for p in range(parts):
        x = tok_ref[p * size : (p + 1) * size, :].astype(F32)
        inv = lax.rsqrt(jnp.mean(x * x, axis=-1, keepdims=True) + 1e-6)
        mine[p * size : (p + 1) * size, :] = (x * inv * gain_ref[...]).astype(BF16)
        for f, far in enumerate(fars):
            remote(mine.at[span(p)], block(me, p), far_s.at[f, p], got.at[me, p], "head", far).start()
        remote(mine.at[span(p)], block(me, p), pair_s.at[p], got.at[me, p], "head", pair).start()
        pltpu.make_async_copy(mine.at[span(p)], block(me, p), keep_s.at[p]).start()

    cots, held = cot_gather(count, cot_ref, cot_rows, cot_sems, local.at[1])
    held.start()
    for p in range(cots.parts):
        cots.send(p)

    def pass_on(p):
        for f, far in enumerate(fars):
            moved = remote(block(far, p), block(far, p), fwd_s.at[f, p], got.at[far, p], "head", pair)
            moved.wait_recv()
            moved.start()

    for i in range(parts):
        pass_on(i)
        if i < lines - 1:
            hop_step(i)
    if lines - 1 > parts:
        pl.loop(parts, lines - 1)(hop_step)
    for p in range(cots.parts):
        cots.pass_on(p)
    arrived()
    last()
    held.wait()
    for p in range(cots.parts):
        cots.arrive(p)
        cots.sent(p)
    for p in range(parts):
        remote(mine.at[span(p)], block(pair, p), pair_s.at[p], got.at[pair, p], "head", pair).wait()
        pltpu.make_async_copy(mine.at[span(p)], block(me, p), keep_s.at[p]).wait()
        for f, far in enumerate(fars):
            remote(mine.at[span(p)], block(me, p), far_s.at[f, p], got.at[me, p], "head", far).wait_send()
            there = lax.rem(pair + 2 * (f + 1), count)
            remote(block(far, p), block(there, p), fwd_s.at[f, p], got.at[there, p], "head", pair).wait()


def start(tokens, gain, w_out, in_ws, cot, n_dp, n_head, parts=4):
    rows, width = tokens.shape
    shard = (in_ws[0].shape[0], w_out.shape[0] + sum(w.shape[1] for w in in_ws))
    lines, far = n_dp // 2, n_head // 2 - 1
    dma = lambda *shape: pltpu.SemaphoreType.DMA(shape)
    anywhere = pl.BlockSpec(memory_space=pl.ANY)
    vmem = pl.BlockSpec(memory_space=pltpu.VMEM)
    return pl.pallas_call(
        partial(start_kernel, lines, n_head, parts),
        out_shape=[jax.ShapeDtypeStruct((n_head, rows, width), BF16),
                   jax.ShapeDtypeStruct((n_dp, *shard), BF16),
                   jax.ShapeDtypeStruct((n_head, *cot.shape), BF16)],
        in_specs=[vmem] * (4 + len(in_ws)),
        out_specs=[anywhere] * 3,
        scratch_shapes=[
            pltpu.VMEM((rows, width), BF16),
            pltpu.VMEM(shard, BF16),
            dma(lines), dma(lines), dma(lines), dma(n_dp), dma(2),
            dma(far, parts), dma(parts), dma(far, parts), dma(n_head, parts), dma(parts),
        ]
        + HeadGather.scratch(n_head, COT_PARTS),
        compiler_params=pltpu.CompilerParams(vmem_limit_bytes=VMEM_LIMIT, has_side_effects=True, collective_id=0),
        name="start",
    )(tokens, gain, w_out, *in_ws, cot)


def when(condition):
    return pl.when(condition) if not isinstance(condition, bool) else (lambda f: f() if condition else None)


class HeadScatter:
    def __init__(self, count, refs):
        self.count = count
        (self.out, self.near, self.onward, self.far, self.own,
         self.out_s, self.near_r, self.onward_s, self.far_r) = refs
        self.me = lax.axis_index("head")
        self.side, self.place = self.me % 2, self.me // 2
        self.pair = self.me + 1 - 2 * self.side
        self.parts, self.depth, self.size = self.near.shape[0], self.own.shape[0], self.own.shape[1]

    @staticmethod
    def scratch(count, parts, size, width, depth):
        half = count // 2
        return [
            pltpu.VMEM((2, 2, half, size, width), BF16),
            pltpu.VMEM((parts, half, size, width), BF16),
            pltpu.VMEM((2, half - 1, size, width), BF16),
            pltpu.VMEM((parts, half - 1, size, width), BF16),
            pltpu.VMEM((depth, size, width), F32),
            pltpu.SemaphoreType.DMA((2,)),
            pltpu.SemaphoreType.DMA((parts,)),
            pltpu.SemaphoreType.DMA((2, half - 1)),
            pltpu.SemaphoreType.DMA((parts, half - 1)),
        ]

    def _near(self, p):
        slot = p % 2
        return remote(self.out.at[slot, 1 - self.side], self.near.at[p], self.out_s.at[slot], self.near_r.at[p], "head", self.pair)

    def _far(self, p, f):
        slot = p % 2
        to = lax.rem(self.me + 2 * (f + 1), self.count)
        return remote(self.onward.at[slot, f], self.far.at[p, f], self.onward_s.at[slot, f], self.far_r.at[p, f], "head", to)

    def offer(self, p, total):
        when(p >= 2)(lambda: self._near(p - 2).wait_send())
        for owner in range(self.count):
            self.out[p % 2, owner % 2, owner // 2] = total[owner * self.size : (owner + 1) * self.size].astype(BF16)
        self._near(p).start()

    def turn(self, p):
        slot, half = p % 2, self.count // 2
        self._near(p).wait_recv()
        both = lambda i: self.out[slot, self.side, i].astype(F32) + self.near[p, i].astype(F32)
        for f in range(half - 1):
            when(p >= 2)(lambda f=f: self._far(p - 2, f).wait_send())
            self.onward[slot, f] = both(lax.rem(self.place + f + 1, half)).astype(BF16)
            self._far(p, f).start()
        self.own[p % self.depth] = both(self.place)

    def take(self, p):
        total = self.own[p % self.depth]
        for f in range(self.count // 2 - 1):
            self._far(p, f).wait_recv()
            total = total + self.far[p, f].astype(F32)
        return total

    def close(self):
        for p in range(max(self.parts - 2, 0), self.parts):
            self._near(p).wait_send()
            for f in range(self.count // 2 - 1):
                self._far(p, f).wait_send()


class OwnerScatter:
    def __init__(self, count, out_ref, refs):
        self.count, self.out_ref = count, out_ref
        self.terms, self.near, self.far, self.near_s, self.near_r, self.far_s, self.far_r = refs
        self.me = lax.axis_index("head")
        self.side = self.me % 2
        self.pair = self.me + 1 - 2 * self.side

    @staticmethod
    def scratch(count, rows, width):
        half = count // 2
        sems = lambda n: pltpu.SemaphoreType.DMA((n,))
        return [
            pltpu.VMEM((count, rows, width), BF16),
            pltpu.VMEM((half, rows, width), BF16),
            pltpu.VMEM((half - 1, rows, width), BF16),
            sems(half), sems(half), sems(count), sems(half - 1),
        ]

    def _near(self, owner):
        at = owner // 2
        return remote(self.terms.at[owner], self.near.at[at], self.near_s.at[at], self.near_r.at[at], "head", self.pair)

    def _far(self, owner):
        at = lax.rem(self.me - owner + self.count, self.count) // 2 - 1
        return remote(self.terms.at[owner], self.far.at[at], self.far_s.at[owner], self.far_r.at[at], "head", owner)

    def _mine(self, owner):
        return owner % 2 == self.side

    def offer(self, owner, total):
        self.terms[owner] = total.astype(BF16)
        pl.when(jnp.logical_not(self._mine(owner)))(lambda: self._near(owner).start())

    def settle(self, owner):
        @pl.when(self._mine(owner))
        def _():
            self._near(owner).wait_recv()
            both = self.terms[owner].astype(F32) + self.near[owner // 2].astype(F32)

            @pl.when(owner == self.me)
            def _():
                self.out_ref[...] = both

            @pl.when(owner != self.me)
            def _():
                self.terms[owner] = both.astype(BF16)
                self._far(owner).start()

    def finish(self):
        for f in range(self.count // 2 - 1):
            sender = lax.rem(self.me + 2 * (f + 1), self.count)
            remote(self.terms.at[0], self.far.at[f], self.far_s.at[0], self.far_r.at[f], "head", sender).wait_recv()
            self.out_ref[...] += self.far[f].astype(F32)

        @pl.loop(0, self.count)
        def _(owner):
            pl.when(jnp.logical_not(self._mine(owner)))(lambda: self._near(owner).wait_send())
            pl.when(jnp.logical_and(self._mine(owner), owner != self.me))(lambda: self._far(owner).wait_send())


class HeadGather:
    def __init__(self, count, parts, own, block, refs, takes=None):
        self.count, self.parts, self.own, self.block, self.takes = count, parts, own, block, takes
        self.far_s, self.pair_s, self.fwd_s, self.got = refs
        self.me = lax.axis_index("head")
        self.pair = self.me + 1 - 2 * (self.me % 2)

    @staticmethod
    def scratch(count, parts):
        far = count // 2 - 1
        return [pltpu.SemaphoreType.DMA(s) for s in ((far, parts), (parts,), (far, parts), (count, parts))]

    def _if(self, owner, action):
        pl.when(self.takes(owner))(action) if self.takes else action()

    def _fars(self, base):
        return [(f, lax.rem(base + 2 * (f + 1), self.count)) for f in range(self.count // 2 - 1)]

    def _far(self, p, f, far):
        return remote(self.own(p), self.block(self.me, p), self.far_s.at[f, p], self.got.at[self.me, p], "head", far)

    def _pair(self, p):
        return remote(self.own(p), self.block(self.me, p), self.pair_s.at[p], self.got.at[self.me, p], "head", self.pair)

    def _on(self, p, f, owner):
        return remote(self.block(owner, p), self.block(owner, p), self.fwd_s.at[f, p], self.got.at[owner, p], "head", self.pair)

    def send(self, p):
        def act():
            for f, far in self._fars(self.me):
                self._far(p, f, far).start()
            self._pair(p).start()

        self._if(self.me, act)

    def pass_on(self, p, ready=None):
        for f, far in self._fars(self.me):

            def act(f=f, far=far):
                self._on(p, f, far).wait_recv()
                self._on(p, f, far).start()

            pl.when(far == ready)(act) if ready is not None else self._if(far, act)

    def arrive(self, p, ready=None):
        def near():
            remote(self.own(p), self.block(self.pair, p), self.pair_s.at[p], self.got.at[self.pair, p], "head", self.pair).wait_recv()

        pl.when(self.pair == ready)(near) if ready is not None else self._if(self.pair, near)
        for f, far in self._fars(self.pair):
            act = lambda f=f, far=far: self._on(p, f, far).wait_recv()
            pl.when(far == ready)(act) if ready is not None else self._if(far, act)

    def sent(self, p):
        def mine():
            self._pair(p).wait_send()
            for f, far in self._fars(self.me):
                self._far(p, f, far).wait_send()

        self._if(self.me, mine)
        for f, far in self._fars(self.me):
            self._if(far, lambda f=f, far=far: self._on(p, f, far).wait_send())


LEAD = 8


def mid_kernel(lines, count, parts, att_ref, tok_ref, gain_ref, cot_early, cot_late, ff_ref, down_mine,
               out_ref, grad_ref, hg_ref, gain_grad_ref, terms_ref, down_terms_ref, *scratch):
    scratch = list(scratch)
    take = lambda n: [scratch.pop(0) for _ in range(n)]
    down_refs, back_refs = take(9), take(9)
    second_sems, hg_sems = take(4), take(4)
    cot_ref, second, hidden, hg_own, total, loads, keep_s, down_all, right_s, left_s, over_s, landed = scratch
    size, width = tok_ref.shape[1:]
    ff = ff_ref.shape[1] // 2
    me = lax.axis_index("head")
    greet(lines, count)
    first, hop_step, arrived, last = shard_line(
        lines, down_mine, down_all, (right_s, left_s, over_s, landed, loads.at[1])
    )
    first()
    half = parts // 2
    loading = [
        pltpu.make_async_copy(src, cot_ref.at[:, at : at + half], loads.at[i])
        for i, (src, at) in ((0, (cot_early, 0)), (2, (cot_late, half)))
    ]
    for m in loading:
        m.start()
    down_w = lambda: down_all[...].reshape(-1, ff)
    down, back = (HeadScatter(count, r) for r in (down_refs, back_refs))
    here = lambda owner, p: second.at[p, owner]
    seconds = HeadGather(count, parts, lambda p: here(me, p), here, second_sems)
    there = lambda owner, p: hg_ref.at[owner, p]
    hgs = HeadGather(count, parts, lambda p: hg_own.at[p], there, hg_sems, lambda owner: owner == count - 1)
    keep = lambda p: pltpu.make_async_copy(hg_own.at[p], there(me, p), keep_s.at[p])
    total[...] = jnp.zeros_like(total)
    gain_grad_ref[...] = jnp.zeros_like(gain_grad_ref)

    def within(p, stage):
        pl.when(jnp.logical_and(p >= 0, p < parts))(lambda: stage(p))

    def norm(p):
        rows = tok_ref[p].astype(F32) + att_ref[p]
        hidden[p] = rows
        inv = lax.rsqrt(jnp.mean(rows * rows, axis=-1, keepdims=True) + 1e-6)
        second[p, me] = (rows * inv * gain_ref[...]).astype(BF16)
        seconds.send(p)

    def feed(p):
        seconds.arrive(p)
        rows = second[p].reshape(count * size, width)
        both = dot(rows, ff_ref[...], ((1,), (0,)))
        gate, up = both[:, :ff], both[:, ff:]
        sig = jax.nn.sigmoid(gate)
        act = gate * sig
        middle = (act * up).astype(BF16)

        @pl.when(p == 0)
        def _():
            hop_step(0)
            pl.loop(1, lines - 1)(hop_step)
            arrived()

        down.offer(p, dot(middle, down_w(), ((1,), (1,))))
        cot = cot_ref[:, p].reshape(count * size, width)
        grad = dot(cot, down_w(), ((1,), (0,))).astype(BF16).astype(F32)
        pair = jnp.concatenate(
            [(grad * up * sig * (1.0 + gate * (1.0 - sig))).astype(BF16), (grad * act).astype(BF16)], axis=1
        )
        back.offer(p, dot(pair, ff_ref[...], ((1,), (1,))))
        total[:, : 2 * ff] += dot(rows, pair, ((0,), (0,)))
        total[:, 2 * ff :] += dot(cot, middle, ((0,), (0,)))

    def turn(p):
        down.turn(p)
        back.turn(p)

    def finish(p):
        rows = hidden[p]
        out_ref[p] = (rows + down.take(p)).astype(BF16)
        second_grad = back.take(p).astype(BF16).astype(F32)
        inv = lax.rsqrt(jnp.mean(rows * rows, axis=-1, keepdims=True) + 1e-6)
        scaled = second_grad * gain_ref[...]
        mean = jnp.mean(scaled * rows, axis=-1, keepdims=True)
        grad = cot_ref[me, p].astype(F32) + inv * scaled - rows * (inv * inv * inv * mean)
        grad_ref[p] = grad
        gain_grad_ref[...] += jnp.sum(second_grad * rows * inv, axis=0, keepdims=True)
        hg_own[p] = grad.astype(BF16)
        hgs.send(p)
        keep(p).start()

    for p in range(LEAD):
        norm(p)
    for m in loading:
        m.wait()

    @pl.loop(0, parts + 2)
    def _(step):
        within(step + LEAD, norm)
        within(step, seconds.pass_on)
        within(step, feed)
        within(step, turn)
        within(step - 1, finish)
        within(step - 2, hgs.pass_on)

    terms_ref[...] = total[:, : 2 * ff].astype(BF16)
    down_terms_ref[...] = total[:, 2 * ff :].astype(BF16)

    @pl.loop(0, parts)
    def _(p):
        hgs.arrive(p)
        keep(p).wait()
        hgs.sent(p)
        seconds.sent(p)

    for s in (down, back):
        s.close()
    last()


def mid(attention, tokens, gain, cot_early, cot_late, ff_set, down_mine, n_dp, count, parts=8):
    rows, width = tokens.shape
    lines, ff = n_dp // 2, down_mine.shape[1]
    dma = lambda *shape: pltpu.SemaphoreType.DMA(shape)
    size = rows // parts
    anywhere = pl.BlockSpec(memory_space=pl.ANY)
    vmem = pl.BlockSpec(memory_space=pltpu.VMEM)
    scatter = HeadScatter.scratch(count, parts, size, width, 2)
    out, grad, hg, gain_grad, terms, down_terms = pl.pallas_call(
        partial(mid_kernel, lines, count, parts),
        out_shape=[
            jax.ShapeDtypeStruct((parts, size, width), BF16),
            jax.ShapeDtypeStruct((parts, size, width), F32),
            jax.ShapeDtypeStruct((count, parts, size, width), BF16),
            jax.ShapeDtypeStruct((1, width), F32),
            jax.ShapeDtypeStruct((width, 2 * ff), BF16),
            jax.ShapeDtypeStruct((width, ff), BF16),
        ],
        in_specs=[vmem] * 3 + [anywhere] * 2 + [vmem] * 2,
        out_specs=[vmem, vmem, anywhere, vmem, vmem, vmem],
        scratch_shapes=scatter * 2
        + HeadGather.scratch(count, parts) * 2
        + [
            pltpu.VMEM((count, parts, size, width), BF16),
            pltpu.VMEM((parts, count, size, width), BF16),
            pltpu.VMEM((parts, size, width), F32),
            pltpu.VMEM((parts, size, width), BF16),
            pltpu.VMEM((width, 3 * ff), F32),
            dma(3),
            dma(parts),
            pltpu.VMEM((n_dp, *down_mine.shape), BF16),
            dma(lines), dma(lines), dma(lines), dma(n_dp),
        ],
        compiler_params=pltpu.CompilerParams(vmem_limit_bytes=61 * 1024 * 1024, has_side_effects=True, collective_id=2),
        name="mid",
    )(
        attention.reshape(parts, size, width), tokens.reshape(parts, size, width), gain,
        *(c.reshape(count, parts // 2, size, width) for c in (cot_early, cot_late)), ff_set, down_mine,
    )
    return out.reshape(rows, width), grad.reshape(rows, width), hg.reshape(count, rows, width), gain_grad, terms, down_terms


class ChainScatter:
    LAG = 2

    def __init__(self, lines, terms, own, refs, by_piece):
        self.lines, self.terms, self.own, self.by_piece = lines, terms, own, by_piece
        self.cross, self.going, self.coming, self.cross_s, self.cross_r, self.go_s, self.come_r = refs
        self.pieces = self.cross_s.shape[1]
        self.size = self.cross.shape[1] // self.pieces
        self.me = lax.axis_index("dp")
        self.spot, self.side = self.me // 2, self.me % 2
        self.across = self.me + 1 - 2 * self.side
        self.items = (lines - 1) * self.pieces
        self.points = self.items + (lines - 1) * self.LAG

    @staticmethod
    def scratch(lines, rows, width):
        pieces = max(1, rows // 32)
        wide = lambda *lead: pltpu.VMEM((*lead, rows, width), BF16)
        sems = lambda *shape: pltpu.SemaphoreType.DMA((*shape, pieces))
        return [
            wide(lines), wide(2, lines), wide(2, lines),
            sems(lines), sems(lines), sems(2, lines), sems(2, lines),
        ]

    def _at(self, k):
        return pl.ds(pl.multiple_of(k * self.size, self.size), self.size)

    def _cross(self, place, k):
        at = self._at(k)
        src = self.terms(2 * place + 1 - self.side).at[at]
        return remote(src, self.cross.at[place, at], self.cross_s.at[place, k], self.cross_r.at[place, k], "dp", self.across)

    def _line(self, way, dest, k):
        to = self.me + 2 if way == 0 else self.me - 2
        at = self._at(k)
        return remote(self.going.at[way, dest, at], self.coming.at[way, dest, at], self.go_s.at[way, dest, k], self.come_r.at[way, dest, k], "dp", to)

    def offer(self, place, k):
        self._cross(place, k).start()

    def offer_all(self):
        for k in range(self.pieces):
            for d in range((self.lines + 1) // 2):
                for place in sorted({self.lines - 1 - d, d}, reverse=True):
                    self.offer(place, k)

    def _both(self, place, k):
        return self.own(place)[self._at(k), :].astype(F32) + self.cross[place, self._at(k), :].astype(F32)

    def _passes(self, way, dest):
        return dest > self.spot if way == 0 else dest < self.spot

    def _fed(self, way):
        return self.spot >= 1 if way == 0 else self.spot + 1 < self.lines

    def point(self, n):
        for way in (0, 1):
            away = self.spot if way == 0 else self.lines - 1 - self.spot
            item = n - away * self.LAG
            safe = jnp.clip(item, 0, self.items - 1)
            if self.by_piece:
                k, d = safe // (self.lines - 1), safe % (self.lines - 1)
            else:
                d, k = safe // self.pieces, safe % self.pieces
            dest = self.lines - 1 - d if way == 0 else d
            live = jnp.logical_and(item >= 0, item < self.items)

            @pl.when(jnp.logical_and(live, self._passes(way, dest)))
            def _(way=way, dest=dest, k=k):
                at = self._at(k)
                self._cross(dest, k).wait_recv()

                @pl.when(self._fed(way))
                def _():
                    self._line(way, dest, k).wait_recv()
                    self.going[way, dest, at, :] = (self._both(dest, k) + self.coming[way, dest, at, :].astype(F32)).astype(BF16)

                @pl.when(jnp.logical_not(self._fed(way)))
                def _():
                    self.going[way, dest, at, :] = self._both(dest, k).astype(BF16)

                self._line(way, dest, k).start()

    def finish(self, out_ref):
        for k in range(self.pieces):
            at = slice(k * self.size, (k + 1) * self.size)
            self._cross(self.spot, k).wait_recv()
            out_ref[at, :] = self._both(self.spot, k)
            for way in (0, 1):
                @pl.when(self._fed(way))
                def _(way=way, k=k, at=at):
                    self._line(way, self.spot, k).wait_recv()
                    out_ref[at, :] += self.coming[way, self.spot, at, :].astype(F32)

    def close(self):
        @pl.loop(0, self.lines * self.pieces)
        def _(i):
            place, k = i // self.pieces, i % self.pieces
            self._cross(place, k).wait_send()
            for way in (0, 1):
                pl.when(self._passes(way, place))(lambda way=way: self._line(way, place, k).wait_send())


class LineScatter:
    def __init__(self, lines, terms, own, refs, order):
        self.lines, self.terms, self.own, self.order = lines, terms, own, order
        self.cross, self.going, self.coming, self.cross_s, self.cross_r, self.go_s, self.come_r = refs
        self.pieces = self.cross_s.shape[1]
        self.size = self.cross.shape[1] // self.pieces
        self.me = lax.axis_index("dp")
        self.spot, self.side = self.me // 2, self.me % 2
        self.across = self.me + 1 - 2 * self.side
        self.points = lines * self.pieces

    @staticmethod
    def scratch(lines, rows, width):
        pieces = max(1, rows // 32)
        wide = pltpu.VMEM((lines, rows, width), BF16)
        sems = pltpu.SemaphoreType.DMA((lines, pieces))
        return [wide, wide, wide, sems, sems, sems, sems]

    def _at(self, k):
        return pl.ds(pl.multiple_of(k * self.size, self.size), self.size)

    def _cross(self, place, k):
        at = self._at(k)
        src = self.terms(2 * place + 1 - self.side).at[at]
        return remote(src, self.cross.at[place, at], self.cross_s.at[place, k], self.cross_r.at[place, k], "dp", self.across)

    def _on(self, sender, dest, k):
        at = self._at(k)
        return remote(self.going.at[dest, at], self.coming.at[sender, at], self.go_s.at[dest, k], self.come_r.at[sender, k], "dp", 2 * dest + self.side)

    def offer(self, place, k):
        self._cross(place, k).start()

    def offer_all(self):
        @pl.loop(0, self.points)
        def _(n):
            k, place = self.order(n)
            self.offer(place, k)

    def _both(self, place, k):
        return self.own(place)[self._at(k), :].astype(F32) + self.cross[place, self._at(k), :].astype(F32)

    def point(self, n):
        k, dest = self.order(jnp.clip(n, 0, self.points - 1))

        @pl.when(jnp.logical_and(jnp.logical_and(n >= 0, n < self.points), dest != self.spot))
        def _():
            self._cross(dest, k).wait_recv()
            self.going[dest, self._at(k), :] = self._both(dest, k).astype(BF16)
            self._on(self.spot, dest, k).start()

    def finish(self, out_ref):
        for k in range(self.pieces):
            at = slice(k * self.size, (k + 1) * self.size)
            self._cross(self.spot, k).wait_recv()
            out_ref[at, :] = self._both(self.spot, k)

            @pl.loop(1, self.lines)
            def _(hop, k=k, at=at):
                sender = lax.rem(self.spot + hop, self.lines)
                self._on(sender, self.spot, k).wait_recv()
                out_ref[at, :] += self.coming[sender, at, :].astype(F32)

    def close(self):
        @pl.loop(0, self.points)
        def _(i):
            place, k = i // self.pieces, i % self.pieces
            self._cross(place, k).wait_send()
            pl.when(place != self.spot)(lambda: self._on(self.spot, place, k).wait_send())


def outside_in(lines, i):
    return jnp.where(i % 2 == 0, lines - 1 - i // 2, i // 2)


class SmallSum:
    def __init__(self, n_dp, count, shared, refs):
        self.n_dp, self.count, self.shared = n_dp, count, shared
        self.mine, self.theirs, self.half, self.halves, self.a_s, self.a_r, self.b_s, self.b_r = refs
        self.dp, self.head = lax.axis_index("dp"), lax.axis_index("head")

    @staticmethod
    def scratch(n_dp, count, rows, shared):
        return [
            pltpu.VMEM((rows, 128), F32),
            pltpu.VMEM((n_dp, rows, 128), F32),
            pltpu.VMEM((shared, 128), F32),
            pltpu.VMEM((count, shared, 128), F32),
            pltpu.SemaphoreType.DMA((n_dp,)),
            pltpu.SemaphoreType.DMA((n_dp,)),
            pltpu.SemaphoreType.DMA((count,)),
            pltpu.SemaphoreType.DMA((count,)),
        ]

    def _a(self, hop):
        to = lax.rem(self.dp + hop, self.n_dp)
        return remote(self.mine, self.theirs.at[self.dp], self.a_s.at[hop], self.a_r.at[self.dp], "dp", to)

    def _b(self, hop):
        to = lax.rem(self.head + hop, self.count)
        return remote(self.half, self.halves.at[self.head], self.b_s.at[hop], self.b_r.at[self.head], "head", to)

    def start(self):
        self.theirs[self.dp] = self.mine[...]

        @pl.loop(1, self.n_dp)
        def _(hop):
            self._a(hop).start()

    def turn(self, out_ref):
        @pl.loop(1, self.n_dp)
        def _(hop):
            sender = lax.rem(self.dp + self.n_dp - hop, self.n_dp)
            remote(self.mine, self.theirs.at[sender], self.a_s.at[hop], self.a_r.at[sender], "dp", sender).wait_recv()

        total = self.theirs[0]
        for i in range(1, self.n_dp):
            total = total + self.theirs[i]
        out_ref[...] = total
        self.half[...] = total[: self.shared]
        self.halves[self.head] = total[: self.shared]
        for hop in range(1, self.count):
            self._b(hop).start()

    def finish(self, out_ref):
        for hop in range(1, self.count):
            sender = lax.rem(self.head + self.count - hop, self.count)
            remote(self.half, self.halves.at[sender], self.b_s.at[hop], self.b_r.at[sender], "head", sender).wait_recv()
        total = self.halves[0]
        for i in range(1, self.count):
            total = total + self.halves[i]
        out_ref[: self.shared, :] = total

        @pl.loop(1, self.n_dp)
        def _(hop):
            self._a(hop).wait_send()

        for hop in range(1, self.count):
            self._b(hop).wait_send()


def greet_all(n_dp, count):
    barrier = pltpu.get_barrier_semaphore()
    dp, head = lax.axis_index("dp"), lax.axis_index("head")

    @pl.loop(1, n_dp)
    def _(hop):
        pl.semaphore_signal(barrier, 1, device_id={"dp": lax.rem(dp + hop, n_dp)}, device_id_type=MESH)

    for hop in range(1, count):
        pl.semaphore_signal(barrier, 1, device_id={"head": lax.rem(head + hop, count)}, device_id_type=MESH)
    pl.semaphore_wait(barrier, n_dp + count - 2)


def end_kernel(n_dp, count, parts, shared,
               dpre_ref, w_ref, normed_ref, hg_ref, mixed_ref, down_ref, tok_ref, gain_ref, grad_ref, small_ref,
               in_ref, mix_ref, sum_ref, down_sum_ref, *scratch):
    scratch = list(scratch)
    take = lambda n: [scratch.pop(0) for _ in range(n)]
    head_refs, dp_refs, down_refs, small_refs = take(9), take(7), take(7), take(8)
    terms, dpre, w, normed, hg, mixed, down_own, loads, down_s = scratch
    rows, width = tok_ref.shape
    block = terms.shape[1]
    hid = mixed.shape[1]
    greet_all(n_dp, count)
    lines = n_dp // 2
    side = lax.axis_index("dp") % 2
    down = ChainScatter(lines, lambda j: down_ref.at[j], lambda place: down_own.at[place], down_refs, True)
    fetch = lambda place: pltpu.make_async_copy(down_ref.at[2 * place + side], down_own.at[place], down_s.at[place])
    moves = [pltpu.make_async_copy(s, d, loads.at[i]) for i, (s, d) in enumerate(
        ((dpre_ref, dpre), (w_ref.at[:, hid:], w), (normed_ref, normed), (mixed_ref, mixed), (hg_ref, hg)))]
    for m in moves:
        m.start()
    down.offer_all()
    for place in range(lines):
        fetch(place).start()
    heads = HeadScatter(count, head_refs)
    line = ChainScatter(lines, lambda j: terms.at[j], lambda place: terms.at[2 * place + side], dp_refs, False)
    small = SmallSum(n_dp, count, shared, small_refs)
    size = rows // parts

    def offer(p):
        part = jnp.concatenate([dpre[o * rows + p * size : o * rows + (p + 1) * size, :] for o in range(count)], axis=0)
        heads.offer(p, dot(part, w[...], ((1,), (1,))))

    tiles = width // 256
    per = 256 // block

    def outer(t):
        cols = slice(t * 256, (t + 1) * 256)
        left = dot(normed[:, cols], dpre[...], ((0,), (0,))).astype(BF16)
        right = dot(hg[:, cols], mixed[...], ((0,), (0,))).astype(BF16)
        for b in range(per):
            terms[t * per + b, :, :hid] = right[b * block : (b + 1) * block]
            terms[t * per + b, :, hid:] = left[b * block : (b + 1) * block]
        for place in range(t * per // 2, (t + 1) * per // 2):
            for k in range(line.pieces):
                line.offer(place, k)

    order = [t // 2 if t % 2 else tiles - 1 - t // 2 for t in range(tiles)]
    moves[0].wait()
    moves[1].wait()
    offer(0)
    for m in moves[2:]:
        m.wait()
    for place in range(lines):
        fetch(place).wait()
    down_done = 0
    for i in range(max(tiles, parts)):
        if i < tiles:
            outer(order[i])
        if i < parts:
            heads.turn(i)
        if i + 1 < parts:
            offer(i + 1)
        for n in range(4):
            if down_done < down.points:
                down.point(down_done)
                down_done += 1
    pl.loop(down_done, down.points)(down.point)
    small.mine[...] = small_ref[...]
    gain_total = jnp.zeros((1, width), F32)
    gain = gain_ref[...]

    def finish(p):
        at = slice(p * size, (p + 1) * size)
        normed_grad = heads.take(p).astype(BF16).astype(F32)
        x = tok_ref[at, :].astype(F32)
        inv = lax.rsqrt(jnp.mean(x * x, axis=-1, keepdims=True) + 1e-6)
        scaled = normed_grad * gain
        mean = jnp.mean(scaled * x, axis=-1, keepdims=True)
        in_ref[at, :] = grad_ref[at, :] + inv * scaled - x * (inv * inv * inv * mean)
        return jnp.sum(normed_grad * x * inv, axis=0, keepdims=True)

    done = 0
    for i in range(parts):
        for n in range(2):
            if done < line.points:
                line.point(done)
                done += 1
        gain_total = gain_total + finish(i)
    for i in range(width // 128):
        small.mine[i : i + 1, :] = gain_total[:, i * 128 : (i + 1) * 128]
    small.start()
    half = (done + line.points) // 2
    pl.loop(done, half)(line.point)
    small.turn(sum_ref)
    pl.loop(half, line.points)(line.point)
    line.finish(mix_ref)
    down.finish(down_sum_ref)
    small.finish(sum_ref)
    down.close()
    heads.close()
    line.close()


def end(dpre, weights, normed_rows, hg_rows, mixed, down_terms, tokens, gain, hidden_grad, small, n_dp, count, shared, parts=4):
    rows, width = tokens.shape
    block = width // n_dp
    wide = weights.shape[1]
    anywhere = pl.BlockSpec(memory_space=pl.ANY)
    vmem = pl.BlockSpec(memory_space=pltpu.VMEM)
    like = lambda a: pltpu.VMEM(a.shape, a.dtype)
    return pl.pallas_call(
        partial(end_kernel, n_dp, count, parts, shared),
        out_shape=[
            jax.ShapeDtypeStruct((rows, width), F32),
            jax.ShapeDtypeStruct((block, wide), F32),
            jax.ShapeDtypeStruct(small.shape, F32),
            jax.ShapeDtypeStruct(down_terms.shape[1:], F32),
        ],
        in_specs=[anywhere] * 6 + [vmem] * 4,
        out_specs=[vmem] * 4,
        scratch_shapes=HeadScatter.scratch(count, parts, rows // parts, width, parts)
        + ChainScatter.scratch(n_dp // 2, block, wide)
        + ChainScatter.scratch(n_dp // 2, block, down_terms.shape[2])
        + SmallSum.scratch(n_dp, count, small.shape[0], shared)
        + [pltpu.VMEM((n_dp, block, wide), BF16), like(dpre), pltpu.VMEM((width, dpre.shape[1]), BF16), like(normed_rows), like(hg_rows), like(mixed),
           pltpu.VMEM((n_dp // 2, *down_terms.shape[1:]), BF16),
           pltpu.SemaphoreType.DMA((5,)), pltpu.SemaphoreType.DMA((n_dp // 2,))],
        compiler_params=pltpu.CompilerParams(vmem_limit_bytes=VMEM_LIMIT, has_side_effects=True, collective_id=1),
        name="end",
    )(dpre, weights, normed_rows, hg_rows, mixed, down_terms, tokens, gain, hidden_grad, small)


def spread_kernel(out_ref, in_ref, mix_ref, ff_ref, down_ref, out_to, in_to, *results):
    to_out, *mixes, beta, ff_gate, ff_up, ff_down = results
    hid, heads, ff = to_out.shape[0], beta.shape[0], ff_gate.shape[0]
    wide = down_ref.shape[1]
    out_to[...] = out_ref[...]
    in_to[...] = in_ref[...]
    to_out[...] = mix_ref[:, :hid].T
    for i, r in enumerate(mixes):
        r[...] = mix_ref[:, (i + 1) * hid : (i + 2) * hid]
    beta[...] = mix_ref[:, 5 * hid :].T[:heads]
    ff_gate[...] = ff_ref[:, :wide].T[:ff]
    ff_up[...] = ff_ref[:, wide:].T[:ff]
    ff_down[...] = down_ref[...].T[:ff]


def spread(output, input_grad, mix, ff_sum, down_sum, hid, heads, ff):
    block = mix.shape[0]
    vmem = pl.BlockSpec(memory_space=pltpu.VMEM)
    shapes = [(hid, block)] + [(block, hid)] * 4 + [(heads, block)] + [(ff, block)] * 3
    return pl.pallas_call(
        spread_kernel,
        out_shape=[jax.ShapeDtypeStruct(a.shape, a.dtype) for a in (output, input_grad)]
        + [jax.ShapeDtypeStruct(s, F32) for s in shapes],
        in_specs=[vmem] * 5,
        out_specs=[vmem] * (2 + len(shapes)),
        compiler_params=pltpu.CompilerParams(vmem_limit_bytes=VMEM_LIMIT),
        name="spread",
    )(output, input_grad, mix, ff_sum, down_sum)


def doc_tables(lengths, length):
    count = lengths.shape[0]
    index = jnp.arange(count)
    ends = jnp.sum(jnp.where(index[None, :] <= index[:, None], lengths[None, :], 0), axis=1)
    position = jnp.arange(length, dtype=jnp.int32)
    doc = jnp.sum((position[:, None] >= ends[None, :]).astype(jnp.int32), axis=1)
    no_doc = lambda n: jnp.full((n,), -1, jnp.int32)
    before = [jnp.concatenate([no_doc(o), doc[:-o]]) == doc for o in (1, 2, 3)]
    after = [jnp.concatenate([doc[o:], no_doc(o)]) == doc for o in (1, 2, 3)]
    blocks = doc.reshape(-1, CHUNK)
    ending = blocks[:, -1:]
    prior = jnp.concatenate([no_doc(1)[:, None], ending[:-1]], axis=0)
    enter = (blocks == prior).reshape(-1)
    leave = (blocks == ending).reshape(-1)
    columns = before + [enter, leave] + after + [doc]
    aux = jnp.stack([c.astype(F32) for c in columns], axis=1)
    return aux, doc.astype(F32).reshape(-1, GROUP, CHUNK)


def on_device(
    tokens,
    lengths,
    attn_gain,
    w_query,
    w_key,
    w_value,
    w_beta,
    w_gate_out,
    conv_weight,
    head_gain,
    w_out,
    mlp_gain,
    w_mlp_gate,
    w_mlp_up,
    w_down,
    cotangent,
):
    hid, heads, ff = w_query.shape[1], w_beta.shape[1], w_mlp_gate.shape[1]
    n_dp, n_head = lax.axis_size("dp"), lax.axis_size("head")
    beta_wide = jnp.pad(w_beta, ((0, 0), (0, HEAD_DIM - heads)))
    in_ws = [w_query, w_key, w_value, w_gate_out, beta_wide]
    half = cotangent.shape[0] // 2
    normed_rows, first_set, cot_early = start(
        tokens, attn_gain[None, :], w_out, in_ws, cotangent[:half], n_dp, n_head
    )
    normed_rows = normed_rows.reshape(-1, normed_rows.shape[2])
    first_set = first_set.reshape(-1, first_set.shape[2])
    wide = -(-ff // 256) * 256
    padded = lambda w: jnp.pad(w, ((0, 0), (0, wide - ff)))
    mine = jnp.concatenate([padded(w_mlp_gate), padded(w_mlp_up)], axis=1)

    length = normed_rows.shape[0]
    aux, docrow = doc_tables(lengths[0], length)
    conv = jnp.swapaxes(conv_weight.astype(F32), 0, 1).reshape(conv_weight.shape[1], 3 * hid)
    gain = head_gain[None, :]
    pre, mixed, *saved, attention, cot_late, ff_set = mixer_fwd(
        normed_rows, first_set, aux, docrow, conv, gain, cotangent[half:], mine, n_dp, n_head
    )
    ff_set = ff_set.reshape(-1, ff_set.shape[2])
    output, hidden_grad, hg_some, mlp_gain_grad, mlp_terms, down_terms = mid(
        attention, tokens, mlp_gain[None, :], cot_early, cot_late, ff_set, padded(w_down.T), n_dp, n_head
    )
    dpre, conv_part, head_gain_grad, mlp_reduced, hg_rows = mixer_bwd(
        hg_some, first_set, aux, docrow, conv, gain, (pre, *saved),
        mlp_terms.reshape(n_dp, -1, mlp_terms.shape[1]),
    )
    taps = conv_part.shape[0]
    shared = 2 * (tokens.shape[1] // 128) + 8
    small = jnp.concatenate(
        [
            jnp.zeros((tokens.shape[1] // 128, 128), F32),
            mlp_gain_grad.reshape(-1, 128),
            jnp.pad(head_gain_grad, ((0, 7), (0, 0))),
            conv_part.reshape(-1, 128),
        ]
    )
    input_grad, mix_reduced, summed, down_reduced = end(
        dpre, first_set, normed_rows, hg_rows, mixed, down_terms.reshape(n_dp, -1, wide), tokens, attn_gain[None, :], hidden_grad, small,
        n_dp, n_head, shared,
    )
    gains = summed[: shared - 8].reshape(2, -1)
    conv_grad = jnp.swapaxes(summed[shared:].reshape(taps, 3, hid), 0, 1)
    spread_out = spread(output, input_grad, mix_reduced, mlp_reduced, down_reduced, hid, heads, ff)
    output, input_grad, to_out, query, key, value, gate, beta, ff_gate, ff_up, ff_down = spread_out
    return (
        output,
        input_grad,
        gains[0],
        query,
        key,
        value,
        beta.T,
        gate,
        conv_grad,
        summed[shared - 8],
        to_out,
        gains[1],
        ff_gate.T,
        ff_up.T,
        ff_down,
    )


def solution(mesh):
    rows = P(("dp", "head"), None)
    in_specs = (
        rows,
        P("dp", None),
        P(),
        P("dp", "head"),
        P("dp", "head"),
        P("dp", "head"),
        P("dp", "head"),
        P("dp", "head"),
        P(None, None, "head"),
        P(),
        P("head", "dp"),
        P(),
        P("dp", "head"),
        P("dp", "head"),
        P("head", "dp"),
        rows,
    )
    out_specs = (
        rows,
        rows,
        P(),
        P("dp", "head"),
        P("dp", "head"),
        P("dp", "head"),
        P("dp", "head"),
        P("dp", "head"),
        P(None, None, "head"),
        P(),
        P("head", "dp"),
        P(),
        P("dp", "head"),
        P("dp", "head"),
        P("head", "dp"),
    )
    return jax.shard_map(
        on_device, mesh=mesh, in_specs=in_specs, out_specs=out_specs, check_vma=False
    )
```

```python
from functools import partial

import jax
import jax.numpy as jnp
from jax import lax
from jax.experimental import pallas as pl
from jax.experimental.pallas import tpu as pltpu
from jax.sharding import PartitionSpec as P

HEAD_DIM = 128
CHUNK = 128
GROUP = 4
STEP = CHUNK * GROUP
PAD = 8
F32 = jnp.float32
BF16 = jnp.bfloat16
COT_PARTS = 2
HG_PARTS = 2
VMEM_LIMIT = 56 * 1024 * 1024


def dot(left, right, dims):
    return lax.dot_general(left, right, (dims, ((), ())), preferred_element_type=F32)


def mul(left, right):
    return dot(left.astype(BF16), right.astype(BF16), ((1,), (0,)))


def mul_t(left, right):
    return dot(left.astype(BF16), right.astype(BF16), ((1,), (1,)))


def t_mul(left, right):
    return dot(left.astype(BF16), right.astype(BF16), ((0,), (0,)))


def unit_inverses(lowers):
    row = lax.broadcasted_iota(jnp.int32, (CHUNK, CHUNK), 0)
    col = lax.broadcasted_iota(jnp.int32, (CHUNK, CHUNK), 1)
    eye = (row == col).astype(F32)
    level = lambda bit: jnp.logical_and(
        (row >> (bit + 1)) == (col >> (bit + 1)), (row >> bit) > (col >> bit)
    )
    first = level(0)
    solved = [eye - jnp.where(first, a, 0.0) for a in lowers]
    for bit in range(1, CHUNK.bit_length() - 1):
        mask = level(bit)
        right = [mul(jnp.where(mask, a, 0.0), t) for a, t in zip(lowers, solved)]
        solved = [t - mul(t, r) for t, r in zip(solved, right)]
    return solved


def conv_parts(pre, ext, conv, aux):
    summed = pre * conv[3:4, :]
    for offset in range(1, 4):
        shifted = ext[PAD - offset : PAD - offset + STEP, :]
        summed = summed + shifted * aux[:, offset - 1 : offset] * conv[3 - offset : 4 - offset, :]
    return summed


def unit_rows(act, scale):
    out = []
    for h in range(act.shape[1] // HEAD_DIM):
        part = act[:, h * HEAD_DIM : (h + 1) * HEAD_DIM]
        inv = lax.rsqrt(jnp.sum(part * part, axis=-1, keepdims=True) + 1e-6)
        out.append((part * inv * scale, inv))
    return out


def chunk_masks(aux, docrow):
    row = lax.broadcasted_iota(jnp.int32, (CHUNK, CHUNK), 0)
    col = lax.broadcasted_iota(jnp.int32, (CHUNK, CHUNK), 1)
    made = []
    for c in range(GROUP):
        same = aux[c * CHUNK : (c + 1) * CHUNK, 8:9] == docrow[c : c + 1, :]
        made.append((jnp.logical_and(same, row > col), jnp.logical_and(same, row >= col)))
    return made


def mixer_fwd_kernel(
    lines, count,
    x_ref, w_ref, aux_ref, docrow_ref, conv_ref, gain_ref, cot_ref, ff_ref,
    pre_ref, mixed_ref, o_ref, t_ref, phi_ref, s_ref, p_ref, d_ref, ew_ref, att_ref, cot_rows, ff_rows,
    ext, state, terms, near, far_terms, near_s, near_r, far_s, far_r, right_s, left_s, over_s, landed, local, *cot_sems,
):
    heads = mixed_ref.shape[1] // HEAD_DIM
    hid = heads * HEAD_DIM
    grid_step, last_step = pl.program_id(0), pl.num_programs(0) - 1
    first, hop_step, arrived, last = shard_line(lines, ff_ref, ff_rows, (right_s, left_s, over_s, landed, local.at[0]))
    cot_half = cot_ref.shape[0] // 2
    cots, held = cot_gather(count, cot_ref.at[pl.ds(cot_half, cot_half)], cot_rows, cot_sems, local.at[1])
    cot_parts = cots.parts

    attend = OwnerScatter(count, att_ref, (terms, near, far_terms, near_s, near_r, far_s, far_r))

    @pl.when(grid_step == 0)
    def _():
        greet(lines, count)
        first()
        held.start()
        for p in range(cot_parts):
            cots.send(p)

    @pl.when(grid_step == 2)
    def _():
        hop_step(0)
        cots.pass_on(0)

    @pl.when(pl.program_id(0) == 0)
    def _():
        ext[0:PAD, :] = jnp.zeros((PAD, 3 * hid), F32)
        state[...] = jnp.zeros_like(state)

    pre_ref[...] = dot(x_ref[...], w_ref[:, hid:], ((1,), (0,)))
    pl.when(grid_step >= 1)(lambda: attend.settle(grid_step - 1))
    aux = aux_ref[...]
    conv = conv_ref[...]
    pre = pre_ref[:, : 3 * hid]
    ext[PAD:, :] = pre
    act = conv_parts(pre, ext, conv, aux)
    act = act * jax.nn.sigmoid(act)
    ext[0:PAD, :] = ext[STEP:, :]
    q = unit_rows(act[:, :hid], HEAD_DIM**-0.5)
    k = unit_rows(act[:, hid : 2 * hid], 1.0)
    beta = jax.nn.sigmoid(pre_ref[:, 4 * hid : 4 * hid + 8])
    masks = chunk_masks(aux, docrow_ref[0])

    items = [(c, h) for c in range(GROUP) for h in range(heads)]
    rows = [slice(c * CHUNK, (c + 1) * CHUNK) for c in range(GROUP)]
    lowers, scores = [], []
    for c, h in items:
        key, query = k[h][0][rows[c]], q[h][0][rows[c]]
        both = mul_t(jnp.concatenate([key, query], axis=0), key)
        lowers.append(jnp.where(masks[c][0], both[:CHUNK] * beta[rows[c], h : h + 1], 0.0))
        scores.append(jnp.where(masks[c][1], both[CHUNK:], 0.0).astype(BF16))
    solved = unit_inverses(lowers)
    parts = []
    for (c, h), inverse, score in zip(items, solved, scores):
        key = k[h][0][rows[c]]
        value = act[rows[c], 2 * hid + h * HEAD_DIM : 2 * hid + (h + 1) * HEAD_DIM]
        b = beta[rows[c], h : h + 1]
        enter, leave = aux[rows[c], 3:4], aux[rows[c], 4:5]
        inverse = inverse.astype(BF16)
        wu = mul(inverse, jnp.concatenate([key * b, value * b], axis=1))
        ew, u = wu[:, :HEAD_DIM] * enter, wu[:, HEAD_DIM:]
        phi_b = t_mul(key * leave, jnp.concatenate([ew, u], axis=1))
        parts.append((ew, u, phi_b[:, :HEAD_DIM].astype(BF16), phi_b[:, HEAD_DIM:]))
        t_ref[c, h] = inverse
        p_ref[c, h] = score
        ew_ref[c, h] = ew.astype(BF16)
        phi_ref[c, h] = parts[-1][2]
    for h in range(heads):
        s = state[h]
        for c in range(GROUP):
            low = s.astype(BF16)
            s_ref[c, h] = low
            _, _, phi, b_term = parts[c * heads + h]
            keep = aux[(c + 1) * CHUNK - 1 : (c + 1) * CHUNK, 3:4]
            s = s * keep - mul(phi, low) + b_term
        state[h] = s
    gain = gain_ref[...]
    for (c, h), (ew, u, _, _), score in zip(items, parts, scores):
        enter = aux[rows[c], 3:4]
        from_state = mul(jnp.concatenate([ew, q[h][0][rows[c]] * enter], axis=0), s_ref[c, h])
        d = (u - from_state[:CHUNK]).astype(BF16)
        d_ref[c, h] = d
        o = from_state[CHUNK:] + mul(score, d)
        cols = slice(h * HEAD_DIM, (h + 1) * HEAD_DIM)
        o_ref[rows[c], cols] = o
        normed = o * lax.rsqrt(jnp.mean(o * o, axis=-1, keepdims=True) + 1e-5) * gain
        gate = pre_ref[rows[c], 3 * hid + h * HEAD_DIM : 3 * hid + (h + 1) * HEAD_DIM]
        mixed_ref[rows[c], cols] = (normed * (gate * jax.nn.sigmoid(gate))).astype(BF16)

    attend.offer(grid_step, dot(mixed_ref[...], w_ref[:, :hid], ((1,), (1,))))

    @pl.when(grid_step == last_step)
    def _():
        attend.settle(grid_step)
        for p in range(1, cot_parts):
            cots.pass_on(p)
        pl.loop(1, lines - 1)(hop_step)
        held.wait()
        for p in range(cot_parts):
            cots.arrive(p)
            cots.sent(p)
        arrived()
        attend.finish()
        last()


def mixer_bwd_kernel(
    lines, steps,
    hg_in, wout_ref, pre_ref, halo_ref, aux_ref, docrow_ref, conv_ref, gain_ref,
    o_ref, t_ref, phi_ref, s_ref, p_ref, d_ref, ew_ref, terms_ref,
    dpre_ref, dconv_ref, dgain_ref, sum_ref, hg_out,
    ext, later, dstate, own, own_s, hg_all, hg_s, *refs,
):
    heads = o_ref.shape[1] // HEAD_DIM
    hid = heads * HEAD_DIM
    grid_step = pl.program_id(0)
    side = lax.axis_index("dp") % 2
    dp_refs, hg_sems = refs[:7], refs[7:]
    me, final = lax.axis_index("head"), hg_all.shape[0] - 1
    hg_parts = hg_sems[1].shape[0]
    hg_size = hg_all.shape[1] // hg_parts
    hg_block = lambda owner, p: hg_all.at[owner, pl.ds(p * hg_size, hg_size)]
    hgs = HeadGather(
        final + 1, hg_parts, lambda p: hg_block(me, p), hg_block, hg_sems, lambda owner: owner != final
    )
    load = lambda owner, i: pltpu.make_async_copy(hg_in.at[owner], hg_all.at[owner], hg_s.at[i])
    order = lambda n: (n // lines, outside_in(lines, n % lines))
    line = LineScatter(lines, lambda j: terms_ref.at[j], lambda place: own.at[place], dp_refs, order)
    fetch = lambda place: pltpu.make_async_copy(terms_ref.at[2 * place + side], own.at[place], own_s.at[place])

    @pl.when(grid_step == 0)
    def _():
        load(final, 0).start()
        pl.when(me != final)(lambda: load(me, 1).start())
        greet_line(lines, final + 1)
        line.offer_all()
        pl.when(me != final)(lambda: load(me, 1).wait())
        for p in range(hg_parts):
            hgs.send(p)
        for place in range(lines):
            fetch(place).start()
        load(final, 0).wait()
        for place in range(lines):
            fetch(place).wait()

    per_step = 5
    base = 3

    def point(i):
        n = grid_step * per_step + i - base
        line.point(n)

    point(0)

    @pl.when(pl.program_id(0) == 0)
    def _():
        later[STEP:, :] = jnp.zeros((PAD, 3 * hid), F32)
        dstate[...] = jnp.zeros_like(dstate)
        dconv_ref[...] = jnp.zeros_like(dconv_ref)
        dgain_ref[...] = jnp.zeros_like(dgain_ref)

    @pl.when(grid_step >= 1)
    def _():
        for p in range(hg_parts):
            hgs.arrive(p, final - grid_step)

    hg_out[...] = hg_all[final - grid_step]
    mixed_grad = dot(hg_out[...], wout_ref[...], ((1,), (0,))).astype(BF16).astype(F32)
    aux = aux_ref[...]
    conv = conv_ref[...]
    pre = pre_ref[:, : 3 * hid]
    ext[0:PAD, :] = halo_ref[:, : 3 * hid]
    ext[PAD:, :] = pre
    lin = conv_parts(pre, ext, conv, aux)
    sig = jax.nn.sigmoid(lin)
    act = lin * sig
    dsilu = sig * (1.0 + lin * (1.0 - sig))
    scale = HEAD_DIM**-0.5
    q = unit_rows(act[:, :hid], 1.0)
    k = unit_rows(act[:, hid : 2 * hid], 1.0)
    beta = jax.nn.sigmoid(pre_ref[:, 4 * hid : 4 * hid + 8])
    masks = chunk_masks(aux, docrow_ref[0])
    gain = gain_ref[...]

    items = [(c, h) for c in range(GROUP) for h in range(heads)]
    rows = [slice(c * CHUNK, (c + 1) * CHUNK) for c in range(GROUP)]
    cols = [slice(h * HEAD_DIM, (h + 1) * HEAD_DIM) for h in range(heads)]

    d_out, d_gain = [], jnp.zeros((1, HEAD_DIM), F32)
    for h in range(heads):
        o = o_ref[:, cols[h]]
        inv = lax.rsqrt(jnp.mean(o * o, axis=-1, keepdims=True) + 1e-5)
        unit = o * inv
        gate = pre_ref[:, 3 * hid + h * HEAD_DIM : 3 * hid + (h + 1) * HEAD_DIM]
        s = jax.nn.sigmoid(gate)
        dm = mixed_grad[:, cols[h]]
        dpre_ref[:, 3 * hid + h * HEAD_DIM : 3 * hid + (h + 1) * HEAD_DIM] = (
            dm * unit * gain * (s * (1.0 + gate * (1.0 - s)))
        ).astype(BF16)
        dn = dm * (gate * s)
        d_gain = d_gain + jnp.sum(dn * unit, axis=0, keepdims=True)
        du = dn * gain
        d_out.append(inv * (du - unit * jnp.mean(du * unit, axis=-1, keepdims=True)))
    dgain_ref[...] += d_gain
    point(1)

    first = []
    for c, h in items:
        enter = aux[rows[c], 3:4]
        do = d_out[h][rows[c]].astype(BF16)
        eq = (q[h][0][rows[c]] * (enter * scale)).astype(BF16)
        x = t_mul(p_ref[c, h], do)
        c_term = t_mul(
            jnp.concatenate([eq, -ew_ref[c, h]], axis=0),
            jnp.concatenate([do, x.astype(BF16)], axis=0),
        )
        first.append((do, x, c_term))
    point(2)
    after = {}
    for h in range(heads):
        ds = dstate[h]
        for c in reversed(range(GROUP)):
            low = ds.astype(BF16)
            after[c, h] = low
            keep = aux[(c + 1) * CHUNK - 1 : (c + 1) * CHUNK, 3:4]
            ds = ds * keep - t_mul(phi_ref[c, h], low) + first[c * heads + h][2]
        dstate[h] = ds
    db_cols = []
    grads = {}
    point(3)
    for (c, h), (do, x, _) in zip(items, first):
        enter, leave = aux[rows[c], 3:4], aux[rows[c], 4:5]
        b = beta[rows[c], h : h + 1]
        key, query = k[h][0][rows[c]], q[h][0][rows[c]] * scale
        value = act[rows[c], 2 * hid + h * HEAD_DIM : 2 * hid + (h + 1) * HEAD_DIM]
        ds = after[c, h]
        d, s = d_ref[c, h], s_ref[c, h]
        dr = t_mul(t_ref[c, h], x + mul(key * leave, ds))
        stacked = jnp.concatenate([do, dr.astype(BF16)], axis=0)
        with_d = mul_t(stacked, d)
        with_s = mul_t(stacked, s) * jnp.concatenate([enter, enter], axis=0)
        dp = jnp.where(masks[c][1], with_d[:CHUNK], 0.0)
        da = jnp.where(masks[c][0], -with_d[CHUNK:], 0.0)
        pair = jnp.concatenate([dp, da], axis=0).astype(BF16)
        with_k = mul(pair, key)
        dq = with_s[:CHUNK] + with_k[:CHUNK]
        row_k = with_k[CHUNK:] - with_s[CHUNK:]
        dk = b * row_k + t_mul(pair, jnp.concatenate([query, key * b], axis=0))
        dk = dk + mul_t(d, ds) * leave
        db = jnp.sum(dr * value + key * row_k, axis=-1, keepdims=True)
        grads[c, h] = (dq * scale, dk, dr * b, db * b * (1.0 - b))
    point(4)
    for h in range(heads):
        whole = [jnp.concatenate([grads[c, h][i] for c in range(GROUP)], axis=0) for i in range(4)]
        for i, unit in ((0, q[h]), (1, k[h])):
            y, inv = unit
            grad = inv * (whole[i] - y * jnp.sum(y * whole[i], axis=-1, keepdims=True))
            at = slice(i * hid + h * HEAD_DIM, i * hid + (h + 1) * HEAD_DIM)
            later[0:STEP, at] = grad * dsilu[:, at]
        at = slice(2 * hid + h * HEAD_DIM, 2 * hid + (h + 1) * HEAD_DIM)
        later[0:STEP, at] = whole[2] * dsilu[:, at]
        db_cols.append(whole[3])
    lane = lax.broadcasted_iota(jnp.int32, (STEP, HEAD_DIM), 1)
    tail = jnp.zeros((STEP, HEAD_DIM), F32)
    for h in range(heads):
        tail = jnp.where(lane == h, db_cols[h], tail)
    dpre_ref[:, 4 * hid :] = tail.astype(BF16)
    dlin = later[0:STEP, :]
    dpre = dlin * conv[3:4, :]
    taps = [jnp.sum(dlin * pre, axis=0, keepdims=True)]
    for offset in range(1, 4):
        ahead = later[offset : offset + STEP, :]
        dpre = dpre + ahead * aux[:, 4 + offset : 5 + offset] * conv[3 - offset : 4 - offset, :]
        behind = ext[PAD - offset : PAD - offset + STEP, :] * aux[:, offset - 1 : offset]
        taps.append(jnp.sum(dlin * behind, axis=0, keepdims=True))
    dpre_ref[:, : 3 * hid] = dpre.astype(BF16)
    for offset in range(4):
        dconv_ref[3 - offset : 4 - offset, :] += taps[offset]
    later[STEP:, :] = later[0:PAD, :]

    @pl.when(grid_step < steps - 1)
    def _():
        for p in range(hg_parts):
            hgs.pass_on(p, final - 1 - grid_step)

    @pl.when(grid_step == steps - 1)
    def _():
        for p in range(hg_parts):
            hgs.sent(p)
        pl.loop(max(steps * per_step - base, 0), line.points)(line.point)
        line.finish(sum_ref)
        line.close()


def mixer_fwd(x_rows, weights, aux, docrow, conv, gain, cotangent, ff_mine, n_dp, count):
    hid = conv.shape[1] // 3
    length, width = x_rows.shape[0], weights.shape[1] - hid
    heads, chunks = hid // HEAD_DIM, length // CHUNK
    lines, dma = n_dp // 2, lambda *shape: pltpu.SemaphoreType.DMA(shape)
    anywhere = pl.BlockSpec(memory_space=pl.ANY)
    rows = lambda n: pl.BlockSpec((STEP, n), lambda i: (i, 0))
    whole = lambda a: pl.BlockSpec(a.shape, lambda i: (0,) * a.ndim)
    square = pl.BlockSpec((GROUP, heads, CHUNK, HEAD_DIM), lambda i: (i, 0, 0, 0))
    squares = jax.ShapeDtypeStruct((chunks, heads, CHUNK, HEAD_DIM), BF16)
    return pl.pallas_call(
        partial(mixer_fwd_kernel, lines, count),
        grid=(length // STEP,),
        in_specs=[
            rows(x_rows.shape[1]), whole(weights), rows(aux.shape[1]),
            pl.BlockSpec((1, GROUP, CHUNK), lambda i: (i, 0, 0)), whole(conv), whole(gain),
            whole(cotangent), whole(ff_mine),
        ],
        out_specs=[rows(width), rows(hid), rows(hid)]
        + [square] * 6
        + [pl.BlockSpec((STEP, x_rows.shape[1]), lambda i: (0, 0))]
        + [anywhere] * 2,
        out_shape=[
            jax.ShapeDtypeStruct((length, width), F32),
            jax.ShapeDtypeStruct((length, hid), BF16),
            jax.ShapeDtypeStruct((length, hid), F32),
        ]
        + [squares] * 6
        + [
            jax.ShapeDtypeStruct((STEP, x_rows.shape[1]), F32),
            jax.ShapeDtypeStruct((count, cotangent.shape[0] // 2, cotangent.shape[1]), BF16),
            jax.ShapeDtypeStruct((n_dp, *ff_mine.shape), BF16),
        ],
        scratch_shapes=[
            pltpu.VMEM((PAD + STEP, 3 * hid), F32),
            pltpu.VMEM((heads, HEAD_DIM, HEAD_DIM), F32),
        ]
        + OwnerScatter.scratch(count, STEP, x_rows.shape[1])
        + [
            dma(lines), dma(lines), dma(lines), dma(n_dp), dma(2),
        ]
        + HeadGather.scratch(count, COT_PARTS),
        compiler_params=pltpu.CompilerParams(vmem_limit_bytes=VMEM_LIMIT, has_side_effects=True, collective_id=3),
        name="mixer_fwd",
    )(x_rows, weights, aux, docrow, conv, gain, cotangent, ff_mine)


def mixer_bwd(hg_rows, weights, aux, docrow, conv, gain, saved, terms):
    pre, o, t, phi, s, p, d, ew = saved
    length, width = pre.shape
    hid = conv.shape[1] // 3
    heads, steps = hid // HEAD_DIM, length // STEP
    last = steps - 1
    n_dp, block, wide = terms.shape
    lines = n_dp // 2
    rows = lambda n: pl.BlockSpec((STEP, n), lambda i: (last - i, 0))
    whole = lambda a: pl.BlockSpec(a.shape, lambda i: (0,) * a.ndim)
    square = pl.BlockSpec((GROUP, heads, CHUNK, HEAD_DIM), lambda i: (last - i, 0, 0, 0))
    halo = pl.BlockSpec(
        (PAD, width), lambda i: (jnp.maximum((last - i) * (STEP // PAD) - 1, 0), 0)
    )
    return pl.pallas_call(
        partial(mixer_bwd_kernel, lines, steps),
        grid=(steps,),
        in_specs=[
            pl.BlockSpec(memory_space=pl.ANY), pl.BlockSpec((weights.shape[0], hid), lambda i: (0, 0)), rows(width), halo, rows(aux.shape[1]),
            pl.BlockSpec((1, GROUP, CHUNK), lambda i: (last - i, 0, 0)), whole(conv), whole(gain),
            rows(hid),
        ]
        + [square] * 6
        + [pl.BlockSpec(memory_space=pl.ANY)],
        out_specs=[
            rows(width),
            pl.BlockSpec((4, 3 * hid), lambda i: (0, 0)),
            pl.BlockSpec((1, HEAD_DIM), lambda i: (0, 0)),
            pl.BlockSpec((block, wide), lambda i: (0, 0)),
            rows(weights.shape[0]),
        ],
        out_shape=[
            jax.ShapeDtypeStruct((length, width), BF16),
            jax.ShapeDtypeStruct((4, 3 * hid), F32),
            jax.ShapeDtypeStruct((1, HEAD_DIM), F32),
            jax.ShapeDtypeStruct((block, wide), F32),
            jax.ShapeDtypeStruct((length, weights.shape[0]), BF16),
        ],
        scratch_shapes=[
            pltpu.VMEM((PAD + STEP, 3 * hid), F32),
            pltpu.VMEM((STEP + PAD, 3 * hid), F32),
            pltpu.VMEM((heads, HEAD_DIM, HEAD_DIM), F32),
            pltpu.VMEM((lines, block, wide), BF16),
            pltpu.SemaphoreType.DMA((lines,)),
            pltpu.VMEM(hg_rows.shape, BF16),
            pltpu.SemaphoreType.DMA((2,)),
        ]
        + LineScatter.scratch(lines, block, wide)
        + HeadGather.scratch(hg_rows.shape[0], HG_PARTS),
        compiler_params=pltpu.CompilerParams(vmem_limit_bytes=VMEM_LIMIT, has_side_effects=True, collective_id=4),
        name="mixer_bwd",
    )(hg_rows, weights, pre, pre, aux, docrow, conv, gain, o, t, phi, s, p, d, ew, terms)


MESH = pl.DeviceIdType.MESH


def remote(src, dst, sent, landed, axis, to):
    return pltpu.make_async_remote_copy(
        src_ref=src, dst_ref=dst, send_sem=sent, recv_sem=landed,
        device_id={axis: to}, device_id_type=MESH,
    )


def shard_line(lines, own, out, sems):
    right_s, left_s, over_s, landed, local = sems
    me = lax.axis_index("dp")
    spot, side = me // 2, me % 2
    slot = lambda place: 2 * place + side
    across = me + 1 - 2 * side

    def hop(step, where):
        return (spot - step, me + 2, right_s) if where == 0 else (spot + step, me - 2, left_s)

    def going(step, where):
        place, to, sent = hop(step, where)
        src = out.at[slot(place)] if not isinstance(step, int) or step else own
        return remote(src, out.at[slot(place)], sent.at[step], landed.at[slot(place)], "dp", to)

    def goes(step, where):
        if where == 0:
            return jnp.logical_and(spot - step >= 0, spot + 1 < lines)
        return jnp.logical_and(spot + step < lines, spot >= 1)

    def over(place):
        return remote(out.at[slot(place)], out.at[slot(place)], over_s.at[place], landed.at[slot(place)], "dp", across)

    def first():
        pltpu.make_async_copy(own, out.at[me], local).start()
        remote(own, out.at[me], over_s.at[spot], landed.at[me], "dp", across).start()
        for where in (0, 1):
            pl.when(goes(0, where))(lambda where=where: going(0, where).start())

    def arrive(step, place):
        @pl.when(jnp.logical_and(place >= 0, place < lines))
        def _():
            over(place).wait_recv()
            over(place).start()

    def hop_step(step):
        for where in (0, 1):
            place = spot - step - 1 if where == 0 else spot + step + 1
            arrive(step, place)
            if isinstance(step, int) and step + 1 >= lines - 1:
                continue
            pl.when(jnp.logical_and(goes(step + 1, where), step + 1 < lines - 1))(
                lambda where=where: going(step + 1, where).start()
            )

    def arrived():
        pltpu.make_async_copy(own, out.at[me], local).wait()

        @pl.loop(0, lines)
        def _(place):
            there = 2 * place + 1 - side
            remote(out.at[there], out.at[there], over_s.at[place], landed.at[there], "dp", across).wait_recv()

    def last():
        pl.loop(0, lines)(lambda place: over(place).wait_send())

        @pl.loop(0, lines - 1)
        def _(step):
            for where in (0, 1):
                pl.when(goes(step, where))(lambda where=where: going(step, where).wait_send())

    return first, hop_step, arrived, last


def greet(lines, count):
    barrier = pltpu.get_barrier_semaphore()
    me = lax.axis_index("dp")
    spot, across = me // 2, me + 1 - 2 * (me % 2)

    def tell(axis, to):
        pl.semaphore_signal(barrier, 1, device_id={axis: to}, device_id_type=MESH)

    tell("dp", across)
    pl.when(spot >= 1)(lambda: tell("dp", me - 2))
    pl.when(spot + 1 < lines)(lambda: tell("dp", me + 2))
    head = lax.axis_index("head")
    tell("head", head + 1 - 2 * (head % 2))
    for f in range(1, count // 2):
        tell("head", lax.rem(head + 2 * f, count))
    beside = jnp.minimum(spot, 1) + jnp.minimum(lines - 1 - spot, 1)
    pl.semaphore_wait(barrier, 1 + count // 2 + beside)


def greet_line(lines, count):
    barrier = pltpu.get_barrier_semaphore()
    head = lax.axis_index("head")
    for to in [head + 1 - 2 * (head % 2)] + [lax.rem(head + hop, count) for hop in range(2, count, 2)]:
        pl.semaphore_signal(barrier, 1, device_id={"head": to}, device_id_type=MESH)
    me = lax.axis_index("dp")

    def tell(to):
        pl.semaphore_signal(barrier, 1, device_id={"dp": to}, device_id_type=MESH)

    tell(me + 1 - 2 * (me % 2))
    pl.loop(1, lines)(lambda hop: tell(lax.rem(me + 2 * hop, 2 * lines)))
    pl.semaphore_wait(barrier, lines + count // 2)


def cot_gather(count, cot_ref, cot_rows, sems, held_s):
    parts = sems[1].shape[0]
    size = cot_ref.shape[0] // parts
    at = lambda p: pl.ds(p * size, size)
    me = lax.axis_index("head")
    cots = HeadGather(count, parts, lambda p: cot_ref.at[at(p)], lambda owner, p: cot_rows.at[owner, at(p)], sems)
    return cots, pltpu.make_async_copy(cot_ref, cot_rows.at[me], held_s)


def start_kernel(lines, count, parts, tok_ref, gain_ref, out_w, *refs):
    *in_ws, cot_ref, rows_ref, wall_ref, cot_rows, mine, w_ref = refs[:11]
    start_body(
        lines, count, parts, tok_ref, gain_ref, out_w, in_ws, cot_ref, rows_ref, wall_ref, cot_rows, mine, w_ref, *refs[11:]
    )


def start_body(lines, count, parts, tok_ref, gain_ref, out_w, in_ws, cot_ref, rows_ref, wall_ref, cot_rows, mine, w_ref,
               right_s, left_s, over_s, landed, local, far_s, pair_s, fwd_s, got, keep_s, *cot_sems):
    first, hop_step, arrived, last = shard_line(lines, w_ref, wall_ref, (right_s, left_s, over_s, landed, local.at[0]))
    at = out_w.shape[0]
    w_ref[:, :at] = out_w[...].T
    for w in in_ws:
        w_ref[:, at : at + w.shape[1]] = w[...]
        at += w.shape[1]
    greet(lines, count)
    first()
    me = lax.axis_index("head")
    pair = me + 1 - 2 * (me % 2)
    fars = [lax.rem(me + 2 * f, count) for f in range(1, count // 2)]
    size = tok_ref.shape[0] // parts
    span = lambda p: pl.ds(p * size, size)

    def block(owner, p):
        return rows_ref.at[owner, span(p)]

    for p in range(parts):
        x = tok_ref[p * size : (p + 1) * size, :].astype(F32)
        inv = lax.rsqrt(jnp.mean(x * x, axis=-1, keepdims=True) + 1e-6)
        mine[p * size : (p + 1) * size, :] = (x * inv * gain_ref[...]).astype(BF16)
        for f, far in enumerate(fars):
            remote(mine.at[span(p)], block(me, p), far_s.at[f, p], got.at[me, p], "head", far).start()
        remote(mine.at[span(p)], block(me, p), pair_s.at[p], got.at[me, p], "head", pair).start()
        pltpu.make_async_copy(mine.at[span(p)], block(me, p), keep_s.at[p]).start()

    cot_half = cot_ref.shape[0] // 2
    cots, held = cot_gather(count, cot_ref.at[pl.ds(0, cot_half)], cot_rows, cot_sems, local.at[1])
    held.start()
    for p in range(cots.parts):
        cots.send(p)

    def pass_on(p):
        for f, far in enumerate(fars):
            moved = remote(block(far, p), block(far, p), fwd_s.at[f, p], got.at[far, p], "head", pair)
            moved.wait_recv()
            moved.start()

    for i in range(parts):
        pass_on(i)
        if i < lines - 1:
            hop_step(i)
    if lines - 1 > parts:
        pl.loop(parts, lines - 1)(hop_step)
    for p in range(cots.parts):
        cots.pass_on(p)
    arrived()
    last()
    held.wait()
    for p in range(cots.parts):
        cots.arrive(p)
        cots.sent(p)
    for p in range(parts):
        remote(mine.at[span(p)], block(pair, p), pair_s.at[p], got.at[pair, p], "head", pair).wait()
        pltpu.make_async_copy(mine.at[span(p)], block(me, p), keep_s.at[p]).wait()
        for f, far in enumerate(fars):
            remote(mine.at[span(p)], block(me, p), far_s.at[f, p], got.at[me, p], "head", far).wait_send()
            there = lax.rem(pair + 2 * (f + 1), count)
            remote(block(far, p), block(there, p), fwd_s.at[f, p], got.at[there, p], "head", pair).wait()


def start(tokens, gain, w_out, in_ws, cot, n_dp, n_head, parts=4):
    rows, width = tokens.shape
    shard = (in_ws[0].shape[0], w_out.shape[0] + sum(w.shape[1] for w in in_ws))
    lines, far = n_dp // 2, n_head // 2 - 1
    dma = lambda *shape: pltpu.SemaphoreType.DMA(shape)
    anywhere = pl.BlockSpec(memory_space=pl.ANY)
    vmem = pl.BlockSpec(memory_space=pltpu.VMEM)
    return pl.pallas_call(
        partial(start_kernel, lines, n_head, parts),
        out_shape=[jax.ShapeDtypeStruct((n_head, rows, width), BF16),
                   jax.ShapeDtypeStruct((n_dp, *shard), BF16),
                   jax.ShapeDtypeStruct((n_head, cot.shape[0] // 2, cot.shape[1]), BF16)],
        in_specs=[vmem] * (4 + len(in_ws)),
        out_specs=[anywhere] * 3,
        scratch_shapes=[
            pltpu.VMEM((rows, width), BF16),
            pltpu.VMEM(shard, BF16),
            dma(lines), dma(lines), dma(lines), dma(n_dp), dma(2),
            dma(far, parts), dma(parts), dma(far, parts), dma(n_head, parts), dma(parts),
        ]
        + HeadGather.scratch(n_head, COT_PARTS),
        compiler_params=pltpu.CompilerParams(vmem_limit_bytes=VMEM_LIMIT, has_side_effects=True, collective_id=0),
        name="start",
    )(tokens, gain, w_out, *in_ws, cot)


def when(condition):
    return pl.when(condition) if not isinstance(condition, bool) else (lambda f: f() if condition else None)


class HeadScatter:
    def __init__(self, count, refs):
        self.count = count
        (self.out, self.near, self.onward, self.far, self.own,
         self.out_s, self.near_r, self.onward_s, self.far_r) = refs
        self.me = lax.axis_index("head")
        self.side, self.place = self.me % 2, self.me // 2
        self.pair = self.me + 1 - 2 * self.side
        self.parts, self.depth, self.size = self.near.shape[0], self.own.shape[0], self.own.shape[1]

    @staticmethod
    def scratch(count, parts, size, width, depth):
        half = count // 2
        return [
            pltpu.VMEM((2, 2, half, size, width), BF16),
            pltpu.VMEM((parts, half, size, width), BF16),
            pltpu.VMEM((2, half - 1, size, width), BF16),
            pltpu.VMEM((parts, half - 1, size, width), BF16),
            pltpu.VMEM((depth, size, width), F32),
            pltpu.SemaphoreType.DMA((2,)),
            pltpu.SemaphoreType.DMA((parts,)),
            pltpu.SemaphoreType.DMA((2, half - 1)),
            pltpu.SemaphoreType.DMA((parts, half - 1)),
        ]

    def _near(self, p):
        slot = p % 2
        return remote(self.out.at[slot, 1 - self.side], self.near.at[p], self.out_s.at[slot], self.near_r.at[p], "head", self.pair)

    def _far(self, p, f):
        slot = p % 2
        to = lax.rem(self.me + 2 * (f + 1), self.count)
        return remote(self.onward.at[slot, f], self.far.at[p, f], self.onward_s.at[slot, f], self.far_r.at[p, f], "head", to)

    def offer(self, p, total):
        when(p >= 2)(lambda: self._near(p - 2).wait_send())
        for owner in range(self.count):
            self.out[p % 2, owner % 2, owner // 2] = total[owner * self.size : (owner + 1) * self.size].astype(BF16)
        self._near(p).start()

    def turn(self, p):
        slot, half = p % 2, self.count // 2
        self._near(p).wait_recv()
        both = lambda i: self.out[slot, self.side, i].astype(F32) + self.near[p, i].astype(F32)
        for f in range(half - 1):
            when(p >= 2)(lambda f=f: self._far(p - 2, f).wait_send())
            self.onward[slot, f] = both(lax.rem(self.place + f + 1, half)).astype(BF16)
            self._far(p, f).start()
        self.own[p % self.depth] = both(self.place)

    def take(self, p):
        total = self.own[p % self.depth]
        for f in range(self.count // 2 - 1):
            self._far(p, f).wait_recv()
            total = total + self.far[p, f].astype(F32)
        return total

    def close(self):
        for p in range(max(self.parts - 2, 0), self.parts):
            self._near(p).wait_send()
            for f in range(self.count // 2 - 1):
                self._far(p, f).wait_send()


class OwnerScatter:
    def __init__(self, count, out_ref, refs):
        self.count, self.out_ref = count, out_ref
        self.terms, self.near, self.far, self.near_s, self.near_r, self.far_s, self.far_r = refs
        self.me = lax.axis_index("head")
        self.side = self.me % 2
        self.pair = self.me + 1 - 2 * self.side

    @staticmethod
    def scratch(count, rows, width):
        half = count // 2
        sems = lambda n: pltpu.SemaphoreType.DMA((n,))
        return [
            pltpu.VMEM((count, rows, width), BF16),
            pltpu.VMEM((half, rows, width), BF16),
            pltpu.VMEM((half - 1, rows, width), BF16),
            sems(half), sems(half), sems(count), sems(half - 1),
        ]

    def _near(self, owner):
        at = owner // 2
        return remote(self.terms.at[owner], self.near.at[at], self.near_s.at[at], self.near_r.at[at], "head", self.pair)

    def _far(self, owner):
        at = lax.rem(self.me - owner + self.count, self.count) // 2 - 1
        return remote(self.terms.at[owner], self.far.at[at], self.far_s.at[owner], self.far_r.at[at], "head", owner)

    def _mine(self, owner):
        return owner % 2 == self.side

    def offer(self, owner, total):
        self.terms[owner] = total.astype(BF16)
        pl.when(jnp.logical_not(self._mine(owner)))(lambda: self._near(owner).start())

    def settle(self, owner):
        @pl.when(self._mine(owner))
        def _():
            self._near(owner).wait_recv()
            both = self.terms[owner].astype(F32) + self.near[owner // 2].astype(F32)

            @pl.when(owner == self.me)
            def _():
                self.out_ref[...] = both

            @pl.when(owner != self.me)
            def _():
                self.terms[owner] = both.astype(BF16)
                self._far(owner).start()

    def finish(self):
        for f in range(self.count // 2 - 1):
            sender = lax.rem(self.me + 2 * (f + 1), self.count)
            remote(self.terms.at[0], self.far.at[f], self.far_s.at[0], self.far_r.at[f], "head", sender).wait_recv()
            self.out_ref[...] += self.far[f].astype(F32)

        @pl.loop(0, self.count)
        def _(owner):
            pl.when(jnp.logical_not(self._mine(owner)))(lambda: self._near(owner).wait_send())
            pl.when(jnp.logical_and(self._mine(owner), owner != self.me))(lambda: self._far(owner).wait_send())


class HeadGather:
    def __init__(self, count, parts, own, block, refs, takes=None):
        self.count, self.parts, self.own, self.block, self.takes = count, parts, own, block, takes
        self.far_s, self.pair_s, self.fwd_s, self.got = refs
        self.me = lax.axis_index("head")
        self.pair = self.me + 1 - 2 * (self.me % 2)

    @staticmethod
    def scratch(count, parts):
        far = count // 2 - 1
        return [pltpu.SemaphoreType.DMA(s) for s in ((far, parts), (parts,), (far, parts), (count, parts))]

    def _if(self, owner, action):
        pl.when(self.takes(owner))(action) if self.takes else action()

    def _fars(self, base):
        return [(f, lax.rem(base + 2 * (f + 1), self.count)) for f in range(self.count // 2 - 1)]

    def _far(self, p, f, far):
        return remote(self.own(p), self.block(self.me, p), self.far_s.at[f, p], self.got.at[self.me, p], "head", far)

    def _pair(self, p):
        return remote(self.own(p), self.block(self.me, p), self.pair_s.at[p], self.got.at[self.me, p], "head", self.pair)

    def _on(self, p, f, owner):
        return remote(self.block(owner, p), self.block(owner, p), self.fwd_s.at[f, p], self.got.at[owner, p], "head", self.pair)

    def send(self, p):
        def act():
            for f, far in self._fars(self.me):
                self._far(p, f, far).start()
            self._pair(p).start()

        self._if(self.me, act)

    def pass_on(self, p, ready=None):
        for f, far in self._fars(self.me):

            def act(f=f, far=far):
                self._on(p, f, far).wait_recv()
                self._on(p, f, far).start()

            pl.when(far == ready)(act) if ready is not None else self._if(far, act)

    def arrive(self, p, ready=None):
        def near():
            remote(self.own(p), self.block(self.pair, p), self.pair_s.at[p], self.got.at[self.pair, p], "head", self.pair).wait_recv()

        pl.when(self.pair == ready)(near) if ready is not None else self._if(self.pair, near)
        for f, far in self._fars(self.pair):
            act = lambda f=f, far=far: self._on(p, f, far).wait_recv()
            pl.when(far == ready)(act) if ready is not None else self._if(far, act)

    def sent(self, p):
        def mine():
            self._pair(p).wait_send()
            for f, far in self._fars(self.me):
                self._far(p, f, far).wait_send()

        self._if(self.me, mine)
        for f, far in self._fars(self.me):
            self._if(far, lambda f=f, far=far: self._on(p, f, far).wait_send())


LEAD = 8


def mid_kernel(lines, count, parts, att_ref, tok_ref, gain_ref, cot_early, cot_late, ff_ref, down_mine,
               out_ref, grad_ref, hg_ref, gain_grad_ref, terms_ref, down_terms_ref, *scratch):
    scratch = list(scratch)
    take = lambda n: [scratch.pop(0) for _ in range(n)]
    down_refs, back_refs = take(9), take(9)
    second_sems, hg_sems = take(4), take(4)
    cot_ref, second, hidden, hg_own, total, loads, keep_s, down_all, right_s, left_s, over_s, landed = scratch
    size, width = tok_ref.shape[1:]
    ff = ff_ref.shape[1] // 2
    me = lax.axis_index("head")
    greet(lines, count)
    first, hop_step, arrived, last = shard_line(
        lines, down_mine, down_all, (right_s, left_s, over_s, landed, loads.at[1])
    )
    first()
    half = parts // 2
    loading = [
        pltpu.make_async_copy(src, cot_ref.at[:, at : at + half], loads.at[i])
        for i, (src, at) in ((0, (cot_early, 0)), (2, (cot_late, half)))
    ]
    for m in loading:
        m.start()
    down_w = lambda: down_all[...].reshape(-1, ff)
    down, back = (HeadScatter(count, r) for r in (down_refs, back_refs))
    here = lambda owner, p: second.at[p, owner]
    seconds = HeadGather(count, parts, lambda p: here(me, p), here, second_sems)
    there = lambda owner, p: hg_ref.at[owner, p]
    hgs = HeadGather(count, parts, lambda p: hg_own.at[p], there, hg_sems, lambda owner: owner == count - 1)
    keep = lambda p: pltpu.make_async_copy(hg_own.at[p], there(me, p), keep_s.at[p])
    total[...] = jnp.zeros_like(total)
    gain_grad_ref[...] = jnp.zeros_like(gain_grad_ref)

    def within(p, stage):
        pl.when(jnp.logical_and(p >= 0, p < parts))(lambda: stage(p))

    def norm(p):
        rows = tok_ref[p].astype(F32) + att_ref[p]
        hidden[p] = rows
        inv = lax.rsqrt(jnp.mean(rows * rows, axis=-1, keepdims=True) + 1e-6)
        second[p, me] = (rows * inv * gain_ref[...]).astype(BF16)
        seconds.send(p)

    def feed(p):
        seconds.arrive(p)
        rows = second[p].reshape(count * size, width)
        both = dot(rows, ff_ref[...], ((1,), (0,)))
        gate, up = both[:, :ff], both[:, ff:]
        sig = jax.nn.sigmoid(gate)
        act = gate * sig
        middle = (act * up).astype(BF16)

        @pl.when(p == 0)
        def _():
            hop_step(0)
            pl.loop(1, lines - 1)(hop_step)
            arrived()

        down.offer(p, dot(middle, down_w(), ((1,), (1,))))
        cot = cot_ref[:, p].reshape(count * size, width)
        grad = dot(cot, down_w(), ((1,), (0,))).astype(BF16).astype(F32)
        pair = jnp.concatenate(
            [(grad * up * sig * (1.0 + gate * (1.0 - sig))).astype(BF16), (grad * act).astype(BF16)], axis=1
        )
        back.offer(p, dot(pair, ff_ref[...], ((1,), (1,))))
        total[:, : 2 * ff] += dot(rows, pair, ((0,), (0,)))
        total[:, 2 * ff :] += dot(cot, middle, ((0,), (0,)))

    def turn(p):
        down.turn(p)
        back.turn(p)

    def finish(p):
        rows = hidden[p]
        out_ref[p] = (rows + down.take(p)).astype(BF16)
        second_grad = back.take(p).astype(BF16).astype(F32)
        inv = lax.rsqrt(jnp.mean(rows * rows, axis=-1, keepdims=True) + 1e-6)
        scaled = second_grad * gain_ref[...]
        mean = jnp.mean(scaled * rows, axis=-1, keepdims=True)
        grad = cot_ref[me, p].astype(F32) + inv * scaled - rows * (inv * inv * inv * mean)
        grad_ref[p] = grad
        gain_grad_ref[...] += jnp.sum(second_grad * rows * inv, axis=0, keepdims=True)
        hg_own[p] = grad.astype(BF16)
        hgs.send(p)
        keep(p).start()

    for p in range(LEAD):
        norm(p)
    for m in loading:
        m.wait()

    @pl.loop(0, parts + 2)
    def _(step):
        within(step + LEAD, norm)
        within(step, seconds.pass_on)
        within(step, feed)
        within(step, turn)
        within(step - 1, finish)
        within(step - 2, hgs.pass_on)

    terms_ref[...] = total[:, : 2 * ff].astype(BF16)
    down_terms_ref[...] = total[:, 2 * ff :].astype(BF16)

    @pl.loop(0, parts)
    def _(p):
        hgs.arrive(p)
        keep(p).wait()
        hgs.sent(p)
        seconds.sent(p)

    for s in (down, back):
        s.close()
    last()


def mid(attention, tokens, gain, cot_early, cot_late, ff_set, down_mine, n_dp, count, parts=8):
    rows, width = tokens.shape
    lines, ff = n_dp // 2, down_mine.shape[1]
    dma = lambda *shape: pltpu.SemaphoreType.DMA(shape)
    size = rows // parts
    anywhere = pl.BlockSpec(memory_space=pl.ANY)
    vmem = pl.BlockSpec(memory_space=pltpu.VMEM)
    scatter = HeadScatter.scratch(count, parts, size, width, 2)
    out, grad, hg, gain_grad, terms, down_terms = pl.pallas_call(
        partial(mid_kernel, lines, count, parts),
        out_shape=[
            jax.ShapeDtypeStruct((parts, size, width), BF16),
            jax.ShapeDtypeStruct((parts, size, width), F32),
            jax.ShapeDtypeStruct((count, parts, size, width), BF16),
            jax.ShapeDtypeStruct((1, width), F32),
            jax.ShapeDtypeStruct((width, 2 * ff), BF16),
            jax.ShapeDtypeStruct((width, ff), BF16),
        ],
        in_specs=[vmem] * 3 + [anywhere] * 2 + [vmem] * 2,
        out_specs=[vmem, vmem, anywhere, vmem, vmem, vmem],
        scratch_shapes=scatter * 2
        + HeadGather.scratch(count, parts) * 2
        + [
            pltpu.VMEM((count, parts, size, width), BF16),
            pltpu.VMEM((parts, count, size, width), BF16),
            pltpu.VMEM((parts, size, width), F32),
            pltpu.VMEM((parts, size, width), BF16),
            pltpu.VMEM((width, 3 * ff), F32),
            dma(3),
            dma(parts),
            pltpu.VMEM((n_dp, *down_mine.shape), BF16),
            dma(lines), dma(lines), dma(lines), dma(n_dp),
        ],
        compiler_params=pltpu.CompilerParams(vmem_limit_bytes=61 * 1024 * 1024, has_side_effects=True, collective_id=2),
        name="mid",
    )(
        attention.reshape(parts, size, width), tokens.reshape(parts, size, width), gain,
        *(c.reshape(count, parts // 2, size, width) for c in (cot_early, cot_late)), ff_set, down_mine,
    )
    return out.reshape(rows, width), grad.reshape(rows, width), hg.reshape(count, rows, width), gain_grad, terms, down_terms


class ChainScatter:
    LAG = 2

    def __init__(self, lines, terms, own, refs, by_piece):
        self.lines, self.terms, self.own, self.by_piece = lines, terms, own, by_piece
        self.cross, self.going, self.coming, self.cross_s, self.cross_r, self.go_s, self.come_r = refs
        self.pieces = self.cross_s.shape[1]
        self.size = self.cross.shape[1] // self.pieces
        self.me = lax.axis_index("dp")
        self.spot, self.side = self.me // 2, self.me % 2
        self.across = self.me + 1 - 2 * self.side
        self.items = (lines - 1) * self.pieces
        self.points = self.items + (lines - 1) * self.LAG

    @staticmethod
    def scratch(lines, rows, width):
        pieces = max(1, rows // 32)
        wide = lambda *lead: pltpu.VMEM((*lead, rows, width), BF16)
        sems = lambda *shape: pltpu.SemaphoreType.DMA((*shape, pieces))
        return [
            wide(lines), wide(2, lines), wide(2, lines),
            sems(lines), sems(lines), sems(2, lines), sems(2, lines),
        ]

    def _at(self, k):
        return pl.ds(pl.multiple_of(k * self.size, self.size), self.size)

    def _cross(self, place, k):
        at = self._at(k)
        src = self.terms(2 * place + 1 - self.side).at[at]
        return remote(src, self.cross.at[place, at], self.cross_s.at[place, k], self.cross_r.at[place, k], "dp", self.across)

    def _line(self, way, dest, k):
        to = self.me + 2 if way == 0 else self.me - 2
        at = self._at(k)
        return remote(self.going.at[way, dest, at], self.coming.at[way, dest, at], self.go_s.at[way, dest, k], self.come_r.at[way, dest, k], "dp", to)

    def offer(self, place, k):
        self._cross(place, k).start()

    def offer_all(self):
        for k in range(self.pieces):
            for d in range((self.lines + 1) // 2):
                for place in sorted({self.lines - 1 - d, d}, reverse=True):
                    self.offer(place, k)

    def _both(self, place, k):
        return self.own(place)[self._at(k), :].astype(F32) + self.cross[place, self._at(k), :].astype(F32)

    def _passes(self, way, dest):
        return dest > self.spot if way == 0 else dest < self.spot

    def _fed(self, way):
        return self.spot >= 1 if way == 0 else self.spot + 1 < self.lines

    def point(self, n):
        for way in (0, 1):
            away = self.spot if way == 0 else self.lines - 1 - self.spot
            item = n - away * self.LAG
            safe = jnp.clip(item, 0, self.items - 1)
            if self.by_piece:
                k, d = safe // (self.lines - 1), safe % (self.lines - 1)
            else:
                d, k = safe // self.pieces, safe % self.pieces
            dest = self.lines - 1 - d if way == 0 else d
            live = jnp.logical_and(item >= 0, item < self.items)

            @pl.when(jnp.logical_and(live, self._passes(way, dest)))
            def _(way=way, dest=dest, k=k):
                at = self._at(k)
                self._cross(dest, k).wait_recv()

                @pl.when(self._fed(way))
                def _():
                    self._line(way, dest, k).wait_recv()
                    self.going[way, dest, at, :] = (self._both(dest, k) + self.coming[way, dest, at, :].astype(F32)).astype(BF16)

                @pl.when(jnp.logical_not(self._fed(way)))
                def _():
                    self.going[way, dest, at, :] = self._both(dest, k).astype(BF16)

                self._line(way, dest, k).start()

    def finish(self, out_ref):
        for k in range(self.pieces):
            at = slice(k * self.size, (k + 1) * self.size)
            self._cross(self.spot, k).wait_recv()
            out_ref[at, :] = self._both(self.spot, k)
            for way in (0, 1):
                @pl.when(self._fed(way))
                def _(way=way, k=k, at=at):
                    self._line(way, self.spot, k).wait_recv()
                    out_ref[at, :] += self.coming[way, self.spot, at, :].astype(F32)

    def close(self):
        @pl.loop(0, self.lines * self.pieces)
        def _(i):
            place, k = i // self.pieces, i % self.pieces
            self._cross(place, k).wait_send()
            for way in (0, 1):
                pl.when(self._passes(way, place))(lambda way=way: self._line(way, place, k).wait_send())


class LineScatter:
    def __init__(self, lines, terms, own, refs, order):
        self.lines, self.terms, self.own, self.order = lines, terms, own, order
        self.cross, self.going, self.coming, self.cross_s, self.cross_r, self.go_s, self.come_r = refs
        self.pieces = self.cross_s.shape[1]
        self.size = self.cross.shape[1] // self.pieces
        self.me = lax.axis_index("dp")
        self.spot, self.side = self.me // 2, self.me % 2
        self.across = self.me + 1 - 2 * self.side
        self.points = lines * self.pieces

    @staticmethod
    def scratch(lines, rows, width):
        pieces = max(1, rows // 32)
        wide = pltpu.VMEM((lines, rows, width), BF16)
        sems = pltpu.SemaphoreType.DMA((lines, pieces))
        return [wide, wide, wide, sems, sems, sems, sems]

    def _at(self, k):
        return pl.ds(pl.multiple_of(k * self.size, self.size), self.size)

    def _cross(self, place, k):
        at = self._at(k)
        src = self.terms(2 * place + 1 - self.side).at[at]
        return remote(src, self.cross.at[place, at], self.cross_s.at[place, k], self.cross_r.at[place, k], "dp", self.across)

    def _on(self, sender, dest, k):
        at = self._at(k)
        return remote(self.going.at[dest, at], self.coming.at[sender, at], self.go_s.at[dest, k], self.come_r.at[sender, k], "dp", 2 * dest + self.side)

    def offer(self, place, k):
        self._cross(place, k).start()

    def offer_all(self):
        @pl.loop(0, self.points)
        def _(n):
            k, place = self.order(n)
            self.offer(place, k)

    def _both(self, place, k):
        return self.own(place)[self._at(k), :].astype(F32) + self.cross[place, self._at(k), :].astype(F32)

    def point(self, n):
        k, dest = self.order(jnp.clip(n, 0, self.points - 1))

        @pl.when(jnp.logical_and(jnp.logical_and(n >= 0, n < self.points), dest != self.spot))
        def _():
            self._cross(dest, k).wait_recv()
            self.going[dest, self._at(k), :] = self._both(dest, k).astype(BF16)
            self._on(self.spot, dest, k).start()

    def finish(self, out_ref):
        for k in range(self.pieces):
            at = slice(k * self.size, (k + 1) * self.size)
            self._cross(self.spot, k).wait_recv()
            out_ref[at, :] = self._both(self.spot, k)

            @pl.loop(1, self.lines)
            def _(hop, k=k, at=at):
                sender = lax.rem(self.spot + hop, self.lines)
                self._on(sender, self.spot, k).wait_recv()
                out_ref[at, :] += self.coming[sender, at, :].astype(F32)

    def close(self):
        @pl.loop(0, self.points)
        def _(i):
            place, k = i // self.pieces, i % self.pieces
            self._cross(place, k).wait_send()
            pl.when(place != self.spot)(lambda: self._on(self.spot, place, k).wait_send())


def outside_in(lines, i):
    return jnp.where(i % 2 == 0, lines - 1 - i // 2, i // 2)


class SmallSum:
    def __init__(self, n_dp, count, shared, refs):
        self.n_dp, self.count, self.shared = n_dp, count, shared
        self.mine, self.theirs, self.half, self.halves, self.a_s, self.a_r, self.b_s, self.b_r = refs
        self.dp, self.head = lax.axis_index("dp"), lax.axis_index("head")

    @staticmethod
    def scratch(n_dp, count, rows, shared):
        return [
            pltpu.VMEM((rows, 128), F32),
            pltpu.VMEM((n_dp, rows, 128), F32),
            pltpu.VMEM((shared, 128), F32),
            pltpu.VMEM((count, shared, 128), F32),
            pltpu.SemaphoreType.DMA((n_dp,)),
            pltpu.SemaphoreType.DMA((n_dp,)),
            pltpu.SemaphoreType.DMA((count,)),
            pltpu.SemaphoreType.DMA((count,)),
        ]

    def _a(self, hop):
        to = lax.rem(self.dp + hop, self.n_dp)
        return remote(self.mine, self.theirs.at[self.dp], self.a_s.at[hop], self.a_r.at[self.dp], "dp", to)

    def _b(self, hop):
        to = lax.rem(self.head + hop, self.count)
        return remote(self.half, self.halves.at[self.head], self.b_s.at[hop], self.b_r.at[self.head], "head", to)

    def start(self):
        self.theirs[self.dp] = self.mine[...]

        @pl.loop(1, self.n_dp)
        def _(hop):
            self._a(hop).start()

    def turn(self, out_ref):
        @pl.loop(1, self.n_dp)
        def _(hop):
            sender = lax.rem(self.dp + self.n_dp - hop, self.n_dp)
            remote(self.mine, self.theirs.at[sender], self.a_s.at[hop], self.a_r.at[sender], "dp", sender).wait_recv()

        total = self.theirs[0]
        for i in range(1, self.n_dp):
            total = total + self.theirs[i]
        out_ref[...] = total
        self.half[...] = total[: self.shared]
        self.halves[self.head] = total[: self.shared]
        for hop in range(1, self.count):
            self._b(hop).start()

    def finish(self, out_ref):
        for hop in range(1, self.count):
            sender = lax.rem(self.head + self.count - hop, self.count)
            remote(self.half, self.halves.at[sender], self.b_s.at[hop], self.b_r.at[sender], "head", sender).wait_recv()
        total = self.halves[0]
        for i in range(1, self.count):
            total = total + self.halves[i]
        out_ref[: self.shared, :] = total

        @pl.loop(1, self.n_dp)
        def _(hop):
            self._a(hop).wait_send()

        for hop in range(1, self.count):
            self._b(hop).wait_send()


def greet_all(n_dp, count):
    barrier = pltpu.get_barrier_semaphore()
    dp, head = lax.axis_index("dp"), lax.axis_index("head")

    @pl.loop(1, n_dp)
    def _(hop):
        pl.semaphore_signal(barrier, 1, device_id={"dp": lax.rem(dp + hop, n_dp)}, device_id_type=MESH)

    for hop in range(1, count):
        pl.semaphore_signal(barrier, 1, device_id={"head": lax.rem(head + hop, count)}, device_id_type=MESH)
    pl.semaphore_wait(barrier, n_dp + count - 2)


def end_kernel(n_dp, count, parts, shared,
               dpre_ref, w_ref, normed_ref, hg_ref, mixed_ref, down_ref, tok_ref, gain_ref, grad_ref, small_ref,
               in_ref, mix_ref, sum_ref, down_sum_ref, *scratch):
    scratch = list(scratch)
    take = lambda n: [scratch.pop(0) for _ in range(n)]
    head_refs, dp_refs, down_refs, small_refs = take(9), take(7), take(7), take(8)
    terms, dpre, w, normed, hg, mixed, down_own, loads, down_s = scratch
    rows, width = tok_ref.shape
    block = terms.shape[1]
    hid = mixed.shape[1]
    greet_all(n_dp, count)
    lines = n_dp // 2
    side = lax.axis_index("dp") % 2
    down = ChainScatter(lines, lambda j: down_ref.at[j], lambda place: down_own.at[place], down_refs, True)
    fetch = lambda place: pltpu.make_async_copy(down_ref.at[2 * place + side], down_own.at[place], down_s.at[place])
    moves = [pltpu.make_async_copy(s, d, loads.at[i]) for i, (s, d) in enumerate(
        ((dpre_ref, dpre), (w_ref.at[:, hid:], w), (normed_ref, normed), (mixed_ref, mixed), (hg_ref, hg)))]
    for m in moves:
        m.start()
    down.offer_all()
    for place in range(lines):
        fetch(place).start()
    heads = HeadScatter(count, head_refs)
    line = ChainScatter(lines, lambda j: terms.at[j], lambda place: terms.at[2 * place + side], dp_refs, False)
    small = SmallSum(n_dp, count, shared, small_refs)
    size = rows // parts

    def offer(p):
        part = jnp.concatenate([dpre[o * rows + p * size : o * rows + (p + 1) * size, :] for o in range(count)], axis=0)
        heads.offer(p, dot(part, w[...], ((1,), (1,))))

    tiles = width // 256
    per = 256 // block

    def outer(t):
        cols = slice(t * 256, (t + 1) * 256)
        left = dot(normed[:, cols], dpre[...], ((0,), (0,))).astype(BF16)
        right = dot(hg[:, cols], mixed[...], ((0,), (0,))).astype(BF16)
        for b in range(per):
            terms[t * per + b, :, :hid] = right[b * block : (b + 1) * block]
            terms[t * per + b, :, hid:] = left[b * block : (b + 1) * block]
        for place in range(t * per // 2, (t + 1) * per // 2):
            for k in range(line.pieces):
                line.offer(place, k)

    order = [t // 2 if t % 2 else tiles - 1 - t // 2 for t in range(tiles)]
    moves[0].wait()
    moves[1].wait()
    offer(0)
    for m in moves[2:]:
        m.wait()
    for place in range(lines):
        fetch(place).wait()
    down_done = 0
    for i in range(max(tiles, parts)):
        if i < tiles:
            outer(order[i])
        if i < parts:
            heads.turn(i)
        if i + 1 < parts:
            offer(i + 1)
        for n in range(4):
            if down_done < down.points:
                down.point(down_done)
                down_done += 1
    pl.loop(down_done, down.points)(down.point)
    small.mine[...] = small_ref[...]
    gain_total = jnp.zeros((1, width), F32)
    gain = gain_ref[...]

    def finish(p):
        at = slice(p * size, (p + 1) * size)
        normed_grad = heads.take(p).astype(BF16).astype(F32)
        x = tok_ref[at, :].astype(F32)
        inv = lax.rsqrt(jnp.mean(x * x, axis=-1, keepdims=True) + 1e-6)
        scaled = normed_grad * gain
        mean = jnp.mean(scaled * x, axis=-1, keepdims=True)
        in_ref[at, :] = grad_ref[at, :] + inv * scaled - x * (inv * inv * inv * mean)
        return jnp.sum(normed_grad * x * inv, axis=0, keepdims=True)

    done = 0
    for i in range(parts):
        for n in range(2):
            if done < line.points:
                line.point(done)
                done += 1
        gain_total = gain_total + finish(i)
    for i in range(width // 128):
        small.mine[i : i + 1, :] = gain_total[:, i * 128 : (i + 1) * 128]
    small.start()
    half = (done + line.points) // 2
    pl.loop(done, half)(line.point)
    small.turn(sum_ref)
    pl.loop(half, line.points)(line.point)
    line.finish(mix_ref)
    down.finish(down_sum_ref)
    small.finish(sum_ref)
    down.close()
    heads.close()
    line.close()


def end(dpre, weights, normed_rows, hg_rows, mixed, down_terms, tokens, gain, hidden_grad, small, n_dp, count, shared, parts=4):
    rows, width = tokens.shape
    block = width // n_dp
    wide = weights.shape[1]
    anywhere = pl.BlockSpec(memory_space=pl.ANY)
    vmem = pl.BlockSpec(memory_space=pltpu.VMEM)
    like = lambda a: pltpu.VMEM(a.shape, a.dtype)
    return pl.pallas_call(
        partial(end_kernel, n_dp, count, parts, shared),
        out_shape=[
            jax.ShapeDtypeStruct((rows, width), F32),
            jax.ShapeDtypeStruct((block, wide), F32),
            jax.ShapeDtypeStruct(small.shape, F32),
            jax.ShapeDtypeStruct(down_terms.shape[1:], F32),
        ],
        in_specs=[anywhere] * 6 + [vmem] * 4,
        out_specs=[vmem] * 4,
        scratch_shapes=HeadScatter.scratch(count, parts, rows // parts, width, parts)
        + ChainScatter.scratch(n_dp // 2, block, wide)
        + ChainScatter.scratch(n_dp // 2, block, down_terms.shape[2])
        + SmallSum.scratch(n_dp, count, small.shape[0], shared)
        + [pltpu.VMEM((n_dp, block, wide), BF16), like(dpre), pltpu.VMEM((width, dpre.shape[1]), BF16), like(normed_rows), like(hg_rows), like(mixed),
           pltpu.VMEM((n_dp // 2, *down_terms.shape[1:]), BF16),
           pltpu.SemaphoreType.DMA((5,)), pltpu.SemaphoreType.DMA((n_dp // 2,))],
        compiler_params=pltpu.CompilerParams(vmem_limit_bytes=VMEM_LIMIT, has_side_effects=True, collective_id=1),
        name="end",
    )(dpre, weights, normed_rows, hg_rows, mixed, down_terms, tokens, gain, hidden_grad, small)


def spread_kernel(out_ref, in_ref, mix_ref, ff_ref, down_ref, out_to, in_to, *results):
    to_out, *mixes, beta, ff_gate, ff_up, ff_down = results
    hid, heads, ff = to_out.shape[0], beta.shape[0], ff_gate.shape[0]
    wide = down_ref.shape[1]
    out_to[...] = out_ref[...]
    in_to[...] = in_ref[...]
    to_out[...] = mix_ref[:, :hid].T
    for i, r in enumerate(mixes):
        r[...] = mix_ref[:, (i + 1) * hid : (i + 2) * hid]
    beta[...] = mix_ref[:, 5 * hid :].T[:heads]
    ff_gate[...] = ff_ref[:, :wide].T[:ff]
    ff_up[...] = ff_ref[:, wide:].T[:ff]
    ff_down[...] = down_ref[...].T[:ff]


def spread(output, input_grad, mix, ff_sum, down_sum, hid, heads, ff):
    block = mix.shape[0]
    vmem = pl.BlockSpec(memory_space=pltpu.VMEM)
    shapes = [(hid, block)] + [(block, hid)] * 4 + [(heads, block)] + [(ff, block)] * 3
    return pl.pallas_call(
        spread_kernel,
        out_shape=[jax.ShapeDtypeStruct(a.shape, a.dtype) for a in (output, input_grad)]
        + [jax.ShapeDtypeStruct(s, F32) for s in shapes],
        in_specs=[vmem] * 5,
        out_specs=[vmem] * (2 + len(shapes)),
        compiler_params=pltpu.CompilerParams(vmem_limit_bytes=VMEM_LIMIT),
        name="spread",
    )(output, input_grad, mix, ff_sum, down_sum)


def doc_tables(lengths, length):
    count = lengths.shape[0]
    index = jnp.arange(count)
    ends = jnp.sum(jnp.where(index[None, :] <= index[:, None], lengths[None, :], 0), axis=1)
    position = jnp.arange(length, dtype=jnp.int32)
    doc = jnp.sum((position[:, None] >= ends[None, :]).astype(jnp.int32), axis=1)
    no_doc = lambda n: jnp.full((n,), -1, jnp.int32)
    before = [jnp.concatenate([no_doc(o), doc[:-o]]) == doc for o in (1, 2, 3)]
    after = [jnp.concatenate([doc[o:], no_doc(o)]) == doc for o in (1, 2, 3)]
    blocks = doc.reshape(-1, CHUNK)
    ending = blocks[:, -1:]
    prior = jnp.concatenate([no_doc(1)[:, None], ending[:-1]], axis=0)
    enter = (blocks == prior).reshape(-1)
    leave = (blocks == ending).reshape(-1)
    columns = before + [enter, leave] + after + [doc]
    aux = jnp.stack([c.astype(F32) for c in columns], axis=1)
    return aux, doc.astype(F32).reshape(-1, GROUP, CHUNK)


def on_device(
    tokens,
    lengths,
    attn_gain,
    w_query,
    w_key,
    w_value,
    w_beta,
    w_gate_out,
    conv_weight,
    head_gain,
    w_out,
    mlp_gain,
    w_mlp_gate,
    w_mlp_up,
    w_down,
    cotangent,
):
    hid, heads, ff = w_query.shape[1], w_beta.shape[1], w_mlp_gate.shape[1]
    n_dp, n_head = lax.axis_size("dp"), lax.axis_size("head")
    beta_wide = jnp.pad(w_beta, ((0, 0), (0, HEAD_DIM - heads)))
    in_ws = [w_query, w_key, w_value, w_gate_out, beta_wide]
    normed_rows, first_set, cot_early = start(
        tokens, attn_gain[None, :], w_out, in_ws, cotangent, n_dp, n_head
    )
    normed_rows = normed_rows.reshape(-1, normed_rows.shape[2])
    first_set = first_set.reshape(-1, first_set.shape[2])
    wide = -(-ff // 256) * 256
    padded = lambda w: jnp.pad(w, ((0, 0), (0, wide - ff)))
    mine = jnp.concatenate([padded(w_mlp_gate), padded(w_mlp_up)], axis=1)

    length = normed_rows.shape[0]
    aux, docrow = doc_tables(lengths[0], length)
    conv = jnp.swapaxes(conv_weight.astype(F32), 0, 1).reshape(conv_weight.shape[1], 3 * hid)
    gain = head_gain[None, :]
    pre, mixed, *saved, attention, cot_late, ff_set = mixer_fwd(
        normed_rows, first_set, aux, docrow, conv, gain, cotangent, mine, n_dp, n_head
    )
    ff_set = ff_set.reshape(-1, ff_set.shape[2])
    output, hidden_grad, hg_some, mlp_gain_grad, mlp_terms, down_terms = mid(
        attention, tokens, mlp_gain[None, :], cot_early, cot_late, ff_set, padded(w_down.T), n_dp, n_head
    )
    dpre, conv_part, head_gain_grad, mlp_reduced, hg_rows = mixer_bwd(
        hg_some, first_set, aux, docrow, conv, gain, (pre, *saved),
        mlp_terms.reshape(n_dp, -1, mlp_terms.shape[1]),
    )
    taps = conv_part.shape[0]
    shared = 2 * (tokens.shape[1] // 128) + 8
    small = jnp.concatenate(
        [
            jnp.zeros((tokens.shape[1] // 128, 128), F32),
            mlp_gain_grad.reshape(-1, 128),
            jnp.pad(head_gain_grad, ((0, 7), (0, 0))),
            conv_part.reshape(-1, 128),
        ]
    )
    input_grad, mix_reduced, summed, down_reduced = end(
        dpre, first_set, normed_rows, hg_rows, mixed, down_terms.reshape(n_dp, -1, wide), tokens, attn_gain[None, :], hidden_grad, small,
        n_dp, n_head, shared,
    )
    gains = summed[: shared - 8].reshape(2, -1)
    conv_grad = jnp.swapaxes(summed[shared:].reshape(taps, 3, hid), 0, 1)
    spread_out = spread(output, input_grad, mix_reduced, mlp_reduced, down_reduced, hid, heads, ff)
    output, input_grad, to_out, query, key, value, gate, beta, ff_gate, ff_up, ff_down = spread_out
    return (
        output,
        input_grad,
        gains[0],
        query,
        key,
        value,
        beta.T,
        gate,
        conv_grad,
        summed[shared - 8],
        to_out,
        gains[1],
        ff_gate.T,
        ff_up.T,
        ff_down,
    )


def solution(mesh):
    rows = P(("dp", "head"), None)
    in_specs = (
        rows,
        P("dp", None),
        P(),
        P("dp", "head"),
        P("dp", "head"),
        P("dp", "head"),
        P("dp", "head"),
        P("dp", "head"),
        P(None, None, "head"),
        P(),
        P("head", "dp"),
        P(),
        P("dp", "head"),
        P("dp", "head"),
        P("head", "dp"),
        rows,
    )
    out_specs = (
        rows,
        rows,
        P(),
        P("dp", "head"),
        P("dp", "head"),
        P("dp", "head"),
        P("dp", "head"),
        P("dp", "head"),
        P(None, None, "head"),
        P(),
        P("head", "dp"),
        P(),
        P("dp", "head"),
        P("dp", "head"),
        P("head", "dp"),
    )
    return jax.shard_map(
        on_device, mesh=mesh, in_specs=in_specs, out_specs=out_specs, check_vma=False
    )
```

```python
from functools import partial

import jax
import jax.numpy as jnp
from jax import lax
from jax.experimental import pallas as pl
from jax.experimental.pallas import tpu as pltpu
from jax.sharding import PartitionSpec as P

HEAD_DIM = 128
CHUNK = 128
GROUP = 4
STEP = CHUNK * GROUP
PAD = 8
F32 = jnp.float32
BF16 = jnp.bfloat16
COT_PARTS = 2
HG_PARTS = 2
VMEM_LIMIT = 56 * 1024 * 1024


def dot(left, right, dims):
    return lax.dot_general(left, right, (dims, ((), ())), preferred_element_type=F32)


def mul(left, right):
    return dot(left.astype(BF16), right.astype(BF16), ((1,), (0,)))


def mul_t(left, right):
    return dot(left.astype(BF16), right.astype(BF16), ((1,), (1,)))


def t_mul(left, right):
    return dot(left.astype(BF16), right.astype(BF16), ((0,), (0,)))


def unit_inverses(lowers):
    row = lax.broadcasted_iota(jnp.int32, (CHUNK, CHUNK), 0)
    col = lax.broadcasted_iota(jnp.int32, (CHUNK, CHUNK), 1)
    eye = (row == col).astype(F32)
    level = lambda bit: jnp.logical_and(
        (row >> (bit + 1)) == (col >> (bit + 1)), (row >> bit) > (col >> bit)
    )
    first = level(0)
    solved = [eye - jnp.where(first, a, 0.0) for a in lowers]
    for bit in range(1, CHUNK.bit_length() - 1):
        mask = level(bit)
        right = [mul(jnp.where(mask, a, 0.0), t) for a, t in zip(lowers, solved)]
        solved = [t - mul(t, r) for t, r in zip(solved, right)]
    return solved


def conv_parts(pre, ext, conv, aux):
    summed = pre * conv[3:4, :]
    for offset in range(1, 4):
        shifted = ext[PAD - offset : PAD - offset + STEP, :]
        summed = summed + shifted * aux[:, offset - 1 : offset] * conv[3 - offset : 4 - offset, :]
    return summed


def unit_rows(act, scale):
    out = []
    for h in range(act.shape[1] // HEAD_DIM):
        part = act[:, h * HEAD_DIM : (h + 1) * HEAD_DIM]
        inv = lax.rsqrt(jnp.sum(part * part, axis=-1, keepdims=True) + 1e-6)
        out.append((part * inv * scale, inv))
    return out


def chunk_masks(aux, docrow):
    row = lax.broadcasted_iota(jnp.int32, (CHUNK, CHUNK), 0)
    col = lax.broadcasted_iota(jnp.int32, (CHUNK, CHUNK), 1)
    made = []
    for c in range(GROUP):
        same = aux[c * CHUNK : (c + 1) * CHUNK, 8:9] == docrow[c : c + 1, :]
        made.append((jnp.logical_and(same, row > col), jnp.logical_and(same, row >= col)))
    return made


def mixer_fwd_kernel(
    lines, count,
    x_ref, w_ref, aux_ref, docrow_ref, conv_ref, gain_ref, cot_ref, ff_ref,
    pre_ref, mixed_ref, o_ref, t_ref, phi_ref, s_ref, p_ref, d_ref, ew_ref, att_ref, cot_rows, ff_rows,
    ext, state, terms, near, far_terms, near_s, near_r, far_s, far_r, right_s, left_s, over_s, landed, local, *cot_sems,
):
    heads = mixed_ref.shape[1] // HEAD_DIM
    hid = heads * HEAD_DIM
    grid_step, last_step = pl.program_id(0), pl.num_programs(0) - 1
    first, hop_step, arrived, last = shard_line(lines, ff_ref, ff_rows, (right_s, left_s, over_s, landed, local.at[0]))
    cot_half = cot_ref.shape[0] // 2
    cots, held = cot_gather(count, cot_ref.at[pl.ds(cot_half, cot_half)], cot_rows, cot_sems, local.at[1])
    cot_parts = cots.parts

    attend = OwnerScatter(count, att_ref, (terms, near, far_terms, near_s, near_r, far_s, far_r))

    @pl.when(grid_step == 0)
    def _():
        greet(lines, count)
        first()
        held.start()
        for p in range(cot_parts):
            cots.send(p)

    @pl.when(grid_step == 2)
    def _():
        hop_step(0)
        cots.pass_on(0)

    @pl.when(pl.program_id(0) == 0)
    def _():
        ext[0:PAD, :] = jnp.zeros((PAD, 3 * hid), F32)
        state[...] = jnp.zeros_like(state)

    pre_ref[...] = dot(x_ref[...], w_ref[:, hid:], ((1,), (0,)))
    pl.when(grid_step >= 1)(lambda: attend.settle(grid_step - 1))
    aux = aux_ref[...]
    conv = conv_ref[...]
    pre = pre_ref[:, : 3 * hid]
    ext[PAD:, :] = pre
    act = conv_parts(pre, ext, conv, aux)
    act = act * jax.nn.sigmoid(act)
    ext[0:PAD, :] = ext[STEP:, :]
    q = unit_rows(act[:, :hid], HEAD_DIM**-0.5)
    k = unit_rows(act[:, hid : 2 * hid], 1.0)
    beta = jax.nn.sigmoid(pre_ref[:, 4 * hid : 4 * hid + 8])
    masks = chunk_masks(aux, docrow_ref[0])

    items = [(c, h) for c in range(GROUP) for h in range(heads)]
    rows = [slice(c * CHUNK, (c + 1) * CHUNK) for c in range(GROUP)]
    lowers, scores = [], []
    for c, h in items:
        key, query = k[h][0][rows[c]], q[h][0][rows[c]]
        both = mul_t(jnp.concatenate([key, query], axis=0), key)
        lowers.append(jnp.where(masks[c][0], both[:CHUNK] * beta[rows[c], h : h + 1], 0.0))
        scores.append(jnp.where(masks[c][1], both[CHUNK:], 0.0).astype(BF16))
    solved = unit_inverses(lowers)
    parts = []
    for (c, h), inverse, score in zip(items, solved, scores):
        key = k[h][0][rows[c]]
        value = act[rows[c], 2 * hid + h * HEAD_DIM : 2 * hid + (h + 1) * HEAD_DIM]
        b = beta[rows[c], h : h + 1]
        enter, leave = aux[rows[c], 3:4], aux[rows[c], 4:5]
        inverse = inverse.astype(BF16)
        wu = mul(inverse, jnp.concatenate([key * b, value * b], axis=1))
        ew, u = wu[:, :HEAD_DIM] * enter, wu[:, HEAD_DIM:]
        phi_b = t_mul(key * leave, jnp.concatenate([ew, u], axis=1))
        parts.append((ew, u, phi_b[:, :HEAD_DIM].astype(BF16), phi_b[:, HEAD_DIM:]))
        t_ref[c, h] = inverse
        p_ref[c, h] = score
        ew_ref[c, h] = ew.astype(BF16)
        phi_ref[c, h] = parts[-1][2]
    for h in range(heads):
        s = state[h]
        for c in range(GROUP):
            low = s.astype(BF16)
            s_ref[c, h] = low
            _, _, phi, b_term = parts[c * heads + h]
            keep = aux[(c + 1) * CHUNK - 1 : (c + 1) * CHUNK, 3:4]
            s = s * keep - mul(phi, low) + b_term
        state[h] = s
    gain = gain_ref[...]
    for (c, h), (ew, u, _, _), score in zip(items, parts, scores):
        enter = aux[rows[c], 3:4]
        from_state = mul(jnp.concatenate([ew, q[h][0][rows[c]] * enter], axis=0), s_ref[c, h])
        d = (u - from_state[:CHUNK]).astype(BF16)
        d_ref[c, h] = d
        o = from_state[CHUNK:] + mul(score, d)
        cols = slice(h * HEAD_DIM, (h + 1) * HEAD_DIM)
        o_ref[rows[c], cols] = o
        normed = o * lax.rsqrt(jnp.mean(o * o, axis=-1, keepdims=True) + 1e-5) * gain
        gate = pre_ref[rows[c], 3 * hid + h * HEAD_DIM : 3 * hid + (h + 1) * HEAD_DIM]
        mixed_ref[rows[c], cols] = (normed * (gate * jax.nn.sigmoid(gate))).astype(BF16)

    attend.offer(grid_step, dot(mixed_ref[...], w_ref[:, :hid], ((1,), (1,))))

    @pl.when(grid_step == last_step)
    def _():
        attend.settle(grid_step)
        for p in range(1, cot_parts):
            cots.pass_on(p)
        pl.loop(1, lines - 1)(hop_step)
        held.wait()
        for p in range(cot_parts):
            cots.arrive(p)
            cots.sent(p)
        arrived()
        attend.finish()
        last()


def mixer_bwd_kernel(
    lines, steps,
    hg_in, wout_ref, pre_ref, halo_ref, aux_ref, docrow_ref, conv_ref, gain_ref,
    o_ref, t_ref, phi_ref, s_ref, p_ref, d_ref, ew_ref, terms_ref,
    dpre_ref, dconv_ref, dgain_ref, sum_ref, hg_out,
    ext, later, dstate, own, own_s, hg_all, hg_s, *refs,
):
    heads = o_ref.shape[1] // HEAD_DIM
    hid = heads * HEAD_DIM
    grid_step = pl.program_id(0)
    side = lax.axis_index("dp") % 2
    dp_refs, hg_sems = refs[:7], refs[7:]
    me, final = lax.axis_index("head"), hg_all.shape[0] - 1
    hg_parts = hg_sems[1].shape[0]
    hg_size = hg_all.shape[1] // hg_parts
    hg_block = lambda owner, p: hg_all.at[owner, pl.ds(p * hg_size, hg_size)]
    hgs = HeadGather(
        final + 1, hg_parts, lambda p: hg_block(me, p), hg_block, hg_sems, lambda owner: owner != final
    )
    load = lambda owner, i: pltpu.make_async_copy(hg_in.at[owner], hg_all.at[owner], hg_s.at[i])
    order = lambda n: (n // lines, outside_in(lines, n % lines))
    line = LineScatter(lines, lambda j: terms_ref.at[j], lambda place: own.at[place], dp_refs, order)
    fetch = lambda place: pltpu.make_async_copy(terms_ref.at[2 * place + side], own.at[place], own_s.at[place])

    @pl.when(grid_step == 0)
    def _():
        load(final, 0).start()
        pl.when(me != final)(lambda: load(me, 1).start())
        greet_line(lines, final + 1)
        line.offer_all()
        pl.when(me != final)(lambda: load(me, 1).wait())
        for p in range(hg_parts):
            hgs.send(p)
        for place in range(lines):
            fetch(place).start()
        load(final, 0).wait()
        for place in range(lines):
            fetch(place).wait()

    per_step = 5
    base = 3

    def point(i):
        n = grid_step * per_step + i - base
        line.point(n)

    point(0)

    @pl.when(pl.program_id(0) == 0)
    def _():
        later[STEP:, :] = jnp.zeros((PAD, 3 * hid), F32)
        dstate[...] = jnp.zeros_like(dstate)
        dconv_ref[...] = jnp.zeros_like(dconv_ref)
        dgain_ref[...] = jnp.zeros_like(dgain_ref)

    @pl.when(grid_step >= 1)
    def _():
        for p in range(hg_parts):
            hgs.arrive(p, final - grid_step)

    hg_out[...] = hg_all[final - grid_step]
    mixed_grad = dot(hg_out[...], wout_ref[...], ((1,), (0,))).astype(BF16).astype(F32)
    aux = aux_ref[...]
    conv = conv_ref[...]
    pre = pre_ref[:, : 3 * hid]
    ext[0:PAD, :] = halo_ref[:, : 3 * hid]
    ext[PAD:, :] = pre
    lin = conv_parts(pre, ext, conv, aux)
    sig = jax.nn.sigmoid(lin)
    act = lin * sig
    dsilu = sig * (1.0 + lin * (1.0 - sig))
    scale = HEAD_DIM**-0.5
    q = unit_rows(act[:, :hid], 1.0)
    k = unit_rows(act[:, hid : 2 * hid], 1.0)
    beta = jax.nn.sigmoid(pre_ref[:, 4 * hid : 4 * hid + 8])
    masks = chunk_masks(aux, docrow_ref[0])
    gain = gain_ref[...]

    items = [(c, h) for c in range(GROUP) for h in range(heads)]
    rows = [slice(c * CHUNK, (c + 1) * CHUNK) for c in range(GROUP)]
    cols = [slice(h * HEAD_DIM, (h + 1) * HEAD_DIM) for h in range(heads)]

    d_out, d_gain = [], jnp.zeros((1, HEAD_DIM), F32)
    for h in range(heads):
        o = o_ref[:, cols[h]]
        inv = lax.rsqrt(jnp.mean(o * o, axis=-1, keepdims=True) + 1e-5)
        unit = o * inv
        gate = pre_ref[:, 3 * hid + h * HEAD_DIM : 3 * hid + (h + 1) * HEAD_DIM]
        s = jax.nn.sigmoid(gate)
        dm = mixed_grad[:, cols[h]]
        dpre_ref[:, 3 * hid + h * HEAD_DIM : 3 * hid + (h + 1) * HEAD_DIM] = (
            dm * unit * gain * (s * (1.0 + gate * (1.0 - s)))
        ).astype(BF16)
        dn = dm * (gate * s)
        d_gain = d_gain + jnp.sum(dn * unit, axis=0, keepdims=True)
        du = dn * gain
        d_out.append(inv * (du - unit * jnp.mean(du * unit, axis=-1, keepdims=True)))
    dgain_ref[...] += d_gain
    point(1)

    first = []
    for c, h in items:
        enter = aux[rows[c], 3:4]
        do = d_out[h][rows[c]].astype(BF16)
        eq = (q[h][0][rows[c]] * (enter * scale)).astype(BF16)
        x = t_mul(p_ref[c, h], do)
        c_term = t_mul(
            jnp.concatenate([eq, -ew_ref[c, h]], axis=0),
            jnp.concatenate([do, x.astype(BF16)], axis=0),
        )
        first.append((do, x, c_term))
    point(2)
    after = {}
    for h in range(heads):
        ds = dstate[h]
        for c in reversed(range(GROUP)):
            low = ds.astype(BF16)
            after[c, h] = low
            keep = aux[(c + 1) * CHUNK - 1 : (c + 1) * CHUNK, 3:4]
            ds = ds * keep - t_mul(phi_ref[c, h], low) + first[c * heads + h][2]
        dstate[h] = ds
    db_cols = []
    grads = {}
    point(3)
    for (c, h), (do, x, _) in zip(items, first):
        enter, leave = aux[rows[c], 3:4], aux[rows[c], 4:5]
        b = beta[rows[c], h : h + 1]
        key, query = k[h][0][rows[c]], q[h][0][rows[c]] * scale
        value = act[rows[c], 2 * hid + h * HEAD_DIM : 2 * hid + (h + 1) * HEAD_DIM]
        ds = after[c, h]
        d, s = d_ref[c, h], s_ref[c, h]
        dr = t_mul(t_ref[c, h], x + mul(key * leave, ds))
        stacked = jnp.concatenate([do, dr.astype(BF16)], axis=0)
        with_d = mul_t(stacked, d)
        with_s = mul_t(stacked, s) * jnp.concatenate([enter, enter], axis=0)
        dp = jnp.where(masks[c][1], with_d[:CHUNK], 0.0)
        da = jnp.where(masks[c][0], -with_d[CHUNK:], 0.0)
        pair = jnp.concatenate([dp, da], axis=0).astype(BF16)
        with_k = mul(pair, key)
        dq = with_s[:CHUNK] + with_k[:CHUNK]
        row_k = with_k[CHUNK:] - with_s[CHUNK:]
        dk = b * row_k + t_mul(pair, jnp.concatenate([query, key * b], axis=0))
        dk = dk + mul_t(d, ds) * leave
        db = jnp.sum(dr * value + key * row_k, axis=-1, keepdims=True)
        grads[c, h] = (dq * scale, dk, dr * b, db * b * (1.0 - b))
    point(4)
    for h in range(heads):
        whole = [jnp.concatenate([grads[c, h][i] for c in range(GROUP)], axis=0) for i in range(4)]
        for i, unit in ((0, q[h]), (1, k[h])):
            y, inv = unit
            grad = inv * (whole[i] - y * jnp.sum(y * whole[i], axis=-1, keepdims=True))
            at = slice(i * hid + h * HEAD_DIM, i * hid + (h + 1) * HEAD_DIM)
            later[0:STEP, at] = grad * dsilu[:, at]
        at = slice(2 * hid + h * HEAD_DIM, 2 * hid + (h + 1) * HEAD_DIM)
        later[0:STEP, at] = whole[2] * dsilu[:, at]
        db_cols.append(whole[3])
    lane = lax.broadcasted_iota(jnp.int32, (STEP, HEAD_DIM), 1)
    tail = jnp.zeros((STEP, HEAD_DIM), F32)
    for h in range(heads):
        tail = jnp.where(lane == h, db_cols[h], tail)
    dpre_ref[:, 4 * hid :] = tail.astype(BF16)
    dlin = later[0:STEP, :]
    dpre = dlin * conv[3:4, :]
    taps = [jnp.sum(dlin * pre, axis=0, keepdims=True)]
    for offset in range(1, 4):
        ahead = later[offset : offset + STEP, :]
        dpre = dpre + ahead * aux[:, 4 + offset : 5 + offset] * conv[3 - offset : 4 - offset, :]
        behind = ext[PAD - offset : PAD - offset + STEP, :] * aux[:, offset - 1 : offset]
        taps.append(jnp.sum(dlin * behind, axis=0, keepdims=True))
    dpre_ref[:, : 3 * hid] = dpre.astype(BF16)
    for offset in range(4):
        dconv_ref[3 - offset : 4 - offset, :] += taps[offset]
    later[STEP:, :] = later[0:PAD, :]

    @pl.when(grid_step < steps - 1)
    def _():
        for p in range(hg_parts):
            hgs.pass_on(p, final - 1 - grid_step)

    @pl.when(grid_step == steps - 1)
    def _():
        for p in range(hg_parts):
            hgs.sent(p)
        pl.loop(max(steps * per_step - base, 0), line.points)(line.point)
        line.finish(sum_ref)
        line.close()


def mixer_fwd(x_rows, weights, aux, docrow, conv, gain, cotangent, ff_mine, n_dp, count):
    hid = conv.shape[1] // 3
    length, width = x_rows.shape[0], weights.shape[1] - hid
    heads, chunks = hid // HEAD_DIM, length // CHUNK
    lines, dma = n_dp // 2, lambda *shape: pltpu.SemaphoreType.DMA(shape)
    anywhere = pl.BlockSpec(memory_space=pl.ANY)
    rows = lambda n: pl.BlockSpec((STEP, n), lambda i: (i, 0))
    whole = lambda a: pl.BlockSpec(a.shape, lambda i: (0,) * a.ndim)
    square = pl.BlockSpec((GROUP, heads, CHUNK, HEAD_DIM), lambda i: (i, 0, 0, 0))
    squares = jax.ShapeDtypeStruct((chunks, heads, CHUNK, HEAD_DIM), BF16)
    return pl.pallas_call(
        partial(mixer_fwd_kernel, lines, count),
        grid=(length // STEP,),
        in_specs=[
            rows(x_rows.shape[1]), whole(weights), rows(aux.shape[1]),
            pl.BlockSpec((1, GROUP, CHUNK), lambda i: (i, 0, 0)), whole(conv), whole(gain),
            whole(cotangent), whole(ff_mine),
        ],
        out_specs=[rows(width), rows(hid), rows(hid)]
        + [square] * 6
        + [pl.BlockSpec((STEP, x_rows.shape[1]), lambda i: (0, 0))]
        + [anywhere] * 2,
        out_shape=[
            jax.ShapeDtypeStruct((length, width), F32),
            jax.ShapeDtypeStruct((length, hid), BF16),
            jax.ShapeDtypeStruct((length, hid), F32),
        ]
        + [squares] * 6
        + [
            jax.ShapeDtypeStruct((STEP, x_rows.shape[1]), F32),
            jax.ShapeDtypeStruct((count, cotangent.shape[0] // 2, cotangent.shape[1]), BF16),
            jax.ShapeDtypeStruct((n_dp, *ff_mine.shape), BF16),
        ],
        scratch_shapes=[
            pltpu.VMEM((PAD + STEP, 3 * hid), F32),
            pltpu.VMEM((heads, HEAD_DIM, HEAD_DIM), F32),
        ]
        + OwnerScatter.scratch(count, STEP, x_rows.shape[1])
        + [
            dma(lines), dma(lines), dma(lines), dma(n_dp), dma(2),
        ]
        + HeadGather.scratch(count, COT_PARTS),
        compiler_params=pltpu.CompilerParams(vmem_limit_bytes=VMEM_LIMIT, has_side_effects=True, collective_id=3),
        name="mixer_fwd",
    )(x_rows, weights, aux, docrow, conv, gain, cotangent, ff_mine)


def mixer_bwd(hg_rows, weights, aux, docrow, conv, gain, saved, terms):
    pre, o, t, phi, s, p, d, ew = saved
    length, width = pre.shape
    hid = conv.shape[1] // 3
    heads, steps = hid // HEAD_DIM, length // STEP
    last = steps - 1
    n_dp, block, wide = terms.shape
    lines = n_dp // 2
    rows = lambda n: pl.BlockSpec((STEP, n), lambda i: (last - i, 0))
    whole = lambda a: pl.BlockSpec(a.shape, lambda i: (0,) * a.ndim)
    square = pl.BlockSpec((GROUP, heads, CHUNK, HEAD_DIM), lambda i: (last - i, 0, 0, 0))
    halo = pl.BlockSpec(
        (PAD, width), lambda i: (jnp.maximum((last - i) * (STEP // PAD) - 1, 0), 0)
    )
    return pl.pallas_call(
        partial(mixer_bwd_kernel, lines, steps),
        grid=(steps,),
        in_specs=[
            pl.BlockSpec(memory_space=pl.ANY), pl.BlockSpec((weights.shape[0], hid), lambda i: (0, 0)), rows(width), halo, rows(aux.shape[1]),
            pl.BlockSpec((1, GROUP, CHUNK), lambda i: (last - i, 0, 0)), whole(conv), whole(gain),
            rows(hid),
        ]
        + [square] * 6
        + [pl.BlockSpec(memory_space=pl.ANY)],
        out_specs=[
            rows(width),
            pl.BlockSpec((4, 3 * hid), lambda i: (0, 0)),
            pl.BlockSpec((1, HEAD_DIM), lambda i: (0, 0)),
            pl.BlockSpec((block, wide), lambda i: (0, 0)),
            rows(weights.shape[0]),
        ],
        out_shape=[
            jax.ShapeDtypeStruct((length, width), BF16),
            jax.ShapeDtypeStruct((4, 3 * hid), F32),
            jax.ShapeDtypeStruct((1, HEAD_DIM), F32),
            jax.ShapeDtypeStruct((block, wide), F32),
            jax.ShapeDtypeStruct((length, weights.shape[0]), BF16),
        ],
        scratch_shapes=[
            pltpu.VMEM((PAD + STEP, 3 * hid), F32),
            pltpu.VMEM((STEP + PAD, 3 * hid), F32),
            pltpu.VMEM((heads, HEAD_DIM, HEAD_DIM), F32),
            pltpu.VMEM((lines, block, wide), BF16),
            pltpu.SemaphoreType.DMA((lines,)),
            pltpu.VMEM(hg_rows.shape, BF16),
            pltpu.SemaphoreType.DMA((2,)),
        ]
        + LineScatter.scratch(lines, block, wide)
        + HeadGather.scratch(hg_rows.shape[0], HG_PARTS),
        compiler_params=pltpu.CompilerParams(vmem_limit_bytes=VMEM_LIMIT, has_side_effects=True, collective_id=4),
        name="mixer_bwd",
    )(hg_rows, weights, pre, pre, aux, docrow, conv, gain, o, t, phi, s, p, d, ew, terms)


MESH = pl.DeviceIdType.MESH


def remote(src, dst, sent, landed, axis, to):
    return pltpu.make_async_remote_copy(
        src_ref=src, dst_ref=dst, send_sem=sent, recv_sem=landed,
        device_id={axis: to}, device_id_type=MESH,
    )


def shard_line(lines, own, out, sems):
    right_s, left_s, over_s, landed, local = sems
    me = lax.axis_index("dp")
    spot, side = me // 2, me % 2
    slot = lambda place: 2 * place + side
    across = me + 1 - 2 * side

    def hop(step, where):
        return (spot - step, me + 2, right_s) if where == 0 else (spot + step, me - 2, left_s)

    def going(step, where):
        place, to, sent = hop(step, where)
        src = out.at[slot(place)] if not isinstance(step, int) or step else own
        return remote(src, out.at[slot(place)], sent.at[step], landed.at[slot(place)], "dp", to)

    def goes(step, where):
        if where == 0:
            return jnp.logical_and(spot - step >= 0, spot + 1 < lines)
        return jnp.logical_and(spot + step < lines, spot >= 1)

    def over(place):
        return remote(out.at[slot(place)], out.at[slot(place)], over_s.at[place], landed.at[slot(place)], "dp", across)

    def first():
        pltpu.make_async_copy(own, out.at[me], local).start()
        remote(own, out.at[me], over_s.at[spot], landed.at[me], "dp", across).start()
        for where in (0, 1):
            pl.when(goes(0, where))(lambda where=where: going(0, where).start())

    def arrive(step, place):
        @pl.when(jnp.logical_and(place >= 0, place < lines))
        def _():
            over(place).wait_recv()
            over(place).start()

    def hop_step(step):
        for where in (0, 1):
            place = spot - step - 1 if where == 0 else spot + step + 1
            arrive(step, place)
            if isinstance(step, int) and step + 1 >= lines - 1:
                continue
            pl.when(jnp.logical_and(goes(step + 1, where), step + 1 < lines - 1))(
                lambda where=where: going(step + 1, where).start()
            )

    def arrived():
        pltpu.make_async_copy(own, out.at[me], local).wait()

        @pl.loop(0, lines)
        def _(place):
            there = 2 * place + 1 - side
            remote(out.at[there], out.at[there], over_s.at[place], landed.at[there], "dp", across).wait_recv()

    def last():
        pl.loop(0, lines)(lambda place: over(place).wait_send())

        @pl.loop(0, lines - 1)
        def _(step):
            for where in (0, 1):
                pl.when(goes(step, where))(lambda where=where: going(step, where).wait_send())

    return first, hop_step, arrived, last


def greet(lines, count):
    barrier = pltpu.get_barrier_semaphore()
    me = lax.axis_index("dp")
    spot, across = me // 2, me + 1 - 2 * (me % 2)

    def tell(axis, to):
        pl.semaphore_signal(barrier, 1, device_id={axis: to}, device_id_type=MESH)

    tell("dp", across)
    pl.when(spot >= 1)(lambda: tell("dp", me - 2))
    pl.when(spot + 1 < lines)(lambda: tell("dp", me + 2))
    head = lax.axis_index("head")
    tell("head", head + 1 - 2 * (head % 2))
    for f in range(1, count // 2):
        tell("head", lax.rem(head + 2 * f, count))
    beside = jnp.minimum(spot, 1) + jnp.minimum(lines - 1 - spot, 1)
    pl.semaphore_wait(barrier, 1 + count // 2 + beside)


def greet_line(lines, count):
    barrier = pltpu.get_barrier_semaphore()
    head = lax.axis_index("head")
    for to in [head + 1 - 2 * (head % 2)] + [lax.rem(head + hop, count) for hop in range(2, count, 2)]:
        pl.semaphore_signal(barrier, 1, device_id={"head": to}, device_id_type=MESH)
    me = lax.axis_index("dp")

    def tell(to):
        pl.semaphore_signal(barrier, 1, device_id={"dp": to}, device_id_type=MESH)

    tell(me + 1 - 2 * (me % 2))
    pl.loop(1, lines)(lambda hop: tell(lax.rem(me + 2 * hop, 2 * lines)))
    pl.semaphore_wait(barrier, lines + count // 2)


def wide_transpose(rows, width):
    rest = jnp.zeros((width - rows.shape[0], rows.shape[1]), F32)
    return jnp.concatenate([rows.astype(F32), rest], axis=0).T.astype(BF16)


def cot_gather(count, cot_ref, cot_rows, sems, held_s):
    parts = sems[1].shape[0]
    size = cot_ref.shape[0] // parts
    at = lambda p: pl.ds(p * size, size)
    me = lax.axis_index("head")
    cots = HeadGather(count, parts, lambda p: cot_ref.at[at(p)], lambda owner, p: cot_rows.at[owner, at(p)], sems)
    return cots, pltpu.make_async_copy(cot_ref, cot_rows.at[me], held_s)


def start_kernel(lines, count, parts, tok_ref, gain_ref, out_w, *refs):
    *in_ws, cot_ref, rows_ref, wall_ref, cot_rows, mine, w_ref = refs[:11]
    start_body(
        lines, count, parts, tok_ref, gain_ref, out_w, in_ws, cot_ref, rows_ref, wall_ref, cot_rows, mine, w_ref, *refs[11:]
    )


def start_body(lines, count, parts, tok_ref, gain_ref, out_w, in_ws, cot_ref, rows_ref, wall_ref, cot_rows, mine, w_ref,
               right_s, left_s, over_s, landed, local, far_s, pair_s, fwd_s, got, keep_s, *cot_sems):
    first, hop_step, arrived, last = shard_line(lines, w_ref, wall_ref, (right_s, left_s, over_s, landed, local.at[0]))
    at = out_w.shape[0]
    w_ref[:, :at] = out_w[...].T
    for w in in_ws[:-1]:
        w_ref[:, at : at + w.shape[1]] = w[...]
        at += w.shape[1]
    w_ref[:, at:] = wide_transpose(in_ws[-1][...], HEAD_DIM)
    greet(lines, count)
    first()
    me = lax.axis_index("head")
    pair = me + 1 - 2 * (me % 2)
    fars = [lax.rem(me + 2 * f, count) for f in range(1, count // 2)]
    size = tok_ref.shape[0] // parts
    span = lambda p: pl.ds(p * size, size)

    def block(owner, p):
        return rows_ref.at[owner, span(p)]

    for p in range(parts):
        x = tok_ref[p * size : (p + 1) * size, :].astype(F32)
        inv = lax.rsqrt(jnp.mean(x * x, axis=-1, keepdims=True) + 1e-6)
        mine[p * size : (p + 1) * size, :] = (x * inv * gain_ref[...]).astype(BF16)
        for f, far in enumerate(fars):
            remote(mine.at[span(p)], block(me, p), far_s.at[f, p], got.at[me, p], "head", far).start()
        remote(mine.at[span(p)], block(me, p), pair_s.at[p], got.at[me, p], "head", pair).start()
        pltpu.make_async_copy(mine.at[span(p)], block(me, p), keep_s.at[p]).start()

    cot_half = cot_ref.shape[0] // 2
    cots, held = cot_gather(count, cot_ref.at[pl.ds(0, cot_half)], cot_rows, cot_sems, local.at[1])
    held.start()
    for p in range(cots.parts):
        cots.send(p)

    def pass_on(p):
        for f, far in enumerate(fars):
            moved = remote(block(far, p), block(far, p), fwd_s.at[f, p], got.at[far, p], "head", pair)
            moved.wait_recv()
            moved.start()

    for i in range(parts):
        pass_on(i)
        if i < lines - 1:
            hop_step(i)
    if lines - 1 > parts:
        pl.loop(parts, lines - 1)(hop_step)
    for p in range(cots.parts):
        cots.pass_on(p)
    arrived()
    last()
    held.wait()
    for p in range(cots.parts):
        cots.arrive(p)
        cots.sent(p)
    for p in range(parts):
        remote(mine.at[span(p)], block(pair, p), pair_s.at[p], got.at[pair, p], "head", pair).wait()
        pltpu.make_async_copy(mine.at[span(p)], block(me, p), keep_s.at[p]).wait()
        for f, far in enumerate(fars):
            remote(mine.at[span(p)], block(me, p), far_s.at[f, p], got.at[me, p], "head", far).wait_send()
            there = lax.rem(pair + 2 * (f + 1), count)
            remote(block(far, p), block(there, p), fwd_s.at[f, p], got.at[there, p], "head", pair).wait()


def start(tokens, gain, w_out, in_ws, cot, n_dp, n_head, parts=4):
    rows, width = tokens.shape
    shard = (in_ws[0].shape[0], w_out.shape[0] + sum(w.shape[1] for w in in_ws[:-1]) + HEAD_DIM)
    lines, far = n_dp // 2, n_head // 2 - 1
    dma = lambda *shape: pltpu.SemaphoreType.DMA(shape)
    anywhere = pl.BlockSpec(memory_space=pl.ANY)
    vmem = pl.BlockSpec(memory_space=pltpu.VMEM)
    return pl.pallas_call(
        partial(start_kernel, lines, n_head, parts),
        out_shape=[jax.ShapeDtypeStruct((n_head, rows, width), BF16),
                   jax.ShapeDtypeStruct((n_dp, *shard), BF16),
                   jax.ShapeDtypeStruct((n_head, cot.shape[0] // 2, cot.shape[1]), BF16)],
        in_specs=[vmem] * (4 + len(in_ws)),
        out_specs=[anywhere] * 3,
        scratch_shapes=[
            pltpu.VMEM((rows, width), BF16),
            pltpu.VMEM(shard, BF16),
            dma(lines), dma(lines), dma(lines), dma(n_dp), dma(2),
            dma(far, parts), dma(parts), dma(far, parts), dma(n_head, parts), dma(parts),
        ]
        + HeadGather.scratch(n_head, COT_PARTS),
        compiler_params=pltpu.CompilerParams(vmem_limit_bytes=VMEM_LIMIT, has_side_effects=True, collective_id=0),
        name="start",
    )(tokens, gain, w_out, *in_ws, cot)


def when(condition):
    return pl.when(condition) if not isinstance(condition, bool) else (lambda f: f() if condition else None)


class HeadScatter:
    def __init__(self, count, refs):
        self.count = count
        (self.out, self.near, self.onward, self.far, self.own,
         self.out_s, self.near_r, self.onward_s, self.far_r) = refs
        self.me = lax.axis_index("head")
        self.side, self.place = self.me % 2, self.me // 2
        self.pair = self.me + 1 - 2 * self.side
        self.parts, self.depth, self.size = self.near.shape[0], self.own.shape[0], self.own.shape[1]

    @staticmethod
    def scratch(count, parts, size, width, depth):
        half = count // 2
        return [
            pltpu.VMEM((2, 2, half, size, width), BF16),
            pltpu.VMEM((parts, half, size, width), BF16),
            pltpu.VMEM((2, half - 1, size, width), BF16),
            pltpu.VMEM((parts, half - 1, size, width), BF16),
            pltpu.VMEM((depth, size, width), F32),
            pltpu.SemaphoreType.DMA((2,)),
            pltpu.SemaphoreType.DMA((parts,)),
            pltpu.SemaphoreType.DMA((2, half - 1)),
            pltpu.SemaphoreType.DMA((parts, half - 1)),
        ]

    def _near(self, p):
        slot = p % 2
        return remote(self.out.at[slot, 1 - self.side], self.near.at[p], self.out_s.at[slot], self.near_r.at[p], "head", self.pair)

    def _far(self, p, f):
        slot = p % 2
        to = lax.rem(self.me + 2 * (f + 1), self.count)
        return remote(self.onward.at[slot, f], self.far.at[p, f], self.onward_s.at[slot, f], self.far_r.at[p, f], "head", to)

    def offer(self, p, total):
        when(p >= 2)(lambda: self._near(p - 2).wait_send())
        for owner in range(self.count):
            self.out[p % 2, owner % 2, owner // 2] = total[owner * self.size : (owner + 1) * self.size].astype(BF16)
        self._near(p).start()

    def turn(self, p):
        slot, half = p % 2, self.count // 2
        self._near(p).wait_recv()
        both = lambda i: self.out[slot, self.side, i].astype(F32) + self.near[p, i].astype(F32)
        for f in range(half - 1):
            when(p >= 2)(lambda f=f: self._far(p - 2, f).wait_send())
            self.onward[slot, f] = both(lax.rem(self.place + f + 1, half)).astype(BF16)
            self._far(p, f).start()
        self.own[p % self.depth] = both(self.place)

    def take(self, p):
        total = self.own[p % self.depth]
        for f in range(self.count // 2 - 1):
            self._far(p, f).wait_recv()
            total = total + self.far[p, f].astype(F32)
        return total

    def close(self):
        for p in range(max(self.parts - 2, 0), self.parts):
            self._near(p).wait_send()
            for f in range(self.count // 2 - 1):
                self._far(p, f).wait_send()


class OwnerScatter:
    def __init__(self, count, out_ref, refs):
        self.count, self.out_ref = count, out_ref
        self.terms, self.near, self.far, self.near_s, self.near_r, self.far_s, self.far_r = refs
        self.me = lax.axis_index("head")
        self.side = self.me % 2
        self.pair = self.me + 1 - 2 * self.side

    @staticmethod
    def scratch(count, rows, width):
        half = count // 2
        sems = lambda n: pltpu.SemaphoreType.DMA((n,))
        return [
            pltpu.VMEM((count, rows, width), BF16),
            pltpu.VMEM((half, rows, width), BF16),
            pltpu.VMEM((half - 1, rows, width), BF16),
            sems(half), sems(half), sems(count), sems(half - 1),
        ]

    def _near(self, owner):
        at = owner // 2
        return remote(self.terms.at[owner], self.near.at[at], self.near_s.at[at], self.near_r.at[at], "head", self.pair)

    def _far(self, owner):
        at = lax.rem(self.me - owner + self.count, self.count) // 2 - 1
        return remote(self.terms.at[owner], self.far.at[at], self.far_s.at[owner], self.far_r.at[at], "head", owner)

    def _mine(self, owner):
        return owner % 2 == self.side

    def offer(self, owner, total):
        self.terms[owner] = total.astype(BF16)
        pl.when(jnp.logical_not(self._mine(owner)))(lambda: self._near(owner).start())

    def settle(self, owner):
        @pl.when(self._mine(owner))
        def _():
            self._near(owner).wait_recv()
            both = self.terms[owner].astype(F32) + self.near[owner // 2].astype(F32)

            @pl.when(owner == self.me)
            def _():
                self.out_ref[...] = both

            @pl.when(owner != self.me)
            def _():
                self.terms[owner] = both.astype(BF16)
                self._far(owner).start()

    def finish(self):
        for f in range(self.count // 2 - 1):
            sender = lax.rem(self.me + 2 * (f + 1), self.count)
            remote(self.terms.at[0], self.far.at[f], self.far_s.at[0], self.far_r.at[f], "head", sender).wait_recv()
            self.out_ref[...] += self.far[f].astype(F32)

        @pl.loop(0, self.count)
        def _(owner):
            pl.when(jnp.logical_not(self._mine(owner)))(lambda: self._near(owner).wait_send())
            pl.when(jnp.logical_and(self._mine(owner), owner != self.me))(lambda: self._far(owner).wait_send())


class HeadGather:
    def __init__(self, count, parts, own, block, refs, takes=None):
        self.count, self.parts, self.own, self.block, self.takes = count, parts, own, block, takes
        self.far_s, self.pair_s, self.fwd_s, self.got = refs
        self.me = lax.axis_index("head")
        self.pair = self.me + 1 - 2 * (self.me % 2)

    @staticmethod
    def scratch(count, parts):
        far = count // 2 - 1
        return [pltpu.SemaphoreType.DMA(s) for s in ((far, parts), (parts,), (far, parts), (count, parts))]

    def _if(self, owner, action):
        pl.when(self.takes(owner))(action) if self.takes else action()

    def _fars(self, base):
        return [(f, lax.rem(base + 2 * (f + 1), self.count)) for f in range(self.count // 2 - 1)]

    def _far(self, p, f, far):
        return remote(self.own(p), self.block(self.me, p), self.far_s.at[f, p], self.got.at[self.me, p], "head", far)

    def _pair(self, p):
        return remote(self.own(p), self.block(self.me, p), self.pair_s.at[p], self.got.at[self.me, p], "head", self.pair)

    def _on(self, p, f, owner):
        return remote(self.block(owner, p), self.block(owner, p), self.fwd_s.at[f, p], self.got.at[owner, p], "head", self.pair)

    def send(self, p):
        def act():
            for f, far in self._fars(self.me):
                self._far(p, f, far).start()
            self._pair(p).start()

        self._if(self.me, act)

    def pass_on(self, p, ready=None):
        for f, far in self._fars(self.me):

            def act(f=f, far=far):
                self._on(p, f, far).wait_recv()
                self._on(p, f, far).start()

            pl.when(far == ready)(act) if ready is not None else self._if(far, act)

    def arrive(self, p, ready=None):
        def near():
            remote(self.own(p), self.block(self.pair, p), self.pair_s.at[p], self.got.at[self.pair, p], "head", self.pair).wait_recv()

        pl.when(self.pair == ready)(near) if ready is not None else self._if(self.pair, near)
        for f, far in self._fars(self.pair):
            act = lambda f=f, far=far: self._on(p, f, far).wait_recv()
            pl.when(far == ready)(act) if ready is not None else self._if(far, act)

    def sent(self, p):
        def mine():
            self._pair(p).wait_send()
            for f, far in self._fars(self.me):
                self._far(p, f, far).wait_send()

        self._if(self.me, mine)
        for f, far in self._fars(self.me):
            self._if(far, lambda f=f, far=far: self._on(p, f, far).wait_send())


LEAD = 8


def mid_kernel(lines, count, parts, att_ref, tok_ref, gain_ref, cot_early, cot_late, ff_ref, down_in,
               out_ref, grad_ref, hg_ref, gain_grad_ref, terms_ref, down_terms_ref, *scratch):
    scratch = list(scratch)
    take = lambda n: [scratch.pop(0) for _ in range(n)]
    down_refs, back_refs = take(9), take(9)
    second_sems, hg_sems = take(4), take(4)
    down_mine, cot_ref, second, hidden, hg_own, total, loads, keep_s, down_all, right_s, left_s, over_s, landed = scratch
    size, width = tok_ref.shape[1:]
    ff = ff_ref.shape[1] // 2
    me = lax.axis_index("head")
    down_mine[...] = wide_transpose(down_in[...], ff)
    greet(lines, count)
    first, hop_step, arrived, last = shard_line(
        lines, down_mine, down_all, (right_s, left_s, over_s, landed, loads.at[1])
    )
    first()
    half = parts // 2
    loading = [
        pltpu.make_async_copy(src, cot_ref.at[:, at : at + half], loads.at[i])
        for i, (src, at) in ((0, (cot_early, 0)), (2, (cot_late, half)))
    ]
    for m in loading:
        m.start()
    down_w = lambda: down_all[...].reshape(-1, ff)
    down, back = (HeadScatter(count, r) for r in (down_refs, back_refs))
    here = lambda owner, p: second.at[p, owner]
    seconds = HeadGather(count, parts, lambda p: here(me, p), here, second_sems)
    there = lambda owner, p: hg_ref.at[owner, p]
    hgs = HeadGather(count, parts, lambda p: hg_own.at[p], there, hg_sems, lambda owner: owner == count - 1)
    keep = lambda p: pltpu.make_async_copy(hg_own.at[p], there(me, p), keep_s.at[p])
    total[...] = jnp.zeros_like(total)
    gain_grad_ref[...] = jnp.zeros_like(gain_grad_ref)

    def within(p, stage):
        pl.when(jnp.logical_and(p >= 0, p < parts))(lambda: stage(p))

    def norm(p):
        rows = tok_ref[p].astype(F32) + att_ref[p]
        hidden[p] = rows
        inv = lax.rsqrt(jnp.mean(rows * rows, axis=-1, keepdims=True) + 1e-6)
        second[p, me] = (rows * inv * gain_ref[...]).astype(BF16)
        seconds.send(p)

    def feed(p):
        seconds.arrive(p)
        rows = second[p].reshape(count * size, width)
        both = dot(rows, ff_ref[...], ((1,), (0,)))
        gate, up = both[:, :ff], both[:, ff:]
        sig = jax.nn.sigmoid(gate)
        act = gate * sig
        middle = (act * up).astype(BF16)

        @pl.when(p == 0)
        def _():
            hop_step(0)
            pl.loop(1, lines - 1)(hop_step)
            arrived()

        down.offer(p, dot(middle, down_w(), ((1,), (1,))))
        cot = cot_ref[:, p].reshape(count * size, width)
        grad = dot(cot, down_w(), ((1,), (0,))).astype(BF16).astype(F32)
        pair = jnp.concatenate(
            [(grad * up * sig * (1.0 + gate * (1.0 - sig))).astype(BF16), (grad * act).astype(BF16)], axis=1
        )
        back.offer(p, dot(pair, ff_ref[...], ((1,), (1,))))
        total[:, : 2 * ff] += dot(rows, pair, ((0,), (0,)))
        total[:, 2 * ff :] += dot(cot, middle, ((0,), (0,)))

    def turn(p):
        down.turn(p)
        back.turn(p)

    def finish(p):
        rows = hidden[p]
        out_ref[p] = (rows + down.take(p)).astype(BF16)
        second_grad = back.take(p).astype(BF16).astype(F32)
        inv = lax.rsqrt(jnp.mean(rows * rows, axis=-1, keepdims=True) + 1e-6)
        scaled = second_grad * gain_ref[...]
        mean = jnp.mean(scaled * rows, axis=-1, keepdims=True)
        grad = cot_ref[me, p].astype(F32) + inv * scaled - rows * (inv * inv * inv * mean)
        grad_ref[p] = grad
        gain_grad_ref[...] += jnp.sum(second_grad * rows * inv, axis=0, keepdims=True)
        hg_own[p] = grad.astype(BF16)
        hgs.send(p)
        keep(p).start()

    for p in range(LEAD):
        norm(p)
    for m in loading:
        m.wait()

    @pl.loop(0, parts + 2)
    def _(step):
        within(step + LEAD, norm)
        within(step, seconds.pass_on)
        within(step, feed)
        within(step, turn)
        within(step - 1, finish)
        within(step - 2, hgs.pass_on)

    terms_ref[...] = total[:, : 2 * ff].astype(BF16)
    down_terms_ref[...] = total[:, 2 * ff :].astype(BF16)

    @pl.loop(0, parts)
    def _(p):
        hgs.arrive(p)
        keep(p).wait()
        hgs.sent(p)
        seconds.sent(p)

    for s in (down, back):
        s.close()
    last()


def mid(attention, tokens, gain, cot_early, cot_late, ff_set, down_w, n_dp, count, parts=8):
    rows, width = tokens.shape
    lines, ff = n_dp // 2, ff_set.shape[1] // 2
    block = down_w.shape[1]
    dma = lambda *shape: pltpu.SemaphoreType.DMA(shape)
    size = rows // parts
    anywhere = pl.BlockSpec(memory_space=pl.ANY)
    vmem = pl.BlockSpec(memory_space=pltpu.VMEM)
    scatter = HeadScatter.scratch(count, parts, size, width, 2)
    out, grad, hg, gain_grad, terms, down_terms = pl.pallas_call(
        partial(mid_kernel, lines, count, parts),
        out_shape=[
            jax.ShapeDtypeStruct((parts, size, width), BF16),
            jax.ShapeDtypeStruct((parts, size, width), F32),
            jax.ShapeDtypeStruct((count, parts, size, width), BF16),
            jax.ShapeDtypeStruct((1, width), F32),
            jax.ShapeDtypeStruct((width, 2 * ff), BF16),
            jax.ShapeDtypeStruct((width, ff), BF16),
        ],
        in_specs=[vmem] * 3 + [anywhere] * 2 + [vmem] * 2,
        out_specs=[vmem, vmem, anywhere, vmem, vmem, vmem],
        scratch_shapes=scatter * 2
        + HeadGather.scratch(count, parts) * 2
        + [
            pltpu.VMEM((block, ff), BF16),
            pltpu.VMEM((count, parts, size, width), BF16),
            pltpu.VMEM((parts, count, size, width), BF16),
            pltpu.VMEM((parts, size, width), F32),
            pltpu.VMEM((parts, size, width), BF16),
            pltpu.VMEM((width, 3 * ff), F32),
            dma(3),
            dma(parts),
            pltpu.VMEM((n_dp, block, ff), BF16),
            dma(lines), dma(lines), dma(lines), dma(n_dp),
        ],
        compiler_params=pltpu.CompilerParams(vmem_limit_bytes=61 * 1024 * 1024, has_side_effects=True, collective_id=2),
        name="mid",
    )(
        attention.reshape(parts, size, width), tokens.reshape(parts, size, width), gain,
        *(c.reshape(count, parts // 2, size, width) for c in (cot_early, cot_late)), ff_set, down_w,
    )
    return out.reshape(rows, width), grad.reshape(rows, width), hg.reshape(count, rows, width), gain_grad, terms, down_terms


class ChainScatter:
    LAG = 2

    def __init__(self, lines, terms, own, refs, by_piece):
        self.lines, self.terms, self.own, self.by_piece = lines, terms, own, by_piece
        self.cross, self.going, self.coming, self.cross_s, self.cross_r, self.go_s, self.come_r = refs
        self.pieces = self.cross_s.shape[1]
        self.size = self.cross.shape[1] // self.pieces
        self.me = lax.axis_index("dp")
        self.spot, self.side = self.me // 2, self.me % 2
        self.across = self.me + 1 - 2 * self.side
        self.items = (lines - 1) * self.pieces
        self.points = self.items + (lines - 1) * self.LAG

    @staticmethod
    def scratch(lines, rows, width):
        pieces = max(1, rows // 32)
        wide = lambda *lead: pltpu.VMEM((*lead, rows, width), BF16)
        sems = lambda *shape: pltpu.SemaphoreType.DMA((*shape, pieces))
        return [
            wide(lines), wide(2, lines), wide(2, lines),
            sems(lines), sems(lines), sems(2, lines), sems(2, lines),
        ]

    def _at(self, k):
        return pl.ds(pl.multiple_of(k * self.size, self.size), self.size)

    def _cross(self, place, k):
        at = self._at(k)
        src = self.terms(2 * place + 1 - self.side).at[at]
        return remote(src, self.cross.at[place, at], self.cross_s.at[place, k], self.cross_r.at[place, k], "dp", self.across)

    def _line(self, way, dest, k):
        to = self.me + 2 if way == 0 else self.me - 2
        at = self._at(k)
        return remote(self.going.at[way, dest, at], self.coming.at[way, dest, at], self.go_s.at[way, dest, k], self.come_r.at[way, dest, k], "dp", to)

    def offer(self, place, k):
        self._cross(place, k).start()

    def offer_all(self):
        for k in range(self.pieces):
            for d in range((self.lines + 1) // 2):
                for place in sorted({self.lines - 1 - d, d}, reverse=True):
                    self.offer(place, k)

    def _both(self, place, k):
        return self.own(place)[self._at(k), :].astype(F32) + self.cross[place, self._at(k), :].astype(F32)

    def _passes(self, way, dest):
        return dest > self.spot if way == 0 else dest < self.spot

    def _fed(self, way):
        return self.spot >= 1 if way == 0 else self.spot + 1 < self.lines

    def point(self, n):
        for way in (0, 1):
            away = self.spot if way == 0 else self.lines - 1 - self.spot
            item = n - away * self.LAG
            safe = jnp.clip(item, 0, self.items - 1)
            if self.by_piece:
                k, d = safe // (self.lines - 1), safe % (self.lines - 1)
            else:
                d, k = safe // self.pieces, safe % self.pieces
            dest = self.lines - 1 - d if way == 0 else d
            live = jnp.logical_and(item >= 0, item < self.items)

            @pl.when(jnp.logical_and(live, self._passes(way, dest)))
            def _(way=way, dest=dest, k=k):
                at = self._at(k)
                self._cross(dest, k).wait_recv()

                @pl.when(self._fed(way))
                def _():
                    self._line(way, dest, k).wait_recv()
                    self.going[way, dest, at, :] = (self._both(dest, k) + self.coming[way, dest, at, :].astype(F32)).astype(BF16)

                @pl.when(jnp.logical_not(self._fed(way)))
                def _():
                    self.going[way, dest, at, :] = self._both(dest, k).astype(BF16)

                self._line(way, dest, k).start()

    def finish(self, out_ref):
        for k in range(self.pieces):
            at = slice(k * self.size, (k + 1) * self.size)
            self._cross(self.spot, k).wait_recv()
            out_ref[at, :] = self._both(self.spot, k)
            for way in (0, 1):
                @pl.when(self._fed(way))
                def _(way=way, k=k, at=at):
                    self._line(way, self.spot, k).wait_recv()
                    out_ref[at, :] += self.coming[way, self.spot, at, :].astype(F32)

    def close(self):
        @pl.loop(0, self.lines * self.pieces)
        def _(i):
            place, k = i // self.pieces, i % self.pieces
            self._cross(place, k).wait_send()
            for way in (0, 1):
                pl.when(self._passes(way, place))(lambda way=way: self._line(way, place, k).wait_send())


class LineScatter:
    def __init__(self, lines, terms, own, refs, order):
        self.lines, self.terms, self.own, self.order = lines, terms, own, order
        self.cross, self.going, self.coming, self.cross_s, self.cross_r, self.go_s, self.come_r = refs
        self.pieces = self.cross_s.shape[1]
        self.size = self.cross.shape[1] // self.pieces
        self.me = lax.axis_index("dp")
        self.spot, self.side = self.me // 2, self.me % 2
        self.across = self.me + 1 - 2 * self.side
        self.points = lines * self.pieces

    @staticmethod
    def scratch(lines, rows, width):
        pieces = max(1, rows // 32)
        wide = pltpu.VMEM((lines, rows, width), BF16)
        sems = pltpu.SemaphoreType.DMA((lines, pieces))
        return [wide, wide, wide, sems, sems, sems, sems]

    def _at(self, k):
        return pl.ds(pl.multiple_of(k * self.size, self.size), self.size)

    def _cross(self, place, k):
        at = self._at(k)
        src = self.terms(2 * place + 1 - self.side).at[at]
        return remote(src, self.cross.at[place, at], self.cross_s.at[place, k], self.cross_r.at[place, k], "dp", self.across)

    def _on(self, sender, dest, k):
        at = self._at(k)
        return remote(self.going.at[dest, at], self.coming.at[sender, at], self.go_s.at[dest, k], self.come_r.at[sender, k], "dp", 2 * dest + self.side)

    def offer(self, place, k):
        self._cross(place, k).start()

    def offer_all(self):
        @pl.loop(0, self.points)
        def _(n):
            k, place = self.order(n)
            self.offer(place, k)

    def _both(self, place, k):
        return self.own(place)[self._at(k), :].astype(F32) + self.cross[place, self._at(k), :].astype(F32)

    def point(self, n):
        k, dest = self.order(jnp.clip(n, 0, self.points - 1))

        @pl.when(jnp.logical_and(jnp.logical_and(n >= 0, n < self.points), dest != self.spot))
        def _():
            self._cross(dest, k).wait_recv()
            self.going[dest, self._at(k), :] = self._both(dest, k).astype(BF16)
            self._on(self.spot, dest, k).start()

    def finish(self, out_ref):
        for k in range(self.pieces):
            at = slice(k * self.size, (k + 1) * self.size)
            self._cross(self.spot, k).wait_recv()
            out_ref[at, :] = self._both(self.spot, k)

            @pl.loop(1, self.lines)
            def _(hop, k=k, at=at):
                sender = lax.rem(self.spot + hop, self.lines)
                self._on(sender, self.spot, k).wait_recv()
                out_ref[at, :] += self.coming[sender, at, :].astype(F32)

    def close(self):
        @pl.loop(0, self.points)
        def _(i):
            place, k = i // self.pieces, i % self.pieces
            self._cross(place, k).wait_send()
            pl.when(place != self.spot)(lambda: self._on(self.spot, place, k).wait_send())


def outside_in(lines, i):
    return jnp.where(i % 2 == 0, lines - 1 - i // 2, i // 2)


class SmallSum:
    def __init__(self, n_dp, count, shared, refs):
        self.n_dp, self.count, self.shared = n_dp, count, shared
        self.mine, self.theirs, self.half, self.halves, self.a_s, self.a_r, self.b_s, self.b_r = refs
        self.dp, self.head = lax.axis_index("dp"), lax.axis_index("head")

    @staticmethod
    def scratch(n_dp, count, rows, shared):
        return [
            pltpu.VMEM((rows, 128), F32),
            pltpu.VMEM((n_dp, rows, 128), F32),
            pltpu.VMEM((shared, 128), F32),
            pltpu.VMEM((count, shared, 128), F32),
            pltpu.SemaphoreType.DMA((n_dp,)),
            pltpu.SemaphoreType.DMA((n_dp,)),
            pltpu.SemaphoreType.DMA((count,)),
            pltpu.SemaphoreType.DMA((count,)),
        ]

    def _a(self, hop):
        to = lax.rem(self.dp + hop, self.n_dp)
        return remote(self.mine, self.theirs.at[self.dp], self.a_s.at[hop], self.a_r.at[self.dp], "dp", to)

    def _b(self, hop):
        to = lax.rem(self.head + hop, self.count)
        return remote(self.half, self.halves.at[self.head], self.b_s.at[hop], self.b_r.at[self.head], "head", to)

    def start(self):
        self.theirs[self.dp] = self.mine[...]

        @pl.loop(1, self.n_dp)
        def _(hop):
            self._a(hop).start()

    def turn(self, out_ref):
        @pl.loop(1, self.n_dp)
        def _(hop):
            sender = lax.rem(self.dp + self.n_dp - hop, self.n_dp)
            remote(self.mine, self.theirs.at[sender], self.a_s.at[hop], self.a_r.at[sender], "dp", sender).wait_recv()

        total = self.theirs[0]
        for i in range(1, self.n_dp):
            total = total + self.theirs[i]
        out_ref[...] = total
        self.half[...] = total[: self.shared]
        self.halves[self.head] = total[: self.shared]
        for hop in range(1, self.count):
            self._b(hop).start()

    def finish(self, out_ref):
        for hop in range(1, self.count):
            sender = lax.rem(self.head + self.count - hop, self.count)
            remote(self.half, self.halves.at[sender], self.b_s.at[hop], self.b_r.at[sender], "head", sender).wait_recv()
        total = self.halves[0]
        for i in range(1, self.count):
            total = total + self.halves[i]
        out_ref[: self.shared, :] = total

        @pl.loop(1, self.n_dp)
        def _(hop):
            self._a(hop).wait_send()

        for hop in range(1, self.count):
            self._b(hop).wait_send()


def greet_all(n_dp, count):
    barrier = pltpu.get_barrier_semaphore()
    dp, head = lax.axis_index("dp"), lax.axis_index("head")

    @pl.loop(1, n_dp)
    def _(hop):
        pl.semaphore_signal(barrier, 1, device_id={"dp": lax.rem(dp + hop, n_dp)}, device_id_type=MESH)

    for hop in range(1, count):
        pl.semaphore_signal(barrier, 1, device_id={"head": lax.rem(head + hop, count)}, device_id_type=MESH)
    pl.semaphore_wait(barrier, n_dp + count - 2)


def end_kernel(n_dp, count, parts, shared,
               dpre_ref, w_ref, normed_ref, hg_ref, mixed_ref, down_ref, tok_ref, gain_ref, grad_ref, small_ref,
               in_ref, mix_ref, sum_ref, down_sum_ref, *scratch):
    scratch = list(scratch)
    take = lambda n: [scratch.pop(0) for _ in range(n)]
    head_refs, dp_refs, down_refs, small_refs = take(9), take(7), take(7), take(8)
    terms, dpre, w, normed, hg, mixed, down_own, loads, down_s = scratch
    rows, width = tok_ref.shape
    block = terms.shape[1]
    hid = mixed.shape[1]
    greet_all(n_dp, count)
    lines = n_dp // 2
    side = lax.axis_index("dp") % 2
    down = ChainScatter(lines, lambda j: down_ref.at[j], lambda place: down_own.at[place], down_refs, True)
    fetch = lambda place: pltpu.make_async_copy(down_ref.at[2 * place + side], down_own.at[place], down_s.at[place])
    moves = [pltpu.make_async_copy(s, d, loads.at[i]) for i, (s, d) in enumerate(
        ((dpre_ref, dpre), (w_ref.at[:, hid:], w), (normed_ref, normed), (mixed_ref, mixed), (hg_ref, hg)))]
    for m in moves:
        m.start()
    down.offer_all()
    for place in range(lines):
        fetch(place).start()
    heads = HeadScatter(count, head_refs)
    line = ChainScatter(lines, lambda j: terms.at[j], lambda place: terms.at[2 * place + side], dp_refs, False)
    small = SmallSum(n_dp, count, shared, small_refs)
    size = rows // parts

    def offer(p):
        part = jnp.concatenate([dpre[o * rows + p * size : o * rows + (p + 1) * size, :] for o in range(count)], axis=0)
        heads.offer(p, dot(part, w[...], ((1,), (1,))))

    tiles = width // 256
    per = 256 // block

    def outer(t):
        cols = slice(t * 256, (t + 1) * 256)
        left = dot(normed[:, cols], dpre[...], ((0,), (0,))).astype(BF16)
        right = dot(hg[:, cols], mixed[...], ((0,), (0,))).astype(BF16)
        for b in range(per):
            terms[t * per + b, :, :hid] = right[b * block : (b + 1) * block]
            terms[t * per + b, :, hid:] = left[b * block : (b + 1) * block]
        for place in range(t * per // 2, (t + 1) * per // 2):
            for k in range(line.pieces):
                line.offer(place, k)

    order = [t // 2 if t % 2 else tiles - 1 - t // 2 for t in range(tiles)]
    moves[0].wait()
    moves[1].wait()
    offer(0)
    for m in moves[2:]:
        m.wait()
    for place in range(lines):
        fetch(place).wait()
    down_done = 0
    for i in range(max(tiles, parts)):
        if i < tiles:
            outer(order[i])
        if i < parts:
            heads.turn(i)
        if i + 1 < parts:
            offer(i + 1)
        for n in range(4):
            if down_done < down.points:
                down.point(down_done)
                down_done += 1
    pl.loop(down_done, down.points)(down.point)
    small.mine[...] = small_ref[...]
    gain_total = jnp.zeros((1, width), F32)
    gain = gain_ref[...]

    def finish(p):
        at = slice(p * size, (p + 1) * size)
        normed_grad = heads.take(p).astype(BF16).astype(F32)
        x = tok_ref[at, :].astype(F32)
        inv = lax.rsqrt(jnp.mean(x * x, axis=-1, keepdims=True) + 1e-6)
        scaled = normed_grad * gain
        mean = jnp.mean(scaled * x, axis=-1, keepdims=True)
        in_ref[at, :] = grad_ref[at, :] + inv * scaled - x * (inv * inv * inv * mean)
        return jnp.sum(normed_grad * x * inv, axis=0, keepdims=True)

    done = 0
    for i in range(parts):
        for n in range(2):
            if done < line.points:
                line.point(done)
                done += 1
        gain_total = gain_total + finish(i)
    for i in range(width // 128):
        small.mine[i : i + 1, :] = gain_total[:, i * 128 : (i + 1) * 128]
    small.start()
    half = (done + line.points) // 2
    pl.loop(done, half)(line.point)
    small.turn(sum_ref)
    pl.loop(half, line.points)(line.point)
    line.finish(mix_ref)
    down.finish(down_sum_ref)
    small.finish(sum_ref)
    down.close()
    heads.close()
    line.close()


def end(dpre, weights, normed_rows, hg_rows, mixed, down_terms, tokens, gain, hidden_grad, small, n_dp, count, shared, parts=4):
    rows, width = tokens.shape
    block = width // n_dp
    wide = weights.shape[1]
    anywhere = pl.BlockSpec(memory_space=pl.ANY)
    vmem = pl.BlockSpec(memory_space=pltpu.VMEM)
    like = lambda a: pltpu.VMEM(a.shape, a.dtype)
    return pl.pallas_call(
        partial(end_kernel, n_dp, count, parts, shared),
        out_shape=[
            jax.ShapeDtypeStruct((rows, width), F32),
            jax.ShapeDtypeStruct((block, wide), F32),
            jax.ShapeDtypeStruct(small.shape, F32),
            jax.ShapeDtypeStruct(down_terms.shape[1:], F32),
        ],
        in_specs=[anywhere] * 6 + [vmem] * 4,
        out_specs=[vmem] * 4,
        scratch_shapes=HeadScatter.scratch(count, parts, rows // parts, width, parts)
        + ChainScatter.scratch(n_dp // 2, block, wide)
        + ChainScatter.scratch(n_dp // 2, block, down_terms.shape[2])
        + SmallSum.scratch(n_dp, count, small.shape[0], shared)
        + [pltpu.VMEM((n_dp, block, wide), BF16), like(dpre), pltpu.VMEM((width, dpre.shape[1]), BF16), like(normed_rows), like(hg_rows), like(mixed),
           pltpu.VMEM((n_dp // 2, *down_terms.shape[1:]), BF16),
           pltpu.SemaphoreType.DMA((5,)), pltpu.SemaphoreType.DMA((n_dp // 2,))],
        compiler_params=pltpu.CompilerParams(vmem_limit_bytes=VMEM_LIMIT, has_side_effects=True, collective_id=1),
        name="end",
    )(dpre, weights, normed_rows, hg_rows, mixed, down_terms, tokens, gain, hidden_grad, small)


def spread_kernel(out_ref, in_ref, mix_ref, ff_ref, down_ref, out_to, in_to, *results):
    to_out, *mixes, beta, ff_gate, ff_up, ff_down = results
    hid, heads, ff = to_out.shape[0], beta.shape[0], ff_gate.shape[0]
    wide = down_ref.shape[1]
    out_to[...] = out_ref[...]
    in_to[...] = in_ref[...]
    to_out[...] = mix_ref[:, :hid].T
    for i, r in enumerate(mixes):
        r[...] = mix_ref[:, (i + 1) * hid : (i + 2) * hid]
    beta[...] = mix_ref[:, 5 * hid :].T[:heads]
    ff_gate[...] = ff_ref[:, :wide].T[:ff]
    ff_up[...] = ff_ref[:, wide:].T[:ff]
    ff_down[...] = down_ref[...].T[:ff]


def spread(output, input_grad, mix, ff_sum, down_sum, hid, heads, ff):
    block = mix.shape[0]
    vmem = pl.BlockSpec(memory_space=pltpu.VMEM)
    shapes = [(hid, block)] + [(block, hid)] * 4 + [(heads, block)] + [(ff, block)] * 3
    return pl.pallas_call(
        spread_kernel,
        out_shape=[jax.ShapeDtypeStruct(a.shape, a.dtype) for a in (output, input_grad)]
        + [jax.ShapeDtypeStruct(s, F32) for s in shapes],
        in_specs=[vmem] * 5,
        out_specs=[vmem] * (2 + len(shapes)),
        compiler_params=pltpu.CompilerParams(vmem_limit_bytes=VMEM_LIMIT),
        name="spread",
    )(output, input_grad, mix, ff_sum, down_sum)


def doc_tables(lengths, length):
    count = lengths.shape[0]
    index = jnp.arange(count)
    ends = jnp.sum(jnp.where(index[None, :] <= index[:, None], lengths[None, :], 0), axis=1)
    position = jnp.arange(length, dtype=jnp.int32)
    doc = jnp.sum((position[:, None] >= ends[None, :]).astype(jnp.int32), axis=1)
    no_doc = lambda n: jnp.full((n,), -1, jnp.int32)
    before = [jnp.concatenate([no_doc(o), doc[:-o]]) == doc for o in (1, 2, 3)]
    after = [jnp.concatenate([doc[o:], no_doc(o)]) == doc for o in (1, 2, 3)]
    blocks = doc.reshape(-1, CHUNK)
    ending = blocks[:, -1:]
    prior = jnp.concatenate([no_doc(1)[:, None], ending[:-1]], axis=0)
    enter = (blocks == prior).reshape(-1)
    leave = (blocks == ending).reshape(-1)
    columns = before + [enter, leave] + after + [doc]
    aux = jnp.stack([c.astype(F32) for c in columns], axis=1)
    return aux, doc.astype(F32).reshape(-1, GROUP, CHUNK)


def on_device(
    tokens,
    lengths,
    attn_gain,
    w_query,
    w_key,
    w_value,
    w_beta,
    w_gate_out,
    conv_weight,
    head_gain,
    w_out,
    mlp_gain,
    w_mlp_gate,
    w_mlp_up,
    w_down,
    cotangent,
):
    hid, heads, ff = w_query.shape[1], w_beta.shape[1], w_mlp_gate.shape[1]
    n_dp, n_head = lax.axis_size("dp"), lax.axis_size("head")
    in_ws = [w_query, w_key, w_value, w_gate_out, w_beta.T]
    normed_rows, first_set, cot_early = start(
        tokens, attn_gain[None, :], w_out, in_ws, cotangent, n_dp, n_head
    )
    normed_rows = normed_rows.reshape(-1, normed_rows.shape[2])
    first_set = first_set.reshape(-1, first_set.shape[2])
    wide = -(-ff // 256) * 256
    padded = lambda w: jnp.pad(w, ((0, 0), (0, wide - ff)))
    mine = jnp.concatenate([padded(w_mlp_gate), padded(w_mlp_up)], axis=1)

    length = normed_rows.shape[0]
    aux, docrow = doc_tables(lengths[0], length)
    conv = jnp.swapaxes(conv_weight.astype(F32), 0, 1).reshape(conv_weight.shape[1], 3 * hid)
    gain = head_gain[None, :]
    pre, mixed, *saved, attention, cot_late, ff_set = mixer_fwd(
        normed_rows, first_set, aux, docrow, conv, gain, cotangent, mine, n_dp, n_head
    )
    ff_set = ff_set.reshape(-1, ff_set.shape[2])
    output, hidden_grad, hg_some, mlp_gain_grad, mlp_terms, down_terms = mid(
        attention, tokens, mlp_gain[None, :], cot_early, cot_late, ff_set, w_down, n_dp, n_head
    )
    dpre, conv_part, head_gain_grad, mlp_reduced, hg_rows = mixer_bwd(
        hg_some, first_set, aux, docrow, conv, gain, (pre, *saved),
        mlp_terms.reshape(n_dp, -1, mlp_terms.shape[1]),
    )
    taps = conv_part.shape[0]
    shared = 2 * (tokens.shape[1] // 128) + 8
    small = jnp.concatenate(
        [
            jnp.zeros((tokens.shape[1] // 128, 128), F32),
            mlp_gain_grad.reshape(-1, 128),
            jnp.pad(head_gain_grad, ((0, 7), (0, 0))),
            conv_part.reshape(-1, 128),
        ]
    )
    input_grad, mix_reduced, summed, down_reduced = end(
        dpre, first_set, normed_rows, hg_rows, mixed, down_terms.reshape(n_dp, -1, wide), tokens, attn_gain[None, :], hidden_grad, small,
        n_dp, n_head, shared,
    )
    gains = summed[: shared - 8].reshape(2, -1)
    conv_grad = jnp.swapaxes(summed[shared:].reshape(taps, 3, hid), 0, 1)
    spread_out = spread(output, input_grad, mix_reduced, mlp_reduced, down_reduced, hid, heads, ff)
    output, input_grad, to_out, query, key, value, gate, beta, ff_gate, ff_up, ff_down = spread_out
    return (
        output,
        input_grad,
        gains[0],
        query,
        key,
        value,
        beta.T,
        gate,
        conv_grad,
        summed[shared - 8],
        to_out,
        gains[1],
        ff_gate.T,
        ff_up.T,
        ff_down,
    )


def solution(mesh):
    rows = P(("dp", "head"), None)
    in_specs = (
        rows,
        P("dp", None),
        P(),
        P("dp", "head"),
        P("dp", "head"),
        P("dp", "head"),
        P("dp", "head"),
        P("dp", "head"),
        P(None, None, "head"),
        P(),
        P("head", "dp"),
        P(),
        P("dp", "head"),
        P("dp", "head"),
        P("head", "dp"),
        rows,
    )
    out_specs = (
        rows,
        rows,
        P(),
        P("dp", "head"),
        P("dp", "head"),
        P("dp", "head"),
        P("dp", "head"),
        P("dp", "head"),
        P(None, None, "head"),
        P(),
        P("head", "dp"),
        P(),
        P("dp", "head"),
        P("dp", "head"),
        P("head", "dp"),
    )
    return jax.shard_map(
        on_device, mesh=mesh, in_specs=in_specs, out_specs=out_specs, check_vma=False
    )
```
